32 devices in a mesh: gx: 2 (over x), gy: 4 (over y, core), gz: 4 (over z).
Axes of the slice: x: 2, y: 2, z: 4, core: 2. Of those that a mesh axis runs over, the one named last changes fastest.
Arguments:
- state: bfloat16 [32, 64, 8, 8, 128], P('gx', 'gy', 'gz'), may hold values from -6 to 6
- cotangent: bfloat16 [32, 64, 8, 8, 128], P('gx', 'gy', 'gz'), may hold values from -6 to 6
- counts: int32 [4], P('gz'), may hold values from 1 to 2, 6 in all
- edge_weights: bfloat16 [2, 2, 128, 128], replicated, may hold values from -0.5 to 0.5
- node_in: bfloat16 [2, 256, 128], replicated, may hold values from -0.375 to 0.375
- node_out: bfloat16 [2, 128, 128], replicated, may hold values from -0.5 to 0.5
- biases: float32 [2, 2, 128], replicated, may hold values from -4 to 4
Outputs:
- state_grad: bfloat16 [32, 64, 8, 8, 128], P('gx', 'gy', 'gz')
- edge_grads: float32 [2, 2, 128, 128], replicated
- node_in_grad: float32 [2, 256, 128], replicated
- node_out_grad: float32 [2, 128, 128], replicated
- bias_grads: float32 [2, 2, 128], replicated
The draws below stay inside these ranges and needn't reach their ends.
Inputs may be any that keep to these rules, and one draw needn't show every extreme that they name: The counts sum to 6; index k of gz holds the element layers that follow those of smaller indices.
All inputs are finite; a program needn't handle non-finite values. No bound on the sum of `counts` on one device may be relied on, other than what follows from the above.
Results may differ from the reference program's by a relative error of at most 0.012.
The reference program's roundings to bfloat16 on the way count: a program that leaves them out, or rounds other values in their place, can miss the bound.
Values sent between devices are 32-bit elements; how exact they have to be, the bound alone decides.
No kernel may reach another device: no remote copies, remote signals or barrier semaphores. Data moves between devices by JAX's collectives and lax.ppermute only.
A program may use at most 128 MiB of HBM per device.

```python
import math
import jax
import jax.numpy as jnp
import numpy as np
from jax import lax

H = 128
NODE = 8
EB = 2
LZ = 2
LAYERS_ALL = 6
NODES_ALL = 98304
N_GX = 2
N_GY = 4
N_GZ = 4


def block_levels(rng, extent, pieces, least, largest):
    def one(axis_at, parts):
        draws = jax.random.uniform(jax.random.fold_in(jax.random.fold_in(rng, 6), axis_at), (parts,), jnp.float32, least / len(pieces), largest / len(pieces))
        return jnp.repeat(jnp.exp(draws), extent[axis_at] // parts).reshape((-1,) + (1,) * (len(extent) - axis_at - 1))

    gain = one(*pieces[0])
    for cut in pieces[1:]:
        gain = gain * one(*cut)
    return gain


def length_profile(amount, total, limit, slope):
    loads = [(1 << 20) // math.isqrt(standing ** slope) + 1 for standing in range(2, amount + 1)]
    rest, given = total - limit - (amount - 1), [1] * (amount - 1)
    while rest > 0:
        free = [i for i in range(amount - 1) if given[i] < limit]
        mass, remaining = sum([loads[i] for i in free]), rest
        for i in free:
            addition = min(limit - given[i], max(1, remaining * loads[i] // mass), rest)
            given[i] = given[i] + addition
            rest = rest - addition
    return np.array([limit] + given)


def ragged_sizes(stream_key, count, total, limit, skew):
    if count == 2:
        one = jax.random.randint(stream_key, (), max(1, total - limit), min(limit, total - 1) + 1)
        return jnp.stack([one, total - one])
    sizes = jnp.asarray(length_profile(count, total, limit, skew), jnp.int32)
    pairs = (count - 1) // 2
    giver, sink = sizes[1:1 + 2 * pairs:2], sizes[2:2 + 2 * pairs:2]
    margin = jnp.minimum(giver - 1, limit - sink)
    moved = jax.random.randint(jax.random.fold_in(stream_key, 1), (pairs,), 0, 1 << 20) % (margin + 1)
    sizes = sizes.at[1:1 + 2 * pairs:2].set(giver - moved).at[2:2 + 2 * pairs:2].set(sink + moved)
    return sizes[jax.random.permutation(jax.random.fold_in(stream_key, 2), count)]


def gaussian(rng, shape, width, bound, cuts=(), kind=jnp.bfloat16):
    values = width * jax.random.normal(rng, shape, jnp.float32)
    if cuts:
        values = values * block_levels(rng, shape, cuts, -0.22, 0.18)
    return jnp.clip(values, -bound, bound).astype(kind)


def setup_inputs(seed: int = 0) -> dict:
    arg_keys = jax.random.split(jax.random.key(seed), 8)
    return {
        "state": gaussian(arg_keys[0], (NODE * EB * N_GX, NODE * EB * N_GY, LZ * N_GZ, NODE, H), 1.0, 6.0, ((0, 2), (1, 4), (2, 4))),
        "cotangent": gaussian(arg_keys[1], (NODE * EB * N_GX, NODE * EB * N_GY, LZ * N_GZ, NODE, H), 1.0, 6.0, ((0, 2), (1, 4), (2, 4))),
        "counts": ragged_sizes(arg_keys[2], N_GZ, LAYERS_ALL, LZ, 2).astype(jnp.int32),
        "edge_weights": gaussian(arg_keys[3], (2, 2, H, H), H ** -0.5, 0.5),
        "node_in": gaussian(arg_keys[4], (2, 2 * H, H), (2 * H) ** -0.5, 0.375),
        "node_out": gaussian(arg_keys[5], (2, H, H), H ** -0.5, 0.5),
        "biases": gaussian(arg_keys[6], (2, 2, H), 1.0, 4.0, (), jnp.float32),
    }


edge_dims = (1, 3, 5)

def slice_along(array, start, stop, dim_no):
    return lax.slice_in_dim(array, start, stop, axis=dim_no)

def matmul_rows(left, weight):
    flattened = left.reshape(-1, left.shape[-1])
    product = jnp.dot(flattened, weight, preferred_element_type=jnp.float32)
    return product.reshape(left.shape[:-1] + (weight.shape[-1],))

def cross_rows(left, right):
    return lax.dot_general(left.reshape(-1, left.shape[-1]), right.reshape(-1, right.shape[-1]), (((0,), (0,)), ((), ())), preferred_element_type=jnp.float32)

def spread_diff(values, dim_no):
    zero_row = jnp.zeros_like(slice_along(values, 0, 1, dim_no))
    return jnp.concatenate([zero_row, values], dim_no) - jnp.concatenate([values, zero_row], dim_no)

def silu_slope(values):
    sig_value = jax.nn.sigmoid(values)
    return sig_value * (1.0 + values * (1.0 - sig_value))

def edges_forward(features, weight_one, weight_two, bias_edge):
    widened = features.astype(jnp.float32)
    messages = jnp.zeros(features.shape, jnp.float32)
    stored = []
    for dim_no in edge_dims:
        length = features.shape[dim_no]
        differ = (slice_along(widened, 1, length, dim_no) - slice_along(widened, 0, length - 1, dim_no)).astype(jnp.bfloat16)
        before = matmul_rows(differ, weight_one) + bias_edge
        active = jax.nn.silu(before).astype(jnp.bfloat16)
        messages = messages + spread_diff(matmul_rows(active, weight_two), dim_no)
        stored.append((differ, before, active))
    return (messages, stored)

def edges_backward(grad_msg, stored, weight_one, weight_two):
    feat_width = grad_msg.shape[-1]
    grad_feat = jnp.zeros(grad_msg.shape, jnp.float32)
    grad_one = jnp.zeros((feat_width, feat_width), jnp.float32)
    grad_two = jnp.zeros((feat_width, feat_width), jnp.float32)
    grad_bias = jnp.zeros((feat_width,), jnp.float32)
    for dim_no, entry in zip(edge_dims, stored):
        differ, before, active = entry
        length = grad_msg.shape[dim_no]
        grad_out = (slice_along(grad_msg, 1, length, dim_no) - slice_along(grad_msg, 0, length - 1, dim_no)).astype(jnp.bfloat16)
        grad_two = grad_two + cross_rows(active, grad_out)
        grad_pre = (matmul_rows(grad_out, weight_two.T) * silu_slope(before)).astype(jnp.bfloat16)
        grad_one = grad_one + cross_rows(differ, grad_pre)
        grad_bias = grad_bias + lax.optimization_barrier(jnp.sum(grad_pre.astype(jnp.float32).reshape(-1, feat_width), 0))
        grad_feat = grad_feat + spread_diff(matmul_rows(grad_pre, weight_one.T), dim_no)
    return (grad_feat, grad_one, grad_two, grad_bias)

def node_forward(features, summed, weight_in, weight_out, bias_node):
    joined = jnp.concatenate([features, summed.astype(jnp.bfloat16)], -1)
    before = matmul_rows(joined, weight_in) + bias_node
    active = jax.nn.silu(before).astype(jnp.bfloat16)
    result = (features.astype(jnp.float32) + matmul_rows(active, weight_out)).astype(jnp.bfloat16)
    return (result, (joined, before, active))

def node_backward(grad_next, stored, weight_in, weight_out):
    joined, before, active = stored
    feat_width = grad_next.shape[-1]
    grad_out_w = cross_rows(active, grad_next)
    grad_pre = (matmul_rows(grad_next, weight_out.T) * silu_slope(before)).astype(jnp.bfloat16)
    grad_in_w = cross_rows(joined, grad_pre)
    grad_bias = lax.optimization_barrier(jnp.sum(grad_pre.astype(jnp.float32).reshape(-1, feat_width), 0))
    grad_joined = matmul_rows(grad_pre, weight_in.T)
    grad_feat = grad_next.astype(jnp.float32) + grad_joined[..., :feat_width]
    return (grad_feat, grad_joined[..., feat_width:], grad_in_w, grad_out_w, grad_bias)

def couple(array, elem_dim, node_dim):
    moved = jnp.moveaxis(array, (elem_dim, node_dim), (0, 1))
    front_face = moved[:, 0]
    back_face = moved[:, -1]
    zero_face = jnp.zeros_like(front_face[:1])
    new_front = front_face + jnp.concatenate([zero_face, back_face[:-1]], 0)
    new_back = back_face + jnp.concatenate([front_face[1:], zero_face], 0)
    joined = jnp.concatenate([new_front[:, None], moved[:, 1:-1], new_back[:, None]], 1)
    return jnp.moveaxis(joined, (0, 1), (elem_dim, node_dim))

def couple_all(array):
    full_shape = array.shape
    along_x = couple(array.reshape((N_GX * EB, NODE) + full_shape[1:]), 0, 1).reshape(full_shape)
    along_y = couple(along_x.reshape(full_shape[:1] + (N_GY * EB, NODE) + full_shape[2:]), 1, 2).reshape(full_shape)
    return couple(along_y, 2, 3)

def reference(state, cotangent, counts, edge_weights, node_in, node_out, biases):
    layer_total = LAYERS_ALL
    slot_place = jnp.arange(N_GZ * LZ, dtype=jnp.int32)
    owner_dev = slot_place // LZ
    within = slot_place % LZ
    starts = (jnp.cumsum(counts) - counts).astype(jnp.int32)
    target = jnp.where(within < counts[owner_dev], starts[owner_dev] + within, layer_total).astype(jnp.int32)

    def compact(array):
        holder = jnp.zeros(array.shape[:2] + (layer_total + 1,) + array.shape[3:], array.dtype)
        return holder.at[:, :, target].set(array)[:, :, :layer_total]

    def expand(array):
        padded = jnp.concatenate([array, jnp.zeros_like(array[:, :, :1])], 2)
        return padded[:, :, target]
    features = compact(state)
    grad_next = compact(cotangent)
    grid_shape = features.shape[:4]

    def to_cells(array):
        return array.reshape((N_GX * EB, NODE, N_GY * EB, NODE, layer_total, NODE, array.shape[-1]))

    def to_grid(array):
        return array.reshape(grid_shape + (array.shape[-1],))
    copies = couple_all(jnp.ones(grid_shape + (1,), jnp.float32))
    saved = []
    for layer_no in range(2):
        messages, edge_store = edges_forward(to_cells(features), edge_weights[layer_no, 0], edge_weights[layer_no, 1], biases[layer_no, 0])
        summed = couple_all(to_grid(messages)) / copies
        result, node_store = node_forward(features, summed, node_in[layer_no], node_out[layer_no], biases[layer_no, 1])
        saved.append((edge_store, node_store))
        features = result
    per_layer = [None, None]
    for layer_no in (1, 0):
        edge_store, node_store = saved[layer_no]
        grad_feat, grad_sum, grad_in_w, grad_out_w, grad_node_b = node_backward(grad_next, node_store, node_in[layer_no], node_out[layer_no])
        grad_msg = couple_all(grad_sum / copies)
        grad_edge, grad_one, grad_two, grad_edge_b = edges_backward(to_cells(grad_msg), edge_store, edge_weights[layer_no, 0], edge_weights[layer_no, 1])
        grad_next = (grad_feat + to_grid(grad_edge)).astype(jnp.bfloat16)
        per_layer[layer_no] = (jnp.stack([grad_one, grad_two]), grad_in_w, grad_out_w, jnp.stack([grad_edge_b, grad_node_b]))
    grad_scale = 1.0 / math.sqrt(NODES_ALL)
    edge_grads = jnp.stack([per_layer[0][0], per_layer[1][0]]) * grad_scale
    node_in_grad = jnp.stack([per_layer[0][1], per_layer[1][1]]) * grad_scale
    node_out_grad = jnp.stack([per_layer[0][2], per_layer[1][2]]) * grad_scale
    bias_grads = jnp.stack([per_layer[0][3], per_layer[1][3]]) * grad_scale
    return (expand(grad_next), edge_grads, node_in_grad, node_out_grad, bias_grads)
```

```python
import functools
import math

import jax
import jax.numpy as jnp
from jax import lax
from jax.experimental import pallas as pl
from jax.experimental.pallas import tpu as pltpu
from jax.sharding import PartitionSpec as P

f32 = jnp.float32
bf16 = jnp.bfloat16
NODES = 8
VM = pl.BlockSpec(memory_space=pltpu.VMEM)
SM = pl.BlockSpec(memory_space=pltpu.SMEM)


def dot(left, right):
    return lax.dot_general(left, right, (((1,), (0,)), ((), ())), preferred_element_type=f32)


def dot_t(left, right):
    return lax.dot_general(left, right, (((0,), (0,)), ((), ())), preferred_element_type=f32)


def silu_half(half):
    th = jnp.tanh(half)
    prod = half * th
    return half + prod, (0.5 + 0.5 * th) * ((1.0 + half) - prod)


def split_cols(value):
    high = value.astype(bf16)
    low = (value - high.astype(f32)).astype(bf16)
    return jnp.concatenate([high, low], -1)


def up(value):
    return pltpu.roll(value, NODES - 1, 1)


def down(value):
    return pltpu.roll(value, 1, 1)


def flat(value):
    return value.reshape(-1, value.shape[-1])


def node_rows(value):
    return value.reshape(-1, NODES, value.shape[-1])


def row_ids():
    return lax.broadcasted_iota(jnp.int32, (1, NODES, 128), 1)


def couple_slots(plane, filled):
    count, rows, width = plane.shape
    slots = rows // NODES
    parts = plane.reshape(count, slots, NODES, width)
    ids = row_ids()
    done = []
    for s in range(slots):
        here = parts[:, s]
        if s + 1 < slots:
            take = (ids == NODES - 1) & (s + 1 < filled)
            here = here + jnp.where(take, up(parts[:, s + 1]), 0.0)
        if s > 0:
            here = here + jnp.where(ids == 0, down(parts[:, s - 1]), 0.0)
            here = jnp.where(s < filled, here, 0.0)
        done.append(here[:, None])
    return jnp.concatenate(done, 1).reshape(plane.shape)


def elements(x_len, y_len, body):
    ey = y_len // NODES
    total = (x_len // NODES) * ey

    def step(e, carry):
        x0 = pl.multiple_of((e // ey) * NODES, NODES)
        y0 = pl.multiple_of((e % ey) * NODES, NODES)
        body(x0, y0)
        return carry

    lax.fori_loop(0, total, step, 0)


def edges_forward(h_ref, w_one, half_bias, filled, sum_ref, slope_ref):
    x_len, y_len, rows, width = h_ref.shape
    inner = row_ids() < NODES - 1

    def body(x0, y0):
        ys = pl.ds(y0, NODES)
        prev = None
        here = h_ref[x0, ys].astype(f32)
        for i in range(NODES):
            parts = []
            nxt = None
            if i < NODES - 1:
                nxt = h_ref[x0 + i + 1, ys].astype(f32)
                parts.append((nxt - here).astype(bf16))
            parts.append((here[1:] - here[:-1]).astype(bf16))
            cols = node_rows(here)
            parts.append((up(cols) - cols).reshape(here.shape).astype(bf16))
            half = dot(flat(jnp.concatenate(parts, 0)), w_one).reshape(-1, rows, width) + half_bias
            act, slope = silu_half(half)
            act = act.astype(bf16).astype(f32)
            at = 0
            total = prev
            prev = None
            if i < NODES - 1:
                prev = act[:NODES]
                total = -prev if total is None else total - prev
                slope_ref[0, x0 + i, ys] = slope[:NODES]
                at = NODES
            along_y = act[at : at + NODES - 1]
            slope_ref[1, x0 + i, pl.ds(y0, NODES - 1)] = slope[at : at + NODES - 1]
            at += NODES - 1
            along_z = jnp.where(inner, node_rows(act[at:]), 0.0)
            slope_z = jnp.where(inner, node_rows(slope[at:]), 0.0)
            slope_ref[2, x0 + i, ys] = slope_z.reshape(here.shape)
            total = total + (down(along_z) - along_z).reshape(here.shape)
            total = jnp.concatenate(
                [
                    total[:1] - along_y[:1],
                    total[1:-1] + (along_y[:-1] - along_y[1:]),
                    total[-1:] + along_y[-1:],
                ],
                0,
            )
            sum_ref[x0 + i, ys] = couple_slots(total, filled)
            here = nxt

    elements(x_len, y_len, body)


def couple_columns(sum_ref):
    x_len, y_len = sum_ref.shape[:2]
    for cut in range(NODES, x_len, NODES):
        both = sum_ref[cut - 1] + sum_ref[cut]
        sum_ref[cut - 1] = both
        sum_ref[cut] = both
    for cut in range(NODES, y_len, NODES):
        both = sum_ref[:, cut - 1] + sum_ref[:, cut]
        sum_ref[:, cut - 1] = both
        sum_ref[:, cut] = both


def pick_top(values, filled):
    top = values[0]
    for s in range(1, len(values)):
        top = jnp.where(filled == s + 1, values[s], top)
    return top


def write_faces(sc_ref, sum_ref, faces):
    x_len, y_len, rows, width = sum_ref.shape
    x_faces, (y_low, y_high, z_low, z_high) = faces[:-4], faces[-4:]
    if len(x_faces) == 1:
        x_faces[0][0] = sum_ref[sc_ref[1]]
    else:
        x_faces[0][0] = sum_ref[0]
        x_faces[1][0] = sum_ref[x_len - 1]
    y_low[...] = sum_ref[:, 0]
    y_high[...] = sum_ref[:, y_len - 1]
    z_low[...] = sum_ref[:, :, 0]
    tops = [sum_ref[:, :, s * NODES + NODES - 1] for s in range(rows // NODES)]
    z_high[...] = pick_top(tops, sc_ref[0])


def x_planes(sc_ref, received, x_len):
    if len(received) == 1:
        return [(sc_ref[1], received[0])]
    return [(0, received[0]), (x_len - 1, received[1])]


def add_halo(sc_ref, from_ref, halo, into_ref):
    x_len, y_len, rows, width = from_ref.shape
    x_recv, (y_low, y_high, z_low, z_high) = halo[:-4], halo[-4:]

    def copy(x, carry):
        into_ref[x] = from_ref[x]
        return carry

    lax.fori_loop(0, x_len, copy, 0)
    for place, ref in x_planes(sc_ref, x_recv, x_len):
        into_ref[place] += ref[0]
    into_ref[:, 0] += y_low[...]
    into_ref[:, y_len - 1] += y_high[...]
    into_ref[:, :, 0] += z_low[...]
    for s in range(rows // NODES):
        add = jnp.where(sc_ref[0] == s + 1, z_high[...], 0.0)
        into_ref[:, :, s * NODES + NODES - 1] += add


def fix_y_kernel(sc_ref, *refs):
    x_recv, (low, high, out_low, out_high) = refs[:-4], refs[-4:]
    x_len = low.shape[0]
    out_low[...] = low[...]
    out_high[...] = high[...]
    for place, ref in x_planes(sc_ref, x_recv, x_len):
        out_low[place] += ref[0, 0]
        out_high[place] += ref[0, ref.shape[1] - 1]


def fix_z_kernel(sc_ref, *refs):
    x_recv, (y_low, y_high, low, high, out_low, out_high) = refs[:-6], refs[-6:]
    x_len, y_len, width = low.shape
    slots = y_low.shape[1] // NODES
    filled = sc_ref[0]
    out_low[...] = low[...]
    out_high[...] = high[...]
    for place, ref in x_planes(sc_ref, x_recv, x_len):
        out_low[place] += ref[0, :, 0]
        out_high[place] += pick_top([ref[0, :, s * NODES + NODES - 1] for s in range(slots)], filled)
    for place, ref in ((0, y_low), (y_len - 1, y_high)):
        out_low[:, place] += ref[:, 0]
        out_high[:, place] += pick_top([ref[:, s * NODES + NODES - 1] for s in range(slots)], filled)


def node_forward(x, fx_ref, inv_ref, sum_ref, h_ref, w_two, w_in, half_bias):
    scaled = sum_ref[x] * (inv_ref[...] * fx_ref[x])
    pair = split_cols(flat(scaled))
    joined = jnp.concatenate([flat(h_ref[x]), dot(pair, w_two).astype(bf16)], -1)
    act, slope = silu_half(dot(joined, w_in) + half_bias)
    return pair[:, :128], act.astype(bf16), slope


def node_backward(x, fx_ref, inv_ref, filled, grad, feat, scaled, act, slope, w_out_t, w_in_t, sum_ref, base_ref, grads):
    out_acc, top_acc, low_acc, bias_acc = grads
    shape = sum_ref.shape[1:]
    dpn = (dot(grad, w_out_t) * slope).astype(bf16)
    out_acc[...] += dot_t(act, grad)
    both = dot_t(dpn, jnp.concatenate([feat, scaled], -1))
    top_acc[...] += both[:, :128]
    low_acc[...] += both[:, 128:]
    bias_acc[...] += jnp.sum(dpn.astype(f32).reshape(-1, NODES, 128), 0)
    dx = dot(dpn, w_in_t)
    base_ref[x] = (grad.astype(f32) + dx[:, :128]).reshape(shape)
    share = dx[:, 128:].reshape(shape) * (inv_ref[...] * fx_ref[x])
    sum_ref[x] = couple_slots(share, filled)


def edges_backward(q_ref, slope_ref, edge_ref, bias_acc):
    x_len, y_len, rows, width = q_ref.shape

    def body(x0, y0):
        ys = pl.ds(y0, NODES)
        prev = None
        here = q_ref[x0, ys]
        bias = jnp.zeros((NODES, width), f32)
        for i in range(NODES):
            total = prev
            prev = None
            nxt = None
            if i < NODES - 1:
                nxt = q_ref[x0 + i + 1, ys]
                prev = ((nxt - here) * slope_ref[0, x0 + i, ys]).astype(bf16).astype(f32)
                total = -prev if total is None else total - prev
                bias = bias + jnp.sum(node_rows(prev), 0)
            along_y = (here[1:] - here[:-1]) * slope_ref[1, x0 + i, pl.ds(y0, NODES - 1)]
            along_y = along_y.astype(bf16).astype(f32)
            cols = node_rows(here)
            along_z = (up(cols) - cols) * node_rows(slope_ref[2, x0 + i, ys])
            along_z = along_z.astype(bf16).astype(f32)
            bias = bias + jnp.sum(node_rows(along_y), 0) + jnp.sum(along_z, 0)
            total = total + (down(along_z) - along_z).reshape(here.shape)
            total = jnp.concatenate(
                [
                    total[:1] - along_y[:1],
                    total[1:-1] + (along_y[:-1] - along_y[1:]),
                    total[-1:] + along_y[-1:],
                ],
                0,
            )
            edge_ref[x0 + i, ys] = total
            here = nxt
        bias_acc[...] += bias

    elements(x_len, y_len, body)


def planes(count, body):
    def step(x, carry):
        body(x)
        return carry

    lax.fori_loop(0, count, step, 0)


def first_kernel(sc, h, w_one, edge_bias, sums, slopes, *faces):
    edges_forward(h, w_one[...], edge_bias[...], sc[0], sums, slopes)
    couple_columns(sums)
    write_faces(sc, sums, faces)


def middle_kernel(nx, sc, fx, inv, sums_in, h, w_two, w_in, node_bias, w_out, w_one, edge_bias, *refs):
    halo, refs = refs[: nx + 4], refs[nx + 4 :]
    scaled_ref, act_ref, slope_ref, next_ref, sums, slopes = refs[:6]
    faces, work = refs[6:-1], refs[-1]
    add_halo(sc, sums_in, halo, work)
    shape = h.shape[1:]

    def body(x):
        scaled, act, slope = node_forward(x, fx, inv, work, h, w_two[...], w_in[...], node_bias[...])
        scaled_ref[x] = scaled.reshape(shape)
        act_ref[x] = act.reshape(shape)
        slope_ref[x] = slope.reshape(shape)
        moved = flat(h[x]).astype(f32) + dot(act, w_out[...])
        next_ref[x] = moved.astype(bf16).reshape(shape)

    planes(h.shape[0], body)
    edges_forward(next_ref, w_one[...], edge_bias[...], sc[0], sums, slopes)
    couple_columns(sums)
    write_faces(sc, sums, faces)


def turn_kernel(nx, sc, fx, inv, sums_in, h, g_ref, w_two, w_in, node_bias, w_out_t, w_in_t, *refs):
    halo, refs = refs[: nx + 4], refs[nx + 4 :]
    base, sums, out_acc, top_acc, low_acc, bias_acc = refs[:6]
    faces, work = refs[6:-1], refs[-1]
    add_halo(sc, sums_in, halo, work)
    grads = (out_acc, top_acc, low_acc, bias_acc)
    for ref in grads:
        ref[...] = jnp.zeros_like(ref)
    slots = h.shape[2] // NODES
    live = (lax.broadcasted_iota(jnp.int32, (1, h.shape[2], 128), 1) < sc[0] * NODES).astype(f32)

    def body(x):
        scaled, act, slope = node_forward(x, fx, inv, work, h, w_two[...], w_in[...], node_bias[...])
        grad = flat((g_ref[x].astype(f32) * live).astype(bf16))
        node_backward(
            x, fx, inv, sc[0], grad, flat(h[x]), scaled, act, slope, w_out_t[...], w_in_t[...], sums, base, grads
        )

    planes(h.shape[0], body)
    couple_columns(sums)
    write_faces(sc, sums, faces)


def back_to_state(sc, sums_in, halo, h, base, slopes, w_two_t, w_one_t, work, edge_acc, bias_acc, use):
    add_halo(sc, sums_in, halo, work)
    edge_acc[...] = jnp.zeros_like(edge_acc)
    bias_acc[...] = jnp.zeros_like(bias_acc)
    shape = h.shape[1:]

    def to_q(x):
        work[x] = dot(split_cols(flat(work[x])), w_two_t[...]).reshape(shape)

    planes(h.shape[0], to_q)
    edges_backward(work, slopes, work, bias_acc)

    def body(x):
        pair = split_cols(flat(work[x]))
        both = dot_t(flat(h[x]), pair)
        edge_acc[...] += both[:, :128] + both[:, 128:]
        use(x, (flat(base[x]) + dot(pair, w_one_t[...])).astype(bf16))

    planes(h.shape[0], body)


def join_kernel(
    nx, sc, fx, inv, sums_in, h, base_in, slopes, w_two_t, w_one_t,
    h0, scaled0, act0, slope0, w_out_t, w_in_t, *refs
):
    halo, refs = refs[: nx + 4], refs[nx + 4 :]
    base, sums, edge_acc, edge_bias_acc, out_acc, top_acc, low_acc, bias_acc = refs[:8]
    faces, work = refs[8:-1], refs[-1]
    grads = (out_acc, top_acc, low_acc, bias_acc)
    for ref in grads:
        ref[...] = jnp.zeros_like(ref)

    def use(x, grad):
        node_backward(
            x, fx, inv, sc[0], grad, flat(h0[x]), flat(scaled0[x]), flat(act0[x]), flat(slope0[x]),
            w_out_t[...], w_in_t[...], sums, base, grads,
        )

    back_to_state(sc, sums_in, halo, h, base_in, slopes, w_two_t, w_one_t, work, edge_acc, edge_bias_acc, use)
    couple_columns(sums)
    write_faces(sc, sums, faces)


def last_kernel(nx, sc, sums_in, h, base_in, slopes, w_two_t, w_one_t, *refs):
    halo, refs = refs[: nx + 4], refs[nx + 4 :]
    grad_ref, edge_acc, edge_bias_acc, work = refs
    shape = h.shape[1:]

    def use(x, grad):
        grad_ref[x] = grad.reshape(shape)

    back_to_state(sc, sums_in, halo, h, base_in, slopes, w_two_t, w_one_t, work, edge_acc, edge_bias_acc, use)


def call(kernel, name, inputs, smem, outs, scratch=(), flops=0):
    total = sum(math.prod(o.shape) * o.dtype.itemsize for o in outs)
    total += sum(math.prod(i.shape) * i.dtype.itemsize for i in inputs)
    return pl.pallas_call(
        kernel,
        name=name,
        out_shape=tuple(outs),
        in_specs=[SM] * smem + [VM] * (len(inputs) - smem),
        out_specs=tuple([VM] * len(outs)),
        scratch_shapes=list(scratch),
        compiler_params=pltpu.CompilerParams(vmem_limit_bytes=40 * 1024 * 1024),
        cost_estimate=pl.CostEstimate(flops=flops, bytes_accessed=total, transcendentals=0),
    )(*inputs)


def on_device(state, cotangent, counts, edge_weights, node_in, node_out, biases):
    x_len, y_len, slots, nodes, width = state.shape
    rows = slots * nodes
    grid = (x_len, y_len, rows, width)
    size_x, size_y, size_z = (lax.axis_size(a) for a in ("gx", "gy", "gz"))
    at_x, at_y, at_z = (lax.axis_index(a) for a in ("gx", "gy", "gz"))
    filled = counts[0]
    h0 = state.reshape(grid)
    g2 = cotangent.reshape(grid)

    def inverse(length, position, size):
        ids = jnp.arange(length, dtype=jnp.int32)
        end = ids + position * length
        shared = ((ids % nodes == 0) & (end > 0)) | ((ids % nodes == nodes - 1) & (end < length * size - 1))
        return jnp.where(shared, 0.5, 1.0).astype(f32)

    fx = inverse(x_len, at_x, size_x)
    inv_y = inverse(y_len, at_y, size_y)
    ids = jnp.arange(rows, dtype=jnp.int32)
    low = (ids % nodes == 0) & ((ids >= nodes) | (at_z > 0))
    high = (ids % nodes == nodes - 1) & ((ids < (filled - 1) * nodes) | (at_z < size_z - 1))
    inv_z = jnp.where(low | high, 0.5, 1.0).astype(f32)
    inv = jnp.broadcast_to((inv_y[:, None] * inv_z[None, :])[:, :, None], (y_len, rows, width))
    single = size_x == 2
    sc = jnp.stack([filled, jnp.where(at_x == 0, x_len - 1, 0).astype(jnp.int32)])
    nx = 1 if single else 2

    def sds(shape, kind=f32):
        return jax.ShapeDtypeStruct(shape, kind)

    face_x = sds((1, y_len, rows, width))
    face_y = sds((x_len, rows, width))
    face_z = sds((x_len, y_len, width))
    face_outs = [face_x] * nx + [face_y] * 2 + [face_z] * 2
    full = sds(grid)
    full16 = sds(grid, bf16)
    full3 = sds((3,) + grid)
    square = sds((width, width))
    strip = sds((NODES, width))
    work = pltpu.VMEM(grid, f32)
    matmul = 2 * math.prod(grid) * width

    def trade(low_face, high_face, axis):
        size = lax.axis_size(axis)
        below = lax.ppermute(high_face, axis, [(i, i + 1) for i in range(size - 1)])
        above = lax.ppermute(low_face, axis, [(i + 1, i) for i in range(size - 1)])
        return below, above

    def exchange(faces):
        x_faces, (y_low, y_high, z_low, z_high) = faces[:nx], faces[nx:]
        if single:
            got_x = (lax.ppermute(x_faces[0], "gx", [(0, 1), (1, 0)]),)
        else:
            got_x = trade(x_faces[0], x_faces[1], "gx")
        y_low, y_high = call(fix_y_kernel, "fix_y", (sc, *got_x, y_low, y_high), 1, [face_y] * 2)
        got_y = trade(y_low, y_high, "gy")
        z_low, z_high = call(fix_z_kernel, "fix_z", (sc, *got_x, *got_y, z_low, z_high), 1, [face_z] * 2)
        got_z = trade(z_low, z_high, "gz")
        return (*got_x, *got_y, *got_z)

    half = jnp.bfloat16(0.5)
    w_one = [edge_weights[l, 0] * half for l in range(2)]
    w_two = [jnp.concatenate([edge_weights[l, 1]] * 2, 0) for l in range(2)]
    w_one_t = [jnp.concatenate([edge_weights[l, 0].T] * 2, 0) for l in range(2)]
    w_two_t = [jnp.concatenate([edge_weights[l, 1].T] * 2, 0) for l in range(2)]
    w_in = [node_in[l] * half for l in range(2)]
    w_in_t = [node_in[l].T for l in range(2)]
    w_out_t = [node_out[l].T for l in range(2)]
    edge_bias = [0.5 * biases[l, 0][None] for l in range(2)]
    node_bias = [0.5 * biases[l, 1][None] for l in range(2)]

    sums, slopes0, *faces = call(
        first_kernel, "edges0", (sc, h0, w_one[0], edge_bias[0]), 1, [full, full3] + face_outs, flops=3 * matmul
    )
    halo = exchange(faces)
    scaled0, act0, slope0, h1, sums, slopes1, *faces = call(
        functools.partial(middle_kernel, nx),
        "nodes0_edges1",
        (sc, fx, inv, sums, h0, w_two[0], w_in[0], node_bias[0], node_out[0], w_one[1], edge_bias[1], *halo),
        2,
        [full16, full16, full, full16, full, full3] + face_outs,
        [work],
        flops=8 * matmul,
    )
    halo = exchange(faces)
    base, sums, out1, top1, low1, nb1, *faces = call(
        functools.partial(turn_kernel, nx),
        "nodes1_back",
        (sc, fx, inv, sums, h1, g2, w_two[1], w_in[1], node_bias[1], w_out_t[1], w_in_t[1], *halo),
        2,
        [full, full, square, square, square, strip] + face_outs,
        [work],
        flops=10 * matmul,
    )
    halo = exchange(faces)
    base, sums, edge1, eb1, out0, top0, low0, nb0, *faces = call(
        functools.partial(join_kernel, nx),
        "edges1_back_nodes0_back",
        (
            sc, fx, inv, sums, h1, base, slopes1, w_two_t[1], w_one_t[1],
            h0, scaled0, act0, slope0, w_out_t[0], w_in_t[0], *halo,
        ),
        2,
        [full, full, square, strip, square, square, square, strip] + face_outs,
        [work],
        flops=12 * matmul,
    )
    halo = exchange(faces)
    grad0, edge0, eb0 = call(
        functools.partial(last_kernel, nx),
        "edges0_back",
        (sc, sums, h0, base, slopes0, w_two_t[0], w_one_t[0], *halo),
        1,
        [full16, square, strip],
        [work],
        flops=6 * matmul,
    )

    def reduce_all(value):
        for axis in ("gx", "gy", "gz"):
            size = lax.axis_size(axis)
            hop = 1
            while hop < size:
                value = value + lax.ppermute(value, axis, [(i, i ^ hop) for i in range(size)])
                hop *= 2
        return value

    summed1 = reduce_all(jnp.concatenate([out1, top1, low1, nb1], 0))
    summed0 = reduce_all(jnp.concatenate([edge1, out0, top0, low0, eb1, nb0], 0))
    last = reduce_all(jnp.concatenate([edge0, eb0], 0))
    layers_all = 3 * slots * size_z // 4
    nodes_all = x_len * size_x * y_len * size_y * layers_all * nodes
    scale = 1.0 / math.sqrt(nodes_all)

    def block(value, index):
        return value[index * width : (index + 1) * width] * scale

    def tail(value, index):
        start = value.shape[0] - (index + 1) * NODES
        return jnp.sum(value[start : start + NODES], 0) * scale

    out_grads = (block(summed0, 1), block(summed1, 0))
    tops = (block(summed0, 2).T, block(summed1, 1).T)
    lows_t = (block(summed0, 3), block(summed1, 2))
    firsts = (block(last, 0), block(summed0, 0))
    edge_biases = (tail(last, 0), tail(summed0, 1))
    node_biases = (tail(summed0, 0), tail(summed1, 0))

    def exact(left, right, dims):
        return lax.dot_general(
            left, right.astype(f32), (dims, ((), ())), precision=lax.Precision.HIGHEST, preferred_element_type=f32
        )

    edge_grads = jnp.stack(
        [jnp.stack([firsts[l], exact(lows_t[l], node_in[l, width:], ((0,), (1,)))]) for l in range(2)]
    )
    in_grads = jnp.stack(
        [
            jnp.concatenate([tops[l], exact(lows_t[l], edge_weights[l, 1], ((1,), (0,))).T], 0)
            for l in range(2)
        ]
    )
    bias_grads = jnp.stack([jnp.stack([edge_biases[l], node_biases[l]]) for l in range(2)])
    return grad0.reshape(state.shape), edge_grads, in_grads, jnp.stack(out_grads), bias_grads


def solution(mesh):
    return jax.shard_map(
        on_device,
        mesh=mesh,
        in_specs=(
            P("gx", "gy", "gz", None, None),
            P("gx", "gy", "gz", None, None),
            P("gz"),
            P(),
            P(),
            P(),
            P(),
        ),
        out_specs=(P("gx", "gy", "gz", None, None), P(), P(), P(), P()),
        check_vma=False,
    )
```

```python
import functools
import math

import jax
import jax.numpy as jnp
from jax import lax
from jax.experimental import pallas as pl
from jax.experimental.pallas import tpu as pltpu
from jax.sharding import PartitionSpec as P

f32 = jnp.float32
bf16 = jnp.bfloat16
NODES = 8
VMEM_LIMIT = 12 * 1024 * 1024
VM = pl.BlockSpec(memory_space=pltpu.VMEM)
SM = pl.BlockSpec(memory_space=pltpu.SMEM)


def dot(left, right):
    return lax.dot_general(left, right, (((1,), (0,)), ((), ())), preferred_element_type=f32)


def dot_t(left, right):
    return lax.dot_general(left, right, (((0,), (0,)), ((), ())), preferred_element_type=f32)


def dot_rt(left, right):
    return lax.dot_general(left, right, (((1,), (1,)), ((), ())), preferred_element_type=f32)


def silu_half(half):
    th = jnp.tanh(half)
    prod = half * th
    return half + prod, (0.5 + 0.5 * th) * ((1.0 + half) - prod)


def split_cols(value):
    high = value.astype(bf16)
    low = (value - high.astype(f32)).astype(bf16)
    return jnp.concatenate([high, low], -1)


def up(value):
    return pltpu.roll(value, NODES - 1, 1)


def down(value):
    return pltpu.roll(value, 1, 1)


def flat(value):
    return value.reshape(-1, value.shape[-1])


def node_rows(value):
    return value.reshape(-1, NODES, value.shape[-1])


def row_ids():
    return lax.broadcasted_iota(jnp.int32, (1, NODES, 128), 1)


def couple_slots(plane, filled):
    count, rows, width = plane.shape
    slots = rows // NODES
    parts = plane.reshape(count, slots, NODES, width)
    ids = row_ids()
    done = []
    for s in range(slots):
        here = parts[:, s]
        if s + 1 < slots:
            take = (ids == NODES - 1) & (s + 1 < filled)
            here = here + jnp.where(take, up(parts[:, s + 1]), 0.0)
        if s > 0:
            here = here + jnp.where(ids == 0, down(parts[:, s - 1]), 0.0)
            here = jnp.where(s < filled, here, 0.0)
        done.append(here[:, None])
    return jnp.concatenate(done, 1).reshape(plane.shape)


def elements(x_len, y_len, body):
    ey = y_len // NODES
    total = (x_len // NODES) * ey

    def step(e, carry):
        x0 = pl.multiple_of((e // ey) * NODES, NODES)
        y0 = pl.multiple_of((e % ey) * NODES, NODES)
        body(x0, y0)
        return carry

    lax.fori_loop(0, total, step, 0)


def edges_forward(h_ref, w_one, half_bias, filled, sum_ref, slope_ref):
    x_len, y_len, rows, width = h_ref.shape
    inner = row_ids() < NODES - 1

    def body(x0, y0):
        ys = pl.ds(y0, NODES)
        prev = None
        here = h_ref[x0, ys].astype(f32)
        for i in range(NODES):
            parts = []
            nxt = None
            if i < NODES - 1:
                nxt = h_ref[x0 + i + 1, ys].astype(f32)
                parts.append((nxt - here).astype(bf16))
            parts.append((here[1:] - here[:-1]).astype(bf16))
            cols = node_rows(here)
            parts.append((up(cols) - cols).reshape(here.shape).astype(bf16))
            half = dot(flat(jnp.concatenate(parts, 0)), w_one).reshape(-1, rows, width) + half_bias
            act, slope = silu_half(half)
            act = act.astype(bf16).astype(f32)
            at = 0
            total = prev
            prev = None
            if i < NODES - 1:
                prev = act[:NODES]
                total = -prev if total is None else total - prev
                slope_ref[0, x0 + i, ys] = slope[:NODES]
                at = NODES
            along_y = act[at : at + NODES - 1]
            slope_ref[1, x0 + i, pl.ds(y0, NODES - 1)] = slope[at : at + NODES - 1]
            at += NODES - 1
            along_z = jnp.where(inner, node_rows(act[at:]), 0.0)
            slope_z = jnp.where(inner, node_rows(slope[at:]), 0.0)
            slope_ref[2, x0 + i, ys] = slope_z.reshape(here.shape)
            total = total + (down(along_z) - along_z).reshape(here.shape)
            total = jnp.concatenate(
                [
                    total[:1] - along_y[:1],
                    total[1:-1] + (along_y[:-1] - along_y[1:]),
                    total[-1:] + along_y[-1:],
                ],
                0,
            )
            sum_ref[x0 + i, ys] = couple_slots(total, filled)
            here = nxt

    elements(x_len, y_len, body)


def couple_columns(sum_ref):
    x_len, y_len = sum_ref.shape[:2]
    for cut in range(NODES, x_len, NODES):
        both = sum_ref[cut - 1] + sum_ref[cut]
        sum_ref[cut - 1] = both
        sum_ref[cut] = both
    for cut in range(NODES, y_len, NODES):
        both = sum_ref[:, cut - 1] + sum_ref[:, cut]
        sum_ref[:, cut - 1] = both
        sum_ref[:, cut] = both


def face_place(sc_ref, axis, kind, last):
    return jnp.where((sc_ref[1 + axis] + kind) % 2 == 0, last, 0)


def end_rows(values, filled, take_top):
    picked = values(0)
    slots = values.slots
    for s in range(slots):
        picked = jnp.where(take_top & (filled == s + 1), values(s * NODES + NODES - 1), picked)
    return picked


class RowReader:
    def __init__(self, slots, read):
        self.slots = slots
        self.read = read

    def __call__(self, row):
        return self.read(row)


def takes_top(sc_ref, kind):
    return (sc_ref[3] + kind) % 2 == 0


def write_faces(sc_ref, sum_ref, faces, counts):
    x_len, y_len, rows, width = sum_ref.shape
    nx, ny, nz = counts
    reader = RowReader(rows // NODES, lambda row: sum_ref[:, :, row])
    for kind in range(nx):
        faces[kind][...] = sum_ref[face_place(sc_ref, 0, kind, x_len - 1)]
    for kind in range(ny):
        faces[nx + kind][...] = sum_ref[:, face_place(sc_ref, 1, kind, y_len - 1)]
    for kind in range(nz):
        faces[nx + ny + kind][...] = end_rows(reader, sc_ref[0], takes_top(sc_ref, kind))


def add_halo(sc_ref, from_ref, halo, into_ref, counts):
    x_len, y_len, rows, width = from_ref.shape
    nx, ny, nz = counts

    def copy(x, carry):
        into_ref[x] = from_ref[x]
        return carry

    lax.fori_loop(0, x_len, copy, 0)
    for kind in range(nx):
        into_ref[face_place(sc_ref, 0, kind, x_len - 1)] += halo[kind][...]
    for kind in range(ny):
        into_ref[:, face_place(sc_ref, 1, kind, y_len - 1)] += halo[nx + kind][...]
    if nz:
        got = [halo[nx + ny + kind][...] for kind in range(nz)]
        tops = [takes_top(sc_ref, kind) for kind in range(nz)]
        from_below = sum(jnp.where(top, 0.0, value) for top, value in zip(tops, got))
        from_above = sum(jnp.where(top, value, 0.0) for top, value in zip(tops, got))
        into_ref[:, :, 0] += from_below
        for s in range(rows // NODES):
            into_ref[:, :, s * NODES + NODES - 1] += jnp.where(sc_ref[0] == s + 1, from_above, 0.0)


def fix_y_kernel(counts, sc_ref, *refs):
    nx, ny, nz = counts
    got, faces, outs = refs[:nx], refs[nx : nx + ny], refs[nx + ny :]
    x_len = faces[0].shape[0]
    for k in range(ny):
        outs[k][...] = faces[k][...]
    for kind in range(nx):
        place = face_place(sc_ref, 0, kind, x_len - 1)
        for k in range(ny):
            y_len = got[kind].shape[0]
            outs[k][place] += got[kind][face_place(sc_ref, 1, k, y_len - 1)]


def fix_z_kernel(counts, sc_ref, *refs):
    nx, ny, nz = counts
    got_x, refs = refs[:nx], refs[nx:]
    got_y, refs = refs[:ny], refs[ny:]
    faces, outs = refs[:nz], refs[nz:]
    x_len, y_len, width = faces[0].shape
    for k in range(nz):
        outs[k][...] = faces[k][...]
    for k in range(nz):
        top = takes_top(sc_ref, k)
        for kind in range(nx):
            ref = got_x[kind]
            reader = RowReader(ref.shape[1] // NODES, lambda row, ref=ref: ref[:, row])
            outs[k][face_place(sc_ref, 0, kind, x_len - 1)] += end_rows(reader, sc_ref[0], top)
        for kind in range(ny):
            ref = got_y[kind]
            reader = RowReader(ref.shape[1] // NODES, lambda row, ref=ref: ref[:, row])
            add = end_rows(reader, sc_ref[0], top)
            first = face_place(sc_ref, 1, kind, 1) == 0
            outs[k][:, 0] += jnp.where(first, add, 0.0)
            outs[k][:, y_len - 1] += jnp.where(first, 0.0, add)


def write_inverse(sc_ref, inv_ref, sizes):
    y_len, rows, width = inv_ref.shape
    filled, at_y, at_z = sc_ref[0], sc_ref[2], sc_ref[3]
    ids = lax.broadcasted_iota(jnp.int32, (rows, width), 0)
    node = ids % NODES
    low = (node == 0) & ((ids >= NODES) | (at_z > 0))
    high = (node == NODES - 1) & ((ids < (filled - 1) * NODES) | (at_z < sizes[2] - 1))
    along_z = jnp.where(low | high, 0.5, 1.0).astype(f32)
    for y in range(y_len):
        inv_ref[y] = along_z * end_factor(y, y_len, at_y, sizes[1])


def end_factor(place, length, position, size):
    whole = place + position * length
    low = (place % NODES == 0) & (whole > 0)
    high = (place % NODES == NODES - 1) & (whole < length * size - 1)
    return jnp.where(low | high, 0.5, 1.0).astype(f32)


CHUNK = 4


def scale_planes(sc_ref, inv_ref, x, block, x_len, size_x):
    inv = inv_ref[...]
    parts = [block[c] * (inv * end_factor(x + c, x_len, sc_ref[1], size_x)) for c in range(CHUNK)]
    return jnp.stack(parts, 0)


def node_forward(sc_ref, x, inv_ref, size_x, sum_ref, h_ref, weights, layer):
    edge_w, node_in, node_out, biases = weights
    at = pl.ds(x, CHUNK)
    scaled = scale_planes(sc_ref, inv_ref, x, sum_ref[at], sum_ref.shape[0], size_x)
    pair = split_cols(flat(scaled))
    w_two = edge_w[layer, 1]
    joined = jnp.concatenate([flat(h_ref[at]), dot(pair, jnp.concatenate([w_two, w_two], 0)).astype(bf16)], -1)
    half = jnp.bfloat16(0.5)
    act, slope = silu_half(dot(joined, node_in[layer] * half) + 0.5 * biases[layer, pl.ds(1, 1)])
    return pair[:, :128], act.astype(bf16), slope


def node_backward(sc_ref, x, inv_ref, size_x, grad, feat, scaled, act, slope, weights, layer, sum_ref, base_ref, grads):
    edge_w, node_in, node_out, biases = weights
    shape = (CHUNK,) + sum_ref.shape[1:]
    at = pl.ds(x, CHUNK)
    dpn = (dot_rt(grad, node_out[layer]) * slope).astype(bf16)
    grads[0, pl.ds(0, 128)] += dot_t(act, grad)
    both = dot_t(dpn, jnp.concatenate([feat, scaled], -1))
    grads[0, pl.ds(128, 128)] += both[:, :128]
    grads[0, pl.ds(256, 128)] += both[:, 128:]
    grads[0, pl.ds(384, NODES)] += jnp.sum(dpn.astype(f32).reshape(-1, NODES, 128), 0)
    dx = dot_rt(dpn, node_in[layer])
    base_ref[at] = (grad.astype(f32) + dx[:, :128]).reshape(shape)
    share = scale_planes(sc_ref, inv_ref, x, dx[:, 128:].reshape(shape), sum_ref.shape[0], size_x)
    joined = couple_slots(share.reshape((-1,) + shape[2:]), sc_ref[0])
    sum_ref[at] = joined.reshape(shape)


def edges_backward(q_ref, slope_ref, edge_ref, bias_acc):
    x_len, y_len, rows, width = q_ref.shape

    def body(x0, y0):
        ys = pl.ds(y0, NODES)
        prev = None
        here = q_ref[x0, ys]
        bias = jnp.zeros((NODES, width), f32)
        for i in range(NODES):
            total = prev
            prev = None
            nxt = None
            if i < NODES - 1:
                nxt = q_ref[x0 + i + 1, ys]
                prev = ((nxt - here) * slope_ref[0, x0 + i, ys]).astype(bf16).astype(f32)
                total = -prev if total is None else total - prev
                bias = bias + jnp.sum(node_rows(prev), 0)
            along_y = (here[1:] - here[:-1]) * slope_ref[1, x0 + i, pl.ds(y0, NODES - 1)]
            along_y = along_y.astype(bf16).astype(f32)
            cols = node_rows(here)
            along_z = (up(cols) - cols) * node_rows(slope_ref[2, x0 + i, ys])
            along_z = along_z.astype(bf16).astype(f32)
            bias = bias + jnp.sum(node_rows(along_y), 0) + jnp.sum(along_z, 0)
            total = total + (down(along_z) - along_z).reshape(here.shape)
            total = jnp.concatenate(
                [
                    total[:1] - along_y[:1],
                    total[1:-1] + (along_y[:-1] - along_y[1:]),
                    total[-1:] + along_y[-1:],
                ],
                0,
            )
            edge_ref[x0 + i, ys] = total
            here = nxt
        bias_acc[...] += bias

    elements(x_len, y_len, body)


def planes(count, body):
    def step(c, carry):
        body(pl.multiple_of(c * CHUNK, CHUNK))
        return carry

    lax.fori_loop(0, count // CHUNK, step, 0)


def half_weights(weights, layer):
    edge_w, node_in, node_out, biases = weights
    return edge_w[layer, 0] * jnp.bfloat16(0.5), 0.5 * biases[layer, pl.ds(0, 1)]


def first_kernel(counts, sizes, sc, edge_w, node_in, node_out, biases, h, *refs):
    weights = (edge_w, node_in, node_out, biases)
    sums, slopes = refs[:2]
    faces = refs[2:]
    w_one, bias = half_weights(weights, 0)
    edges_forward(h, w_one, bias, sc[0], sums, slopes)
    couple_columns(sums)
    write_faces(sc, sums, faces, counts)


def middle_kernel(counts, sizes, sc, edge_w, node_in, node_out, biases, sums_in, h, *refs):
    weights = (edge_w, node_in, node_out, biases)
    n = sum(counts)
    halo, refs = refs[:n], refs[n:]
    scaled_ref, act_ref, slope_ref, next_ref, sums, slopes = refs[:6]
    faces, (work, inv) = refs[6:-2], refs[-2:]
    add_halo(sc, sums_in, halo, work, counts)
    write_inverse(sc, inv, sizes)
    shape = (CHUNK,) + h.shape[1:]

    def body(x):
        at = pl.ds(x, CHUNK)
        scaled, act, slope = node_forward(sc, x, inv, sizes[0], work, h, weights, 0)
        scaled_ref[at] = scaled.reshape(shape)
        act_ref[at] = act.reshape(shape)
        slope_ref[at] = slope.reshape(shape)
        moved = flat(h[at]).astype(f32) + dot(act, node_out[0])
        next_ref[at] = moved.astype(bf16).reshape(shape)

    planes(h.shape[0], body)
    w_one, bias = half_weights(weights, 1)
    edges_forward(next_ref, w_one, bias, sc[0], sums, slopes)
    couple_columns(sums)
    write_faces(sc, sums, faces, counts)


def turn_kernel(counts, sizes, sc, edge_w, node_in, node_out, biases, sums_in, h, g_ref, *refs):
    weights = (edge_w, node_in, node_out, biases)
    n = sum(counts)
    halo, refs = refs[:n], refs[n:]
    base, sums, grads = refs[:3]
    faces, (work, inv) = refs[3:-2], refs[-2:]
    add_halo(sc, sums_in, halo, work, counts)
    write_inverse(sc, inv, sizes)
    grads[...] = jnp.zeros_like(grads)
    live = (lax.broadcasted_iota(jnp.int32, (1, 1, h.shape[2], 128), 2) < sc[0] * NODES).astype(f32)

    def body(x):
        at = pl.ds(x, CHUNK)
        scaled, act, slope = node_forward(sc, x, inv, sizes[0], work, h, weights, 1)
        grad = flat((g_ref[at].astype(f32) * live).astype(bf16))
        node_backward(
            sc, x, inv, sizes[0], grad, flat(h[at]), scaled, act, slope, weights, 1, sums, base, grads
        )

    planes(h.shape[0], body)
    couple_columns(sums)
    write_faces(sc, sums, faces, counts)


def back_to_state(counts, sc, weights, layer, sums_in, halo, h, base, slopes, work, grads, row, use):
    edge_w = weights[0]
    add_halo(sc, sums_in, halo, work, counts)
    shape = (CHUNK,) + h.shape[1:]
    w_two = edge_w[layer, 1]
    w_two = jnp.concatenate([w_two, w_two], 1)
    w_one = edge_w[layer, 0]
    w_one = jnp.concatenate([w_one, w_one], 1)

    def to_q(x):
        at = pl.ds(x, CHUNK)
        work[at] = dot_rt(split_cols(flat(work[at])), w_two).reshape(shape)

    planes(h.shape[0], to_q)
    edges_backward(work, slopes, work, grads.at[0, pl.ds(row + 128, NODES)])

    def body(x):
        at = pl.ds(x, CHUNK)
        pair = split_cols(flat(work[at]))
        both = dot_t(flat(h[at]), pair)
        grads[0, pl.ds(row, 128)] += both[:, :128] + both[:, 128:]
        use(x, (flat(base[at]) + dot_rt(pair, w_one)).astype(bf16))

    planes(h.shape[0], body)


def join_kernel(
    counts, sizes, sc, edge_w, node_in, node_out, biases,
    sums_in, h, base_in, slopes, h0, scaled0, act0, slope0, *refs
):
    weights = (edge_w, node_in, node_out, biases)
    n = sum(counts)
    halo, refs = refs[:n], refs[n:]
    base, sums, grads = refs[:3]
    faces, (work, inv) = refs[3:-2], refs[-2:]
    write_inverse(sc, inv, sizes)
    grads[...] = jnp.zeros_like(grads)

    def use(x, grad):
        at = pl.ds(x, CHUNK)
        node_backward(
            sc, x, inv, sizes[0], grad, flat(h0[at]), flat(scaled0[at]), flat(act0[at]), flat(slope0[at]),
            weights, 0, sums, base, grads,
        )

    back_to_state(counts, sc, weights, 1, sums_in, halo, h, base_in, slopes, work, grads, 384 + NODES, use)
    couple_columns(sums)
    write_faces(sc, sums, faces, counts)


def last_kernel(counts, sizes, sc, edge_w, node_in, node_out, biases, sums_in, h, base_in, slopes, *refs):
    weights = (edge_w, node_in, node_out, biases)
    n = sum(counts)
    halo, refs = refs[:n], refs[n:]
    grad_ref, grads, work = refs
    grads[...] = jnp.zeros_like(grads)
    shape = (CHUNK,) + h.shape[1:]

    def use(x, grad):
        grad_ref[pl.ds(x, CHUNK)] = grad.reshape(shape)

    back_to_state(counts, sc, weights, 0, sums_in, halo, h, base_in, slopes, work, grads, 0, use)


def finish_kernel(scale, edge_w, node_in, sum0, sum1, last, edge_grads, in_grads, out_grads, bias_grads):
    width = edge_w.shape[-1]

    def rows_of(ref, start, count=width):
        return ref[pl.ds(start, count)] * scale

    def bias_of(ref, start):
        return jnp.sum(rows_of(ref, start, NODES), 0, keepdims=True)

    end = 3 * width
    firsts = ((last, 0), (sum0, end + NODES))
    for layer, ref in enumerate((sum0, sum1)):
        out_grads[layer] = rows_of(ref, 0)
        in_grads[layer, pl.ds(0, width)] = rows_of(ref, width).T
        bias_grads[layer, pl.ds(1, 1)] = bias_of(ref, end)
        source, start = firsts[layer]
        edge_grads[layer, 0] = rows_of(source, start)
        bias_grads[layer, pl.ds(0, 1)] = bias_of(source, start + width)
        mixed = rows_of(ref, 2 * width).T
        high = mixed.astype(bf16)
        low = (mixed - high.astype(f32)).astype(bf16)
        lower = node_in[layer, pl.ds(width, width)]
        edge_grads[layer, 1] = dot_rt(high, lower) + dot_rt(low, lower)
        w_two = edge_w[layer, 1]
        in_grads[layer, pl.ds(width, width)] = dot_t(w_two, high) + dot_t(w_two, low)


def call(kernel, name, inputs, outs, scratch=(), flops=0):
    total = sum(math.prod(o.shape) * o.dtype.itemsize for o in outs)
    total += sum(math.prod(i.shape) * i.dtype.itemsize for i in inputs)
    return pl.pallas_call(
        kernel,
        name=name,
        out_shape=tuple(outs),
        in_specs=[SM] + [VM] * (len(inputs) - 1),
        out_specs=tuple([VM] * len(outs)),
        scratch_shapes=list(scratch),
        compiler_params=pltpu.CompilerParams(vmem_limit_bytes=VMEM_LIMIT),
        cost_estimate=pl.CostEstimate(flops=flops, bytes_accessed=total, transcendentals=0),
    )(*inputs)


def pairs(size, kind):
    return [
        pair for low in range(kind, size - 1, 2) for pair in ((low, low + 1), (low + 1, low))
    ]


def double(value, axis, hop):
    size = lax.axis_size(axis)
    return value + lax.ppermute(value, axis, [(i, i ^ hop) for i in range(size)])


def hops(size):
    found = []
    hop = 1
    while hop < size:
        found.append(hop)
        hop *= 2
    return found


def sum_steps(value):
    steps = [("gy", 1)] + [("gx", hop) for hop in hops(lax.axis_size("gx"))]
    steps += [("gy", hop) for hop in hops(lax.axis_size("gy"))[1:]]
    steps = [step for step in steps if lax.axis_size(step[0]) > 1]
    rows, width = value.shape
    unit = NODES << len(steps)
    padded = -(-rows // unit) * unit
    value = jnp.pad(value, ((0, padded - rows), (0, 0))).reshape((2,) * len(steps) + (-1, width))
    for axis, hop in steps:
        size = lax.axis_size(axis)
        bit = (lax.axis_index(axis) // hop) % 2
        keep = lax.dynamic_index_in_dim(value, bit, 0, keepdims=False)
        send = lax.dynamic_index_in_dim(value, 1 - bit, 0, keepdims=False)
        value = yield keep + lax.ppermute(send, axis, [(i, i ^ hop) for i in range(size)])
    for hop in hops(lax.axis_size("gz")):
        value = yield double(value, "gz", hop)
    for axis, hop in reversed(steps):
        size = lax.axis_size(axis)
        bit = (lax.axis_index(axis) // hop) % 2
        other = lax.ppermute(value, axis, [(i, i ^ hop) for i in range(size)])
        value = yield jnp.where(bit == 0, jnp.stack([value, other]), jnp.stack([other, value]))
    yield value.reshape(padded, width)[:rows]


class Background:
    def __init__(self):
        self.active = []

    def add(self, value):
        entry = [sum_steps(value), None, None]
        entry[2] = "ready"
        self.active.append(entry)
        return entry

    def advance(self, entry, tied):
        steps, value, state = entry
        try:
            entry[1] = next(steps) if state == "ready" else steps.send(tied)
            entry[2] = "going"
        except StopIteration:
            entry[2] = "done"

    def beside(self, anchor):
        for entry in self.active:
            if entry[2] == "going":
                anchor, tied = lax.optimization_barrier((anchor, entry[1]))
                self.advance(entry, tied)
            elif entry[2] == "ready":
                self.advance(entry, None)
        return anchor

    def finish(self, entry):
        while entry[2] != "done":
            self.advance(entry, entry[1])
        return entry[1]


def on_device(state, cotangent, counts, edge_weights, node_in, node_out, biases):
    x_len, y_len, slots, nodes, width = state.shape
    rows = slots * nodes
    grid = (x_len, y_len, rows, width)
    axes = ("gx", "gy", "gz")
    sizes = tuple(lax.axis_size(a) for a in axes)
    trades = tuple(min(size - 1, 2) for size in sizes)
    nx, ny, nz = trades
    h0 = state.reshape(grid)
    g2 = cotangent.reshape(grid)
    sc = jnp.stack([counts[0]] + [lax.axis_index(a).astype(jnp.int32) for a in axes])

    def sds(shape, kind=f32):
        return jax.ShapeDtypeStruct(shape, kind)

    face_x = sds((y_len, rows, width))
    face_y = sds((x_len, rows, width))
    face_z = sds((x_len, y_len, width))
    face_outs = [face_x] * nx + [face_y] * ny + [face_z] * nz
    full = sds(grid)
    full16 = sds(grid, bf16)
    full3 = sds((3,) + grid)
    work = pltpu.VMEM(grid, f32)
    inv = pltpu.VMEM((y_len, rows, width), f32)
    matmul = 2 * math.prod(grid) * width
    weights = (edge_weights, node_in, node_out, biases)

    def run(kernel, name, inputs, outs, scratch, flops):
        body = functools.partial(kernel, trades, sizes)
        return call(body, name, (sc, *weights, *inputs), outs, scratch, flops * matmul)

    def trade(faces, axis):
        size = lax.axis_size(axis)
        return [lax.ppermute(face, axis, pairs(size, kind)) for kind, face in enumerate(faces)]

    background = Background()

    def exchange(faces):
        got_x = trade(faces[:nx], "gx")
        fix = functools.partial(fix_y_kernel, trades)
        faces_y = call(fix, "fix_y", (sc, *got_x, *faces[nx : nx + ny]), [face_y] * ny)
        got_y = trade(background.beside(faces_y), "gy")
        fix = functools.partial(fix_z_kernel, trades)
        faces_z = call(fix, "fix_z", (sc, *got_x, *got_y, *faces[nx + ny :]), [face_z] * nz)
        faces_z = background.beside(faces_z)
        got_z = background.beside(trade(faces_z, "gz"))
        return (*got_x, *got_y, *got_z)

    sums, slopes0, *faces = run(first_kernel, "edges0", (h0,), [full, full3] + face_outs, [], 3)
    halo = exchange(faces)
    scaled0, act0, slope0, h1, sums, slopes1, *faces = run(
        middle_kernel, "nodes0_edges1", (sums, h0, *halo),
        [full16, full16, full, full16, full, full3] + face_outs, [work, inv], 8,
    )
    halo = exchange(faces)
    turn_rows = sds((1, 3 * width + NODES, width))
    base, sums, grads1, *faces = run(
        turn_kernel, "nodes1_back", (sums, h1, g2, *halo), [full, full, turn_rows] + face_outs, [work, inv], 10
    )
    sum1 = background.add(grads1[0])
    halo = exchange(faces)
    join_rows = sds((1, 4 * width + 2 * NODES, width))
    base, sums, grads0, *faces = run(
        join_kernel, "edges1_back_nodes0_back", (sums, h1, base, slopes1, h0, scaled0, act0, slope0, *halo),
        [full, full, join_rows] + face_outs, [work, inv], 12,
    )
    sum0 = background.add(grads0[0])
    halo = exchange(faces)
    last_rows = sds((1, width + NODES, width))
    grad0, last = run(last_kernel, "edges0_back", (sums, h0, base, slopes0, *halo), [full16, last_rows], [work], 6)

    last = last[0]
    for axis in ("gz", "gy", "gx"):
        for hop in reversed(hops(lax.axis_size(axis))):
            last = double(background.beside(last), axis, hop)
    summed1, summed0 = background.finish(sum1), background.finish(sum0)
    layers_all = 3 * slots * sizes[2] // 4
    nodes_all = x_len * sizes[0] * y_len * sizes[1] * layers_all * nodes
    scale = 1.0 / math.sqrt(nodes_all)

    edge_grads, in_grads, out_grads, bias_grads = pl.pallas_call(
        functools.partial(finish_kernel, scale),
        name="finish",
        out_shape=(
            sds(edge_weights.shape),
            sds(node_in.shape),
            sds(node_out.shape),
            sds(biases.shape),
        ),
        in_specs=[VM] * 5,
        out_specs=(VM, VM, VM, VM),
        compiler_params=pltpu.CompilerParams(vmem_limit_bytes=VMEM_LIMIT),
    )(edge_weights, node_in, summed0, summed1, last)
    return grad0.reshape(state.shape), edge_grads, in_grads, out_grads, bias_grads


def solution(mesh):
    return jax.shard_map(
        on_device,
        mesh=mesh,
        in_specs=(
            P("gx", "gy", "gz", None, None),
            P("gx", "gy", "gz", None, None),
            P("gz"),
            P(),
            P(),
            P(),
            P(),
        ),
        out_specs=(P("gx", "gy", "gz", None, None), P(), P(), P(), P()),
        check_vma=False,
    )
```

```python
import functools
import math

import jax
import jax.numpy as jnp
from jax import lax
from jax.experimental import pallas as pl
from jax.experimental.pallas import tpu as pltpu
from jax.sharding import PartitionSpec as P

f32 = jnp.float32
bf16 = jnp.bfloat16
NODES = 8
VMEM_LIMIT = 12 * 1024 * 1024
VM = pl.BlockSpec(memory_space=pltpu.VMEM)
SM = pl.BlockSpec(memory_space=pltpu.SMEM)


def dot(left, right):
    return lax.dot_general(left, right, (((1,), (0,)), ((), ())), preferred_element_type=f32)


def dot_t(left, right):
    return lax.dot_general(left, right, (((0,), (0,)), ((), ())), preferred_element_type=f32)


def dot_rt(left, right):
    return lax.dot_general(left, right, (((1,), (1,)), ((), ())), preferred_element_type=f32)


def silu_half(half):
    th = jnp.tanh(half)
    prod = half * th
    return half + prod, (0.5 + 0.5 * th) * ((1.0 + half) - prod)


def split_cols(value):
    high = value.astype(bf16)
    low = (value - high.astype(f32)).astype(bf16)
    return jnp.concatenate([high, low], -1)


def up(value):
    return pltpu.roll(value, NODES - 1, 1)


def down(value):
    return pltpu.roll(value, 1, 1)


def flat(value):
    return value.reshape(-1, value.shape[-1])


def node_rows(value):
    return value.reshape(-1, NODES, value.shape[-1])


def row_ids():
    return lax.broadcasted_iota(jnp.int32, (1, NODES, 128), 1)


def couple_slots(plane, filled):
    count, rows, width = plane.shape
    slots = rows // NODES
    parts = plane.reshape(count, slots, NODES, width)
    ids = row_ids()
    done = []
    for s in range(slots):
        here = parts[:, s]
        if s + 1 < slots:
            take = (ids == NODES - 1) & (s + 1 < filled)
            here = here + jnp.where(take, up(parts[:, s + 1]), 0.0)
        if s > 0:
            here = here + jnp.where(ids == 0, down(parts[:, s - 1]), 0.0)
            here = jnp.where(s < filled, here, 0.0)
        done.append(here[:, None])
    return jnp.concatenate(done, 1).reshape(plane.shape)


def elements(x_len, y_len, body):
    ey = y_len // NODES
    total = (x_len // NODES) * ey

    def step(e, carry):
        x0 = pl.multiple_of((e // ey) * NODES, NODES)
        y0 = pl.multiple_of((e % ey) * NODES, NODES)
        body(x0, y0)
        return carry

    lax.fori_loop(0, total, step, 0)


def edges_forward(h_ref, w_one, half_bias, filled, sum_ref, slope_ref):
    x_len, y_len, rows, width = h_ref.shape
    inner = row_ids() < NODES - 1

    def body(x0, y0):
        ys = pl.ds(y0, NODES)
        prev = None
        here = h_ref[x0, ys].astype(f32)
        for i in range(NODES):
            parts = []
            nxt = None
            if i < NODES - 1:
                nxt = h_ref[x0 + i + 1, ys].astype(f32)
                parts.append((nxt - here).astype(bf16))
            parts.append((here[1:] - here[:-1]).astype(bf16))
            cols = node_rows(here)
            parts.append((up(cols) - cols).reshape(here.shape).astype(bf16))
            half = dot(flat(jnp.concatenate(parts, 0)), w_one).reshape(-1, rows, width) + half_bias
            act, slope = silu_half(half)
            act = act.astype(bf16).astype(f32)
            at = 0
            total = prev
            prev = None
            if i < NODES - 1:
                prev = act[:NODES]
                total = -prev if total is None else total - prev
                slope_ref[0, x0 + i, ys] = slope[:NODES]
                at = NODES
            along_y = act[at : at + NODES - 1]
            slope_ref[1, x0 + i, pl.ds(y0, NODES - 1)] = slope[at : at + NODES - 1]
            at += NODES - 1
            along_z = jnp.where(inner, node_rows(act[at:]), 0.0)
            slope_z = jnp.where(inner, node_rows(slope[at:]), 0.0)
            slope_ref[2, x0 + i, ys] = slope_z.reshape(here.shape)
            total = total + (down(along_z) - along_z).reshape(here.shape)
            total = jnp.concatenate(
                [
                    total[:1] - along_y[:1],
                    total[1:-1] + (along_y[:-1] - along_y[1:]),
                    total[-1:] + along_y[-1:],
                ],
                0,
            )
            sum_ref[x0 + i, ys] = couple_slots(total, filled)
            here = nxt

    elements(x_len, y_len, body)


def couple_columns(sum_ref):
    x_len, y_len = sum_ref.shape[:2]
    for cut in range(NODES, x_len, NODES):
        both = sum_ref[cut - 1] + sum_ref[cut]
        sum_ref[cut - 1] = both
        sum_ref[cut] = both
    for cut in range(NODES, y_len, NODES):
        both = sum_ref[:, cut - 1] + sum_ref[:, cut]
        sum_ref[:, cut - 1] = both
        sum_ref[:, cut] = both


def face_place(sc_ref, axis, kind, last):
    return jnp.where((sc_ref[1 + axis] + kind) % 2 == 0, last, 0)


def end_rows(values, filled, take_top):
    picked = values(0)
    slots = values.slots
    for s in range(slots):
        picked = jnp.where(take_top & (filled == s + 1), values(s * NODES + NODES - 1), picked)
    return picked


class RowReader:
    def __init__(self, slots, read):
        self.slots = slots
        self.read = read

    def __call__(self, row):
        return self.read(row)


def takes_top(sc_ref, kind):
    return (sc_ref[3] + kind) % 2 == 0


def write_faces(sc_ref, sum_ref, faces, counts):
    x_len, y_len, rows, width = sum_ref.shape
    nx, ny, nz = counts
    reader = RowReader(rows // NODES, lambda row: sum_ref[:, :, row])
    for kind in range(nx):
        faces[kind][...] = sum_ref[face_place(sc_ref, 0, kind, x_len - 1)]
    for kind in range(ny):
        faces[nx + kind][...] = sum_ref[:, face_place(sc_ref, 1, kind, y_len - 1)]
    for kind in range(nz):
        faces[nx + ny + kind][...] = end_rows(reader, sc_ref[0], takes_top(sc_ref, kind))


def add_halo(sc_ref, from_ref, halo, into_ref, counts):
    x_len, y_len, rows, width = from_ref.shape
    nx, ny, nz = counts

    def copy(x, carry):
        into_ref[x] = from_ref[x]
        return carry

    lax.fori_loop(0, x_len, copy, 0)
    for kind in range(nx):
        into_ref[face_place(sc_ref, 0, kind, x_len - 1)] += halo[kind][...]
    for kind in range(ny):
        into_ref[:, face_place(sc_ref, 1, kind, y_len - 1)] += halo[nx + kind][...]
    if nz:
        got = [halo[nx + ny + kind][...] for kind in range(nz)]
        tops = [takes_top(sc_ref, kind) for kind in range(nz)]
        from_below = sum(jnp.where(top, 0.0, value) for top, value in zip(tops, got))
        from_above = sum(jnp.where(top, value, 0.0) for top, value in zip(tops, got))
        into_ref[:, :, 0] += from_below
        for s in range(rows // NODES):
            into_ref[:, :, s * NODES + NODES - 1] += jnp.where(sc_ref[0] == s + 1, from_above, 0.0)


def fix_y_kernel(counts, sc_ref, *refs):
    nx, ny, nz = counts
    got, faces, outs = refs[:nx], refs[nx : nx + ny], refs[nx + ny :]
    x_len = faces[0].shape[0]
    for k in range(ny):
        outs[k][...] = faces[k][...]
    for kind in range(nx):
        place = face_place(sc_ref, 0, kind, x_len - 1)
        for k in range(ny):
            y_len = got[kind].shape[0]
            outs[k][place] += got[kind][face_place(sc_ref, 1, k, y_len - 1)]


def fix_z_kernel(counts, sc_ref, *refs):
    nx, ny, nz = counts
    got_x, refs = refs[:nx], refs[nx:]
    got_y, refs = refs[:ny], refs[ny:]
    faces, outs = refs[:nz], refs[nz:]
    x_len, y_len, width = faces[0].shape
    for k in range(nz):
        outs[k][...] = faces[k][...]
    for k in range(nz):
        top = takes_top(sc_ref, k)
        for kind in range(nx):
            ref = got_x[kind]
            reader = RowReader(ref.shape[1] // NODES, lambda row, ref=ref: ref[:, row])
            outs[k][face_place(sc_ref, 0, kind, x_len - 1)] += end_rows(reader, sc_ref[0], top)
        for kind in range(ny):
            ref = got_y[kind]
            reader = RowReader(ref.shape[1] // NODES, lambda row, ref=ref: ref[:, row])
            add = end_rows(reader, sc_ref[0], top)
            first = face_place(sc_ref, 1, kind, 1) == 0
            outs[k][:, 0] += jnp.where(first, add, 0.0)
            outs[k][:, y_len - 1] += jnp.where(first, 0.0, add)


def write_inverse(sc_ref, inv_ref, sizes):
    y_len, rows, width = inv_ref.shape
    filled, at_y, at_z = sc_ref[0], sc_ref[2], sc_ref[3]
    ids = lax.broadcasted_iota(jnp.int32, (rows, width), 0)
    node = ids % NODES
    low = (node == 0) & ((ids >= NODES) | (at_z > 0))
    high = (node == NODES - 1) & ((ids < (filled - 1) * NODES) | (at_z < sizes[2] - 1))
    along_z = jnp.where(low | high, 0.5, 1.0).astype(f32)
    for y in range(y_len):
        inv_ref[y] = along_z * end_factor(y, y_len, at_y, sizes[1])


def end_factor(place, length, position, size):
    whole = place + position * length
    low = (place % NODES == 0) & (whole > 0)
    high = (place % NODES == NODES - 1) & (whole < length * size - 1)
    return jnp.where(low | high, 0.5, 1.0).astype(f32)


CHUNK = 4


def scale_planes(sc_ref, inv_ref, x, block, x_len, size_x):
    inv = inv_ref[...]
    parts = [block[c] * (inv * end_factor(x + c, x_len, sc_ref[1], size_x)) for c in range(CHUNK)]
    return jnp.stack(parts, 0)


def node_forward(sc_ref, x, inv_ref, size_x, sum_ref, h_ref, weights, layer):
    edge_w, node_in, node_out, biases = weights
    at = pl.ds(x, CHUNK)
    scaled = scale_planes(sc_ref, inv_ref, x, sum_ref[at], sum_ref.shape[0], size_x)
    pair = split_cols(flat(scaled))
    w_two = edge_w[layer, 1]
    joined = jnp.concatenate([flat(h_ref[at]), dot(pair, jnp.concatenate([w_two, w_two], 0)).astype(bf16)], -1)
    half = jnp.bfloat16(0.5)
    act, slope = silu_half(dot(joined, node_in[layer] * half) + 0.5 * biases[layer, pl.ds(1, 1)])
    return pair[:, :128], act.astype(bf16), slope


def node_backward(sc_ref, x, inv_ref, size_x, grad, feat, scaled, act, slope, weights, layer, sum_ref, base_ref, grads):
    edge_w, node_in, node_out, biases = weights
    shape = (CHUNK,) + sum_ref.shape[1:]
    at = pl.ds(x, CHUNK)
    dpn = (dot_rt(grad, node_out[layer]) * slope).astype(bf16)
    grads[pl.ds(0, 128)] += dot_t(act, grad)
    both = dot_t(dpn, jnp.concatenate([feat, scaled], -1))
    grads[pl.ds(128, 128)] += both[:, :128]
    grads[pl.ds(256, 128)] += both[:, 128:]
    grads[pl.ds(384, NODES)] += jnp.sum(dpn.astype(f32).reshape(-1, NODES, 128), 0)
    dx = dot_rt(dpn, node_in[layer])
    base_ref[at] = (grad.astype(f32) + dx[:, :128]).reshape(shape)
    share = scale_planes(sc_ref, inv_ref, x, dx[:, 128:].reshape(shape), sum_ref.shape[0], size_x)
    joined = couple_slots(share.reshape((-1,) + shape[2:]), sc_ref[0])
    sum_ref[at] = joined.reshape(shape)


def edges_backward(q_ref, slope_ref, edge_ref, bias_acc):
    x_len, y_len, rows, width = q_ref.shape

    def body(x0, y0):
        ys = pl.ds(y0, NODES)
        prev = None
        here = q_ref[x0, ys]
        bias = jnp.zeros((NODES, width), f32)
        for i in range(NODES):
            total = prev
            prev = None
            nxt = None
            if i < NODES - 1:
                nxt = q_ref[x0 + i + 1, ys]
                prev = ((nxt - here) * slope_ref[0, x0 + i, ys]).astype(bf16).astype(f32)
                total = -prev if total is None else total - prev
                bias = bias + jnp.sum(node_rows(prev), 0)
            along_y = (here[1:] - here[:-1]) * slope_ref[1, x0 + i, pl.ds(y0, NODES - 1)]
            along_y = along_y.astype(bf16).astype(f32)
            cols = node_rows(here)
            along_z = (up(cols) - cols) * node_rows(slope_ref[2, x0 + i, ys])
            along_z = along_z.astype(bf16).astype(f32)
            bias = bias + jnp.sum(node_rows(along_y), 0) + jnp.sum(along_z, 0)
            total = total + (down(along_z) - along_z).reshape(here.shape)
            total = jnp.concatenate(
                [
                    total[:1] - along_y[:1],
                    total[1:-1] + (along_y[:-1] - along_y[1:]),
                    total[-1:] + along_y[-1:],
                ],
                0,
            )
            edge_ref[x0 + i, ys] = total
            here = nxt
        bias_acc[...] += bias

    elements(x_len, y_len, body)


def planes(count, body):
    def step(c, carry):
        body(pl.multiple_of(c * CHUNK, CHUNK))
        return carry

    lax.fori_loop(0, count // CHUNK, step, 0)


def half_weights(weights, layer):
    edge_w, node_in, node_out, biases = weights
    return edge_w[layer, 0] * jnp.bfloat16(0.5), 0.5 * biases[layer, pl.ds(0, 1)]


def first_kernel(counts, sizes, sc, edge_w_in, biases_in, h_in, *refs):
    sums, slopes = refs[:2]
    faces, (h, edge_w, biases, sems) = refs[2:-4], refs[-4:]
    moves = [
        pltpu.make_async_copy(source, target, sems.at[k])
        for k, (source, target) in enumerate(((h_in, h), (edge_w_in, edge_w), (biases_in, biases)))
    ]
    for move in moves:
        move.start()
    for move in moves:
        move.wait()
    w_one, bias = half_weights((edge_w, None, None, biases), 0)
    edges_forward(h, w_one, bias, sc[0], sums, slopes)
    couple_columns(sums)
    write_faces(sc, sums, faces, counts)


def middle_kernel(counts, sizes, sc, edge_w, node_in, node_out, biases, sums_in, h, *refs):
    weights = (edge_w, node_in, node_out, biases)
    n = sum(counts)
    halo, refs = refs[:n], refs[n:]
    scaled_ref, act_ref, slope_ref, next_ref, sums, slopes = refs[:6]
    faces, (work, inv) = refs[6:-2], refs[-2:]
    add_halo(sc, sums_in, halo, work, counts)
    write_inverse(sc, inv, sizes)
    shape = (CHUNK,) + h.shape[1:]

    def body(x):
        at = pl.ds(x, CHUNK)
        scaled, act, slope = node_forward(sc, x, inv, sizes[0], work, h, weights, 0)
        scaled_ref[at] = scaled.reshape(shape)
        act_ref[at] = act.reshape(shape)
        slope_ref[at] = slope.reshape(shape)
        moved = flat(h[at]).astype(f32) + dot(act, node_out[0])
        next_ref[at] = moved.astype(bf16).reshape(shape)

    planes(h.shape[0], body)
    w_one, bias = half_weights(weights, 1)
    edges_forward(next_ref, w_one, bias, sc[0], sums, slopes)
    couple_columns(sums)
    write_faces(sc, sums, faces, counts)


def turn_kernel(counts, sizes, sc, edge_w, node_in, node_out, biases, sums_in, h, g_ref, *refs):
    weights = (edge_w, node_in, node_out, biases)
    n = sum(counts)
    halo, refs = refs[:n], refs[n:]
    base, sums, keep, send = refs[:4]
    faces, (work, inv, grads) = refs[4:-3], refs[-3:]
    add_halo(sc, sums_in, halo, work, counts)
    write_inverse(sc, inv, sizes)
    grads[...] = jnp.zeros_like(grads)
    live = (lax.broadcasted_iota(jnp.int32, (1, 1, h.shape[2], 128), 2) < sc[0] * NODES).astype(f32)

    def body(x):
        at = pl.ds(x, CHUNK)
        scaled, act, slope = node_forward(sc, x, inv, sizes[0], work, h, weights, 1)
        grad = flat((g_ref[at].astype(f32) * live).astype(bf16))
        node_backward(
            sc, x, inv, sizes[0], grad, flat(h[at]), scaled, act, slope, weights, 1, sums, base, grads
        )

    planes(h.shape[0], body)
    couple_columns(sums)
    write_faces(sc, sums, faces, counts)
    write_halves(sc, halving_steps(sizes)[0], grads, keep, send)


def back_to_state(counts, sc, weights, layer, sums_in, halo, h, base, slopes, work, grads, row, use):
    edge_w = weights[0]
    add_halo(sc, sums_in, halo, work, counts)
    shape = (CHUNK,) + h.shape[1:]
    w_two = edge_w[layer, 1]
    w_two = jnp.concatenate([w_two, w_two], 1)
    w_one = edge_w[layer, 0]
    w_one = jnp.concatenate([w_one, w_one], 1)

    def to_q(x):
        at = pl.ds(x, CHUNK)
        work[at] = dot_rt(split_cols(flat(work[at])), w_two).reshape(shape)

    planes(h.shape[0], to_q)
    edges_backward(work, slopes, work, grads.at[pl.ds(row + 128, NODES)])

    def body(x):
        at = pl.ds(x, CHUNK)
        pair = split_cols(flat(work[at]))
        both = dot_t(flat(h[at]), pair)
        grads[pl.ds(row, 128)] += both[:, :128] + both[:, 128:]
        use(x, (flat(base[at]) + dot_rt(pair, w_one)).astype(bf16))

    planes(h.shape[0], body)


def join_kernel(
    counts, sizes, sc, edge_w, node_in, node_out, biases,
    sums_in, h, base_in, slopes, h0, scaled0, act0, slope0, *refs
):
    weights = (edge_w, node_in, node_out, biases)
    n = sum(counts)
    halo, refs = refs[:n], refs[n:]
    base, sums, keep, send = refs[:4]
    faces, (work, inv, grads) = refs[4:-3], refs[-3:]
    write_inverse(sc, inv, sizes)
    grads[...] = jnp.zeros_like(grads)

    def use(x, grad):
        at = pl.ds(x, CHUNK)
        node_backward(
            sc, x, inv, sizes[0], grad, flat(h0[at]), flat(scaled0[at]), flat(act0[at]), flat(slope0[at]),
            weights, 0, sums, base, grads,
        )

    back_to_state(counts, sc, weights, 1, sums_in, halo, h, base_in, slopes, work, grads, 384 + NODES, use)
    couple_columns(sums)
    write_faces(sc, sums, faces, counts)
    write_halves(sc, halving_steps(sizes)[0], grads, keep, send)


def last_kernel(counts, sizes, sc, edge_w, node_in, node_out, biases, sums_in, h, base_in, slopes, *refs):
    weights = (edge_w, node_in, node_out, biases)
    n = sum(counts)
    halo, refs = refs[:n], refs[n:]
    grad_ref, grads, work = refs
    grads[...] = jnp.zeros_like(grads)
    shape = (CHUNK,) + h.shape[1:]

    def use(x, grad):
        grad_ref[pl.ds(x, CHUNK)] = grad.reshape(shape)

    back_to_state(counts, sc, weights, 0, sums_in, halo, h, base_in, slopes, work, grads, 0, use)


def finish_kernel(scale, last_rows, sc, edge_w, node_in, both, sum1, edge_grads, in_grads, out_grads, bias_grads):
    width = edge_w.shape[-1]

    def rows_of(part, start, count=width):
        ref, offset = part
        return ref[pl.ds(offset + start, count)] * scale

    def bias_of(part, start):
        return jnp.sum(rows_of(part, start, NODES), 0, keepdims=True)

    end = 3 * width
    last, sum0 = (both, 0), (both, last_rows)
    firsts = ((last, 0), (sum0, end + NODES))
    for layer, part in enumerate((sum0, (sum1, 0))):
        out_grads[layer] = rows_of(part, 0)
        in_grads[layer, pl.ds(0, width)] = rows_of(part, width).T
        bias_grads[layer, pl.ds(1, 1)] = bias_of(part, end)
        source, start = firsts[layer]
        edge_grads[layer, 0] = rows_of(source, start)
        bias_grads[layer, pl.ds(0, 1)] = bias_of(source, start + width)
        mixed = rows_of(part, 2 * width).T
        high = mixed.astype(bf16)
        low = (mixed - high.astype(f32)).astype(bf16)
        lower = node_in[layer, pl.ds(width, width)]
        edge_grads[layer, 1] = dot_rt(high, lower) + dot_rt(low, lower)
        w_two = edge_w[layer, 1]
        in_grads[layer, pl.ds(width, width)] = dot_t(w_two, high) + dot_t(w_two, low)


def call(kernel, name, inputs, outs, scratch=(), flops=0, where=VM):
    total = sum(math.prod(o.shape) * o.dtype.itemsize for o in outs)
    total += sum(math.prod(i.shape) * i.dtype.itemsize for i in inputs)
    return pl.pallas_call(
        kernel,
        name=name,
        out_shape=tuple(outs),
        in_specs=[SM] + [where] * (len(inputs) - 1),
        out_specs=tuple([VM] * len(outs)),
        scratch_shapes=list(scratch),
        compiler_params=pltpu.CompilerParams(vmem_limit_bytes=VMEM_LIMIT),
        cost_estimate=pl.CostEstimate(flops=flops, bytes_accessed=total, transcendentals=0),
    )(*inputs)


def pairs(size, kind):
    return [
        pair for low in range(kind, size - 1, 2) for pair in ((low, low + 1), (low + 1, low))
    ]


def hops(size):
    found = []
    hop = 1
    while hop < size:
        found.append(hop)
        hop *= 2
    return found


def halving_steps(sizes):
    steps = [(1, hop) for hop in hops(sizes[1])[:1]]
    steps += [(0, hop) for hop in hops(sizes[0])]
    return steps + [(1, hop) for hop in hops(sizes[1])[1:]]


def padded_rows(rows, sizes):
    unit = NODES << len(halving_steps(sizes))
    return -(-rows // unit) * unit


def bit_of(sc_ref, step):
    axis, hop = step
    return (sc_ref[1 + axis] // hop) % 2


def write_halves(sc_ref, step, from_ref, keep, send):
    half = keep.shape[0]
    bit = bit_of(sc_ref, step)
    keep[...] = from_ref[pl.ds(pl.multiple_of(bit * half, NODES), half)]
    send[...] = from_ref[pl.ds(pl.multiple_of((1 - bit) * half, NODES), half)]


def halve_kernel(step, sc, keep_in, got, keep, send, total):
    total[...] = keep_in[...] + got[...]
    write_halves(sc, step, total, keep, send)


def add_kernel(sc, left, right, out):
    out[...] = left[...] + right[...]


def join_kernel_of(step, start, sc, value, got, out):
    half = value.shape[0] - start
    bit = bit_of(sc, step)
    if start:
        out[pl.ds(0, start)] = value[pl.ds(0, start)] + got[pl.ds(0, start)]
    out[pl.ds(pl.multiple_of(start + bit * half, NODES), half)] = value[pl.ds(start, half)]
    out[pl.ds(pl.multiple_of(start + (1 - bit) * half, NODES), half)] = got[pl.ds(start, half)]


def stack_kernel(sc, first, left, right, out):
    rows = first.shape[0]
    out[pl.ds(0, rows)] = first[...]
    out[pl.ds(rows, left.shape[0])] = left[...] + right[...]


def swap(value, step):
    axis = ("gx", "gy", "gz")[step[0]]
    return lax.ppermute(value, axis, [(i, i ^ step[1]) for i in range(lax.axis_size(axis))])


def rows_like(rows, width=128):
    return jax.ShapeDtypeStruct((rows, width), f32)


def halve(sc, sizes, keep, send):
    steps = halving_steps(sizes)
    got = swap(send, steps[0])
    for step in steps[1:]:
        keep, got = yield keep, got
        half = rows_like(keep.shape[0] // 2)
        keep, send = call(
            functools.partial(halve_kernel, step), "halve", (sc, keep, got), [half, half],
            [pltpu.VMEM(keep.shape, f32)],
        )
        got = swap(send, step)
    keep, got = yield keep, got
    return keep, got


def sum_all(sc, sizes, keep, send):
    keep, got = yield from halve(sc, sizes, keep, send)
    (value,) = call(add_kernel, "add", (sc, keep, got), [rows_like(keep.shape[0])])
    for hop in hops(sizes[2]):
        got = swap(value, (2, hop))
        value, got = yield value, got
        (value,) = call(add_kernel, "add", (sc, value, got), [rows_like(value.shape[0])])
    for step in reversed(halving_steps(sizes)):
        got = swap(value, step)
        value, got = yield value, got
        out = rows_like(2 * value.shape[0])
        (value,) = call(functools.partial(join_kernel_of, step, 0), "join", (sc, value, got), [out])
    yield value, None


class Background:
    def __init__(self):
        self.active = {}

    def add(self, name, steps):
        self.active[name] = [steps, None]

    def advance(self, entry, tied):
        steps, pending = entry
        try:
            entry[1] = next(steps) if pending is None else steps.send(tied)
        except StopIteration:
            entry[0] = None

    def beside(self, anchor):
        for entry in self.active.values():
            steps, pending = entry
            if steps is None:
                continue
            if pending is None:
                self.advance(entry, None)
            elif pending[1] is not None:
                anchor, tied = lax.optimization_barrier((anchor, pending))
                self.advance(entry, tied)
        return anchor

    def finish(self, name):
        entry = self.active[name]
        while entry[0] is not None:
            done = entry[1]
            if done is not None and done[1] is None:
                return done[0]
            self.advance(entry, done)
        return entry[1]


def on_device(state, cotangent, counts, edge_weights, node_in, node_out, biases):
    x_len, y_len, slots, nodes, width = state.shape
    rows = slots * nodes
    grid = (x_len, y_len, rows, width)
    axes = ("gx", "gy", "gz")
    sizes = tuple(lax.axis_size(a) for a in axes)
    trades = tuple(min(size - 1, 2) for size in sizes)
    nx, ny, nz = trades
    h0 = state.reshape(grid)
    g2 = cotangent.reshape(grid)
    sc = jnp.stack([counts[0]] + [lax.axis_index(a).astype(jnp.int32) for a in axes])

    def sds(shape, kind=f32):
        return jax.ShapeDtypeStruct(shape, kind)

    face_x = sds((y_len, rows, width))
    face_y = sds((x_len, rows, width))
    face_z = sds((x_len, y_len, width))
    face_outs = [face_x] * nx + [face_y] * ny + [face_z] * nz
    full = sds(grid)
    full16 = sds(grid, bf16)
    full3 = sds((3,) + grid)
    work = pltpu.VMEM(grid, f32)
    inv = pltpu.VMEM((y_len, rows, width), f32)
    matmul = 2 * math.prod(grid) * width
    weights = (edge_weights, node_in, node_out, biases)

    def run(kernel, name, inputs, outs, scratch, flops):
        body = functools.partial(kernel, trades, sizes)
        return call(body, name, (sc, *weights, *inputs), outs, scratch, flops * matmul)

    def trade(faces, axis):
        size = lax.axis_size(axis)
        got = [lax.ppermute(face, axis, pairs(size, kind)) for kind, face in reversed(list(enumerate(faces)))]
        return got[::-1]

    background = Background()

    def exchange(faces):
        got_x = trade(background.beside(faces[:nx]), "gx")
        fix = functools.partial(fix_y_kernel, trades)
        faces_y = call(fix, "fix_y", (sc, *got_x, *faces[nx : nx + ny]), [face_y] * ny)
        got_y = trade(background.beside(faces_y), "gy")
        fix = functools.partial(fix_z_kernel, trades)
        faces_z = call(fix, "fix_z", (sc, *got_x, *got_y, *faces[nx + ny :]), [face_z] * nz)
        got_z = background.beside(trade(background.beside(faces_z), "gz"))
        return (*got_x, *got_y, *got_z)

    sums, slopes0, *faces = call(
        functools.partial(first_kernel, trades, sizes), "edges0", (sc, edge_weights, biases, h0), [full, full3] + face_outs,
        [
            pltpu.VMEM(grid, bf16),
            pltpu.VMEM(edge_weights.shape, bf16),
            pltpu.VMEM(biases.shape, f32),
            pltpu.SemaphoreType.DMA((3,)),
        ],
        3 * matmul, pl.BlockSpec(memory_space=pltpu.HBM),
    )
    halo = exchange(faces)
    scaled0, act0, slope0, h1, sums, slopes1, *faces = run(
        middle_kernel, "nodes0_edges1", (sums, h0, *halo),
        [full16, full16, full, full16, full, full3] + face_outs, [work, inv], 8,
    )
    halo = exchange(faces)
    def sum_rows(rows):
        total = padded_rows(rows, sizes)
        return [rows_like(total // 2)] * 2, pltpu.VMEM((total, width), f32)

    halves, scratch = sum_rows(3 * width + NODES)
    base, sums, keep, send, *faces = run(
        turn_kernel, "nodes1_back", (sums, h1, g2, *halo), [full, full] + halves + face_outs, [work, inv, scratch], 10
    )
    background.add("layer1", sum_all(sc, sizes, keep, send))
    halo = exchange(faces)
    halves, scratch = sum_rows(4 * width + 2 * NODES)
    base, sums, keep, send, *faces = run(
        join_kernel, "edges1_back_nodes0_back", (sums, h1, base, slopes1, h0, scaled0, act0, slope0, *halo),
        [full, full] + halves + face_outs, [work, inv, scratch], 12,
    )
    background.add("layer0", halve(sc, sizes, keep, send))
    halo = exchange(faces)
    tail_rows = width + NODES
    grad0, last = run(
        last_kernel, "edges0_back", (sums, h0, base, slopes0, *halo), [full16, rows_like(tail_rows)], [work], 6
    )
    last = background.beside(last)
    summed1 = background.finish("layer1")
    keep, got = background.finish("layer0")
    (value,) = call(stack_kernel, "stack", (sc, last, keep, got), [rows_like(tail_rows + keep.shape[0])])
    for hop in hops(sizes[2]):
        (value,) = call(add_kernel, "add", (sc, value, swap(value, (2, hop))), [rows_like(value.shape[0])])
    for step in reversed(halving_steps(sizes)):
        out = rows_like(2 * value.shape[0] - tail_rows)
        body = functools.partial(join_kernel_of, step, tail_rows)
        (value,) = call(body, "join", (sc, value, swap(value, step)), [out])
    layers_all = 3 * slots * sizes[2] // 4
    nodes_all = x_len * sizes[0] * y_len * sizes[1] * layers_all * nodes
    scale = 1.0 / math.sqrt(nodes_all)
    edge_grads, in_grads, out_grads, bias_grads = call(
        functools.partial(finish_kernel, scale, tail_rows), "finish", (sc, edge_weights, node_in, value, summed1),
        [sds(edge_weights.shape), sds(node_in.shape), sds(node_out.shape), sds(biases.shape)],
    )
    return grad0.reshape(state.shape), edge_grads, in_grads, out_grads, bias_grads


def solution(mesh):
    return jax.shard_map(
        on_device,
        mesh=mesh,
        in_specs=(
            P("gx", "gy", "gz", None, None),
            P("gx", "gy", "gz", None, None),
            P("gz"),
            P(),
            P(),
            P(),
            P(),
        ),
        out_specs=(P("gx", "gy", "gz", None, None), P(), P(), P(), P()),
        check_vma=False,
    )
```

```python
import functools
import math

import jax
import jax.numpy as jnp
from jax import lax
from jax.experimental import pallas as pl
from jax.experimental.pallas import tpu as pltpu
from jax.sharding import PartitionSpec as P

f32 = jnp.float32
bf16 = jnp.bfloat16
NODES = 8
VMEM_LIMIT = 12 * 1024 * 1024
VM = pl.BlockSpec(memory_space=pltpu.VMEM)
SM = pl.BlockSpec(memory_space=pltpu.SMEM)


def dot(left, right):
    return lax.dot_general(left, right, (((1,), (0,)), ((), ())), preferred_element_type=f32)


def dot_t(left, right):
    return lax.dot_general(left, right, (((0,), (0,)), ((), ())), preferred_element_type=f32)


def dot_rt(left, right):
    return lax.dot_general(left, right, (((1,), (1,)), ((), ())), preferred_element_type=f32)


def silu_half(half):
    th = jnp.tanh(half)
    prod = half * th
    return half + prod, (0.5 + 0.5 * th) * ((1.0 + half) - prod)


def split_cols(value):
    high = value.astype(bf16)
    low = (value - high.astype(f32)).astype(bf16)
    return jnp.concatenate([high, low], -1)


def up(value):
    return pltpu.roll(value, NODES - 1, 1)


def down(value):
    return pltpu.roll(value, 1, 1)


def flat(value):
    return value.reshape(-1, value.shape[-1])


def node_rows(value):
    return value.reshape(-1, NODES, value.shape[-1])


def row_ids():
    return lax.broadcasted_iota(jnp.int32, (1, NODES, 128), 1)


def couple_slots(plane, filled):
    count, rows, width = plane.shape
    slots = rows // NODES
    parts = plane.reshape(count, slots, NODES, width)
    ids = row_ids()
    done = []
    for s in range(slots):
        here = parts[:, s]
        if s + 1 < slots:
            take = (ids == NODES - 1) & (s + 1 < filled)
            here = here + jnp.where(take, up(parts[:, s + 1]), 0.0)
        if s > 0:
            here = here + jnp.where(ids == 0, down(parts[:, s - 1]), 0.0)
            here = jnp.where(s < filled, here, 0.0)
        done.append(here[:, None])
    return jnp.concatenate(done, 1).reshape(plane.shape)


def elements(x_len, y_len, body):
    ey = y_len // NODES
    total = (x_len // NODES) * ey

    def step(e, carry):
        x0 = pl.multiple_of((e // ey) * NODES, NODES)
        y0 = pl.multiple_of((e % ey) * NODES, NODES)
        body(x0, y0)
        return carry

    lax.fori_loop(0, total, step, 0)


def edges_forward(h_ref, w_one, half_bias, filled, sum_ref, slope_ref):
    x_len, y_len, rows, width = h_ref.shape
    inner = row_ids() < NODES - 1

    def body(x0, y0):
        ys = pl.ds(y0, NODES)
        prev = None
        here = h_ref[x0, ys].astype(f32)
        for i in range(NODES):
            parts = []
            nxt = None
            if i < NODES - 1:
                nxt = h_ref[x0 + i + 1, ys].astype(f32)
                parts.append((nxt - here).astype(bf16))
            parts.append((here[1:] - here[:-1]).astype(bf16))
            cols = node_rows(here)
            parts.append((up(cols) - cols).reshape(here.shape).astype(bf16))
            half = dot(flat(jnp.concatenate(parts, 0)), w_one).reshape(-1, rows, width) + half_bias
            act, slope = silu_half(half)
            act = act.astype(bf16).astype(f32)
            at = 0
            total = prev
            prev = None
            if i < NODES - 1:
                prev = act[:NODES]
                total = -prev if total is None else total - prev
                slope_ref[0, x0 + i, ys] = slope[:NODES]
                at = NODES
            along_y = act[at : at + NODES - 1]
            slope_ref[1, x0 + i, pl.ds(y0, NODES - 1)] = slope[at : at + NODES - 1]
            at += NODES - 1
            along_z = jnp.where(inner, node_rows(act[at:]), 0.0)
            slope_z = jnp.where(inner, node_rows(slope[at:]), 0.0)
            slope_ref[2, x0 + i, ys] = slope_z.reshape(here.shape)
            total = total + (down(along_z) - along_z).reshape(here.shape)
            total = jnp.concatenate(
                [
                    total[:1] - along_y[:1],
                    total[1:-1] + (along_y[:-1] - along_y[1:]),
                    total[-1:] + along_y[-1:],
                ],
                0,
            )
            sum_ref[x0 + i, ys] = couple_slots(total, filled)
            here = nxt

    elements(x_len, y_len, body)


def couple_columns(sum_ref):
    x_len, y_len = sum_ref.shape[:2]
    for cut in range(NODES, x_len, NODES):
        both = sum_ref[cut - 1] + sum_ref[cut]
        sum_ref[cut - 1] = both
        sum_ref[cut] = both
    for cut in range(NODES, y_len, NODES):
        both = sum_ref[:, cut - 1] + sum_ref[:, cut]
        sum_ref[:, cut - 1] = both
        sum_ref[:, cut] = both


def face_place(sc_ref, axis, kind, last):
    return jnp.where((sc_ref[1 + axis] + kind) % 2 == 0, last, 0)


def end_rows(values, filled, take_top):
    picked = values(0)
    slots = values.slots
    for s in range(slots):
        picked = jnp.where(take_top & (filled == s + 1), values(s * NODES + NODES - 1), picked)
    return picked


class RowReader:
    def __init__(self, slots, read):
        self.slots = slots
        self.read = read

    def __call__(self, row):
        return self.read(row)


def takes_top(sc_ref, kind):
    return (sc_ref[3] + kind) % 2 == 0


def write_faces(sc_ref, sum_ref, faces, counts):
    x_len, y_len, rows, width = sum_ref.shape
    nx, ny, nz = counts
    reader = RowReader(rows // NODES, lambda row: sum_ref[:, :, row])
    for kind in range(ny):
        faces[kind][...] = sum_ref[:, face_place(sc_ref, 1, kind, y_len - 1)]
    for kind in range(nz):
        faces[ny + kind][...] = end_rows(reader, sc_ref[0], takes_top(sc_ref, kind))


def add_halo(sc_ref, from_ref, halo, into_ref, counts):
    x_len, y_len, rows, width = from_ref.shape
    nx, ny, nz = counts

    def copy(x, carry):
        into_ref[x] = from_ref[x]
        return carry

    lax.fori_loop(0, x_len, copy, 0)
    for kind in range(nx):
        into_ref[face_place(sc_ref, 0, kind, x_len - 1)] += halo[kind][...]
    for kind in range(ny):
        into_ref[:, face_place(sc_ref, 1, kind, y_len - 1)] += halo[nx + kind][...]
    if nz:
        got = [halo[nx + ny + kind][...] for kind in range(nz)]
        tops = [takes_top(sc_ref, kind) for kind in range(nz)]
        from_below = sum(jnp.where(top, 0.0, value) for top, value in zip(tops, got))
        from_above = sum(jnp.where(top, value, 0.0) for top, value in zip(tops, got))
        into_ref[:, :, 0] += from_below
        for s in range(rows // NODES):
            into_ref[:, :, s * NODES + NODES - 1] += jnp.where(sc_ref[0] == s + 1, from_above, 0.0)


def fix_y_kernel(counts, sc_ref, *refs):
    nx, ny, nz = counts
    got, faces, outs = refs[:nx], refs[nx : nx + ny], refs[nx + ny :]
    x_len = faces[0].shape[0]
    for k in range(ny):
        outs[k][...] = faces[k][...]
    for kind in range(nx):
        place = face_place(sc_ref, 0, kind, x_len - 1)
        for k in range(ny):
            y_len = got[kind].shape[0]
            outs[k][place] += got[kind][face_place(sc_ref, 1, k, y_len - 1)]


def fix_z_kernel(counts, sc_ref, *refs):
    nx, ny, nz = counts
    got_x, refs = refs[:nx], refs[nx:]
    got_y, refs = refs[:ny], refs[ny:]
    faces, outs = refs[:nz], refs[nz:]
    x_len, y_len, width = faces[0].shape
    for k in range(nz):
        outs[k][...] = faces[k][...]
    for k in range(nz):
        top = takes_top(sc_ref, k)
        for kind in range(nx):
            ref = got_x[kind]
            reader = RowReader(ref.shape[1] // NODES, lambda row, ref=ref: ref[:, row])
            outs[k][face_place(sc_ref, 0, kind, x_len - 1)] += end_rows(reader, sc_ref[0], top)
        for kind in range(ny):
            ref = got_y[kind]
            reader = RowReader(ref.shape[1] // NODES, lambda row, ref=ref: ref[:, row])
            add = end_rows(reader, sc_ref[0], top)
            first = face_place(sc_ref, 1, kind, 1) == 0
            outs[k][:, 0] += jnp.where(first, add, 0.0)
            outs[k][:, y_len - 1] += jnp.where(first, 0.0, add)


def write_inverse(sc_ref, inv_ref, sizes):
    y_len, rows, width = inv_ref.shape
    filled, at_y, at_z = sc_ref[0], sc_ref[2], sc_ref[3]
    ids = lax.broadcasted_iota(jnp.int32, (rows, width), 0)
    node = ids % NODES
    low = (node == 0) & ((ids >= NODES) | (at_z > 0))
    high = (node == NODES - 1) & ((ids < (filled - 1) * NODES) | (at_z < sizes[2] - 1))
    along_z = jnp.where(low | high, 0.5, 1.0).astype(f32)
    for y in range(y_len):
        inv_ref[y] = along_z * end_factor(y, y_len, at_y, sizes[1])


def end_factor(place, length, position, size):
    whole = place + position * length
    low = (place % NODES == 0) & (whole > 0)
    high = (place % NODES == NODES - 1) & (whole < length * size - 1)
    return jnp.where(low | high, 0.5, 1.0).astype(f32)


CHUNK = 4


def scale_planes(sc_ref, inv_ref, x, block, x_len, size_x):
    inv = inv_ref[...]
    parts = [block[c] * (inv * end_factor(x + c, x_len, sc_ref[1], size_x)) for c in range(block.shape[0])]
    return jnp.stack(parts, 0)


def node_forward(scaled, feat, weights, layer):
    edge_w, node_in, node_out, biases = weights
    pair = split_cols(scaled)
    w_two = edge_w[layer, 1]
    joined = jnp.concatenate([feat, dot(pair, jnp.concatenate([w_two, w_two], 0)).astype(bf16)], -1)
    half = jnp.bfloat16(0.5)
    act, slope = silu_half(dot(joined, node_in[layer] * half) + 0.5 * biases[layer, pl.ds(1, 1)])
    return pair[:, :128], act.astype(bf16), slope


def node_slopes(grad, slope, weights, layer):
    return (dot_rt(grad, weights[2][layer]) * slope).astype(bf16)


def node_backward(sc_ref, x, inv_ref, size_x, grad, feat, scaled, act, slope, weights, layer, sum_ref, base_ref, grads):
    shape = (CHUNK,) + sum_ref.shape[1:]
    at = pl.ds(x, CHUNK)
    dpn = node_slopes(grad, slope, weights, layer)
    grads[pl.ds(0, 128)] += dot_t(act, grad)
    both = dot_t(dpn, jnp.concatenate([feat, scaled], -1))
    grads[pl.ds(128, 128)] += both[:, :128]
    grads[pl.ds(256, 128)] += both[:, 128:]
    grads[pl.ds(384, NODES)] += jnp.sum(dpn.astype(f32).reshape(-1, NODES, 128), 0)
    dx = dot_rt(dpn, weights[1][layer])
    base_ref[at] = (grad.astype(f32) + dx[:, :128]).reshape(shape)
    share = scale_planes(sc_ref, inv_ref, x, dx[:, 128:].reshape(shape), sum_ref.shape[0], size_x)
    joined = couple_slots(share.reshape((-1,) + shape[2:]), sc_ref[0])
    sum_ref[at] = joined.reshape(shape)


def couple_plane(plane):
    y_len = plane.shape[0]
    parts = [plane[y] for y in range(y_len)]
    for cut in range(NODES, y_len, NODES):
        both = parts[cut - 1] + parts[cut]
        parts[cut - 1] = parts[cut] = both
    return jnp.stack(parts, 0)


def along_y(plane, combine):
    return [
        combine(plane[y : y + NODES - 1], plane[y + 1 : y + NODES], y) for y in range(0, plane.shape[0], NODES)
    ]


def spread_plane(sign, edge_x, edges_y, edge_z):
    total = sign * edge_x + (down(edge_z) - edge_z).reshape(edge_x.shape)
    parts = []
    for k, edge in enumerate(edges_y):
        here = total[k * NODES : (k + 1) * NODES]
        parts += [here[:1] - edge[:1], here[1:-1] + (edge[:-1] - edge[1:]), here[-1:] + edge[-1:]]
    return jnp.concatenate(parts, 0)


def plane_forward(low, high, at_high, w_one, half_bias, filled):
    y_len, rows, width = low.shape
    here = jnp.where(at_high, high, low)
    cols = node_rows(here)
    parts = [(high - low).astype(bf16)]
    parts += along_y(here, lambda lower, upper, y: (upper - lower).astype(bf16))
    parts.append((up(cols) - cols).reshape(here.shape).astype(bf16))
    half = dot(flat(jnp.concatenate(parts, 0)), w_one).reshape(-1, rows, width) + half_bias
    act = silu_half(half)[0].astype(bf16).astype(f32)
    at = y_len
    edges_y = []
    for _ in range(y_len // NODES):
        edges_y.append(act[at : at + NODES - 1])
        at += NODES - 1
    edge_z = jnp.where(row_ids() < NODES - 1, node_rows(act[at:]), 0.0)
    total = spread_plane(jnp.where(at_high, 1.0, -1.0), act[:y_len], edges_y, edge_z)
    return couple_plane(couple_slots(total, filled))


def plane_backward(low, high, at_high, slope_x, slope_y, slope_z):
    here = jnp.where(at_high, high, low)
    cols = node_rows(here)
    edge_x = ((high - low) * slope_x).astype(bf16).astype(f32)
    edges_y = along_y(
        here, lambda lower, upper, y: ((upper - lower) * slope_y[y : y + NODES - 1]).astype(bf16).astype(f32)
    )
    edge_z = ((up(cols) - cols) * node_rows(slope_z)).astype(bf16).astype(f32)
    return spread_plane(jnp.where(at_high, 1.0, -1.0), edge_x, edges_y, edge_z)


def face_planes(sc_ref, kind, x_len):
    place = face_place(sc_ref, 0, kind, x_len - 1)
    at_high = place > 0
    return place, jnp.where(at_high, x_len - 2, 0), at_high


def halo_planes(sc_ref, from_ref, halo, kind, start, into_ref, counts):
    x_len, y_len, rows, width = from_ref.shape
    nx, ny, nz = counts
    for c in range(2):
        into_ref[c] = from_ref[start + c]
    into_ref[face_place(sc_ref, 0, kind, x_len - 1) - start] += halo[kind][...]
    for c in range(2):
        for k in range(ny):
            into_ref[c, face_place(sc_ref, 1, k, y_len - 1)] += halo[nx + k][start + c]
        for k in range(nz):
            got = halo[nx + ny + k][start + c]
            top = takes_top(sc_ref, k)
            into_ref[c, :, 0] += jnp.where(top, 0.0, got)
            for s in range(rows // NODES):
                into_ref[c, :, s * NODES + NODES - 1] += jnp.where(top & (sc_ref[0] == s + 1), got, 0.0)


def edges_backward(q_ref, slope_ref, edge_ref, bias_acc):
    x_len, y_len, rows, width = q_ref.shape

    def body(x0, y0):
        ys = pl.ds(y0, NODES)
        prev = None
        here = q_ref[x0, ys]
        bias = jnp.zeros((NODES, width), f32)
        for i in range(NODES):
            total = prev
            prev = None
            nxt = None
            if i < NODES - 1:
                nxt = q_ref[x0 + i + 1, ys]
                prev = ((nxt - here) * slope_ref[0, x0 + i, ys]).astype(bf16).astype(f32)
                total = -prev if total is None else total - prev
                bias = bias + jnp.sum(node_rows(prev), 0)
            along_y = (here[1:] - here[:-1]) * slope_ref[1, x0 + i, pl.ds(y0, NODES - 1)]
            along_y = along_y.astype(bf16).astype(f32)
            cols = node_rows(here)
            along_z = (up(cols) - cols) * node_rows(slope_ref[2, x0 + i, ys])
            along_z = along_z.astype(bf16).astype(f32)
            bias = bias + jnp.sum(node_rows(along_y), 0) + jnp.sum(along_z, 0)
            total = total + (down(along_z) - along_z).reshape(here.shape)
            total = jnp.concatenate(
                [
                    total[:1] - along_y[:1],
                    total[1:-1] + (along_y[:-1] - along_y[1:]),
                    total[-1:] + along_y[-1:],
                ],
                0,
            )
            edge_ref[x0 + i, ys] = total
            here = nxt
        bias_acc[...] += bias

    elements(x_len, y_len, body)


def planes(count, body):
    def step(c, carry):
        body(pl.multiple_of(c * CHUNK, CHUNK))
        return carry

    lax.fori_loop(0, count // CHUNK, step, 0)


def half_weights(weights, layer):
    edge_w, node_in, node_out, biases = weights
    return edge_w[layer, 0] * jnp.bfloat16(0.5), 0.5 * biases[layer, pl.ds(0, 1)]


def first_kernel(counts, sizes, sc, edge_w, biases, h, sums, slopes, *faces):
    w_one, bias = half_weights((edge_w, None, None, biases), 0)
    edges_forward(h, w_one, bias, sc[0], sums, slopes)
    couple_columns(sums)
    write_faces(sc, sums, faces, counts)


def first_face_kernel(counts, sizes, sc, edge_w, biases, h, *faces):
    w_one, bias = half_weights((edge_w, None, None, biases), 0)
    for kind, face in enumerate(faces):
        place, start, at_high = face_planes(sc, kind, h.shape[0])
        face[...] = plane_forward(
            h[start].astype(f32), h[start + 1].astype(f32), at_high, w_one, bias, sc[0]
        )


def middle_face_kernel(counts, sizes, sc, edge_w, node_in, node_out, biases, sums_in, h, *refs):
    weights = (edge_w, node_in, node_out, biases)
    n = sum(counts)
    halo, faces, (pair, inv) = refs[:n], refs[n:-2], refs[-2:]
    write_inverse(sc, inv, sizes)
    w_one, bias = half_weights(weights, 1)
    x_len = h.shape[0]
    for kind, face in enumerate(faces):
        place, start, at_high = face_planes(sc, kind, x_len)
        halo_planes(sc, sums_in, halo, kind, start, pair, counts)
        sums_at = flat(scale_planes(sc, inv, start, pair[...], x_len, sizes[0]))
        feat = flat(h[pl.ds(start, 2)])
        scaled, act, slope = node_forward(sums_at, feat, weights, 0)
        moved = (feat.astype(f32) + dot(act, node_out[0])).astype(bf16).astype(f32).reshape(pair.shape)
        face[...] = plane_forward(moved[0], moved[1], at_high, w_one, bias, sc[0])


def face_share(sc, sizes, inv, place, x_len, grad, slope, weights, layer, shape):
    dpn = node_slopes(grad, slope, weights, layer)
    dx = dot_rt(dpn, weights[1][layer, pl.ds(128, 128)]).reshape((1,) + shape)
    share = scale_planes(sc, inv, place, dx, x_len, sizes[0])
    return couple_plane(couple_slots(share[0], sc[0]))


def turn_face_kernel(counts, sizes, sc, edge_w, node_in, node_out, biases, sums_in, h, g_ref, *refs):
    weights = (edge_w, node_in, node_out, biases)
    n = sum(counts)
    halo, faces, (pair, inv) = refs[:n], refs[n:-2], refs[-2:]
    write_inverse(sc, inv, sizes)
    x_len, shape = h.shape[0], h.shape[1:]
    live = (lax.broadcasted_iota(jnp.int32, (1, h.shape[2], 128), 1) < sc[0] * NODES).astype(f32)
    for kind, face in enumerate(faces):
        place, start, at_high = face_planes(sc, kind, x_len)
        halo_planes(sc, sums_in, halo, kind, start, pair, counts)
        plane = pair[place - start][None]
        sums_at = flat(scale_planes(sc, inv, place, plane, x_len, sizes[0]))
        scaled, act, slope = node_forward(sums_at, flat(h[place]), weights, 1)
        grad = flat((g_ref[place].astype(f32) * live).astype(bf16))
        face[...] = face_share(sc, sizes, inv, place, x_len, grad, slope, weights, 1, shape)


def join_face_kernel(counts, sizes, sc, edge_w, node_in, node_out, biases, sums_in, base_in, slopes, slope0, *refs):
    weights = (edge_w, node_in, node_out, biases)
    n = sum(counts)
    halo, faces, (pair, inv) = refs[:n], refs[n:-2], refs[-2:]
    write_inverse(sc, inv, sizes)
    x_len, shape = base_in.shape[0], base_in.shape[1:]
    w_two, w_one = twice(edge_w[1, 1]), twice(edge_w[1, 0])
    for kind, face in enumerate(faces):
        place, start, at_high = face_planes(sc, kind, x_len)
        halo_planes(sc, sums_in, halo, kind, start, pair, counts)
        q = dot_rt(split_cols(flat(pair[...])), w_two).reshape(pair.shape)
        edge = plane_backward(q[0], q[1], at_high, slopes[0, start], slopes[1, place], slopes[2, place])
        grad = (flat(base_in[place]) + dot_rt(split_cols(flat(edge)), w_one)).astype(bf16)
        face[...] = face_share(sc, sizes, inv, place, x_len, grad, flat(slope0[place]), weights, 0, shape)


def twice(weight):
    return jnp.concatenate([weight, weight], 1)


def middle_kernel(counts, sizes, sc, edge_w, node_in, node_out, biases, sums_in, h, *refs):
    weights = (edge_w, node_in, node_out, biases)
    n = sum(counts)
    halo, refs = refs[:n], refs[n:]
    scaled_ref, act_ref, slope_ref, next_ref, sums, slopes = refs[:6]
    faces, (work, inv) = refs[6:-2], refs[-2:]
    add_halo(sc, sums_in, halo, work, counts)
    write_inverse(sc, inv, sizes)
    shape = (CHUNK,) + h.shape[1:]

    def body(x):
        at = pl.ds(x, CHUNK)
        sums_at = flat(scale_planes(sc, inv, x, work[at], h.shape[0], sizes[0]))
        scaled, act, slope = node_forward(sums_at, flat(h[at]), weights, 0)
        scaled_ref[at] = scaled.reshape(shape)
        act_ref[at] = act.reshape(shape)
        slope_ref[at] = slope.reshape(shape)
        moved = flat(h[at]).astype(f32) + dot(act, node_out[0])
        next_ref[at] = moved.astype(bf16).reshape(shape)

    planes(h.shape[0], body)
    w_one, bias = half_weights(weights, 1)
    edges_forward(next_ref, w_one, bias, sc[0], sums, slopes)
    couple_columns(sums)
    write_faces(sc, sums, faces, counts)


def turn_kernel(counts, sizes, sc, edge_w, node_in, node_out, biases, sums_in, h, g_ref, *refs):
    weights = (edge_w, node_in, node_out, biases)
    n = sum(counts)
    halo, refs = refs[:n], refs[n:]
    base, sums, grads = refs[:3]
    faces, (work, inv) = refs[3:-2], refs[-2:]
    add_halo(sc, sums_in, halo, work, counts)
    write_inverse(sc, inv, sizes)
    grads[...] = jnp.zeros_like(grads)
    live = (lax.broadcasted_iota(jnp.int32, (1, 1, h.shape[2], 128), 2) < sc[0] * NODES).astype(f32)

    def body(x):
        at = pl.ds(x, CHUNK)
        sums_at = flat(scale_planes(sc, inv, x, work[at], h.shape[0], sizes[0]))
        scaled, act, slope = node_forward(sums_at, flat(h[at]), weights, 1)
        grad = flat((g_ref[at].astype(f32) * live).astype(bf16))
        node_backward(
            sc, x, inv, sizes[0], grad, flat(h[at]), scaled, act, slope, weights, 1, sums, base, grads
        )

    planes(h.shape[0], body)
    couple_columns(sums)
    write_faces(sc, sums, faces, counts)


def edge_parts(counts, sc, weights, layer, sums_in, halo, h, slopes, work, grads, row):
    add_halo(sc, sums_in, halo, work, counts)
    shape = (CHUNK,) + h.shape[1:]
    w_two = twice(weights[0][layer, 1])

    def to_q(x):
        at = pl.ds(x, CHUNK)
        work[at] = dot_rt(split_cols(flat(work[at])), w_two).reshape(shape)

    planes(h.shape[0], to_q)
    edges_backward(work, slopes, work, grads.at[pl.ds(row + 128, NODES)])


def edge_product(h, x, pair, grads, row):
    both = dot_t(flat(h[pl.ds(x, CHUNK)]), pair)
    grads[pl.ds(row, 128)] += both[:, :128] + both[:, 128:]


def join_kernel(
    counts, sizes, sc, edge_w, node_in, node_out, biases,
    sums_in, h, base_in, slopes, h0, scaled0, act0, slope0, grads1, *refs
):
    weights = (edge_w, node_in, node_out, biases)
    n = sum(counts)
    halo, refs = refs[:n], refs[n:]
    base, sums, keep, send = refs[:4]
    faces, (work, inv, grads) = refs[4:-3], refs[-3:]
    write_inverse(sc, inv, sizes)
    grads[...] = jnp.zeros_like(grads)
    grads[pl.ds(512 + 2 * NODES, grads1.shape[0])] = grads1[...]

    row = 384 + NODES
    edge_parts(counts, sc, weights, 1, sums_in, halo, h, slopes, work, grads, row)
    w_one = twice(edge_w[1, 0])

    def body(x):
        at = pl.ds(x, CHUNK)
        pair = split_cols(flat(work[at]))
        edge_product(h, x, pair, grads, row)
        grad = (flat(base_in[at]) + dot_rt(pair, w_one)).astype(bf16)
        node_backward(
            sc, x, inv, sizes[0], grad, flat(h0[at]), flat(scaled0[at]), flat(act0[at]), flat(slope0[at]),
            weights, 0, sums, base, grads,
        )

    planes(h.shape[0], body)
    couple_columns(sums)
    write_faces(sc, sums, faces, counts)
    write_halves(sc, halving_steps(sizes)[0], grads, keep, send)


def last_kernel(counts, sizes, sc, edge_w, node_in, node_out, biases, sums_in, h, slopes, *refs):
    n = sum(counts)
    halo, (edges, grads) = refs[:n], refs[n:]
    grads[...] = jnp.zeros_like(grads)
    edge_parts(counts, sc, (edge_w,), 0, sums_in, halo, h, slopes, edges, grads, 0)

    def body(x):
        edge_product(h, x, split_cols(flat(edges[pl.ds(x, CHUNK)])), grads, 0)

    planes(h.shape[0], body)


def state_kernel(sc, edge_w, base_in, edges, grad_ref):
    shape = (CHUNK,) + edges.shape[1:]
    w_one = twice(edge_w[0, 0])

    def body(x):
        at = pl.ds(x, CHUNK)
        pair = split_cols(flat(edges[at]))
        grad_ref[at] = (flat(base_in[at]) + dot_rt(pair, w_one)).astype(bf16).reshape(shape)

    planes(edges.shape[0], body)


def finish_kernel(scale, last_rows, sc, edge_w, node_in, both, edge_grads, in_grads, out_grads, bias_grads):
    width = edge_w.shape[-1]

    def rows_of(part, start, count=width):
        ref, offset = part
        return ref[pl.ds(offset + start, count)] * scale

    def bias_of(part, start):
        return jnp.sum(rows_of(part, start, NODES), 0, keepdims=True)

    end = 3 * width
    last, sum0 = (both, 0), (both, last_rows)
    sum1 = (both, last_rows + 512 + 2 * NODES)
    firsts = ((last, 0), (sum0, end + NODES))
    for layer, part in enumerate((sum0, sum1)):
        out_grads[layer] = rows_of(part, 0)
        in_grads[layer, pl.ds(0, width)] = rows_of(part, width).T
        bias_grads[layer, pl.ds(1, 1)] = bias_of(part, end)
        source, start = firsts[layer]
        edge_grads[layer, 0] = rows_of(source, start)
        bias_grads[layer, pl.ds(0, 1)] = bias_of(source, start + width)
        mixed = rows_of(part, 2 * width).T
        high = mixed.astype(bf16)
        low = (mixed - high.astype(f32)).astype(bf16)
        lower = node_in[layer, pl.ds(width, width)]
        edge_grads[layer, 1] = dot_rt(high, lower) + dot_rt(low, lower)
        w_two = edge_w[layer, 1]
        in_grads[layer, pl.ds(width, width)] = dot_t(w_two, high) + dot_t(w_two, low)


def call(kernel, name, inputs, outs, scratch=(), flops=0):
    total = sum(math.prod(o.shape) * o.dtype.itemsize for o in outs)
    total += sum(math.prod(i.shape) * i.dtype.itemsize for i in inputs)
    return pl.pallas_call(
        kernel,
        name=name,
        out_shape=tuple(outs),
        in_specs=[SM] + [VM] * (len(inputs) - 1),
        out_specs=tuple([VM] * len(outs)),
        scratch_shapes=list(scratch),
        compiler_params=pltpu.CompilerParams(vmem_limit_bytes=VMEM_LIMIT),
        cost_estimate=pl.CostEstimate(flops=flops, bytes_accessed=total, transcendentals=0),
    )(*inputs)


def pairs(size, kind):
    return [
        pair for low in range(kind, size - 1, 2) for pair in ((low, low + 1), (low + 1, low))
    ]


def hops(size):
    found = []
    hop = 1
    while hop < size:
        found.append(hop)
        hop *= 2
    return found


def halving_steps(sizes):
    steps = [(1, hop) for hop in hops(sizes[1])[:1]]
    steps += [(0, hop) for hop in hops(sizes[0])]
    return steps + [(1, hop) for hop in hops(sizes[1])[1:]]


def padded_rows(rows, sizes):
    unit = NODES << len(halving_steps(sizes))
    return -(-rows // unit) * unit


def bit_of(sc_ref, step):
    axis, hop = step
    return (sc_ref[1 + axis] // hop) % 2


def write_halves(sc_ref, step, from_ref, keep, send):
    half = keep.shape[0]
    bit = bit_of(sc_ref, step)
    keep[...] = from_ref[pl.ds(pl.multiple_of(bit * half, NODES), half)]
    send[...] = from_ref[pl.ds(pl.multiple_of((1 - bit) * half, NODES), half)]


def halve_kernel(step, sc, keep_in, got, keep, send, total):
    total[...] = keep_in[...] + got[...]
    write_halves(sc, step, total, keep, send)


def add_kernel(sc, left, right, out):
    out[...] = left[...] + right[...]


def join_kernel_of(step, start, sc, value, got, out):
    half = value.shape[0] - start
    bit = bit_of(sc, step)
    if start:
        out[pl.ds(0, start)] = value[pl.ds(0, start)] + got[pl.ds(0, start)]
    out[pl.ds(pl.multiple_of(start + bit * half, NODES), half)] = value[pl.ds(start, half)]
    out[pl.ds(pl.multiple_of(start + (1 - bit) * half, NODES), half)] = got[pl.ds(start, half)]


def stack_kernel(sc, first, left, right, out):
    rows = first.shape[0]
    out[pl.ds(0, rows)] = first[...]
    out[pl.ds(rows, left.shape[0])] = left[...] + right[...]


def swap(value, step):
    axis = ("gx", "gy", "gz")[step[0]]
    return lax.ppermute(value, axis, [(i, i ^ step[1]) for i in range(lax.axis_size(axis))])


def rows_like(rows, width=128):
    return jax.ShapeDtypeStruct((rows, width), f32)


def halve(sc, sizes, keep, send):
    steps = halving_steps(sizes)
    got = swap(send, steps[0])
    for step in steps[1:]:
        keep, got = yield keep, got
        half = rows_like(keep.shape[0] // 2)
        keep, send = call(
            functools.partial(halve_kernel, step), "halve", (sc, keep, got), [half, half],
            [pltpu.VMEM(keep.shape, f32)],
        )
        got = swap(send, step)
    keep, got = yield keep, got
    return keep, got


class Background:
    def __init__(self):
        self.active = {}

    def add(self, name, steps):
        self.active[name] = [steps, None]

    def advance(self, entry, tied):
        steps, pending = entry
        try:
            entry[1] = next(steps) if pending is None else steps.send(tied)
        except StopIteration:
            entry[0] = None

    def beside(self, anchor):
        for entry in self.active.values():
            steps, pending = entry
            if steps is None:
                continue
            if pending is None:
                self.advance(entry, None)
            elif pending[1] is not None:
                anchor, tied = lax.optimization_barrier((anchor, pending))
                self.advance(entry, tied)
        return anchor

    def finish(self, name):
        entry = self.active[name]
        while entry[0] is not None:
            done = entry[1]
            if done is not None and done[1] is None:
                return done[0]
            self.advance(entry, done)
        return entry[1]


def on_device(state, cotangent, counts, edge_weights, node_in, node_out, biases):
    x_len, y_len, slots, nodes, width = state.shape
    rows = slots * nodes
    grid = (x_len, y_len, rows, width)
    axes = ("gx", "gy", "gz")
    sizes = tuple(lax.axis_size(a) for a in axes)
    trades = tuple(min(size - 1, 2) for size in sizes)
    nx, ny, nz = trades
    h0 = state.reshape(grid)
    g2 = cotangent.reshape(grid)
    sc = jnp.stack([counts[0]] + [lax.axis_index(a).astype(jnp.int32) for a in axes])

    def sds(shape, kind=f32):
        return jax.ShapeDtypeStruct(shape, kind)

    face_x = sds((y_len, rows, width))
    face_y = sds((x_len, rows, width))
    face_z = sds((x_len, y_len, width))
    face_outs = [face_y] * ny + [face_z] * nz
    full = sds(grid)
    full16 = sds(grid, bf16)
    full3 = sds((3,) + grid)
    work = pltpu.VMEM(grid, f32)
    inv = pltpu.VMEM((y_len, rows, width), f32)
    matmul = 2 * math.prod(grid) * width
    weights = (edge_weights, node_in, node_out, biases)

    def run(kernel, name, inputs, outs, scratch, flops):
        body = functools.partial(kernel, trades, sizes)
        return call(body, name, (sc, *weights, *inputs), outs, scratch, flops * matmul)

    def trade(faces, axis):
        size = lax.axis_size(axis)
        got = [lax.ppermute(face, axis, pairs(size, kind)) for kind, face in reversed(list(enumerate(faces)))]
        return got[::-1]

    background = Background()

    pair = pltpu.VMEM((2,) + grid[1:], f32)

    def first_trade(kernel, name, inputs, scratch, flops):
        faces = call(functools.partial(kernel, trades, sizes), name, (sc, *inputs), [face_x] * nx, scratch, flops)
        return trade(faces, "gx")

    def exchange(got_x, faces):
        fix = functools.partial(fix_y_kernel, trades)
        faces_y = call(fix, "fix_y", (sc, *got_x, *faces[:ny]), [face_y] * ny)
        got_y = trade(background.beside(faces_y), "gy")
        fix = functools.partial(fix_z_kernel, trades)
        faces_z = call(fix, "fix_z", (sc, *got_x, *got_y, *faces[ny:]), [face_z] * nz)
        got_z = background.beside(trade(background.beside(faces_z), "gz"))
        return (*got_x, *got_y, *got_z)

    got_x = first_trade(first_face_kernel, "face0", (edge_weights, biases, h0), [], matmul // 8)
    sums, slopes0, *faces = call(
        functools.partial(first_kernel, trades, sizes), "edges0", (sc, edge_weights, biases, h0),
        [full, full3] + face_outs, [], 3 * matmul,
    )
    halo = exchange(got_x, faces)
    inputs = (*weights, sums, h0, *halo)
    got_x = first_trade(middle_face_kernel, "face1", inputs, [pair, inv], matmul // 4)
    scaled0, act0, slope0, h1, sums, slopes1, *faces = run(
        middle_kernel, "nodes0_edges1", (sums, h0, *halo),
        [full16, full16, full, full16, full, full3] + face_outs, [work, inv], 8,
    )
    halo = exchange(got_x, faces)
    inputs = (*weights, sums, h1, g2, *halo)
    got_x = first_trade(turn_face_kernel, "face2", inputs, [pair, inv], matmul // 4)
    base, sums, grads1, *faces = run(
        turn_kernel, "nodes1_back", (sums, h1, g2, *halo), [full, full, rows_like(3 * width + NODES)] + face_outs,
        [work, inv], 10,
    )
    halo = exchange(got_x, faces)
    inputs = (*weights, sums, base, slopes1, slope0, *halo)
    got_x = first_trade(join_face_kernel, "face3", inputs, [pair, inv], matmul // 4)
    grad_rows = padded_rows(7 * width + 3 * NODES, sizes)
    half = rows_like(grad_rows // 2)
    base, sums, keep, send, *faces = run(
        join_kernel, "edges1_back_nodes0_back",
        (sums, h1, base, slopes1, h0, scaled0, act0, slope0, grads1, *halo),
        [full, full, half, half] + face_outs, [work, inv, pltpu.VMEM((grad_rows, width), f32)], 12,
    )
    background.add("sums", halve(sc, sizes, keep, send))
    halo = exchange(got_x, faces)
    tail_rows = width + NODES
    edges, last = run(last_kernel, "edges0_back", (sums, h0, slopes0, *halo), [full, rows_like(tail_rows)], [], 6)
    (grad0,) = call(state_kernel, "state_grad", (sc, edge_weights, base, edges), [full16], [], 2 * matmul)
    keep, got = background.finish("sums")
    (value,) = call(stack_kernel, "stack", (sc, last, keep, got), [rows_like(tail_rows + keep.shape[0])])
    for hop in hops(sizes[2]):
        (value,) = call(add_kernel, "add", (sc, value, swap(value, (2, hop))), [rows_like(value.shape[0])])
    for step in reversed(halving_steps(sizes)):
        out = rows_like(2 * value.shape[0] - tail_rows)
        body = functools.partial(join_kernel_of, step, tail_rows)
        (value,) = call(body, "join", (sc, value, swap(value, step)), [out])
    layers_all = 3 * slots * sizes[2] // 4
    nodes_all = x_len * sizes[0] * y_len * sizes[1] * layers_all * nodes
    scale = 1.0 / math.sqrt(nodes_all)
    edge_grads, in_grads, out_grads, bias_grads = call(
        functools.partial(finish_kernel, scale, tail_rows), "finish", (sc, edge_weights, node_in, value),
        [sds(edge_weights.shape), sds(node_in.shape), sds(node_out.shape), sds(biases.shape)],
    )
    return grad0.reshape(state.shape), edge_grads, in_grads, out_grads, bias_grads


def solution(mesh):
    return jax.shard_map(
        on_device,
        mesh=mesh,
        in_specs=(
            P("gx", "gy", "gz", None, None),
            P("gx", "gy", "gz", None, None),
            P("gz"),
            P(),
            P(),
            P(),
            P(),
        ),
        out_specs=(P("gx", "gy", "gz", None, None), P(), P(), P(), P()),
        check_vma=False,
    )
```

```python
import functools
import math

import jax
import jax.numpy as jnp
from jax import lax
from jax.experimental import pallas as pl
from jax.experimental.pallas import tpu as pltpu
from jax.sharding import PartitionSpec as P

f32 = jnp.float32
bf16 = jnp.bfloat16
NODES = 8
VMEM_LIMIT = 12 * 1024 * 1024
VM = pl.BlockSpec(memory_space=pltpu.VMEM)
SM = pl.BlockSpec(memory_space=pltpu.SMEM)


def dot(left, right):
    return lax.dot_general(left, right, (((1,), (0,)), ((), ())), preferred_element_type=f32)


def dot_t(left, right):
    return lax.dot_general(left, right, (((0,), (0,)), ((), ())), preferred_element_type=f32)


def dot_rt(left, right):
    return lax.dot_general(left, right, (((1,), (1,)), ((), ())), preferred_element_type=f32)


def silu_half(half):
    th = jnp.tanh(half)
    prod = half * th
    return half + prod, (0.5 + 0.5 * th) * ((1.0 + half) - prod)


def split_cols(value):
    high = value.astype(bf16)
    low = (value - high.astype(f32)).astype(bf16)
    return jnp.concatenate([high, low], -1)


def up(value):
    return pltpu.roll(value, NODES - 1, 1)


def down(value):
    return pltpu.roll(value, 1, 1)


def flat(value):
    return value.reshape(-1, value.shape[-1])


def node_rows(value):
    return value.reshape(-1, NODES, value.shape[-1])


def row_ids():
    return lax.broadcasted_iota(jnp.int32, (1, NODES, 128), 1)


def couple_slots(plane, filled):
    count, rows, width = plane.shape
    slots = rows // NODES
    parts = plane.reshape(count, slots, NODES, width)
    ids = row_ids()
    done = []
    for s in range(slots):
        here = parts[:, s]
        if s + 1 < slots:
            take = (ids == NODES - 1) & (s + 1 < filled)
            here = here + jnp.where(take, up(parts[:, s + 1]), 0.0)
        if s > 0:
            here = here + jnp.where(ids == 0, down(parts[:, s - 1]), 0.0)
            here = jnp.where(s < filled, here, 0.0)
        done.append(here[:, None])
    return jnp.concatenate(done, 1).reshape(plane.shape)


def elements(x_len, y_len, body):
    ey = y_len // NODES
    total = (x_len // NODES) * ey

    def step(e, carry):
        x0 = pl.multiple_of((e // ey) * NODES, NODES)
        y0 = pl.multiple_of((e % ey) * NODES, NODES)
        body(x0, y0)
        return carry

    lax.fori_loop(0, total, step, 0)


def edges_forward(h_ref, w_one, half_bias, filled, sum_ref, half_ref):
    x_len, y_len, rows, width = h_ref.shape
    inner = row_ids() < NODES - 1

    def body(x0, y0):
        ys = pl.ds(y0, NODES)
        prev = None
        here = h_ref[x0, ys].astype(f32)
        for i in range(NODES):
            parts = []
            nxt = None
            if i < NODES - 1:
                nxt = h_ref[x0 + i + 1, ys].astype(f32)
                parts.append((nxt - here).astype(bf16))
            parts.append((here[1:] - here[:-1]).astype(bf16))
            cols = node_rows(here)
            parts.append((up(cols) - cols).reshape(here.shape).astype(bf16))
            half = dot(flat(jnp.concatenate(parts, 0)), w_one).reshape(-1, rows, width) + half_bias
            act = (half + half * jnp.tanh(half)).astype(bf16).astype(f32)
            at = 0
            total = prev
            prev = None
            if i < NODES - 1:
                prev = act[:NODES]
                total = -prev if total is None else total - prev
                half_ref[0, x0 + i, ys] = half[:NODES]
                at = NODES
            along_y = act[at : at + NODES - 1]
            half_ref[1, x0 + i, pl.ds(y0, NODES - 1)] = half[at : at + NODES - 1]
            at += NODES - 1
            along_z = jnp.where(inner, node_rows(act[at:]), 0.0)
            half_ref[2, x0 + i, ys] = half[at:]
            total = total + (down(along_z) - along_z).reshape(here.shape)
            total = jnp.concatenate(
                [
                    total[:1] - along_y[:1],
                    total[1:-1] + (along_y[:-1] - along_y[1:]),
                    total[-1:] + along_y[-1:],
                ],
                0,
            )
            sum_ref[x0 + i, ys] = couple_slots(total, filled)
            here = nxt

    elements(x_len, y_len, body)


def slope_kernel(sc, half_in, slope_out):
    inner = row_ids() < NODES - 1

    def step(x, carry):
        for k in range(3):
            slope = silu_half(half_in[k, x])[1]
            if k == 2:
                slope = jnp.where(inner, node_rows(slope), 0.0).reshape(slope.shape)
            slope_out[k, x] = slope
        return carry

    lax.fori_loop(0, half_in.shape[1], step, 0)


def couple_columns(sum_ref):
    x_len, y_len = sum_ref.shape[:2]
    for cut in range(NODES, x_len, NODES):
        both = sum_ref[cut - 1] + sum_ref[cut]
        sum_ref[cut - 1] = both
        sum_ref[cut] = both
    for cut in range(NODES, y_len, NODES):
        both = sum_ref[:, cut - 1] + sum_ref[:, cut]
        sum_ref[:, cut - 1] = both
        sum_ref[:, cut] = both


def face_place(sc_ref, axis, kind, last):
    return jnp.where((sc_ref[1 + axis] + kind) % 2 == 0, last, 0)


def end_rows(values, filled, take_top):
    picked = values(0)
    slots = values.slots
    for s in range(slots):
        picked = jnp.where(take_top & (filled == s + 1), values(s * NODES + NODES - 1), picked)
    return picked


class RowReader:
    def __init__(self, slots, read):
        self.slots = slots
        self.read = read

    def __call__(self, row):
        return self.read(row)


def takes_top(sc_ref, kind):
    return (sc_ref[3] + kind) % 2 == 0


def write_faces(sc_ref, sum_ref, faces, counts):
    x_len, y_len, rows, width = sum_ref.shape
    nx, ny, nz = counts
    reader = RowReader(rows // NODES, lambda row: sum_ref[:, :, row])
    for kind in range(ny):
        faces[kind][...] = sum_ref[:, face_place(sc_ref, 1, kind, y_len - 1)]
    for kind in range(nz):
        faces[ny + kind][...] = end_rows(reader, sc_ref[0], takes_top(sc_ref, kind))


def add_halo(sc_ref, from_ref, halo, into_ref, counts):
    x_len, y_len, rows, width = from_ref.shape
    nx, ny, nz = counts

    def copy(x, carry):
        into_ref[x] = from_ref[x]
        return carry

    lax.fori_loop(0, x_len, copy, 0)
    for kind in range(nx):
        into_ref[face_place(sc_ref, 0, kind, x_len - 1)] += halo[kind][...]
    for kind in range(ny):
        into_ref[:, face_place(sc_ref, 1, kind, y_len - 1)] += halo[nx + kind][...]
    if nz:
        got = [halo[nx + ny + kind][...] for kind in range(nz)]
        tops = [takes_top(sc_ref, kind) for kind in range(nz)]
        from_below = sum(jnp.where(top, 0.0, value) for top, value in zip(tops, got))
        from_above = sum(jnp.where(top, value, 0.0) for top, value in zip(tops, got))
        into_ref[:, :, 0] += from_below
        for s in range(rows // NODES):
            into_ref[:, :, s * NODES + NODES - 1] += jnp.where(sc_ref[0] == s + 1, from_above, 0.0)


def fix_y_kernel(counts, sc_ref, *refs):
    nx, ny, nz = counts
    got, faces, outs = refs[:nx], refs[nx : nx + ny], refs[nx + ny :]
    x_len = faces[0].shape[0]
    for k in range(ny):
        outs[k][...] = faces[k][...]
    for kind in range(nx):
        place = face_place(sc_ref, 0, kind, x_len - 1)
        for k in range(ny):
            y_len = got[kind].shape[0]
            outs[k][place] += got[kind][face_place(sc_ref, 1, k, y_len - 1)]


def fix_z_kernel(counts, sc_ref, *refs):
    nx, ny, nz = counts
    got_x, refs = refs[:nx], refs[nx:]
    got_y, refs = refs[:ny], refs[ny:]
    faces, outs = refs[:nz], refs[nz:]
    x_len, y_len, width = faces[0].shape
    for k in range(nz):
        outs[k][...] = faces[k][...]
    for k in range(nz):
        top = takes_top(sc_ref, k)
        for kind in range(nx):
            ref = got_x[kind]
            reader = RowReader(ref.shape[1] // NODES, lambda row, ref=ref: ref[:, row])
            outs[k][face_place(sc_ref, 0, kind, x_len - 1)] += end_rows(reader, sc_ref[0], top)
        for kind in range(ny):
            ref = got_y[kind]
            reader = RowReader(ref.shape[1] // NODES, lambda row, ref=ref: ref[:, row])
            add = end_rows(reader, sc_ref[0], top)
            first = face_place(sc_ref, 1, kind, 1) == 0
            outs[k][:, 0] += jnp.where(first, add, 0.0)
            outs[k][:, y_len - 1] += jnp.where(first, 0.0, add)


def write_inverse(sc_ref, inv_ref, sizes):
    y_len, rows, width = inv_ref.shape
    filled, at_y, at_z = sc_ref[0], sc_ref[2], sc_ref[3]
    ids = lax.broadcasted_iota(jnp.int32, (rows, width), 0)
    node = ids % NODES
    low = (node == 0) & ((ids >= NODES) | (at_z > 0))
    high = (node == NODES - 1) & ((ids < (filled - 1) * NODES) | (at_z < sizes[2] - 1))
    along_z = jnp.where(low | high, 0.5, 1.0).astype(f32)
    for y in range(y_len):
        inv_ref[y] = along_z * end_factor(y, y_len, at_y, sizes[1])


def end_factor(place, length, position, size):
    whole = place + position * length
    low = (place % NODES == 0) & (whole > 0)
    high = (place % NODES == NODES - 1) & (whole < length * size - 1)
    return jnp.where(low | high, 0.5, 1.0).astype(f32)


CHUNK = 4


def scale_planes(sc_ref, inv_ref, x, block, x_len, size_x):
    inv = inv_ref[...]
    parts = [block[c] * (inv * end_factor(x + c, x_len, sc_ref[1], size_x)) for c in range(block.shape[0])]
    return jnp.stack(parts, 0)


def node_forward(scaled, feat, weights, layer):
    edge_w, node_in, node_out, biases = weights
    pair = split_cols(scaled)
    w_two = edge_w[layer, 1]
    joined = jnp.concatenate([feat, dot(pair, jnp.concatenate([w_two, w_two], 0)).astype(bf16)], -1)
    half = jnp.bfloat16(0.5)
    act, slope = silu_half(dot(joined, node_in[layer] * half) + 0.5 * biases[layer, pl.ds(1, 1)])
    return pair[:, :128], act.astype(bf16), slope


def node_slopes(grad, slope, weights, layer):
    return (dot_rt(grad, weights[2][layer]) * slope).astype(bf16)


def node_share(sc_ref, x, inv_ref, size_x, dpn, weights, layer, sum_ref):
    shape = (CHUNK,) + sum_ref.shape[1:]
    dx = dot_rt(dpn, weights[1][layer, pl.ds(128, 128)]).reshape(shape)
    share = scale_planes(sc_ref, inv_ref, x, dx, sum_ref.shape[0], size_x)
    joined = couple_slots(share.reshape((-1,) + shape[2:]), sc_ref[0])
    sum_ref[pl.ds(x, CHUNK)] = joined.reshape(shape)


def node_products(grad, feat, scaled, act, dpn, grads):
    grads[pl.ds(0, 128)] += dot_t(act, grad)
    both = dot_t(dpn, jnp.concatenate([feat, scaled], -1))
    grads[pl.ds(128, 128)] += both[:, :128]
    grads[pl.ds(256, 128)] += both[:, 128:]
    grads[pl.ds(384, NODES)] += jnp.sum(dpn.astype(f32).reshape(-1, NODES, 128), 0)


def couple_plane(plane):
    y_len = plane.shape[0]
    parts = [plane[y] for y in range(y_len)]
    for cut in range(NODES, y_len, NODES):
        both = parts[cut - 1] + parts[cut]
        parts[cut - 1] = parts[cut] = both
    return jnp.stack(parts, 0)


def along_y(plane, combine):
    return [
        combine(plane[y : y + NODES - 1], plane[y + 1 : y + NODES], y) for y in range(0, plane.shape[0], NODES)
    ]


def spread_plane(sign, edge_x, edges_y, edge_z):
    total = sign * edge_x + (down(edge_z) - edge_z).reshape(edge_x.shape)
    parts = []
    for k, edge in enumerate(edges_y):
        here = total[k * NODES : (k + 1) * NODES]
        parts += [here[:1] - edge[:1], here[1:-1] + (edge[:-1] - edge[1:]), here[-1:] + edge[-1:]]
    return jnp.concatenate(parts, 0)


def plane_forward(low, high, at_high, w_one, half_bias, filled):
    y_len, rows, width = low.shape
    here = jnp.where(at_high, high, low)
    cols = node_rows(here)
    parts = [(high - low).astype(bf16)]
    parts += along_y(here, lambda lower, upper, y: (upper - lower).astype(bf16))
    parts.append((up(cols) - cols).reshape(here.shape).astype(bf16))
    half = dot(flat(jnp.concatenate(parts, 0)), w_one).reshape(-1, rows, width) + half_bias
    act = silu_half(half)[0].astype(bf16).astype(f32)
    at = y_len
    edges_y = []
    for _ in range(y_len // NODES):
        edges_y.append(act[at : at + NODES - 1])
        at += NODES - 1
    edge_z = jnp.where(row_ids() < NODES - 1, node_rows(act[at:]), 0.0)
    total = spread_plane(jnp.where(at_high, 1.0, -1.0), act[:y_len], edges_y, edge_z)
    return couple_plane(couple_slots(total, filled))


def plane_backward(low, high, at_high, slope_x, slope_y, slope_z):
    here = jnp.where(at_high, high, low)
    cols = node_rows(here)
    edge_x = ((high - low) * slope_x).astype(bf16).astype(f32)
    edges_y = along_y(
        here, lambda lower, upper, y: ((upper - lower) * slope_y[y : y + NODES - 1]).astype(bf16).astype(f32)
    )
    edge_z = ((up(cols) - cols) * node_rows(slope_z)).astype(bf16).astype(f32)
    return spread_plane(jnp.where(at_high, 1.0, -1.0), edge_x, edges_y, edge_z)


def face_planes(sc_ref, kind, x_len):
    place = face_place(sc_ref, 0, kind, x_len - 1)
    at_high = place > 0
    return place, jnp.where(at_high, x_len - 2, 0), at_high


def halo_planes(sc_ref, from_ref, halo, kind, start, into_ref, counts):
    x_len, y_len, rows, width = from_ref.shape
    nx, ny, nz = counts
    for c in range(2):
        into_ref[c] = from_ref[start + c]
    into_ref[face_place(sc_ref, 0, kind, x_len - 1) - start] += halo[kind][...]
    for c in range(2):
        for k in range(ny):
            into_ref[c, face_place(sc_ref, 1, k, y_len - 1)] += halo[nx + k][start + c]
        for k in range(nz):
            got = halo[nx + ny + k][start + c]
            top = takes_top(sc_ref, k)
            into_ref[c, :, 0] += jnp.where(top, 0.0, got)
            for s in range(rows // NODES):
                into_ref[c, :, s * NODES + NODES - 1] += jnp.where(top & (sc_ref[0] == s + 1), got, 0.0)


def edges_backward(q_ref, slope_ref, edge_ref, bias_acc):
    x_len, y_len, rows, width = q_ref.shape

    def body(x0, y0):
        ys = pl.ds(y0, NODES)
        prev = None
        here = q_ref[x0, ys]
        bias = jnp.zeros((NODES, width), f32)
        for i in range(NODES):
            total = prev
            prev = None
            nxt = None
            if i < NODES - 1:
                nxt = q_ref[x0 + i + 1, ys]
                prev = ((nxt - here) * slope_ref[0, x0 + i, ys]).astype(bf16).astype(f32)
                total = -prev if total is None else total - prev
                bias = bias + jnp.sum(node_rows(prev), 0)
            along_y = (here[1:] - here[:-1]) * slope_ref[1, x0 + i, pl.ds(y0, NODES - 1)]
            along_y = along_y.astype(bf16).astype(f32)
            cols = node_rows(here)
            along_z = (up(cols) - cols) * node_rows(slope_ref[2, x0 + i, ys])
            along_z = along_z.astype(bf16).astype(f32)
            bias = bias + jnp.sum(node_rows(along_y), 0) + jnp.sum(along_z, 0)
            total = total + (down(along_z) - along_z).reshape(here.shape)
            total = jnp.concatenate(
                [
                    total[:1] - along_y[:1],
                    total[1:-1] + (along_y[:-1] - along_y[1:]),
                    total[-1:] + along_y[-1:],
                ],
                0,
            )
            edge_ref[x0 + i, ys] = total
            here = nxt
        bias_acc[...] += bias

    elements(x_len, y_len, body)


def planes(count, body):
    def step(c, carry):
        body(pl.multiple_of(c * CHUNK, CHUNK))
        return carry

    lax.fori_loop(0, count // CHUNK, step, 0)


def half_weights(weights, layer):
    edge_w, node_in, node_out, biases = weights
    return edge_w[layer, 0] * jnp.bfloat16(0.5), 0.5 * biases[layer, pl.ds(0, 1)]


def first_kernel(counts, sizes, sc, edge_w, biases, h, sums, slopes, *faces):
    w_one, bias = half_weights((edge_w, None, None, biases), 0)
    edges_forward(h, w_one, bias, sc[0], sums, slopes)
    couple_columns(sums)
    write_faces(sc, sums, faces, counts)


def first_face_kernel(counts, sizes, sc, edge_w, biases, h, *faces):
    w_one, bias = half_weights((edge_w, None, None, biases), 0)
    for kind, face in enumerate(faces):
        place, start, at_high = face_planes(sc, kind, h.shape[0])
        face[...] = plane_forward(
            h[start].astype(f32), h[start + 1].astype(f32), at_high, w_one, bias, sc[0]
        )


def middle_face_kernel(counts, sizes, sc, edge_w, node_in, node_out, biases, sums_in, h, *refs):
    weights = (edge_w, node_in, node_out, biases)
    n = sum(counts)
    halo, faces, (pair, inv) = refs[:n], refs[n:-2], refs[-2:]
    write_inverse(sc, inv, sizes)
    w_one, bias = half_weights(weights, 1)
    x_len = h.shape[0]
    for kind, face in enumerate(faces):
        place, start, at_high = face_planes(sc, kind, x_len)
        halo_planes(sc, sums_in, halo, kind, start, pair, counts)
        sums_at = flat(scale_planes(sc, inv, start, pair[...], x_len, sizes[0]))
        feat = flat(h[pl.ds(start, 2)])
        scaled, act, slope = node_forward(sums_at, feat, weights, 0)
        moved = (feat.astype(f32) + dot(act, node_out[0])).astype(bf16).astype(f32).reshape(pair.shape)
        face[...] = plane_forward(moved[0], moved[1], at_high, w_one, bias, sc[0])


def face_share(sc, sizes, inv, place, x_len, grad, slope, weights, layer, shape):
    dpn = node_slopes(grad, slope, weights, layer)
    dx = dot_rt(dpn, weights[1][layer, pl.ds(128, 128)]).reshape((1,) + shape)
    share = scale_planes(sc, inv, place, dx, x_len, sizes[0])
    return couple_plane(couple_slots(share[0], sc[0]))


def turn_face_kernel(counts, sizes, sc, edge_w, node_in, node_out, biases, sums_in, h, g_ref, *refs):
    weights = (edge_w, node_in, node_out, biases)
    n = sum(counts)
    halo, faces, (pair, inv) = refs[:n], refs[n:-2], refs[-2:]
    write_inverse(sc, inv, sizes)
    x_len, shape = h.shape[0], h.shape[1:]
    live = (lax.broadcasted_iota(jnp.int32, (1, h.shape[2], 128), 1) < sc[0] * NODES).astype(f32)
    for kind, face in enumerate(faces):
        place, start, at_high = face_planes(sc, kind, x_len)
        halo_planes(sc, sums_in, halo, kind, start, pair, counts)
        plane = pair[place - start][None]
        sums_at = flat(scale_planes(sc, inv, place, plane, x_len, sizes[0]))
        scaled, act, slope = node_forward(sums_at, flat(h[place]), weights, 1)
        grad = flat((g_ref[place].astype(f32) * live).astype(bf16))
        face[...] = face_share(sc, sizes, inv, place, x_len, grad, slope, weights, 1, shape)


def join_face_kernel(counts, sizes, sc, edge_w, node_in, node_out, biases, sums_in, base_in, slopes, slope0, *refs):
    weights = (edge_w, node_in, node_out, biases)
    n = sum(counts)
    halo, faces, (pair, inv) = refs[:n], refs[n:-2], refs[-2:]
    write_inverse(sc, inv, sizes)
    x_len, shape = base_in.shape[0], base_in.shape[1:]
    w_two, w_one = twice(edge_w[1, 1]), twice(edge_w[1, 0])
    for kind, face in enumerate(faces):
        place, start, at_high = face_planes(sc, kind, x_len)
        halo_planes(sc, sums_in, halo, kind, start, pair, counts)
        q = dot_rt(split_cols(flat(pair[...])), w_two).reshape(pair.shape)
        edge = plane_backward(q[0], q[1], at_high, slopes[0, start], slopes[1, place], slopes[2, place])
        grad = (flat(base_in[place]) + dot_rt(split_cols(flat(edge)), w_one)).astype(bf16)
        face[...] = face_share(sc, sizes, inv, place, x_len, grad, flat(slope0[place]), weights, 0, shape)


def twice(weight):
    return jnp.concatenate([weight, weight], 1)


def middle_kernel(counts, sizes, sc, edge_w, node_in, node_out, biases, sums_in, h, *refs):
    weights = (edge_w, node_in, node_out, biases)
    n = sum(counts)
    halo, refs = refs[:n], refs[n:]
    scaled_ref, act_ref, slope_ref, next_ref, sums, slopes = refs[:6]
    faces, (work, inv) = refs[6:-2], refs[-2:]
    add_halo(sc, sums_in, halo, work, counts)
    write_inverse(sc, inv, sizes)
    shape = (CHUNK,) + h.shape[1:]

    def body(x):
        at = pl.ds(x, CHUNK)
        sums_at = flat(scale_planes(sc, inv, x, work[at], h.shape[0], sizes[0]))
        scaled, act, slope = node_forward(sums_at, flat(h[at]), weights, 0)
        scaled_ref[at] = scaled.reshape(shape)
        act_ref[at] = act.reshape(shape)
        slope_ref[at] = slope.reshape(shape)
        moved = flat(h[at]).astype(f32) + dot(act, node_out[0])
        next_ref[at] = moved.astype(bf16).reshape(shape)

    planes(h.shape[0], body)
    w_one, bias = half_weights(weights, 1)
    edges_forward(next_ref, w_one, bias, sc[0], sums, slopes)
    couple_columns(sums)
    write_faces(sc, sums, faces, counts)


def turn_kernel(counts, sizes, sc, edge_w, node_in, node_out, biases, sums_in, h, g_ref, *refs):
    weights = (edge_w, node_in, node_out, biases)
    n = sum(counts)
    halo, refs = refs[:n], refs[n:]
    scaled_ref, act_ref, dpn_ref, sums = refs[:4]
    faces, (work, inv) = refs[4:-2], refs[-2:]
    add_halo(sc, sums_in, halo, work, counts)
    write_inverse(sc, inv, sizes)
    shape = (CHUNK,) + h.shape[1:]
    live = live_rows(sc, h)

    def body(x):
        at = pl.ds(x, CHUNK)
        sums_at = flat(scale_planes(sc, inv, x, work[at], h.shape[0], sizes[0]))
        scaled, act, slope = node_forward(sums_at, flat(h[at]), weights, 1)
        scaled_ref[at] = scaled.reshape(shape)
        act_ref[at] = act.reshape(shape)
        grad = flat((g_ref[at].astype(f32) * live).astype(bf16))
        dpn = node_slopes(grad, slope, weights, 1)
        dpn_ref[at] = dpn.reshape(shape)
        node_share(sc, x, inv, sizes[0], dpn, weights, 1, sums)

    planes(h.shape[0], body)
    couple_columns(sums)
    write_faces(sc, sums, faces, counts)


def live_rows(sc, h):
    return (lax.broadcasted_iota(jnp.int32, (1, 1, h.shape[2], 128), 2) < sc[0] * NODES).astype(f32)


def products_kernel(sc, node_in, h, g_ref, scaled, act, dpn, base, grads):
    grads[...] = jnp.zeros_like(grads)
    live = live_rows(sc, h)

    def body(x):
        at = pl.ds(x, CHUNK)
        grad = (g_ref[at].astype(f32) * live).astype(bf16)
        node_products(flat(grad), flat(h[at]), flat(scaled[at]), flat(act[at]), flat(dpn[at]), grads)
        dx = dot_rt(flat(dpn[at]), node_in[1, pl.ds(0, 128)])
        base[at] = grad.astype(f32) + dx.reshape(grad.shape)

    planes(h.shape[0], body)


def edge_parts(counts, sc, weights, layer, sums_in, halo, h, slopes, work, grads, row):
    add_halo(sc, sums_in, halo, work, counts)
    shape = (CHUNK,) + h.shape[1:]
    w_two = twice(weights[0][layer, 1])

    def to_q(x):
        at = pl.ds(x, CHUNK)
        work[at] = dot_rt(split_cols(flat(work[at])), w_two).reshape(shape)

    planes(h.shape[0], to_q)
    edges_backward(work, slopes, work, grads.at[pl.ds(row + 128, NODES)])


def edge_product(h, x, pair, grads, row):
    both = dot_t(flat(h[pl.ds(x, CHUNK)]), pair)
    grads[pl.ds(row, 128)] += both[:, :128] + both[:, 128:]


def join_kernel(
    counts, sizes, sc, edge_w, node_in, node_out, biases,
    sums_in, h, base_in, slopes, h0, scaled0, act0, slope0, grads1, *refs
):
    weights = (edge_w, node_in, node_out, biases)
    n = sum(counts)
    halo, refs = refs[:n], refs[n:]
    grad_ref, dpn_ref, sums, keep, send = refs[:5]
    faces, (work, inv, grads) = refs[5:-3], refs[-3:]
    write_inverse(sc, inv, sizes)
    grads[...] = jnp.zeros_like(grads)
    grads[pl.ds(512 + 2 * NODES, grads1.shape[0])] = grads1[...]

    row = 384 + NODES
    shape = (CHUNK,) + h.shape[1:]
    edge_parts(counts, sc, weights, 1, sums_in, halo, h, slopes, work, grads, row)
    w_one = twice(edge_w[1, 0])

    def body(x):
        at = pl.ds(x, CHUNK)
        pair = split_cols(flat(work[at]))
        edge_product(h, x, pair, grads, row)
        grad = (flat(base_in[at]) + dot_rt(pair, w_one)).astype(bf16)
        dpn = node_slopes(grad, flat(slope0[at]), weights, 0)
        node_products(grad, flat(h0[at]), flat(scaled0[at]), flat(act0[at]), dpn, grads)
        grad_ref[at] = grad.reshape(shape)
        dpn_ref[at] = dpn.reshape(shape)
        node_share(sc, x, inv, sizes[0], dpn, weights, 0, sums)

    planes(h.shape[0], body)
    couple_columns(sums)
    write_faces(sc, sums, faces, counts)
    write_halves(sc, halving_steps(sizes)[0], grads, keep, send)


def last_kernel(counts, sizes, sc, edge_w, node_in, node_out, biases, sums_in, h, slopes, *refs):
    n = sum(counts)
    halo, (edges, grads) = refs[:n], refs[n:]
    grads[...] = jnp.zeros_like(grads)
    edge_parts(counts, sc, (edge_w,), 0, sums_in, halo, h, slopes, edges, grads, 0)

    def body(x):
        edge_product(h, x, split_cols(flat(edges[pl.ds(x, CHUNK)])), grads, 0)

    planes(h.shape[0], body)


def state_kernel(sc, edge_w, node_in, grad_in, dpn, edges, grad_ref):
    shape = (CHUNK,) + edges.shape[1:]
    weight = jnp.concatenate([twice(edge_w[0, 0]), node_in[0, pl.ds(0, 128)]], 1)

    def body(x):
        at = pl.ds(x, CHUNK)
        parts = jnp.concatenate([split_cols(flat(edges[at])), flat(dpn[at])], -1)
        grad_ref[at] = (flat(grad_in[at]).astype(f32) + dot_rt(parts, weight)).astype(bf16).reshape(shape)

    planes(edges.shape[0], body)


def finish_kernel(scale, last_rows, step, sc, edge_w, node_in, value, got, *refs):
    edge_grads, in_grads, out_grads, bias_grads, both = refs
    width = edge_w.shape[-1]
    join_kernel_of(step, last_rows, sc, value, got, both)

    def rows_of(part, start, count=width):
        ref, offset = part
        return ref[pl.ds(offset + start, count)] * scale

    def bias_of(part, start):
        return jnp.sum(rows_of(part, start, NODES), 0, keepdims=True)

    end = 3 * width
    last, sum0 = (both, 0), (both, last_rows)
    sum1 = (both, last_rows + 512 + 2 * NODES)
    firsts = ((last, 0), (sum0, end + NODES))
    for layer, part in enumerate((sum0, sum1)):
        out_grads[layer] = rows_of(part, 0)
        in_grads[layer, pl.ds(0, width)] = rows_of(part, width).T
        bias_grads[layer, pl.ds(1, 1)] = bias_of(part, end)
        source, start = firsts[layer]
        edge_grads[layer, 0] = rows_of(source, start)
        bias_grads[layer, pl.ds(0, 1)] = bias_of(source, start + width)
        mixed = rows_of(part, 2 * width).T
        high = mixed.astype(bf16)
        low = (mixed - high.astype(f32)).astype(bf16)
        lower = node_in[layer, pl.ds(width, width)]
        edge_grads[layer, 1] = dot_rt(high, lower) + dot_rt(low, lower)
        w_two = edge_w[layer, 1]
        in_grads[layer, pl.ds(width, width)] = dot_t(w_two, high) + dot_t(w_two, low)


def call(kernel, name, inputs, outs, scratch=(), flops=0, aliases=None):
    total = sum(math.prod(o.shape) * o.dtype.itemsize for o in outs)
    total += sum(math.prod(i.shape) * i.dtype.itemsize for i in inputs)
    return pl.pallas_call(
        kernel,
        name=name,
        out_shape=tuple(outs),
        in_specs=[SM] + [VM] * (len(inputs) - 1),
        out_specs=tuple([VM] * len(outs)),
        scratch_shapes=list(scratch),
        input_output_aliases=aliases or {},
        compiler_params=pltpu.CompilerParams(vmem_limit_bytes=VMEM_LIMIT),
        cost_estimate=pl.CostEstimate(flops=flops, bytes_accessed=total, transcendentals=0),
    )(*inputs)


def pairs(size, kind):
    return [
        pair for low in range(kind, size - 1, 2) for pair in ((low, low + 1), (low + 1, low))
    ]


def hops(size):
    found = []
    hop = 1
    while hop < size:
        found.append(hop)
        hop *= 2
    return found


def halving_steps(sizes):
    steps = [(1, hop) for hop in hops(sizes[1])[:1]]
    steps += [(0, hop) for hop in hops(sizes[0])]
    return steps + [(1, hop) for hop in hops(sizes[1])[1:]]


def padded_rows(rows, sizes):
    unit = NODES << len(halving_steps(sizes))
    return -(-rows // unit) * unit


def bit_of(sc_ref, step):
    axis, hop = step
    return (sc_ref[1 + axis] // hop) % 2


def write_halves(sc_ref, step, from_ref, keep, send):
    half = keep.shape[0]
    bit = bit_of(sc_ref, step)
    keep[...] = from_ref[pl.ds(pl.multiple_of(bit * half, NODES), half)]
    send[...] = from_ref[pl.ds(pl.multiple_of((1 - bit) * half, NODES), half)]


def halve_kernel(step, sc, keep_in, got, keep, send, total):
    total[...] = keep_in[...] + got[...]
    write_halves(sc, step, total, keep, send)


def add_kernel(sc, left, right, out):
    out[...] = left[...] + right[...]


def join_kernel_of(step, start, sc, value, got, out):
    half = value.shape[0] - start
    bit = bit_of(sc, step)
    if start:
        out[pl.ds(0, start)] = value[pl.ds(0, start)] + got[pl.ds(0, start)]
    out[pl.ds(pl.multiple_of(start + bit * half, NODES), half)] = value[pl.ds(start, half)]
    out[pl.ds(pl.multiple_of(start + (1 - bit) * half, NODES), half)] = got[pl.ds(start, half)]


def stack_kernel(sc, first, left, right, out):
    rows = first.shape[0]
    out[pl.ds(0, rows)] = first[...]
    out[pl.ds(rows, left.shape[0])] = left[...] + right[...]


def swap(value, step):
    axis = ("gx", "gy", "gz")[step[0]]
    return lax.ppermute(value, axis, [(i, i ^ step[1]) for i in range(lax.axis_size(axis))])


def rows_like(rows, width=128):
    return jax.ShapeDtypeStruct((rows, width), f32)


def halve(sc, sizes, keep, send):
    steps = halving_steps(sizes)
    got = swap(send, steps[0])
    for step in steps[1:]:
        keep, got = yield keep, got
        half = rows_like(keep.shape[0] // 2)
        keep, send = call(
            functools.partial(halve_kernel, step), "halve", (sc, keep, got), [half, half],
            [pltpu.VMEM(keep.shape, f32)],
        )
        got = swap(send, step)
    keep, got = yield keep, got
    return keep, got


class Background:
    def __init__(self):
        self.active = {}

    def add(self, name, steps):
        self.active[name] = [steps, None]

    def advance(self, entry, tied):
        steps, pending = entry
        try:
            entry[1] = next(steps) if pending is None else steps.send(tied)
        except StopIteration:
            entry[0] = None

    def beside(self, anchor):
        for entry in self.active.values():
            steps, pending = entry
            if steps is None:
                continue
            if pending is None:
                self.advance(entry, None)
            elif pending[1] is not None:
                anchor, tied = lax.optimization_barrier((anchor, pending))
                self.advance(entry, tied)
        return anchor

    def finish(self, name):
        entry = self.active[name]
        while entry[0] is not None:
            done = entry[1]
            if done is not None and done[1] is None:
                return done[0]
            self.advance(entry, done)
        return entry[1]


def on_device(state, cotangent, counts, edge_weights, node_in, node_out, biases):
    x_len, y_len, slots, nodes, width = state.shape
    rows = slots * nodes
    grid = (x_len, y_len, rows, width)
    axes = ("gx", "gy", "gz")
    sizes = tuple(lax.axis_size(a) for a in axes)
    trades = tuple(min(size - 1, 2) for size in sizes)
    nx, ny, nz = trades
    h0 = state.reshape(grid)
    g2 = cotangent.reshape(grid)
    sc = jnp.stack([counts[0]] + [lax.axis_index(a).astype(jnp.int32) for a in axes])

    def sds(shape, kind=f32):
        return jax.ShapeDtypeStruct(shape, kind)

    face_x = sds((y_len, rows, width))
    face_y = sds((x_len, rows, width))
    face_z = sds((x_len, y_len, width))
    face_outs = [face_y] * ny + [face_z] * nz
    full = sds(grid)
    full16 = sds(grid, bf16)
    full3 = sds((3,) + grid)
    work = pltpu.VMEM(grid, f32)
    inv = pltpu.VMEM((y_len, rows, width), f32)
    matmul = 2 * math.prod(grid) * width
    weights = (edge_weights, node_in, node_out, biases)

    def run(kernel, name, inputs, outs, scratch, flops):
        body = functools.partial(kernel, trades, sizes)
        return call(body, name, (sc, *weights, *inputs), outs, scratch, flops * matmul)

    def trade(faces, axis):
        size = lax.axis_size(axis)
        got = [lax.ppermute(face, axis, pairs(size, kind)) for kind, face in reversed(list(enumerate(faces)))]
        return got[::-1]

    background = Background()

    pair = pltpu.VMEM((2,) + grid[1:], f32)

    def first_trade(kernel, name, inputs, scratch, flops):
        faces = call(functools.partial(kernel, trades, sizes), name, (sc, *inputs), [face_x] * nx, scratch, flops)
        return trade(faces, "gx")

    def exchange(got_x, faces, work=None, held=()):
        fix = functools.partial(fix_y_kernel, trades)
        faces_y = call(fix, "fix_y", (sc, *got_x, *faces[:ny]), [face_y] * ny)
        got_y = trade(background.beside(faces_y), "gy")
        fix = functools.partial(fix_z_kernel, trades)
        faces_z = call(fix, "fix_z", (sc, *got_x, *got_y, *faces[ny:]), [face_z] * nz)
        faces_z = background.beside(faces_z)
        done = None
        if work is not None:
            faces_z, held = lax.optimization_barrier((faces_z, held))
            done = work(*held)
        got_z = background.beside(trade(faces_z, "gz"))
        got_z, done = lax.optimization_barrier((got_z, done))
        return (*got_x, *got_y, *got_z), done

    def to_slopes(half):
        return call(slope_kernel, "slopes", (sc, half), [full3], [], matmul, {1: 0})[0]

    def products(*held):
        return call(
            products_kernel, "nodes1_products", (sc, node_in, *held), [full, rows_like(3 * width + NODES)], [], 6 * matmul
        )

    got_x = first_trade(first_face_kernel, "face0", (edge_weights, biases, h0), [], matmul // 8)
    sums, slopes0, *faces = call(
        functools.partial(first_kernel, trades, sizes), "edges0", (sc, edge_weights, biases, h0),
        [full, full3] + face_outs, [], 3 * matmul,
    )
    halo, slopes0 = exchange(got_x, faces, to_slopes, (slopes0,))
    inputs = (*weights, sums, h0, *halo)
    got_x = first_trade(middle_face_kernel, "face1", inputs, [pair, inv], matmul // 4)
    scaled0, act0, slope0, h1, sums, slopes1, *faces = run(
        middle_kernel, "nodes0_edges1", (sums, h0, *halo),
        [full16, full16, full, full16, full, full3] + face_outs, [work, inv], 8,
    )
    halo, slopes1 = exchange(got_x, faces, to_slopes, (slopes1,))
    inputs = (*weights, sums, h1, g2, *halo)
    got_x = first_trade(turn_face_kernel, "face2", inputs, [pair, inv], matmul // 4)
    scaled1, act1, dpn1, sums, *faces = run(
        turn_kernel, "nodes1_back", (sums, h1, g2, *halo), [full16] * 3 + [full] + face_outs, [work, inv], 7
    )
    halo, (base, grads1) = exchange(got_x, faces, products, (h1, g2, scaled1, act1, dpn1))
    inputs = (*weights, sums, base, slopes1, slope0, *halo)
    got_x = first_trade(join_face_kernel, "face3", inputs, [pair, inv], matmul // 4)
    grad_rows = padded_rows(7 * width + 3 * NODES, sizes)
    half = rows_like(grad_rows // 2)
    grad_in, dpn0, sums, keep, send, *faces = run(
        join_kernel, "edges1_back_nodes0_back",
        (sums, h1, base, slopes1, h0, scaled0, act0, slope0, grads1, *halo),
        [full16, full16, full, half, half] + face_outs, [work, inv, pltpu.VMEM((grad_rows, width), f32)], 12,
    )
    background.add("sums", halve(sc, sizes, keep, send))
    halo, _ = exchange(got_x, faces)
    tail_rows = width + NODES
    edges, last = run(last_kernel, "edges0_back", (sums, h0, slopes0, *halo), [full, rows_like(tail_rows)], [], 6)
    keep, got = background.finish("sums")
    (value,) = call(stack_kernel, "stack", (sc, last, keep, got), [rows_like(tail_rows + keep.shape[0])])
    value, grad_in, dpn0, edges = lax.optimization_barrier((value, grad_in, dpn0, edges))
    (grad0,) = call(
        state_kernel, "state_grad", (sc, edge_weights, node_in, grad_in, dpn0, edges), [full16], [], 4 * matmul
    )
    for hop in reversed(hops(sizes[2])):
        (value,) = call(add_kernel, "add", (sc, value, swap(value, (2, hop))), [rows_like(value.shape[0])])
        value, grad0 = lax.optimization_barrier((value, grad0))
    first, *rest = halving_steps(sizes)
    for step in reversed(rest):
        out = rows_like(2 * value.shape[0] - tail_rows)
        body = functools.partial(join_kernel_of, step, tail_rows)
        (value,) = call(body, "join", (sc, value, swap(value, step)), [out])
    layers_all = 3 * slots * sizes[2] // 4
    nodes_all = x_len * sizes[0] * y_len * sizes[1] * layers_all * nodes
    scale = 1.0 / math.sqrt(nodes_all)
    edge_grads, in_grads, out_grads, bias_grads = call(
        functools.partial(finish_kernel, scale, tail_rows, first), "finish",
        (sc, edge_weights, node_in, value, swap(value, first)),
        [sds(edge_weights.shape), sds(node_in.shape), sds(node_out.shape), sds(biases.shape)],
        [pltpu.VMEM((2 * value.shape[0] - tail_rows, width), f32)],
    )
    return grad0.reshape(state.shape), edge_grads, in_grads, out_grads, bias_grads


def solution(mesh):
    return jax.shard_map(
        on_device,
        mesh=mesh,
        in_specs=(
            P("gx", "gy", "gz", None, None),
            P("gx", "gy", "gz", None, None),
            P("gz"),
            P(),
            P(),
            P(),
            P(),
        ),
        out_specs=(P("gx", "gy", "gz", None, None), P(), P(), P(), P()),
        check_vma=False,
    )
```

```python
import functools
import math

import jax
import jax.numpy as jnp
from jax import lax
from jax.experimental import pallas as pl
from jax.experimental.pallas import tpu as pltpu
from jax.sharding import PartitionSpec as P

f32 = jnp.float32
bf16 = jnp.bfloat16
NODES = 8
VMEM_LIMIT = 12 * 1024 * 1024
VM = pl.BlockSpec(memory_space=pltpu.VMEM)
SM = pl.BlockSpec(memory_space=pltpu.SMEM)


def dot(left, right):
    return lax.dot_general(left, right, (((1,), (0,)), ((), ())), preferred_element_type=f32)


def dot_t(left, right):
    return lax.dot_general(left, right, (((0,), (0,)), ((), ())), preferred_element_type=f32)


def dot_rt(left, right):
    return lax.dot_general(left, right, (((1,), (1,)), ((), ())), preferred_element_type=f32)


def silu_half(half):
    th = jnp.tanh(half)
    prod = half * th
    return half + prod, (0.5 + 0.5 * th) * ((1.0 + half) - prod)


def split_cols(value):
    high = value.astype(bf16)
    low = (value - high.astype(f32)).astype(bf16)
    return jnp.concatenate([high, low], -1)


def up(value):
    return pltpu.roll(value, NODES - 1, 1)


def down(value):
    return pltpu.roll(value, 1, 1)


def flat(value):
    return value.reshape(-1, value.shape[-1])


def node_rows(value):
    return value.reshape(-1, NODES, value.shape[-1])


def row_ids():
    return lax.broadcasted_iota(jnp.int32, (1, NODES, 128), 1)


def couple_slots(plane, filled):
    count, rows, width = plane.shape
    slots = rows // NODES
    parts = plane.reshape(count, slots, NODES, width)
    ids = row_ids()
    done = []
    for s in range(slots):
        here = parts[:, s]
        if s + 1 < slots:
            take = (ids == NODES - 1) & (s + 1 < filled)
            here = here + jnp.where(take, up(parts[:, s + 1]), 0.0)
        if s > 0:
            here = here + jnp.where(ids == 0, down(parts[:, s - 1]), 0.0)
            here = jnp.where(s < filled, here, 0.0)
        done.append(here[:, None])
    return jnp.concatenate(done, 1).reshape(plane.shape)


def elements(x_len, y_len, body):
    ey = y_len // NODES
    total = (x_len // NODES) * ey

    def step(e, carry):
        x0 = pl.multiple_of((e // ey) * NODES, NODES)
        y0 = pl.multiple_of((e % ey) * NODES, NODES)
        body(x0, y0)
        return carry

    lax.fori_loop(0, total, step, 0)


def edges_forward(h_ref, w_one, half_bias, filled, sum_ref, half_ref):
    x_len, y_len, rows, width = h_ref.shape
    inner = row_ids() < NODES - 1

    def body(x0, y0):
        ys = pl.ds(y0, NODES)
        prev = None
        here = h_ref[x0, ys].astype(f32)
        for i in range(NODES):
            parts = []
            nxt = None
            if i < NODES - 1:
                nxt = h_ref[x0 + i + 1, ys].astype(f32)
                parts.append((nxt - here).astype(bf16))
            parts.append((here[1:] - here[:-1]).astype(bf16))
            cols = node_rows(here)
            parts.append((up(cols) - cols).reshape(here.shape).astype(bf16))
            half = dot(flat(jnp.concatenate(parts, 0)), w_one).reshape(-1, rows, width) + half_bias
            act = (half + half * jnp.tanh(half)).astype(bf16).astype(f32)
            at = 0
            total = prev
            prev = None
            if i < NODES - 1:
                prev = act[:NODES]
                total = -prev if total is None else total - prev
                half_ref[0, x0 + i, ys] = half[:NODES]
                at = NODES
            along_y = act[at : at + NODES - 1]
            half_ref[1, x0 + i, pl.ds(y0, NODES - 1)] = half[at : at + NODES - 1]
            at += NODES - 1
            along_z = jnp.where(inner, node_rows(act[at:]), 0.0)
            half_ref[2, x0 + i, ys] = half[at:]
            total = total + (down(along_z) - along_z).reshape(here.shape)
            total = jnp.concatenate(
                [
                    total[:1] - along_y[:1],
                    total[1:-1] + (along_y[:-1] - along_y[1:]),
                    total[-1:] + along_y[-1:],
                ],
                0,
            )
            sum_ref[x0 + i, ys] = couple_slots(total, filled)
            here = nxt

    elements(x_len, y_len, body)


def slope_kernel(sc, half_in, slope_out):
    inner = row_ids() < NODES - 1

    def step(x, carry):
        for k in range(3):
            slope = silu_half(half_in[k, x])[1]
            if k == 2:
                slope = jnp.where(inner, node_rows(slope), 0.0).reshape(slope.shape)
            slope_out[k, x] = slope
        return carry

    lax.fori_loop(0, half_in.shape[1], step, 0)


def couple_columns(sum_ref):
    x_len, y_len = sum_ref.shape[:2]
    for cut in range(NODES, x_len, NODES):
        both = sum_ref[cut - 1] + sum_ref[cut]
        sum_ref[cut - 1] = both
        sum_ref[cut] = both
    for cut in range(NODES, y_len, NODES):
        both = sum_ref[:, cut - 1] + sum_ref[:, cut]
        sum_ref[:, cut - 1] = both
        sum_ref[:, cut] = both


def face_place(sc_ref, axis, kind, last):
    return jnp.where((sc_ref[1 + axis] + kind) % 2 == 0, last, 0)


def end_rows(values, filled, take_top):
    picked = values(0)
    slots = values.slots
    for s in range(slots):
        picked = jnp.where(take_top & (filled == s + 1), values(s * NODES + NODES - 1), picked)
    return picked


class RowReader:
    def __init__(self, slots, read):
        self.slots = slots
        self.read = read

    def __call__(self, row):
        return self.read(row)


def takes_top(sc_ref, kind):
    return (sc_ref[3] + kind) % 2 == 0


def write_faces(sc_ref, sum_ref, faces, counts):
    x_len, y_len, rows, width = sum_ref.shape
    nx, ny, nz = counts
    reader = RowReader(rows // NODES, lambda row: sum_ref[:, :, row])
    for kind in range(ny):
        faces[kind][...] = sum_ref[:, face_place(sc_ref, 1, kind, y_len - 1)]
    for kind in range(nz):
        faces[ny + kind][...] = end_rows(reader, sc_ref[0], takes_top(sc_ref, kind))


def add_halo(sc_ref, from_ref, halo, into_ref, counts):
    x_len, y_len, rows, width = from_ref.shape
    nx, ny, nz = counts

    def copy(x, carry):
        into_ref[x] = from_ref[x]
        return carry

    lax.fori_loop(0, x_len, copy, 0)
    for kind in range(nx):
        into_ref[face_place(sc_ref, 0, kind, x_len - 1)] += halo[kind][...]
    for kind in range(ny):
        into_ref[:, face_place(sc_ref, 1, kind, y_len - 1)] += halo[nx + kind][...]
    if nz:
        got = [halo[nx + ny + kind][...] for kind in range(nz)]
        tops = [takes_top(sc_ref, kind) for kind in range(nz)]
        from_below = sum(jnp.where(top, 0.0, value) for top, value in zip(tops, got))
        from_above = sum(jnp.where(top, value, 0.0) for top, value in zip(tops, got))
        into_ref[:, :, 0] += from_below
        for s in range(rows // NODES):
            into_ref[:, :, s * NODES + NODES - 1] += jnp.where(sc_ref[0] == s + 1, from_above, 0.0)


def fix_y_kernel(counts, sc_ref, *refs):
    nx, ny, nz = counts
    got, faces, outs = refs[:nx], refs[nx : nx + ny], refs[nx + ny :]
    x_len = faces[0].shape[0]
    for k in range(ny):
        outs[k][...] = faces[k][...]
    for kind in range(nx):
        place = face_place(sc_ref, 0, kind, x_len - 1)
        for k in range(ny):
            y_len = got[kind].shape[0]
            outs[k][place] += got[kind][face_place(sc_ref, 1, k, y_len - 1)]


def fix_z_kernel(counts, sc_ref, *refs):
    nx, ny, nz = counts
    got_x, refs = refs[:nx], refs[nx:]
    got_y, refs = refs[:ny][::-1], refs[ny:]
    faces, outs = refs[:nz], refs[nz:]
    x_len, y_len, width = faces[0].shape
    for k in range(nz):
        outs[k][...] = faces[k][...]
    for k in range(nz):
        top = takes_top(sc_ref, k)
        for kind in range(nx):
            ref = got_x[kind]
            reader = RowReader(ref.shape[1] // NODES, lambda row, ref=ref: ref[:, row])
            outs[k][face_place(sc_ref, 0, kind, x_len - 1)] += end_rows(reader, sc_ref[0], top)
        for kind in range(ny):
            ref = got_y[kind]
            reader = RowReader(ref.shape[1] // NODES, lambda row, ref=ref: ref[:, row])
            add = end_rows(reader, sc_ref[0], top)
            first = face_place(sc_ref, 1, kind, 1) == 0
            outs[k][:, 0] += jnp.where(first, add, 0.0)
            outs[k][:, y_len - 1] += jnp.where(first, 0.0, add)


def write_inverse(sc_ref, inv_ref, sizes):
    y_len, rows, width = inv_ref.shape
    filled, at_y, at_z = sc_ref[0], sc_ref[2], sc_ref[3]
    ids = lax.broadcasted_iota(jnp.int32, (rows, width), 0)
    node = ids % NODES
    low = (node == 0) & ((ids >= NODES) | (at_z > 0))
    high = (node == NODES - 1) & ((ids < (filled - 1) * NODES) | (at_z < sizes[2] - 1))
    along_z = jnp.where(low | high, 0.5, 1.0).astype(f32)
    for y in range(y_len):
        inv_ref[y] = along_z * end_factor(y, y_len, at_y, sizes[1])


def end_factor(place, length, position, size):
    whole = place + position * length
    low = (place % NODES == 0) & (whole > 0)
    high = (place % NODES == NODES - 1) & (whole < length * size - 1)
    return jnp.where(low | high, 0.5, 1.0).astype(f32)


CHUNK = 8


def scale_planes(sc_ref, inv_ref, x, block, x_len, size_x):
    inv = inv_ref[...]
    parts = [block[c] * (inv * end_factor(x + c, x_len, sc_ref[1], size_x)) for c in range(block.shape[0])]
    return jnp.stack(parts, 0)


def node_forward(scaled, feat, weights, layer):
    edge_w, node_in, node_out, biases = weights
    pair = split_cols(scaled)
    w_two = edge_w[layer, 1]
    joined = jnp.concatenate([feat, dot(pair, jnp.concatenate([w_two, w_two], 0)).astype(bf16)], -1)
    half = jnp.bfloat16(0.5)
    act, slope = silu_half(dot(joined, node_in[layer] * half) + 0.5 * biases[layer, pl.ds(1, 1)])
    return pair[:, :128], act.astype(bf16), slope


def node_slopes(grad, slope, weights, layer):
    return (dot_rt(grad, weights[2][layer]) * slope).astype(bf16)


def node_share(sc_ref, x, inv_ref, size_x, dpn, weights, layer, sum_ref):
    shape = (CHUNK,) + sum_ref.shape[1:]
    dx = dot_rt(dpn, weights[1][layer, pl.ds(128, 128)]).reshape(shape)
    share = scale_planes(sc_ref, inv_ref, x, dx, sum_ref.shape[0], size_x)
    joined = couple_slots(share.reshape((-1,) + shape[2:]), sc_ref[0])
    sum_ref[pl.ds(x, CHUNK)] = joined.reshape(shape)


def node_products(grad, feat, scaled, act, dpn, grads):
    grads[pl.ds(0, 128)] += dot_t(act, grad)
    both = dot_t(dpn, jnp.concatenate([feat, scaled], -1))
    grads[pl.ds(128, 128)] += both[:, :128]
    grads[pl.ds(256, 128)] += both[:, 128:]
    grads[pl.ds(384, NODES)] += jnp.sum(dpn.astype(f32).reshape(-1, NODES, 128), 0)


def couple_plane(plane):
    y_len = plane.shape[0]
    parts = [plane[y] for y in range(y_len)]
    for cut in range(NODES, y_len, NODES):
        both = parts[cut - 1] + parts[cut]
        parts[cut - 1] = parts[cut] = both
    return jnp.stack(parts, 0)


def along_y(plane, combine):
    return [
        combine(plane[y : y + NODES - 1], plane[y + 1 : y + NODES], y) for y in range(0, plane.shape[0], NODES)
    ]


def spread_plane(sign, edge_x, edges_y, edge_z):
    total = sign * edge_x + (down(edge_z) - edge_z).reshape(edge_x.shape)
    parts = []
    for k, edge in enumerate(edges_y):
        here = total[k * NODES : (k + 1) * NODES]
        parts += [here[:1] - edge[:1], here[1:-1] + (edge[:-1] - edge[1:]), here[-1:] + edge[-1:]]
    return jnp.concatenate(parts, 0)


def plane_forward(low, high, at_high, w_one, half_bias, filled):
    y_len, rows, width = low.shape
    here = jnp.where(at_high, high, low)
    cols = node_rows(here)
    parts = [(high - low).astype(bf16)]
    parts += along_y(here, lambda lower, upper, y: (upper - lower).astype(bf16))
    parts.append((up(cols) - cols).reshape(here.shape).astype(bf16))
    half = dot(flat(jnp.concatenate(parts, 0)), w_one).reshape(-1, rows, width) + half_bias
    act = silu_half(half)[0].astype(bf16).astype(f32)
    at = y_len
    edges_y = []
    for _ in range(y_len // NODES):
        edges_y.append(act[at : at + NODES - 1])
        at += NODES - 1
    edge_z = jnp.where(row_ids() < NODES - 1, node_rows(act[at:]), 0.0)
    total = spread_plane(jnp.where(at_high, 1.0, -1.0), act[:y_len], edges_y, edge_z)
    return couple_plane(couple_slots(total, filled))


def plane_backward(low, high, at_high, slope_x, slope_y, slope_z):
    here = jnp.where(at_high, high, low)
    cols = node_rows(here)
    edge_x = ((high - low) * slope_x).astype(bf16).astype(f32)
    edges_y = along_y(
        here, lambda lower, upper, y: ((upper - lower) * slope_y[y : y + NODES - 1]).astype(bf16).astype(f32)
    )
    edge_z = ((up(cols) - cols) * node_rows(slope_z)).astype(bf16).astype(f32)
    return spread_plane(jnp.where(at_high, 1.0, -1.0), edge_x, edges_y, edge_z)


def face_planes(sc_ref, kind, x_len):
    place = face_place(sc_ref, 0, kind, x_len - 1)
    at_high = place > 0
    return place, jnp.where(at_high, x_len - 2, 0), at_high


def halo_planes(sc_ref, from_ref, halo, kind, start, into_ref, counts):
    x_len, y_len, rows, width = from_ref.shape
    nx, ny, nz = counts
    for c in range(2):
        into_ref[c] = from_ref[start + c]
    into_ref[face_place(sc_ref, 0, kind, x_len - 1) - start] += halo[kind][...]
    for c in range(2):
        for k in range(ny):
            into_ref[c, face_place(sc_ref, 1, k, y_len - 1)] += halo[nx + k][start + c]
        for k in range(nz):
            got = halo[nx + ny + k][start + c]
            top = takes_top(sc_ref, k)
            into_ref[c, :, 0] += jnp.where(top, 0.0, got)
            for s in range(rows // NODES):
                into_ref[c, :, s * NODES + NODES - 1] += jnp.where(top & (sc_ref[0] == s + 1), got, 0.0)


def edges_backward(q_ref, slope_ref, edge_ref, bias_acc):
    x_len, y_len, rows, width = q_ref.shape

    def body(x0, y0):
        ys = pl.ds(y0, NODES)
        prev = None
        here = q_ref[x0, ys]
        bias = jnp.zeros((NODES, width), f32)
        for i in range(NODES):
            total = prev
            prev = None
            nxt = None
            if i < NODES - 1:
                nxt = q_ref[x0 + i + 1, ys]
                prev = ((nxt - here) * slope_ref[0, x0 + i, ys]).astype(bf16).astype(f32)
                total = -prev if total is None else total - prev
                bias = bias + jnp.sum(node_rows(prev), 0)
            along_y = (here[1:] - here[:-1]) * slope_ref[1, x0 + i, pl.ds(y0, NODES - 1)]
            along_y = along_y.astype(bf16).astype(f32)
            cols = node_rows(here)
            along_z = (up(cols) - cols) * node_rows(slope_ref[2, x0 + i, ys])
            along_z = along_z.astype(bf16).astype(f32)
            bias = bias + jnp.sum(node_rows(along_y), 0) + jnp.sum(along_z, 0)
            total = total + (down(along_z) - along_z).reshape(here.shape)
            total = jnp.concatenate(
                [
                    total[:1] - along_y[:1],
                    total[1:-1] + (along_y[:-1] - along_y[1:]),
                    total[-1:] + along_y[-1:],
                ],
                0,
            )
            edge_ref[x0 + i, ys] = total
            here = nxt
        bias_acc[...] += bias

    elements(x_len, y_len, body)


def planes(count, body):
    def step(c, carry):
        body(pl.multiple_of(c * CHUNK, CHUNK))
        return carry

    lax.fori_loop(0, count // CHUNK, step, 0)


def half_weights(weights, layer):
    edge_w, node_in, node_out, biases = weights
    return edge_w[layer, 0] * jnp.bfloat16(0.5), 0.5 * biases[layer, pl.ds(0, 1)]


def first_kernel(counts, sizes, sc, edge_w, biases, h, sums, slopes, *faces):
    w_one, bias = half_weights((edge_w, None, None, biases), 0)
    edges_forward(h, w_one, bias, sc[0], sums, slopes)
    couple_columns(sums)
    write_faces(sc, sums, faces, counts)


def first_face_kernel(counts, sizes, sc, edge_w, biases, h, *faces):
    w_one, bias = half_weights((edge_w, None, None, biases), 0)
    for kind, face in enumerate(faces):
        place, start, at_high = face_planes(sc, kind, h.shape[0])
        face[...] = plane_forward(
            h[start].astype(f32), h[start + 1].astype(f32), at_high, w_one, bias, sc[0]
        )


def middle_face_kernel(counts, sizes, sc, edge_w, node_in, node_out, biases, sums_in, h, *refs):
    weights = (edge_w, node_in, node_out, biases)
    n = sum(counts)
    halo, faces, (pair, inv) = refs[:n], refs[n:-2], refs[-2:]
    write_inverse(sc, inv, sizes)
    w_one, bias = half_weights(weights, 1)
    x_len = h.shape[0]
    for kind, face in enumerate(faces):
        place, start, at_high = face_planes(sc, kind, x_len)
        halo_planes(sc, sums_in, halo, kind, start, pair, counts)
        sums_at = flat(scale_planes(sc, inv, start, pair[...], x_len, sizes[0]))
        feat = flat(h[pl.ds(start, 2)])
        scaled, act, slope = node_forward(sums_at, feat, weights, 0)
        moved = (feat.astype(f32) + dot(act, node_out[0])).astype(bf16).astype(f32).reshape(pair.shape)
        face[...] = plane_forward(moved[0], moved[1], at_high, w_one, bias, sc[0])


def face_share(sc, sizes, inv, place, x_len, grad, slope, weights, layer, shape):
    dpn = node_slopes(grad, slope, weights, layer)
    dx = dot_rt(dpn, weights[1][layer, pl.ds(128, 128)]).reshape((1,) + shape)
    share = scale_planes(sc, inv, place, dx, x_len, sizes[0])
    return couple_plane(couple_slots(share[0], sc[0]))


def turn_face_kernel(counts, sizes, sc, edge_w, node_in, node_out, biases, sums_in, h, g_ref, *refs):
    weights = (edge_w, node_in, node_out, biases)
    n = sum(counts)
    halo, faces, (pair, inv) = refs[:n], refs[n:-2], refs[-2:]
    write_inverse(sc, inv, sizes)
    x_len, shape = h.shape[0], h.shape[1:]
    live = (lax.broadcasted_iota(jnp.int32, (1, h.shape[2], 128), 1) < sc[0] * NODES).astype(f32)
    for kind, face in enumerate(faces):
        place, start, at_high = face_planes(sc, kind, x_len)
        halo_planes(sc, sums_in, halo, kind, start, pair, counts)
        plane = pair[place - start][None]
        sums_at = flat(scale_planes(sc, inv, place, plane, x_len, sizes[0]))
        scaled, act, slope = node_forward(sums_at, flat(h[place]), weights, 1)
        grad = flat((g_ref[place].astype(f32) * live).astype(bf16))
        face[...] = face_share(sc, sizes, inv, place, x_len, grad, slope, weights, 1, shape)


def join_face_kernel(counts, sizes, sc, edge_w, node_in, node_out, biases, sums_in, base_in, slopes, slope0, *refs):
    weights = (edge_w, node_in, node_out, biases)
    n = sum(counts)
    halo, faces, (pair, inv) = refs[:n], refs[n:-2], refs[-2:]
    write_inverse(sc, inv, sizes)
    x_len, shape = base_in.shape[0], base_in.shape[1:]
    w_two, w_one = twice(edge_w[1, 1]), twice(edge_w[1, 0])
    for kind, face in enumerate(faces):
        place, start, at_high = face_planes(sc, kind, x_len)
        halo_planes(sc, sums_in, halo, kind, start, pair, counts)
        q = dot_rt(split_cols(flat(pair[...])), w_two).reshape(pair.shape)
        edge = plane_backward(q[0], q[1], at_high, slopes[0, start], slopes[1, place], slopes[2, place])
        grad = (flat(base_in[place]) + dot_rt(split_cols(flat(edge)), w_one)).astype(bf16)
        face[...] = face_share(sc, sizes, inv, place, x_len, grad, flat(slope0[place]), weights, 0, shape)


def twice(weight):
    return jnp.concatenate([weight, weight], 1)


def middle_kernel(counts, sizes, sc, edge_w, node_in, node_out, biases, sums_in, h, *refs):
    weights = (edge_w, node_in, node_out, biases)
    n = sum(counts)
    halo, refs = refs[:n], refs[n:]
    scaled_ref, act_ref, slope_ref, next_ref, sums, slopes = refs[:6]
    faces, (work, inv) = refs[6:-2], refs[-2:]
    add_halo(sc, sums_in, halo, work, counts)
    write_inverse(sc, inv, sizes)
    shape = (CHUNK,) + h.shape[1:]

    def body(x):
        at = pl.ds(x, CHUNK)
        sums_at = flat(scale_planes(sc, inv, x, work[at], h.shape[0], sizes[0]))
        scaled, act, slope = node_forward(sums_at, flat(h[at]), weights, 0)
        scaled_ref[at] = scaled.reshape(shape)
        act_ref[at] = act.reshape(shape)
        slope_ref[at] = slope.reshape(shape)
        moved = flat(h[at]).astype(f32) + dot(act, node_out[0])
        next_ref[at] = moved.astype(bf16).reshape(shape)

    planes(h.shape[0], body)
    w_one, bias = half_weights(weights, 1)
    edges_forward(next_ref, w_one, bias, sc[0], sums, slopes)
    couple_columns(sums)
    write_faces(sc, sums, faces, counts)


def turn_kernel(counts, sizes, sc, edge_w, node_in, node_out, biases, sums_in, h, g_ref, *refs):
    weights = (edge_w, node_in, node_out, biases)
    n = sum(counts)
    halo, refs = refs[:n], refs[n:]
    scaled_ref, act_ref, dpn_ref, sums = refs[:4]
    faces, (work, inv) = refs[4:-2], refs[-2:]
    add_halo(sc, sums_in, halo, work, counts)
    write_inverse(sc, inv, sizes)
    shape = (CHUNK,) + h.shape[1:]
    live = live_rows(sc, h)

    def body(x):
        at = pl.ds(x, CHUNK)
        sums_at = flat(scale_planes(sc, inv, x, work[at], h.shape[0], sizes[0]))
        scaled, act, slope = node_forward(sums_at, flat(h[at]), weights, 1)
        scaled_ref[at] = scaled.reshape(shape)
        act_ref[at] = act.reshape(shape)
        grad = flat((g_ref[at].astype(f32) * live).astype(bf16))
        dpn = node_slopes(grad, slope, weights, 1)
        dpn_ref[at] = dpn.reshape(shape)
        node_share(sc, x, inv, sizes[0], dpn, weights, 1, sums)

    planes(h.shape[0], body)
    couple_columns(sums)
    write_faces(sc, sums, faces, counts)


def live_rows(sc, h):
    return (lax.broadcasted_iota(jnp.int32, (1, 1, h.shape[2], 128), 2) < sc[0] * NODES).astype(f32)


def products_kernel(sc, node_in, h, g_ref, scaled, act, dpn, base, grads):
    grads[...] = jnp.zeros_like(grads)
    live = live_rows(sc, h)

    def body(x):
        at = pl.ds(x, CHUNK)
        grad = (g_ref[at].astype(f32) * live).astype(bf16)
        node_products(flat(grad), flat(h[at]), flat(scaled[at]), flat(act[at]), flat(dpn[at]), grads)
        dx = dot_rt(flat(dpn[at]), node_in[1, pl.ds(0, 128)])
        base[at] = grad.astype(f32) + dx.reshape(grad.shape)

    planes(h.shape[0], body)


def edge_parts(counts, sc, weights, layer, sums_in, halo, h, slopes, work, grads, row):
    add_halo(sc, sums_in, halo, work, counts)
    shape = (CHUNK,) + h.shape[1:]
    w_two = twice(weights[0][layer, 1])

    def to_q(x):
        at = pl.ds(x, CHUNK)
        work[at] = dot_rt(split_cols(flat(work[at])), w_two).reshape(shape)

    planes(h.shape[0], to_q)
    edges_backward(work, slopes, work, grads.at[pl.ds(row + 128, NODES)])


def edge_product(h, x, pair, grads, row):
    both = dot_t(flat(h[pl.ds(x, CHUNK)]), pair)
    grads[pl.ds(row, 128)] += both[:, :128] + both[:, 128:]


def join_kernel(
    counts, sizes, sc, edge_w, node_in, node_out, biases,
    sums_in, h, base_in, slopes, h0, scaled0, act0, slope0, grads1, *refs
):
    weights = (edge_w, node_in, node_out, biases)
    n = sum(counts)
    halo, refs = refs[:n], refs[n:]
    grad_ref, dpn_ref, sums, keep, send = refs[:5]
    faces, (work, inv, grads) = refs[5:-3], refs[-3:]
    write_inverse(sc, inv, sizes)
    grads[...] = jnp.zeros_like(grads)
    grads[pl.ds(512 + 2 * NODES, grads1.shape[0])] = grads1[...]

    row = 384 + NODES
    shape = (CHUNK,) + h.shape[1:]
    edge_parts(counts, sc, weights, 1, sums_in, halo, h, slopes, work, grads, row)
    w_one = twice(edge_w[1, 0])

    def body(x):
        at = pl.ds(x, CHUNK)
        pair = split_cols(flat(work[at]))
        edge_product(h, x, pair, grads, row)
        grad = (flat(base_in[at]) + dot_rt(pair, w_one)).astype(bf16)
        dpn = node_slopes(grad, flat(slope0[at]), weights, 0)
        node_products(grad, flat(h0[at]), flat(scaled0[at]), flat(act0[at]), dpn, grads)
        grad_ref[at] = grad.reshape(shape)
        dpn_ref[at] = dpn.reshape(shape)
        node_share(sc, x, inv, sizes[0], dpn, weights, 0, sums)

    planes(h.shape[0], body)
    couple_columns(sums)
    write_faces(sc, sums, faces, counts)
    write_halves(sc, halving_steps(sizes)[0], grads, keep, send)


def last_kernel(counts, sizes, sc, edge_w, node_in, node_out, biases, sums_in, h, slopes, *refs):
    n = sum(counts)
    halo, (edges, grads) = refs[:n], refs[n:]
    grads[...] = jnp.zeros_like(grads)
    edge_parts(counts, sc, (edge_w,), 0, sums_in, halo, h, slopes, edges, grads, 0)

    def body(x):
        edge_product(h, x, split_cols(flat(edges[pl.ds(x, CHUNK)])), grads, 0)

    planes(h.shape[0], body)


def state_kernel(sc, edge_w, node_in, grad_in, dpn, edges, grad_ref):
    shape = (CHUNK,) + edges.shape[1:]
    weight = jnp.concatenate([twice(edge_w[0, 0]), node_in[0, pl.ds(0, 128)]], 1)

    def body(x):
        at = pl.ds(x, CHUNK)
        parts = jnp.concatenate([split_cols(flat(edges[at])), flat(dpn[at])], -1)
        grad_ref[at] = (flat(grad_in[at]).astype(f32) + dot_rt(parts, weight)).astype(bf16).reshape(shape)

    planes(edges.shape[0], body)


def finish_kernel(scale, last_rows, step, sc, edge_w, node_in, value, got, *refs):
    edge_grads, in_grads, out_grads, bias_grads, both = refs
    width = edge_w.shape[-1]
    join_kernel_of(step, last_rows, sc, value, got, both)

    def rows_of(part, start, count=width):
        ref, offset = part
        return ref[pl.ds(offset + start, count)] * scale

    def bias_of(part, start):
        return jnp.sum(rows_of(part, start, NODES), 0, keepdims=True)

    end = 3 * width
    last, sum0 = (both, 0), (both, last_rows)
    sum1 = (both, last_rows + 512 + 2 * NODES)
    firsts = ((last, 0), (sum0, end + NODES))
    for layer, part in enumerate((sum0, sum1)):
        out_grads[layer] = rows_of(part, 0)
        in_grads[layer, pl.ds(0, width)] = rows_of(part, width).T
        bias_grads[layer, pl.ds(1, 1)] = bias_of(part, end)
        source, start = firsts[layer]
        edge_grads[layer, 0] = rows_of(source, start)
        bias_grads[layer, pl.ds(0, 1)] = bias_of(source, start + width)
        mixed = rows_of(part, 2 * width).T
        high = mixed.astype(bf16)
        low = (mixed - high.astype(f32)).astype(bf16)
        lower = node_in[layer, pl.ds(width, width)]
        edge_grads[layer, 1] = dot_rt(high, lower) + dot_rt(low, lower)
        w_two = edge_w[layer, 1]
        in_grads[layer, pl.ds(width, width)] = dot_t(w_two, high) + dot_t(w_two, low)


def call(kernel, name, inputs, outs, scratch=(), flops=0, aliases=None):
    total = sum(math.prod(o.shape) * o.dtype.itemsize for o in outs)
    total += sum(math.prod(i.shape) * i.dtype.itemsize for i in inputs)
    return pl.pallas_call(
        kernel,
        name=name,
        out_shape=tuple(outs),
        in_specs=[SM] + [VM] * (len(inputs) - 1),
        out_specs=tuple([VM] * len(outs)),
        scratch_shapes=list(scratch),
        input_output_aliases=aliases or {},
        compiler_params=pltpu.CompilerParams(vmem_limit_bytes=VMEM_LIMIT),
        cost_estimate=pl.CostEstimate(flops=flops, bytes_accessed=total, transcendentals=0),
    )(*inputs)


def pairs(size, kind):
    return [
        pair for low in range(kind, size - 1, 2) for pair in ((low, low + 1), (low + 1, low))
    ]


def hops(size):
    found = []
    hop = 1
    while hop < size:
        found.append(hop)
        hop *= 2
    return found


def halving_steps(sizes):
    steps = [(1, hop) for hop in hops(sizes[1])[:1]]
    steps += [(0, hop) for hop in hops(sizes[0])]
    return steps + [(1, hop) for hop in hops(sizes[1])[1:]]


def padded_rows(rows, sizes):
    unit = NODES << len(halving_steps(sizes))
    return -(-rows // unit) * unit


def bit_of(sc_ref, step):
    axis, hop = step
    return (sc_ref[1 + axis] // hop) % 2


def write_halves(sc_ref, step, from_ref, keep, send):
    half = keep.shape[0]
    bit = bit_of(sc_ref, step)
    keep[...] = from_ref[pl.ds(pl.multiple_of(bit * half, NODES), half)]
    send[...] = from_ref[pl.ds(pl.multiple_of((1 - bit) * half, NODES), half)]


def halve_kernel(step, sc, keep_in, got, keep, send, total):
    total[...] = keep_in[...] + got[...]
    write_halves(sc, step, total, keep, send)


def add_kernel(sc, left, right, out):
    out[...] = left[...] + right[...]


def join_kernel_of(step, start, sc, value, got, out):
    half = value.shape[0] - start
    bit = bit_of(sc, step)
    if start:
        out[pl.ds(0, start)] = value[pl.ds(0, start)] + got[pl.ds(0, start)]
    out[pl.ds(pl.multiple_of(start + bit * half, NODES), half)] = value[pl.ds(start, half)]
    out[pl.ds(pl.multiple_of(start + (1 - bit) * half, NODES), half)] = got[pl.ds(start, half)]


def stack_kernel(sc, first, left, right, out):
    rows = first.shape[0]
    out[pl.ds(0, rows)] = first[...]
    out[pl.ds(rows, left.shape[0])] = left[...] + right[...]


def swap(value, step):
    axis = ("gx", "gy", "gz")[step[0]]
    return lax.ppermute(value, axis, [(i, i ^ step[1]) for i in range(lax.axis_size(axis))])


def rows_like(rows, width=128):
    return jax.ShapeDtypeStruct((rows, width), f32)


def halve(sc, sizes, keep, send):
    steps = halving_steps(sizes)
    got = swap(send, steps[0])
    for step in steps[1:]:
        keep, got = yield keep, got
        half = rows_like(keep.shape[0] // 2)
        keep, send = call(
            functools.partial(halve_kernel, step), "halve", (sc, keep, got), [half, half],
            [pltpu.VMEM(keep.shape, f32)],
        )
        got = swap(send, step)
    keep, got = yield keep, got
    return keep, got


class Background:
    def __init__(self):
        self.active = {}

    def add(self, name, steps):
        self.active[name] = [steps, None]

    def advance(self, entry, tied):
        steps, pending = entry
        try:
            entry[1] = next(steps) if pending is None else steps.send(tied)
        except StopIteration:
            entry[0] = None

    def beside(self, anchor):
        for entry in self.active.values():
            steps, pending = entry
            if steps is None:
                continue
            if pending is None:
                self.advance(entry, None)
            elif pending[1] is not None:
                anchor, tied = lax.optimization_barrier((anchor, pending))
                self.advance(entry, tied)
        return anchor

    def finish(self, name):
        entry = self.active[name]
        while entry[0] is not None:
            done = entry[1]
            if done is not None and done[1] is None:
                return done[0]
            self.advance(entry, done)
        return entry[1]


def on_device(state, cotangent, counts, edge_weights, node_in, node_out, biases):
    x_len, y_len, slots, nodes, width = state.shape
    rows = slots * nodes
    grid = (x_len, y_len, rows, width)
    axes = ("gx", "gy", "gz")
    sizes = tuple(lax.axis_size(a) for a in axes)
    trades = tuple(min(size - 1, 2) for size in sizes)
    nx, ny, nz = trades
    h0 = state.reshape(grid)
    g2 = cotangent.reshape(grid)
    sc = jnp.stack([counts[0]] + [lax.axis_index(a).astype(jnp.int32) for a in axes])

    def sds(shape, kind=f32):
        return jax.ShapeDtypeStruct(shape, kind)

    face_x = sds((y_len, rows, width))
    face_y = sds((x_len, rows, width))
    face_z = sds((x_len, y_len, width))
    face_outs = [face_y] * ny + [face_z] * nz
    full = sds(grid)
    full16 = sds(grid, bf16)
    full3 = sds((3,) + grid)
    work = pltpu.VMEM(grid, f32)
    inv = pltpu.VMEM((y_len, rows, width), f32)
    matmul = 2 * math.prod(grid) * width
    weights = (edge_weights, node_in, node_out, biases)

    def run(kernel, name, inputs, outs, scratch, flops):
        body = functools.partial(kernel, trades, sizes)
        return call(body, name, (sc, *weights, *inputs), outs, scratch, flops * matmul)

    def trade(faces, axis):
        size = lax.axis_size(axis)
        got = [lax.ppermute(face, axis, pairs(size, kind)) for kind, face in reversed(list(enumerate(faces)))]
        return got[::-1]

    background = Background()

    pair = pltpu.VMEM((2,) + grid[1:], f32)

    def first_trade(kernel, name, inputs, scratch, flops):
        faces = call(functools.partial(kernel, trades, sizes), name, (sc, *inputs), [face_x] * nx, scratch, flops)
        return trade(faces, "gx")

    def exchange(got_x, faces, work=None, held=()):
        fix = functools.partial(fix_y_kernel, trades)
        faces_y = call(fix, "fix_y", (sc, *got_x, *faces[:ny]), [face_y] * ny)
        got_y = trade(background.beside(faces_y), "gy")
        fix = functools.partial(fix_z_kernel, trades)
        faces_z = call(fix, "fix_z", (sc, *got_x, *got_y[::-1], *faces[ny:]), [face_z] * nz)
        faces_z = background.beside(faces_z)
        done = None
        if work is not None:
            faces_z, held = lax.optimization_barrier((faces_z, held))
            done = work(*held)
        got_z = background.beside(trade(faces_z, "gz"))
        got_z, done = lax.optimization_barrier((got_z, done))
        return (*got_x, *got_y, *got_z), done

    def to_slopes(half):
        return call(slope_kernel, "slopes", (sc, half), [full3], [], matmul, {1: 0})[0]

    def products(*held):
        return call(
            products_kernel, "nodes1_products", (sc, node_in, *held), [full, rows_like(3 * width + NODES)], [], 6 * matmul
        )

    got_x = first_trade(first_face_kernel, "face0", (edge_weights, biases, h0), [], matmul // 8)
    sums, slopes0, *faces = call(
        functools.partial(first_kernel, trades, sizes), "edges0", (sc, edge_weights, biases, h0),
        [full, full3] + face_outs, [], 3 * matmul,
    )
    halo, slopes0 = exchange(got_x, faces, to_slopes, (slopes0,))
    inputs = (*weights, sums, h0, *halo)
    got_x = first_trade(middle_face_kernel, "face1", inputs, [pair, inv], matmul // 4)
    scaled0, act0, slope0, h1, sums, slopes1, *faces = run(
        middle_kernel, "nodes0_edges1", (sums, h0, *halo),
        [full16, full16, full, full16, full, full3] + face_outs, [work, inv], 8,
    )
    halo, slopes1 = exchange(got_x, faces, to_slopes, (slopes1,))
    inputs = (*weights, sums, h1, g2, *halo)
    got_x = first_trade(turn_face_kernel, "face2", inputs, [pair, inv], matmul // 4)
    scaled1, act1, dpn1, sums, *faces = run(
        turn_kernel, "nodes1_back", (sums, h1, g2, *halo), [full16] * 3 + [full] + face_outs, [work, inv], 7
    )
    halo, (base, grads1) = exchange(got_x, faces, products, (h1, g2, scaled1, act1, dpn1))
    inputs = (*weights, sums, base, slopes1, slope0, *halo)
    got_x = first_trade(join_face_kernel, "face3", inputs, [pair, inv], matmul // 4)
    grad_rows = padded_rows(7 * width + 3 * NODES, sizes)
    half = rows_like(grad_rows // 2)
    grad_in, dpn0, sums, keep, send, *faces = run(
        join_kernel, "edges1_back_nodes0_back",
        (sums, h1, base, slopes1, h0, scaled0, act0, slope0, grads1, *halo),
        [full16, full16, full, half, half] + face_outs, [work, inv, pltpu.VMEM((grad_rows, width), f32)], 12,
    )
    background.add("sums", halve(sc, sizes, keep, send))
    halo, _ = exchange(got_x, faces)
    tail_rows = width + NODES
    edges, last = run(last_kernel, "edges0_back", (sums, h0, slopes0, *halo), [full, rows_like(tail_rows)], [], 6)
    keep, got = background.finish("sums")
    (value,) = call(stack_kernel, "stack", (sc, last, keep, got), [rows_like(tail_rows + keep.shape[0])])
    value, grad_in, dpn0, edges = lax.optimization_barrier((value, grad_in, dpn0, edges))
    (grad0,) = call(
        state_kernel, "state_grad", (sc, edge_weights, node_in, grad_in, dpn0, edges), [full16], [], 4 * matmul
    )
    for hop in reversed(hops(sizes[2])):
        (value,) = call(add_kernel, "add", (sc, value, swap(value, (2, hop))), [rows_like(value.shape[0])])
        value, grad0 = lax.optimization_barrier((value, grad0))
    first, *rest = halving_steps(sizes)
    for step in reversed(rest):
        out = rows_like(2 * value.shape[0] - tail_rows)
        body = functools.partial(join_kernel_of, step, tail_rows)
        (value,) = call(body, "join", (sc, value, swap(value, step)), [out])
    layers_all = 3 * slots * sizes[2] // 4
    nodes_all = x_len * sizes[0] * y_len * sizes[1] * layers_all * nodes
    scale = 1.0 / math.sqrt(nodes_all)
    edge_grads, in_grads, out_grads, bias_grads = call(
        functools.partial(finish_kernel, scale, tail_rows, first), "finish",
        (sc, edge_weights, node_in, value, swap(value, first)),
        [sds(edge_weights.shape), sds(node_in.shape), sds(node_out.shape), sds(biases.shape)],
        [pltpu.VMEM((2 * value.shape[0] - tail_rows, width), f32)],
    )
    return grad0.reshape(state.shape), edge_grads, in_grads, out_grads, bias_grads


def solution(mesh):
    return jax.shard_map(
        on_device,
        mesh=mesh,
        in_specs=(
            P("gx", "gy", "gz", None, None),
            P("gx", "gy", "gz", None, None),
            P("gz"),
            P(),
            P(),
            P(),
            P(),
        ),
        out_specs=(P("gx", "gy", "gz", None, None), P(), P(), P(), P()),
        check_vma=False,
    )
```

```python
import functools
import itertools
import math

import jax
import jax.numpy as jnp
from jax import lax
from jax.experimental import pallas as pl
from jax.experimental.pallas import tpu as pltpu
from jax.sharding import PartitionSpec as P

f32 = jnp.float32
bf16 = jnp.bfloat16
NODES = 8
VMEM_LIMIT = 12 * 1024 * 1024
VM = pl.BlockSpec(memory_space=pltpu.VMEM)
SM = pl.BlockSpec(memory_space=pltpu.SMEM)


def dot(left, right):
    return lax.dot_general(left, right, (((1,), (0,)), ((), ())), preferred_element_type=f32)


def dot_t(left, right):
    return lax.dot_general(left, right, (((0,), (0,)), ((), ())), preferred_element_type=f32)


def dot_rt(left, right):
    return lax.dot_general(left, right, (((1,), (1,)), ((), ())), preferred_element_type=f32)


def silu_half(half):
    th = jnp.tanh(half)
    prod = half * th
    return half + prod, (0.5 + 0.5 * th) * ((1.0 + half) - prod)


def split_cols(value):
    high = value.astype(bf16)
    low = (value - high.astype(f32)).astype(bf16)
    return jnp.concatenate([high, low], -1)


def up(value):
    return pltpu.roll(value, NODES - 1, 1)


def down(value):
    return pltpu.roll(value, 1, 1)


def flat(value):
    return value.reshape(-1, value.shape[-1])


def node_rows(value):
    return value.reshape(-1, NODES, value.shape[-1])


def row_ids():
    return lax.broadcasted_iota(jnp.int32, (1, NODES, 128), 1)


def couple_slots(plane, filled):
    count, rows, width = plane.shape
    slots = rows // NODES
    parts = plane.reshape(count, slots, NODES, width)
    ids = row_ids()
    done = []
    for s in range(slots):
        here = parts[:, s]
        if s + 1 < slots:
            take = (ids == NODES - 1) & (s + 1 < filled)
            here = here + jnp.where(take, up(parts[:, s + 1]), 0.0)
        if s > 0:
            here = here + jnp.where(ids == 0, down(parts[:, s - 1]), 0.0)
            here = jnp.where(s < filled, here, 0.0)
        done.append(here[:, None])
    return jnp.concatenate(done, 1).reshape(plane.shape)


def elements(x_len, y_len, body):
    ey = y_len // NODES
    total = (x_len // NODES) * ey

    def step(e, carry):
        x0 = pl.multiple_of((e // ey) * NODES, NODES)
        y0 = pl.multiple_of((e % ey) * NODES, NODES)
        body(x0, y0)
        return carry

    lax.fori_loop(0, total, step, 0)


def edges_forward(h_ref, w_one, half_bias, filled, sum_ref, half_ref):
    x_len, y_len, rows, width = h_ref.shape
    inner = row_ids() < NODES - 1

    def body(x0, y0):
        ys = pl.ds(y0, NODES)
        prev = None
        here = h_ref[x0, ys].astype(f32)
        for i in range(NODES):
            parts = []
            nxt = None
            if i < NODES - 1:
                nxt = h_ref[x0 + i + 1, ys].astype(f32)
                parts.append((nxt - here).astype(bf16))
            parts.append((here[1:] - here[:-1]).astype(bf16))
            cols = node_rows(here)
            parts.append((up(cols) - cols).reshape(here.shape).astype(bf16))
            half = dot(flat(jnp.concatenate(parts, 0)), w_one).reshape(-1, rows, width) + half_bias
            act = (half + half * jnp.tanh(half)).astype(bf16).astype(f32)
            at = 0
            total = prev
            prev = None
            if i < NODES - 1:
                prev = act[:NODES]
                total = -prev if total is None else total - prev
                half_ref[0, x0 + i, ys] = half[:NODES]
                at = NODES
            along_y = act[at : at + NODES - 1]
            half_ref[1, x0 + i, pl.ds(y0, NODES - 1)] = half[at : at + NODES - 1]
            at += NODES - 1
            along_z = jnp.where(inner, node_rows(act[at:]), 0.0)
            half_ref[2, x0 + i, ys] = half[at:]
            total = total + (down(along_z) - along_z).reshape(here.shape)
            total = jnp.concatenate(
                [
                    total[:1] - along_y[:1],
                    total[1:-1] + (along_y[:-1] - along_y[1:]),
                    total[-1:] + along_y[-1:],
                ],
                0,
            )
            sum_ref[x0 + i, ys] = couple_slots(total, filled)
            here = nxt

    elements(x_len, y_len, body)


def slope_kernel(sc, half_in, slope_out):
    inner = row_ids() < NODES - 1

    def step(x, carry):
        for k in range(3):
            slope = silu_half(half_in[k, x])[1]
            if k == 2:
                slope = jnp.where(inner, node_rows(slope), 0.0).reshape(slope.shape)
            slope_out[k, x] = slope
        return carry

    lax.fori_loop(0, half_in.shape[1], step, 0)


def couple_columns(sum_ref):
    x_len, y_len = sum_ref.shape[:2]
    for cut in range(NODES, x_len, NODES):
        both = sum_ref[cut - 1] + sum_ref[cut]
        sum_ref[cut - 1] = both
        sum_ref[cut] = both
    for cut in range(NODES, y_len, NODES):
        both = sum_ref[:, cut - 1] + sum_ref[:, cut]
        sum_ref[:, cut - 1] = both
        sum_ref[:, cut] = both


def face_place(sc_ref, axis, kind, last):
    return jnp.where((sc_ref[1 + axis] + kind) % 2 == 0, last, 0)


def end_rows(values, filled, take_top):
    picked = values(0)
    slots = values.slots
    for s in range(slots):
        picked = jnp.where(take_top & (filled == s + 1), values(s * NODES + NODES - 1), picked)
    return picked


class RowReader:
    def __init__(self, slots, read):
        self.slots = slots
        self.read = read

    def __call__(self, row):
        return self.read(row)


def takes_top(sc_ref, kind):
    return (sc_ref[3] + kind) % 2 == 0


def write_faces(sc_ref, sum_ref, faces, counts):
    x_len, y_len, rows, width = sum_ref.shape
    nx, ny, nz = counts
    reader = RowReader(rows // NODES, lambda row: sum_ref[:, :, row])
    for kind in range(ny):
        faces[kind][...] = sum_ref[:, face_place(sc_ref, 1, kind, y_len - 1)]
    for kind in range(nz):
        faces[ny + kind][...] = end_rows(reader, sc_ref[0], takes_top(sc_ref, kind))


def add_halo(sc_ref, from_ref, halo, into_ref, counts):
    x_len, y_len, rows, width = from_ref.shape
    nx, ny, nz = counts

    def copy(x, carry):
        into_ref[x] = from_ref[x]
        return carry

    lax.fori_loop(0, x_len, copy, 0)
    for kind in range(nx):
        into_ref[face_place(sc_ref, 0, kind, x_len - 1)] += halo[kind][...]
    for kind in range(ny):
        into_ref[:, face_place(sc_ref, 1, kind, y_len - 1)] += halo[nx + kind][...]
    if nz:
        got = [halo[nx + ny + kind][...] for kind in range(nz)]
        tops = [takes_top(sc_ref, kind) for kind in range(nz)]
        from_below = sum(jnp.where(top, 0.0, value) for top, value in zip(tops, got))
        from_above = sum(jnp.where(top, value, 0.0) for top, value in zip(tops, got))
        into_ref[:, :, 0] += from_below
        for s in range(rows // NODES):
            into_ref[:, :, s * NODES + NODES - 1] += jnp.where(sc_ref[0] == s + 1, from_above, 0.0)


def fix_y_kernel(counts, sc_ref, *refs):
    nx, ny, nz = counts
    got, faces, outs = refs[:nx], refs[nx : nx + ny], refs[nx + ny :]
    x_len = faces[0].shape[0]
    for k in range(ny):
        outs[k][...] = faces[k][...]
    for kind in range(nx):
        place = face_place(sc_ref, 0, kind, x_len - 1)
        for k in range(ny):
            y_len = got[kind].shape[0]
            outs[k][place] += got[kind][face_place(sc_ref, 1, k, y_len - 1)]


def fix_z_kernel(counts, sc_ref, *refs):
    nx, ny, nz = counts
    got_x, refs = refs[:nx], refs[nx:]
    got_y, refs = refs[:ny][::-1], refs[ny:]
    faces, outs = refs[:nz], refs[nz:]
    x_len, y_len, width = faces[0].shape
    for k in range(nz):
        outs[k][...] = faces[k][...]
    for k in range(nz):
        top = takes_top(sc_ref, k)
        for kind in range(nx):
            ref = got_x[kind]
            reader = RowReader(ref.shape[1] // NODES, lambda row, ref=ref: ref[:, row])
            outs[k][face_place(sc_ref, 0, kind, x_len - 1)] += end_rows(reader, sc_ref[0], top)
        for kind in range(ny):
            ref = got_y[kind]
            reader = RowReader(ref.shape[1] // NODES, lambda row, ref=ref: ref[:, row])
            add = end_rows(reader, sc_ref[0], top)
            first = face_place(sc_ref, 1, kind, 1) == 0
            outs[k][:, 0] += jnp.where(first, add, 0.0)
            outs[k][:, y_len - 1] += jnp.where(first, 0.0, add)


def write_inverse(sc_ref, inv_ref, sizes):
    y_len, rows, width = inv_ref.shape
    filled, at_y, at_z = sc_ref[0], sc_ref[2], sc_ref[3]
    ids = lax.broadcasted_iota(jnp.int32, (rows, width), 0)
    node = ids % NODES
    low = (node == 0) & ((ids >= NODES) | (at_z > 0))
    high = (node == NODES - 1) & ((ids < (filled - 1) * NODES) | (at_z < sizes[2] - 1))
    along_z = jnp.where(low | high, 0.5, 1.0).astype(f32)
    for y in range(y_len):
        inv_ref[y] = along_z * end_factor(y, y_len, at_y, sizes[1])


def end_factor(place, length, position, size):
    whole = place + position * length
    low = (place % NODES == 0) & (whole > 0)
    high = (place % NODES == NODES - 1) & (whole < length * size - 1)
    return jnp.where(low | high, 0.5, 1.0).astype(f32)


def chunk_of(x_len):
    return 2 * NODES if x_len % (2 * NODES) == 0 else NODES


def scale_planes(sc_ref, inv_ref, x, block, x_len, size_x):
    inv = inv_ref[...]
    parts = [block[c] * (inv * end_factor(x + c, x_len, sc_ref[1], size_x)) for c in range(block.shape[0])]
    return jnp.stack(parts, 0)


def node_forward(scaled, feat, weights, layer):
    edge_w, node_in, node_out, biases = weights
    pair = split_cols(scaled)
    w_two = edge_w[layer, 1]
    joined = jnp.concatenate([feat, dot(pair, jnp.concatenate([w_two, w_two], 0)).astype(bf16)], -1)
    half = jnp.bfloat16(0.5)
    act, slope = silu_half(dot(joined, node_in[layer] * half) + 0.5 * biases[layer, pl.ds(1, 1)])
    return pair[:, :128], act.astype(bf16), slope


def node_slopes(grad, slope, weights, layer):
    return (dot_rt(grad, weights[2][layer]) * slope).astype(bf16)


def node_share(sc_ref, x, inv_ref, size_x, dpn, weights, layer, sum_ref):
    shape = (chunk_of(sum_ref.shape[0]),) + sum_ref.shape[1:]
    dx = dot_rt(dpn, weights[1][layer, pl.ds(128, 128)]).reshape(shape)
    share = scale_planes(sc_ref, inv_ref, x, dx, sum_ref.shape[0], size_x)
    joined = couple_slots(share.reshape((-1,) + shape[2:]), sc_ref[0])
    sum_ref[pl.ds(x, shape[0])] = joined.reshape(shape)


def node_products(grad, feat, scaled, act, dpn, grads):
    grads[pl.ds(0, 128)] += dot_t(act, grad)
    both = dot_t(dpn, jnp.concatenate([feat, scaled], -1))
    grads[pl.ds(128, 128)] += both[:, :128]
    grads[pl.ds(256, 128)] += both[:, 128:]
    grads[pl.ds(384, NODES)] += jnp.sum(dpn.astype(f32).reshape(-1, NODES, 128), 0)


def couple_plane(plane):
    y_len = plane.shape[0]
    parts = [plane[y] for y in range(y_len)]
    for cut in range(NODES, y_len, NODES):
        both = parts[cut - 1] + parts[cut]
        parts[cut - 1] = parts[cut] = both
    return jnp.stack(parts, 0)


def along_y(plane, combine):
    return [
        combine(plane[y : y + NODES - 1], plane[y + 1 : y + NODES], y) for y in range(0, plane.shape[0], NODES)
    ]


def spread_plane(sign, edge_x, edges_y, edge_z):
    total = sign * edge_x + (down(edge_z) - edge_z).reshape(edge_x.shape)
    parts = []
    for k, edge in enumerate(edges_y):
        here = total[k * NODES : (k + 1) * NODES]
        parts += [here[:1] - edge[:1], here[1:-1] + (edge[:-1] - edge[1:]), here[-1:] + edge[-1:]]
    return jnp.concatenate(parts, 0)


def plane_forward(low, high, at_high, w_one, half_bias, filled):
    y_len, rows, width = low.shape
    here = jnp.where(at_high, high, low)
    cols = node_rows(here)
    parts = [(high - low).astype(bf16)]
    parts += along_y(here, lambda lower, upper, y: (upper - lower).astype(bf16))
    parts.append((up(cols) - cols).reshape(here.shape).astype(bf16))
    half = dot(flat(jnp.concatenate(parts, 0)), w_one).reshape(-1, rows, width) + half_bias
    act = silu_half(half)[0].astype(bf16).astype(f32)
    at = y_len
    edges_y = []
    for _ in range(y_len // NODES):
        edges_y.append(act[at : at + NODES - 1])
        at += NODES - 1
    edge_z = jnp.where(row_ids() < NODES - 1, node_rows(act[at:]), 0.0)
    total = spread_plane(jnp.where(at_high, 1.0, -1.0), act[:y_len], edges_y, edge_z)
    return couple_plane(couple_slots(total, filled))


def plane_backward(low, high, at_high, slope_x, slope_y, slope_z):
    here = jnp.where(at_high, high, low)
    cols = node_rows(here)
    edge_x = ((high - low) * slope_x).astype(bf16).astype(f32)
    edges_y = along_y(
        here, lambda lower, upper, y: ((upper - lower) * slope_y[y : y + NODES - 1]).astype(bf16).astype(f32)
    )
    edge_z = ((up(cols) - cols) * node_rows(slope_z)).astype(bf16).astype(f32)
    return spread_plane(jnp.where(at_high, 1.0, -1.0), edge_x, edges_y, edge_z)


def face_planes(sc_ref, kind, x_len):
    place = face_place(sc_ref, 0, kind, x_len - 1)
    at_high = place > 0
    return place, jnp.where(at_high, x_len - 2, 0), at_high


def halo_planes(sc_ref, from_ref, halo, kind, start, into_ref, counts):
    x_len, y_len, rows, width = from_ref.shape
    nx, ny, nz = counts
    for c in range(2):
        into_ref[c] = from_ref[start + c]
    into_ref[face_place(sc_ref, 0, kind, x_len - 1) - start] += halo[kind][...]
    for c in range(2):
        for k in range(ny):
            into_ref[c, face_place(sc_ref, 1, k, y_len - 1)] += halo[nx + k][start + c]
        for k in range(nz):
            got = halo[nx + ny + k][start + c]
            top = takes_top(sc_ref, k)
            into_ref[c, :, 0] += jnp.where(top, 0.0, got)
            for s in range(rows // NODES):
                into_ref[c, :, s * NODES + NODES - 1] += jnp.where(top & (sc_ref[0] == s + 1), got, 0.0)


def edges_backward(q_ref, slope_ref, edge_ref, bias_acc):
    x_len, y_len, rows, width = q_ref.shape

    def body(x0, y0):
        ys = pl.ds(y0, NODES)
        prev = None
        here = q_ref[x0, ys]
        bias = jnp.zeros((NODES, width), f32)
        for i in range(NODES):
            total = prev
            prev = None
            nxt = None
            if i < NODES - 1:
                nxt = q_ref[x0 + i + 1, ys]
                prev = ((nxt - here) * slope_ref[0, x0 + i, ys]).astype(bf16).astype(f32)
                total = -prev if total is None else total - prev
                bias = bias + jnp.sum(node_rows(prev), 0)
            along_y = (here[1:] - here[:-1]) * slope_ref[1, x0 + i, pl.ds(y0, NODES - 1)]
            along_y = along_y.astype(bf16).astype(f32)
            cols = node_rows(here)
            along_z = (up(cols) - cols) * node_rows(slope_ref[2, x0 + i, ys])
            along_z = along_z.astype(bf16).astype(f32)
            bias = bias + jnp.sum(node_rows(along_y), 0) + jnp.sum(along_z, 0)
            total = total + (down(along_z) - along_z).reshape(here.shape)
            total = jnp.concatenate(
                [
                    total[:1] - along_y[:1],
                    total[1:-1] + (along_y[:-1] - along_y[1:]),
                    total[-1:] + along_y[-1:],
                ],
                0,
            )
            edge_ref[x0 + i, ys] = total
            here = nxt
        bias_acc[...] += bias

    elements(x_len, y_len, body)


def planes(count, body):
    chunk = chunk_of(count)

    def step(c, carry):
        body(pl.multiple_of(c * chunk, chunk))
        return carry

    lax.fori_loop(0, count // chunk, step, 0)


def half_weights(weights, layer):
    edge_w, node_in, node_out, biases = weights
    return edge_w[layer, 0] * jnp.bfloat16(0.5), 0.5 * biases[layer, pl.ds(0, 1)]


def first_kernel(counts, sizes, sc, edge_w, biases, h, sums, slopes, *faces):
    w_one, bias = half_weights((edge_w, None, None, biases), 0)
    edges_forward(h, w_one, bias, sc[0], sums, slopes)
    couple_columns(sums)
    write_faces(sc, sums, faces, counts)


def first_face_kernel(counts, sizes, sc, edge_w, biases, h, *faces):
    w_one, bias = half_weights((edge_w, None, None, biases), 0)
    for kind, face in enumerate(faces):
        place, start, at_high = face_planes(sc, kind, h.shape[0])
        face[...] = plane_forward(
            h[start].astype(f32), h[start + 1].astype(f32), at_high, w_one, bias, sc[0]
        )


def middle_face_kernel(counts, sizes, sc, edge_w, node_in, node_out, biases, sums_in, h, *refs):
    weights = (edge_w, node_in, node_out, biases)
    n = sum(counts)
    halo, faces, (pair, inv) = refs[:n], refs[n:-2], refs[-2:]
    write_inverse(sc, inv, sizes)
    w_one, bias = half_weights(weights, 1)
    x_len = h.shape[0]
    for kind, face in enumerate(faces):
        place, start, at_high = face_planes(sc, kind, x_len)
        halo_planes(sc, sums_in, halo, kind, start, pair, counts)
        sums_at = flat(scale_planes(sc, inv, start, pair[...], x_len, sizes[0]))
        feat = flat(h[pl.ds(start, 2)])
        scaled, act, slope = node_forward(sums_at, feat, weights, 0)
        moved = (feat.astype(f32) + dot(act, node_out[0])).astype(bf16).astype(f32).reshape(pair.shape)
        face[...] = plane_forward(moved[0], moved[1], at_high, w_one, bias, sc[0])


def face_share(sc, sizes, inv, place, x_len, grad, slope, weights, layer, shape):
    dpn = node_slopes(grad, slope, weights, layer)
    dx = dot_rt(dpn, weights[1][layer, pl.ds(128, 128)]).reshape((1,) + shape)
    share = scale_planes(sc, inv, place, dx, x_len, sizes[0])
    return couple_plane(couple_slots(share[0], sc[0]))


def turn_face_kernel(counts, sizes, sc, edge_w, node_in, node_out, biases, sums_in, h, g_ref, *refs):
    weights = (edge_w, node_in, node_out, biases)
    n = sum(counts)
    halo, faces, (pair, inv) = refs[:n], refs[n:-2], refs[-2:]
    write_inverse(sc, inv, sizes)
    x_len, shape = h.shape[0], h.shape[1:]
    live = (lax.broadcasted_iota(jnp.int32, (1, h.shape[2], 128), 1) < sc[0] * NODES).astype(f32)
    for kind, face in enumerate(faces):
        place, start, at_high = face_planes(sc, kind, x_len)
        halo_planes(sc, sums_in, halo, kind, start, pair, counts)
        plane = pair[place - start][None]
        sums_at = flat(scale_planes(sc, inv, place, plane, x_len, sizes[0]))
        scaled, act, slope = node_forward(sums_at, flat(h[place]), weights, 1)
        grad = flat((g_ref[place].astype(f32) * live).astype(bf16))
        face[...] = face_share(sc, sizes, inv, place, x_len, grad, slope, weights, 1, shape)


def join_face_kernel(counts, sizes, sc, edge_w, node_in, node_out, biases, sums_in, base_in, slopes, slope0, *refs):
    weights = (edge_w, node_in, node_out, biases)
    n = sum(counts)
    halo, faces, (pair, inv) = refs[:n], refs[n:-2], refs[-2:]
    write_inverse(sc, inv, sizes)
    x_len, shape = base_in.shape[0], base_in.shape[1:]
    w_two, w_one = twice(edge_w[1, 1]), twice(edge_w[1, 0])
    for kind, face in enumerate(faces):
        place, start, at_high = face_planes(sc, kind, x_len)
        halo_planes(sc, sums_in, halo, kind, start, pair, counts)
        q = dot_rt(split_cols(flat(pair[...])), w_two).reshape(pair.shape)
        edge = plane_backward(q[0], q[1], at_high, slopes[0, start], slopes[1, place], slopes[2, place])
        grad = (flat(base_in[place]) + dot_rt(split_cols(flat(edge)), w_one)).astype(bf16)
        face[...] = face_share(sc, sizes, inv, place, x_len, grad, flat(slope0[place]), weights, 0, shape)


def twice(weight):
    return jnp.concatenate([weight, weight], 1)


def middle_kernel(counts, sizes, sc, edge_w, node_in, node_out, biases, sums_in, h, *refs):
    weights = (edge_w, node_in, node_out, biases)
    n = sum(counts)
    halo, refs = refs[:n], refs[n:]
    scaled_ref, act_ref, slope_ref, next_ref, sums, slopes = refs[:6]
    faces, (work, inv) = refs[6:-2], refs[-2:]
    add_halo(sc, sums_in, halo, work, counts)
    write_inverse(sc, inv, sizes)
    shape = (chunk_of(h.shape[0]),) + h.shape[1:]

    def body(x):
        at = pl.ds(x, chunk_of(h.shape[0]))
        sums_at = flat(scale_planes(sc, inv, x, work[at], h.shape[0], sizes[0]))
        scaled, act, slope = node_forward(sums_at, flat(h[at]), weights, 0)
        scaled_ref[at] = scaled.reshape(shape)
        act_ref[at] = act.reshape(shape)
        slope_ref[at] = slope.reshape(shape)
        moved = flat(h[at]).astype(f32) + dot(act, node_out[0])
        next_ref[at] = moved.astype(bf16).reshape(shape)

    planes(h.shape[0], body)
    w_one, bias = half_weights(weights, 1)
    edges_forward(next_ref, w_one, bias, sc[0], sums, slopes)
    couple_columns(sums)
    write_faces(sc, sums, faces, counts)


def turn_kernel(counts, sizes, sc, edge_w, node_in, node_out, biases, sums_in, h, g_ref, *refs):
    weights = (edge_w, node_in, node_out, biases)
    n = sum(counts)
    halo, refs = refs[:n], refs[n:]
    scaled_ref, act_ref, dpn_ref, sums = refs[:4]
    faces, (work, inv) = refs[4:-2], refs[-2:]
    add_halo(sc, sums_in, halo, work, counts)
    write_inverse(sc, inv, sizes)
    shape = (chunk_of(h.shape[0]),) + h.shape[1:]
    live = live_rows(sc, h)

    def body(x):
        at = pl.ds(x, chunk_of(h.shape[0]))
        sums_at = flat(scale_planes(sc, inv, x, work[at], h.shape[0], sizes[0]))
        scaled, act, slope = node_forward(sums_at, flat(h[at]), weights, 1)
        scaled_ref[at] = scaled.reshape(shape)
        act_ref[at] = act.reshape(shape)
        grad = flat((g_ref[at].astype(f32) * live).astype(bf16))
        dpn = node_slopes(grad, slope, weights, 1)
        dpn_ref[at] = dpn.reshape(shape)
        node_share(sc, x, inv, sizes[0], dpn, weights, 1, sums)

    planes(h.shape[0], body)
    couple_columns(sums)
    write_faces(sc, sums, faces, counts)


def live_rows(sc, h):
    return (lax.broadcasted_iota(jnp.int32, (1, 1, h.shape[2], 128), 2) < sc[0] * NODES).astype(f32)


def products_kernel(sc, node_in, h, g_ref, scaled, act, dpn, base, grads):
    grads[...] = jnp.zeros_like(grads)
    live = live_rows(sc, h)

    def body(x):
        at = pl.ds(x, chunk_of(h.shape[0]))
        grad = (g_ref[at].astype(f32) * live).astype(bf16)
        node_products(flat(grad), flat(h[at]), flat(scaled[at]), flat(act[at]), flat(dpn[at]), grads)
        dx = dot_rt(flat(dpn[at]), node_in[1, pl.ds(0, 128)])
        base[at] = grad.astype(f32) + dx.reshape(grad.shape)

    planes(h.shape[0], body)


def edge_parts(counts, sc, weights, layer, sums_in, halo, h, slopes, work, grads, row):
    add_halo(sc, sums_in, halo, work, counts)
    shape = (chunk_of(h.shape[0]),) + h.shape[1:]
    w_two = twice(weights[0][layer, 1])

    def to_q(x):
        at = pl.ds(x, chunk_of(h.shape[0]))
        work[at] = dot_rt(split_cols(flat(work[at])), w_two).reshape(shape)

    planes(h.shape[0], to_q)
    edges_backward(work, slopes, work, grads.at[pl.ds(row + 128, NODES)])


def edge_product(h, x, pair, grads, row):
    both = dot_t(flat(h[pl.ds(x, chunk_of(h.shape[0]))]), pair)
    grads[pl.ds(row, 128)] += both[:, :128] + both[:, 128:]


def join_kernel(
    counts, sizes, sc, edge_w, node_in, node_out, biases,
    sums_in, h, base_in, slopes, h0, scaled0, act0, slope0, grads1, *refs
):
    weights = (edge_w, node_in, node_out, biases)
    n = sum(counts)
    halo, refs = refs[:n], refs[n:]
    grad_ref, dpn_ref, sums, keep, send = refs[:5]
    faces, (work, inv, grads) = refs[5:-3], refs[-3:]
    write_inverse(sc, inv, sizes)
    grads[...] = jnp.zeros_like(grads)
    grads[pl.ds(512 + 2 * NODES, grads1.shape[0])] = grads1[...]

    row = 384 + NODES
    shape = (chunk_of(h.shape[0]),) + h.shape[1:]
    edge_parts(counts, sc, weights, 1, sums_in, halo, h, slopes, work, grads, row)
    w_one = twice(edge_w[1, 0])

    def body(x):
        at = pl.ds(x, chunk_of(h.shape[0]))
        pair = split_cols(flat(work[at]))
        edge_product(h, x, pair, grads, row)
        grad = (flat(base_in[at]) + dot_rt(pair, w_one)).astype(bf16)
        dpn = node_slopes(grad, flat(slope0[at]), weights, 0)
        node_products(grad, flat(h0[at]), flat(scaled0[at]), flat(act0[at]), dpn, grads)
        grad_ref[at] = grad.reshape(shape)
        dpn_ref[at] = dpn.reshape(shape)
        node_share(sc, x, inv, sizes[0], dpn, weights, 0, sums)

    planes(h.shape[0], body)
    couple_columns(sums)
    write_faces(sc, sums, faces, counts)
    write_halves(sc, halving_steps(sizes)[0], grads, keep, send)


def last_kernel(counts, sizes, sc, edge_w, node_in, node_out, biases, sums_in, h, slopes, *refs):
    n = sum(counts)
    halo, (edges, grads) = refs[:n], refs[n:]
    grads[...] = jnp.zeros_like(grads)
    edge_parts(counts, sc, (edge_w,), 0, sums_in, halo, h, slopes, edges, grads, 0)

    def body(x):
        edge_product(h, x, split_cols(flat(edges[pl.ds(x, chunk_of(edges.shape[0]))])), grads, 0)

    planes(h.shape[0], body)


def state_kernel(sc, edge_w, node_in, grad_in, dpn, edges, grad_ref):
    shape = (chunk_of(edges.shape[0]),) + edges.shape[1:]
    weight = jnp.concatenate([twice(edge_w[0, 0]), node_in[0, pl.ds(0, 128)]], 1)

    def body(x):
        at = pl.ds(x, chunk_of(edges.shape[0]))
        parts = jnp.concatenate([split_cols(flat(edges[at])), flat(dpn[at])], -1)
        grad_ref[at] = (flat(grad_in[at]).astype(f32) + dot_rt(parts, weight)).astype(bf16).reshape(shape)

    planes(edges.shape[0], body)


def finish_kernel(scale, last_rows, step, sc, edge_w, node_in, value, got, *refs):
    edge_grads, in_grads, out_grads, bias_grads, both = refs
    width = edge_w.shape[-1]
    join_kernel_of(step, last_rows, sc, value, got, both)

    def rows_of(part, start, count=width):
        ref, offset = part
        return ref[pl.ds(offset + start, count)] * scale

    def bias_of(part, start):
        return jnp.sum(rows_of(part, start, NODES), 0, keepdims=True)

    end = 3 * width
    last, sum0 = (both, 0), (both, last_rows)
    sum1 = (both, last_rows + 512 + 2 * NODES)
    firsts = ((last, 0), (sum0, end + NODES))
    for layer, part in enumerate((sum0, sum1)):
        out_grads[layer] = rows_of(part, 0)
        in_grads[layer, pl.ds(0, width)] = rows_of(part, width).T
        bias_grads[layer, pl.ds(1, 1)] = bias_of(part, end)
        source, start = firsts[layer]
        edge_grads[layer, 0] = rows_of(source, start)
        bias_grads[layer, pl.ds(0, 1)] = bias_of(source, start + width)
        mixed = rows_of(part, 2 * width).T
        high = mixed.astype(bf16)
        low = (mixed - high.astype(f32)).astype(bf16)
        lower = node_in[layer, pl.ds(width, width)]
        edge_grads[layer, 1] = dot_rt(high, lower) + dot_rt(low, lower)
        w_two = edge_w[layer, 1]
        in_grads[layer, pl.ds(width, width)] = dot_t(w_two, high) + dot_t(w_two, low)


def call(kernel, name, inputs, outs, scratch=(), flops=0, aliases=None):
    total = sum(math.prod(o.shape) * o.dtype.itemsize for o in outs)
    total += sum(math.prod(i.shape) * i.dtype.itemsize for i in inputs)
    return pl.pallas_call(
        kernel,
        name=name,
        out_shape=tuple(outs),
        in_specs=[SM] + [VM] * (len(inputs) - 1),
        out_specs=tuple([VM] * len(outs)),
        scratch_shapes=list(scratch),
        input_output_aliases=aliases or {},
        compiler_params=pltpu.CompilerParams(vmem_limit_bytes=VMEM_LIMIT),
        cost_estimate=pl.CostEstimate(flops=flops, bytes_accessed=total, transcendentals=0),
    )(*inputs)


def pairs(size, kind):
    return [
        pair for low in range(kind, size - 1, 2) for pair in ((low, low + 1), (low + 1, low))
    ]


def hops(size):
    found = []
    hop = 1
    while hop < size:
        found.append(hop)
        hop *= 2
    return found


def halving_steps(sizes):
    return [(1, hop) for hop in hops(sizes[1])[:1]] + [(0, hop) for hop in hops(sizes[0])]


def whole_steps(sizes):
    along_z = hops(sizes[2])
    steps = [(2, along_z[k : k + 2]) for k in range(0, len(along_z), 2)]
    return steps + [(1, [hop]) for hop in hops(sizes[1])[1:]]


def padded_rows(rows, sizes):
    unit = NODES << len(halving_steps(sizes))
    return -(-rows // unit) * unit


def bit_of(sc_ref, step):
    axis, hop = step
    return (sc_ref[1 + axis] // hop) % 2


def write_halves(sc_ref, step, from_ref, keep, send):
    half = keep.shape[0]
    bit = bit_of(sc_ref, step)
    keep[...] = from_ref[pl.ds(pl.multiple_of(bit * half, NODES), half)]
    send[...] = from_ref[pl.ds(pl.multiple_of((1 - bit) * half, NODES), half)]


def halve_kernel(step, sc, keep_in, got, keep, send, total):
    total[...] = keep_in[...] + got[...]
    write_halves(sc, step, total, keep, send)


def add_kernel(sc, *refs):
    total = refs[0][...] + refs[1][...]
    for ref in refs[2:-1]:
        total = total + ref[...]
    refs[-1][...] = total


def join_kernel_of(step, start, sc, value, got, out):
    half = value.shape[0] - start
    bit = bit_of(sc, step)
    if start:
        out[pl.ds(0, start)] = value[pl.ds(0, start)] + got[pl.ds(0, start)]
    out[pl.ds(pl.multiple_of(start + bit * half, NODES), half)] = value[pl.ds(start, half)]
    out[pl.ds(pl.multiple_of(start + (1 - bit) * half, NODES), half)] = got[pl.ds(start, half)]


def stack_kernel(sc, first, left, right, out):
    rows = first.shape[0]
    out[pl.ds(0, rows)] = first[...]
    out[pl.ds(rows, left.shape[0])] = left[...] + right[...]


def swap(value, step):
    axis = ("gx", "gy", "gz")[step[0]]
    return lax.ppermute(value, axis, [(i, i ^ step[1]) for i in range(lax.axis_size(axis))])


def rows_like(rows, width=128):
    return jax.ShapeDtypeStruct((rows, width), f32)


def halve(sc, sizes, keep, send):
    steps = halving_steps(sizes)
    got = swap(send, steps[0])
    for step in steps[1:]:
        keep, got = yield keep, got
        half = rows_like(keep.shape[0] // 2)
        keep, send = call(
            functools.partial(halve_kernel, step), "halve", (sc, keep, got), [half, half],
            [pltpu.VMEM(keep.shape, f32)],
        )
        got = swap(send, step)
    keep, got = yield keep, got
    return keep, got


class Background:
    def __init__(self):
        self.active = {}

    def add(self, name, steps):
        self.active[name] = [steps, None]

    def advance(self, entry, tied):
        steps, pending = entry
        try:
            entry[1] = next(steps) if pending is None else steps.send(tied)
        except StopIteration:
            entry[0] = None

    def beside(self, anchor):
        for entry in self.active.values():
            steps, pending = entry
            if steps is None:
                continue
            if pending is None:
                self.advance(entry, None)
            elif pending[1] is not None:
                anchor, tied = lax.optimization_barrier((anchor, pending))
                self.advance(entry, tied)
        return anchor

    def finish(self, name):
        entry = self.active[name]
        while entry[0] is not None:
            done = entry[1]
            if done is not None and done[1] is None:
                return done[0]
            self.advance(entry, done)
        return entry[1]


def on_device(state, cotangent, counts, edge_weights, node_in, node_out, biases):
    x_len, y_len, slots, nodes, width = state.shape
    rows = slots * nodes
    grid = (x_len, y_len, rows, width)
    axes = ("gx", "gy", "gz")
    sizes = tuple(lax.axis_size(a) for a in axes)
    trades = tuple(min(size - 1, 2) for size in sizes)
    nx, ny, nz = trades
    h0 = state.reshape(grid)
    g2 = cotangent.reshape(grid)
    sc = jnp.stack([counts[0]] + [lax.axis_index(a).astype(jnp.int32) for a in axes])

    def sds(shape, kind=f32):
        return jax.ShapeDtypeStruct(shape, kind)

    face_x = sds((y_len, rows, width))
    face_y = sds((x_len, rows, width))
    face_z = sds((x_len, y_len, width))
    face_outs = [face_y] * ny + [face_z] * nz
    full = sds(grid)
    full16 = sds(grid, bf16)
    full3 = sds((3,) + grid)
    work = pltpu.VMEM(grid, f32)
    inv = pltpu.VMEM((y_len, rows, width), f32)
    matmul = 2 * math.prod(grid) * width
    weights = (edge_weights, node_in, node_out, biases)

    def run(kernel, name, inputs, outs, scratch, flops):
        body = functools.partial(kernel, trades, sizes)
        return call(body, name, (sc, *weights, *inputs), outs, scratch, flops * matmul)

    def trade(faces, axis):
        size = lax.axis_size(axis)
        got = [lax.ppermute(face, axis, pairs(size, kind)) for kind, face in reversed(list(enumerate(faces)))]
        return got[::-1]

    background = Background()

    pair = pltpu.VMEM((2,) + grid[1:], f32)

    def first_trade(kernel, name, inputs, scratch, flops):
        faces = call(functools.partial(kernel, trades, sizes), name, (sc, *inputs), [face_x] * nx, scratch, flops)
        return trade(faces, "gx")

    def exchange(got_x, faces, work=None, held=()):
        fix = functools.partial(fix_y_kernel, trades)
        faces_y = call(fix, "fix_y", (sc, *got_x, *faces[:ny]), [face_y] * ny)
        got_y = trade(background.beside(faces_y), "gy")
        fix = functools.partial(fix_z_kernel, trades)
        faces_z = call(fix, "fix_z", (sc, *got_x, *got_y[::-1], *faces[ny:]), [face_z] * nz)
        faces_z = background.beside(faces_z)
        done = None
        if work is not None:
            faces_z, held = lax.optimization_barrier((faces_z, held))
            done = work(*held)
        got_z = trade(faces_z, "gz")
        got_z, done = lax.optimization_barrier((got_z, done))
        return (*got_x, *got_y, *got_z), done

    def to_slopes(half):
        return call(slope_kernel, "slopes", (sc, half), [full3], [], matmul, {1: 0})[0]

    def products(*held):
        return call(
            products_kernel, "nodes1_products", (sc, node_in, *held), [full, rows_like(3 * width + NODES)], [], 6 * matmul
        )

    got_x = first_trade(first_face_kernel, "face0", (edge_weights, biases, h0), [], matmul // 8)
    sums, slopes0, *faces = call(
        functools.partial(first_kernel, trades, sizes), "edges0", (sc, edge_weights, biases, h0),
        [full, full3] + face_outs, [], 3 * matmul,
    )
    halo, slopes0 = exchange(got_x, faces, to_slopes, (slopes0,))
    inputs = (*weights, sums, h0, *halo)
    got_x = first_trade(middle_face_kernel, "face1", inputs, [pair, inv], matmul // 4)
    scaled0, act0, slope0, h1, sums, slopes1, *faces = run(
        middle_kernel, "nodes0_edges1", (sums, h0, *halo),
        [full16, full16, full, full16, full, full3] + face_outs, [work, inv], 8,
    )
    halo, slopes1 = exchange(got_x, faces, to_slopes, (slopes1,))
    inputs = (*weights, sums, h1, g2, *halo)
    got_x = first_trade(turn_face_kernel, "face2", inputs, [pair, inv], matmul // 4)
    scaled1, act1, dpn1, sums, *faces = run(
        turn_kernel, "nodes1_back", (sums, h1, g2, *halo), [full16] * 3 + [full] + face_outs, [work, inv], 7
    )
    halo, (base, grads1) = exchange(got_x, faces, products, (h1, g2, scaled1, act1, dpn1))
    inputs = (*weights, sums, base, slopes1, slope0, *halo)
    got_x = first_trade(join_face_kernel, "face3", inputs, [pair, inv], matmul // 4)
    grad_rows = padded_rows(7 * width + 3 * NODES, sizes)
    half = rows_like(grad_rows // 2)
    grad_in, dpn0, sums, keep, send, *faces = run(
        join_kernel, "edges1_back_nodes0_back",
        (sums, h1, base, slopes1, h0, scaled0, act0, slope0, grads1, *halo),
        [full16, full16, full, half, half] + face_outs, [work, inv, pltpu.VMEM((grad_rows, width), f32)], 12,
    )
    background.add("sums", halve(sc, sizes, keep, send))
    halo, _ = exchange(got_x, faces)
    tail_rows = width + NODES
    edges, last = run(last_kernel, "edges0_back", (sums, h0, slopes0, *halo), [full, rows_like(tail_rows)], [], 6)
    keep, got = background.finish("sums")
    (value,) = call(stack_kernel, "stack", (sc, last, keep, got), [rows_like(tail_rows + keep.shape[0])])
    value, grad_in, dpn0, edges = lax.optimization_barrier((value, grad_in, dpn0, edges))
    (grad0,) = call(
        state_kernel, "state_grad", (sc, edge_weights, node_in, grad_in, dpn0, edges), [full16], [], 4 * matmul
    )
    for axis, together in whole_steps(sizes):
        partners = [sum(c) for n in range(1, len(together) + 1) for c in itertools.combinations(together, n)]
        got = [swap(value, (axis, partner)) for partner in partners]
        (value,) = call(add_kernel, "add", (sc, value, *got), [rows_like(value.shape[0])])
        value, grad0 = lax.optimization_barrier((value, grad0))
    first, *rest = halving_steps(sizes)
    for step in reversed(rest):
        out = rows_like(2 * value.shape[0] - tail_rows)
        body = functools.partial(join_kernel_of, step, tail_rows)
        (value,) = call(body, "join", (sc, value, swap(value, step)), [out])
    layers_all = 3 * slots * sizes[2] // 4
    nodes_all = x_len * sizes[0] * y_len * sizes[1] * layers_all * nodes
    scale = 1.0 / math.sqrt(nodes_all)
    edge_grads, in_grads, out_grads, bias_grads = call(
        functools.partial(finish_kernel, scale, tail_rows, first), "finish",
        (sc, edge_weights, node_in, value, swap(value, first)),
        [sds(edge_weights.shape), sds(node_in.shape), sds(node_out.shape), sds(biases.shape)],
        [pltpu.VMEM((2 * value.shape[0] - tail_rows, width), f32)],
    )
    return grad0.reshape(state.shape), edge_grads, in_grads, out_grads, bias_grads


def solution(mesh):
    return jax.shard_map(
        on_device,
        mesh=mesh,
        in_specs=(
            P("gx", "gy", "gz", None, None),
            P("gx", "gy", "gz", None, None),
            P("gz"),
            P(),
            P(),
            P(),
            P(),
        ),
        out_specs=(P("gx", "gy", "gz", None, None), P(), P(), P(), P()),
        check_vma=False,
    )
```

```python
import functools
import itertools
import math

import jax
import jax.numpy as jnp
from jax import lax
from jax.experimental import pallas as pl
from jax.experimental.pallas import tpu as pltpu
from jax.sharding import PartitionSpec as P

f32 = jnp.float32
bf16 = jnp.bfloat16
NODES = 8
VMEM_LIMIT = 12 * 1024 * 1024
VM = pl.BlockSpec(memory_space=pltpu.VMEM)
SM = pl.BlockSpec(memory_space=pltpu.SMEM)


def dot(left, right):
    return lax.dot_general(left, right, (((1,), (0,)), ((), ())), preferred_element_type=f32)


def dot_t(left, right):
    return lax.dot_general(left, right, (((0,), (0,)), ((), ())), preferred_element_type=f32)


def dot_rt(left, right):
    return lax.dot_general(left, right, (((1,), (1,)), ((), ())), preferred_element_type=f32)


def silu_half(half):
    th = jnp.tanh(half)
    prod = half * th
    return half + prod, (0.5 + 0.5 * th) * ((1.0 + half) - prod)


def split_cols(value):
    high = value.astype(bf16)
    low = (value - high.astype(f32)).astype(bf16)
    return jnp.concatenate([high, low], -1)


def up(value):
    return pltpu.roll(value, NODES - 1, 1)


def down(value):
    return pltpu.roll(value, 1, 1)


def flat(value):
    return value.reshape(-1, value.shape[-1])


def node_rows(value):
    return value.reshape(-1, NODES, value.shape[-1])


def row_ids():
    return lax.broadcasted_iota(jnp.int32, (1, NODES, 128), 1)


def couple_slots(plane, filled):
    count, rows, width = plane.shape
    slots = rows // NODES
    parts = plane.reshape(count, slots, NODES, width)
    ids = row_ids()
    done = []
    for s in range(slots):
        here = parts[:, s]
        if s + 1 < slots:
            take = (ids == NODES - 1) & (s + 1 < filled)
            here = here + jnp.where(take, up(parts[:, s + 1]), 0.0)
        if s > 0:
            here = here + jnp.where(ids == 0, down(parts[:, s - 1]), 0.0)
            here = jnp.where(s < filled, here, 0.0)
        done.append(here[:, None])
    return jnp.concatenate(done, 1).reshape(plane.shape)


def elements(x_len, y_len, body):
    ey = y_len // NODES
    total = (x_len // NODES) * ey

    def step(e, carry):
        x0 = pl.multiple_of((e // ey) * NODES, NODES)
        y0 = pl.multiple_of((e % ey) * NODES, NODES)
        body(x0, y0)
        return carry

    lax.fori_loop(0, total, step, 0)


def edges_forward(h_ref, w_one, half_bias, filled, sum_ref, half_ref):
    x_len, y_len, rows, width = h_ref.shape
    inner = row_ids() < NODES - 1

    def body(x0, y0):
        ys = pl.ds(y0, NODES)
        prev = None
        here = h_ref[x0, ys].astype(f32)
        for i in range(NODES):
            parts = []
            nxt = None
            if i < NODES - 1:
                nxt = h_ref[x0 + i + 1, ys].astype(f32)
                parts.append((nxt - here).astype(bf16))
            parts.append((here[1:] - here[:-1]).astype(bf16))
            cols = node_rows(here)
            parts.append((up(cols) - cols).reshape(here.shape).astype(bf16))
            half = dot(flat(jnp.concatenate(parts, 0)), w_one).reshape(-1, rows, width) + half_bias
            act = (half + half * jnp.tanh(half)).astype(bf16).astype(f32)
            at = 0
            total = prev
            prev = None
            if i < NODES - 1:
                prev = act[:NODES]
                total = -prev if total is None else total - prev
                half_ref[0, x0 + i, ys] = half[:NODES]
                at = NODES
            along_y = act[at : at + NODES - 1]
            half_ref[1, x0 + i, pl.ds(y0, NODES - 1)] = half[at : at + NODES - 1]
            at += NODES - 1
            along_z = jnp.where(inner, node_rows(act[at:]), 0.0)
            half_ref[2, x0 + i, ys] = half[at:]
            total = total + (down(along_z) - along_z).reshape(here.shape)
            total = jnp.concatenate(
                [
                    total[:1] - along_y[:1],
                    total[1:-1] + (along_y[:-1] - along_y[1:]),
                    total[-1:] + along_y[-1:],
                ],
                0,
            )
            sum_ref[x0 + i, ys] = couple_slots(total, filled)
            here = nxt

    elements(x_len, y_len, body)


def slope_kernel(sc, half_in, slope_out):
    inner = row_ids() < NODES - 1

    def step(x, carry):
        for k in range(3):
            slope = silu_half(half_in[k, x])[1]
            if k == 2:
                slope = jnp.where(inner, node_rows(slope), 0.0).reshape(slope.shape)
            slope_out[k, x] = slope
        return carry

    lax.fori_loop(0, half_in.shape[1], step, 0)


def couple_columns(sum_ref):
    x_len, y_len = sum_ref.shape[:2]
    for cut in range(NODES, x_len, NODES):
        both = sum_ref[cut - 1] + sum_ref[cut]
        sum_ref[cut - 1] = both
        sum_ref[cut] = both
    for cut in range(NODES, y_len, NODES):
        both = sum_ref[:, cut - 1] + sum_ref[:, cut]
        sum_ref[:, cut - 1] = both
        sum_ref[:, cut] = both


def face_place(sc_ref, axis, kind, last):
    return jnp.where((sc_ref[1 + axis] + kind) % 2 == 0, last, 0)


class Trades(tuple):
    sizes = ()


def from_partner(sc_ref, counts, axis, kind, value):
    size = counts.sizes[axis]
    if kind == 0 and size % 2 == 0:
        return value
    at = sc_ref[1 + axis]
    partner = at + jnp.where((at + kind) % 2 == 0, 1, -1)
    return jnp.where((partner >= 0) & (partner < size), value, 0.0)


def end_rows(values, filled, take_top):
    picked = values(0)
    slots = values.slots
    for s in range(slots):
        picked = jnp.where(take_top & (filled == s + 1), values(s * NODES + NODES - 1), picked)
    return picked


class RowReader:
    def __init__(self, slots, read):
        self.slots = slots
        self.read = read

    def __call__(self, row):
        return self.read(row)


def takes_top(sc_ref, kind):
    return (sc_ref[3] + kind) % 2 == 0


def write_faces(sc_ref, sum_ref, faces, counts):
    x_len, y_len, rows, width = sum_ref.shape
    nx, ny, nz = counts
    reader = RowReader(rows // NODES, lambda row: sum_ref[:, :, row])
    for kind in range(ny):
        faces[kind][...] = sum_ref[:, face_place(sc_ref, 1, kind, y_len - 1)]
    for kind in range(nz):
        faces[ny + kind][...] = end_rows(reader, sc_ref[0], takes_top(sc_ref, kind))


def add_halo(sc_ref, from_ref, halo, into_ref, counts):
    x_len, y_len, rows, width = from_ref.shape
    nx, ny, nz = counts

    def copy(x, carry):
        into_ref[x] = from_ref[x]
        return carry

    lax.fori_loop(0, x_len, copy, 0)
    for kind in range(nx):
        got = from_partner(sc_ref, counts, 0, kind, halo[kind][...])
        into_ref[face_place(sc_ref, 0, kind, x_len - 1)] += got
    for kind in range(ny):
        got = from_partner(sc_ref, counts, 1, kind, halo[nx + kind][...])
        into_ref[:, face_place(sc_ref, 1, kind, y_len - 1)] += got
    if nz:
        got = [from_partner(sc_ref, counts, 2, kind, halo[nx + ny + kind][...]) for kind in range(nz)]
        tops = [takes_top(sc_ref, kind) for kind in range(nz)]
        from_below = sum(jnp.where(top, 0.0, value) for top, value in zip(tops, got))
        from_above = sum(jnp.where(top, value, 0.0) for top, value in zip(tops, got))
        into_ref[:, :, 0] += from_below
        for s in range(rows // NODES):
            into_ref[:, :, s * NODES + NODES - 1] += jnp.where(sc_ref[0] == s + 1, from_above, 0.0)


def fix_y_kernel(counts, sc_ref, *refs):
    nx, ny, nz = counts
    got, faces, outs = refs[:nx], refs[nx : nx + ny], refs[nx + ny :]
    x_len = faces[0].shape[0]
    for k in range(ny):
        outs[k][...] = faces[k][...]
    for kind in range(nx):
        place = face_place(sc_ref, 0, kind, x_len - 1)
        for k in range(ny):
            y_len = got[kind].shape[0]
            line = got[kind][face_place(sc_ref, 1, k, y_len - 1)]
            outs[k][place] += from_partner(sc_ref, counts, 0, kind, line)


def fix_z_kernel(counts, sc_ref, *refs):
    nx, ny, nz = counts
    got_x, refs = refs[:nx], refs[nx:]
    got_y, refs = refs[:ny][::-1], refs[ny:]
    faces, outs = refs[:nz], refs[nz:]
    x_len, y_len, width = faces[0].shape
    for k in range(nz):
        outs[k][...] = faces[k][...]
    for k in range(nz):
        top = takes_top(sc_ref, k)
        for kind in range(nx):
            ref = got_x[kind]
            reader = RowReader(ref.shape[1] // NODES, lambda row, ref=ref: ref[:, row])
            line = from_partner(sc_ref, counts, 0, kind, end_rows(reader, sc_ref[0], top))
            outs[k][face_place(sc_ref, 0, kind, x_len - 1)] += line
        for kind in range(ny):
            ref = got_y[kind]
            reader = RowReader(ref.shape[1] // NODES, lambda row, ref=ref: ref[:, row])
            add = from_partner(sc_ref, counts, 1, kind, end_rows(reader, sc_ref[0], top))
            first = face_place(sc_ref, 1, kind, 1) == 0
            outs[k][:, 0] += jnp.where(first, add, 0.0)
            outs[k][:, y_len - 1] += jnp.where(first, 0.0, add)


def write_inverse(sc_ref, inv_ref, sizes):
    y_len, rows, width = inv_ref.shape
    filled, at_y, at_z = sc_ref[0], sc_ref[2], sc_ref[3]
    ids = lax.broadcasted_iota(jnp.int32, (rows, width), 0)
    node = ids % NODES
    low = (node == 0) & ((ids >= NODES) | (at_z > 0))
    high = (node == NODES - 1) & ((ids < (filled - 1) * NODES) | (at_z < sizes[2] - 1))
    along_z = jnp.where(low | high, 0.5, 1.0).astype(f32)
    for y in range(y_len):
        inv_ref[y] = along_z * end_factor(y, y_len, at_y, sizes[1])


def end_factor(place, length, position, size):
    whole = place + position * length
    low = (place % NODES == 0) & (whole > 0)
    high = (place % NODES == NODES - 1) & (whole < length * size - 1)
    return jnp.where(low | high, 0.5, 1.0).astype(f32)


def chunk_of(x_len):
    return 2 * NODES if x_len % (2 * NODES) == 0 else NODES


def scale_planes(sc_ref, inv_ref, x, block, x_len, size_x):
    inv = inv_ref[...]
    parts = [block[c] * (inv * end_factor(x + c, x_len, sc_ref[1], size_x)) for c in range(block.shape[0])]
    return jnp.stack(parts, 0)


def node_forward(scaled, feat, weights, layer):
    edge_w, node_in, node_out, biases = weights
    pair = split_cols(scaled)
    w_two = edge_w[layer, 1]
    joined = jnp.concatenate([feat, dot(pair, jnp.concatenate([w_two, w_two], 0)).astype(bf16)], -1)
    half = jnp.bfloat16(0.5)
    act, slope = silu_half(dot(joined, node_in[layer] * half) + 0.5 * biases[layer, pl.ds(1, 1)])
    return pair[:, :128], act.astype(bf16), slope


def node_slopes(grad, slope, weights, layer):
    return (dot_rt(grad, weights[2][layer]) * slope).astype(bf16)


def node_share(sc_ref, x, inv_ref, size_x, dpn, weights, layer, sum_ref):
    shape = (chunk_of(sum_ref.shape[0]),) + sum_ref.shape[1:]
    dx = dot_rt(dpn, weights[1][layer, pl.ds(128, 128)]).reshape(shape)
    share = scale_planes(sc_ref, inv_ref, x, dx, sum_ref.shape[0], size_x)
    joined = couple_slots(share.reshape((-1,) + shape[2:]), sc_ref[0])
    sum_ref[pl.ds(x, shape[0])] = joined.reshape(shape)


def node_products(grad, feat, scaled, act, dpn, grads):
    grads[pl.ds(0, 128)] += dot_t(act, grad)
    both = dot_t(dpn, jnp.concatenate([feat, scaled], -1))
    grads[pl.ds(128, 128)] += both[:, :128]
    grads[pl.ds(256, 128)] += both[:, 128:]
    grads[pl.ds(384, NODES)] += jnp.sum(dpn.astype(f32).reshape(-1, NODES, 128), 0)


def couple_plane(plane):
    y_len = plane.shape[0]
    parts = [plane[y] for y in range(y_len)]
    for cut in range(NODES, y_len, NODES):
        both = parts[cut - 1] + parts[cut]
        parts[cut - 1] = parts[cut] = both
    return jnp.stack(parts, 0)


def along_y(plane, combine):
    return [
        combine(plane[y : y + NODES - 1], plane[y + 1 : y + NODES], y) for y in range(0, plane.shape[0], NODES)
    ]


def spread_plane(sign, edge_x, edges_y, edge_z):
    total = sign * edge_x + (down(edge_z) - edge_z).reshape(edge_x.shape)
    parts = []
    for k, edge in enumerate(edges_y):
        here = total[k * NODES : (k + 1) * NODES]
        parts += [here[:1] - edge[:1], here[1:-1] + (edge[:-1] - edge[1:]), here[-1:] + edge[-1:]]
    return jnp.concatenate(parts, 0)


def plane_forward(low, high, at_high, w_one, half_bias, filled):
    y_len, rows, width = low.shape
    here = jnp.where(at_high, high, low)
    cols = node_rows(here)
    parts = [(high - low).astype(bf16)]
    parts += along_y(here, lambda lower, upper, y: (upper - lower).astype(bf16))
    parts.append((up(cols) - cols).reshape(here.shape).astype(bf16))
    half = dot(flat(jnp.concatenate(parts, 0)), w_one).reshape(-1, rows, width) + half_bias
    act = silu_half(half)[0].astype(bf16).astype(f32)
    at = y_len
    edges_y = []
    for _ in range(y_len // NODES):
        edges_y.append(act[at : at + NODES - 1])
        at += NODES - 1
    edge_z = jnp.where(row_ids() < NODES - 1, node_rows(act[at:]), 0.0)
    total = spread_plane(jnp.where(at_high, 1.0, -1.0), act[:y_len], edges_y, edge_z)
    return couple_plane(couple_slots(total, filled))


def plane_backward(low, high, at_high, slope_x, slope_y, slope_z):
    here = jnp.where(at_high, high, low)
    cols = node_rows(here)
    edge_x = ((high - low) * slope_x).astype(bf16).astype(f32)
    edges_y = along_y(
        here, lambda lower, upper, y: ((upper - lower) * slope_y[y : y + NODES - 1]).astype(bf16).astype(f32)
    )
    edge_z = ((up(cols) - cols) * node_rows(slope_z)).astype(bf16).astype(f32)
    return spread_plane(jnp.where(at_high, 1.0, -1.0), edge_x, edges_y, edge_z)


def face_planes(sc_ref, kind, x_len):
    place = face_place(sc_ref, 0, kind, x_len - 1)
    at_high = place > 0
    return place, jnp.where(at_high, x_len - 2, 0), at_high


def halo_planes(sc_ref, from_ref, halo, kind, start, into_ref, counts):
    x_len, y_len, rows, width = from_ref.shape
    nx, ny, nz = counts
    for c in range(2):
        into_ref[c] = from_ref[start + c]
    into_ref[face_place(sc_ref, 0, kind, x_len - 1) - start] += from_partner(sc_ref, counts, 0, kind, halo[kind][...])
    for c in range(2):
        for k in range(ny):
            got = from_partner(sc_ref, counts, 1, k, halo[nx + k][start + c])
            into_ref[c, face_place(sc_ref, 1, k, y_len - 1)] += got
        for k in range(nz):
            got = from_partner(sc_ref, counts, 2, k, halo[nx + ny + k][start + c])
            top = takes_top(sc_ref, k)
            into_ref[c, :, 0] += jnp.where(top, 0.0, got)
            for s in range(rows // NODES):
                into_ref[c, :, s * NODES + NODES - 1] += jnp.where(top & (sc_ref[0] == s + 1), got, 0.0)


def edges_backward(q_ref, slope_ref, edge_ref, bias_acc):
    x_len, y_len, rows, width = q_ref.shape

    def body(x0, y0):
        ys = pl.ds(y0, NODES)
        prev = None
        here = q_ref[x0, ys]
        bias = jnp.zeros((NODES, width), f32)
        for i in range(NODES):
            total = prev
            prev = None
            nxt = None
            if i < NODES - 1:
                nxt = q_ref[x0 + i + 1, ys]
                prev = ((nxt - here) * slope_ref[0, x0 + i, ys]).astype(bf16).astype(f32)
                total = -prev if total is None else total - prev
                bias = bias + jnp.sum(node_rows(prev), 0)
            along_y = (here[1:] - here[:-1]) * slope_ref[1, x0 + i, pl.ds(y0, NODES - 1)]
            along_y = along_y.astype(bf16).astype(f32)
            cols = node_rows(here)
            along_z = (up(cols) - cols) * node_rows(slope_ref[2, x0 + i, ys])
            along_z = along_z.astype(bf16).astype(f32)
            bias = bias + jnp.sum(node_rows(along_y), 0) + jnp.sum(along_z, 0)
            total = total + (down(along_z) - along_z).reshape(here.shape)
            total = jnp.concatenate(
                [
                    total[:1] - along_y[:1],
                    total[1:-1] + (along_y[:-1] - along_y[1:]),
                    total[-1:] + along_y[-1:],
                ],
                0,
            )
            edge_ref[x0 + i, ys] = total
            here = nxt
        bias_acc[...] += bias

    elements(x_len, y_len, body)


def planes(count, body):
    chunk = chunk_of(count)

    def step(c, carry):
        body(pl.multiple_of(c * chunk, chunk))
        return carry

    lax.fori_loop(0, count // chunk, step, 0)


def half_weights(weights, layer):
    edge_w, node_in, node_out, biases = weights
    return edge_w[layer, 0] * jnp.bfloat16(0.5), 0.5 * biases[layer, pl.ds(0, 1)]


def first_kernel(counts, sizes, sc, edge_w, biases, h, sums, slopes, *faces):
    w_one, bias = half_weights((edge_w, None, None, biases), 0)
    edges_forward(h, w_one, bias, sc[0], sums, slopes)
    couple_columns(sums)
    write_faces(sc, sums, faces, counts)


def first_face_kernel(counts, sizes, sc, edge_w, biases, h, *faces):
    w_one, bias = half_weights((edge_w, None, None, biases), 0)
    for kind, face in enumerate(faces):
        place, start, at_high = face_planes(sc, kind, h.shape[0])
        face[...] = plane_forward(
            h[start].astype(f32), h[start + 1].astype(f32), at_high, w_one, bias, sc[0]
        )


def middle_face_kernel(counts, sizes, sc, edge_w, node_in, node_out, biases, sums_in, h, *refs):
    weights = (edge_w, node_in, node_out, biases)
    n = sum(counts)
    halo, faces, (pair, inv) = refs[:n], refs[n:-2], refs[-2:]
    write_inverse(sc, inv, sizes)
    w_one, bias = half_weights(weights, 1)
    x_len = h.shape[0]
    for kind, face in enumerate(faces):
        place, start, at_high = face_planes(sc, kind, x_len)
        halo_planes(sc, sums_in, halo, kind, start, pair, counts)
        sums_at = flat(scale_planes(sc, inv, start, pair[...], x_len, sizes[0]))
        feat = flat(h[pl.ds(start, 2)])
        scaled, act, slope = node_forward(sums_at, feat, weights, 0)
        moved = (feat.astype(f32) + dot(act, node_out[0])).astype(bf16).astype(f32).reshape(pair.shape)
        face[...] = plane_forward(moved[0], moved[1], at_high, w_one, bias, sc[0])


def face_share(sc, sizes, inv, place, x_len, grad, slope, weights, layer, shape):
    dpn = node_slopes(grad, slope, weights, layer)
    dx = dot_rt(dpn, weights[1][layer, pl.ds(128, 128)]).reshape((1,) + shape)
    share = scale_planes(sc, inv, place, dx, x_len, sizes[0])
    return couple_plane(couple_slots(share[0], sc[0]))


def turn_face_kernel(counts, sizes, sc, edge_w, node_in, node_out, biases, sums_in, h, g_ref, *refs):
    weights = (edge_w, node_in, node_out, biases)
    n = sum(counts)
    halo, faces, (pair, inv) = refs[:n], refs[n:-2], refs[-2:]
    write_inverse(sc, inv, sizes)
    x_len, shape = h.shape[0], h.shape[1:]
    live = (lax.broadcasted_iota(jnp.int32, (1, h.shape[2], 128), 1) < sc[0] * NODES).astype(f32)
    for kind, face in enumerate(faces):
        place, start, at_high = face_planes(sc, kind, x_len)
        halo_planes(sc, sums_in, halo, kind, start, pair, counts)
        plane = pair[place - start][None]
        sums_at = flat(scale_planes(sc, inv, place, plane, x_len, sizes[0]))
        scaled, act, slope = node_forward(sums_at, flat(h[place]), weights, 1)
        grad = flat((g_ref[place].astype(f32) * live).astype(bf16))
        face[...] = face_share(sc, sizes, inv, place, x_len, grad, slope, weights, 1, shape)


def join_face_kernel(counts, sizes, sc, edge_w, node_in, node_out, biases, sums_in, base_in, slopes, slope0, *refs):
    weights = (edge_w, node_in, node_out, biases)
    n = sum(counts)
    halo, faces, (pair, inv) = refs[:n], refs[n:-2], refs[-2:]
    write_inverse(sc, inv, sizes)
    x_len, shape = base_in.shape[0], base_in.shape[1:]
    w_two, w_one = twice(edge_w[1, 1]), twice(edge_w[1, 0])
    for kind, face in enumerate(faces):
        place, start, at_high = face_planes(sc, kind, x_len)
        halo_planes(sc, sums_in, halo, kind, start, pair, counts)
        q = dot_rt(split_cols(flat(pair[...])), w_two).reshape(pair.shape)
        edge = plane_backward(q[0], q[1], at_high, slopes[0, start], slopes[1, place], slopes[2, place])
        grad = (flat(base_in[place]) + dot_rt(split_cols(flat(edge)), w_one)).astype(bf16)
        face[...] = face_share(sc, sizes, inv, place, x_len, grad, flat(slope0[place]), weights, 0, shape)


def twice(weight):
    return jnp.concatenate([weight, weight], 1)


def middle_kernel(counts, sizes, sc, edge_w, node_in, node_out, biases, sums_in, h, *refs):
    weights = (edge_w, node_in, node_out, biases)
    n = sum(counts)
    halo, refs = refs[:n], refs[n:]
    scaled_ref, act_ref, slope_ref, next_ref, sums, slopes = refs[:6]
    faces, (work, inv) = refs[6:-2], refs[-2:]
    add_halo(sc, sums_in, halo, work, counts)
    write_inverse(sc, inv, sizes)
    shape = (chunk_of(h.shape[0]),) + h.shape[1:]

    def body(x):
        at = pl.ds(x, chunk_of(h.shape[0]))
        sums_at = flat(scale_planes(sc, inv, x, work[at], h.shape[0], sizes[0]))
        scaled, act, slope = node_forward(sums_at, flat(h[at]), weights, 0)
        scaled_ref[at] = scaled.reshape(shape)
        act_ref[at] = act.reshape(shape)
        slope_ref[at] = slope.reshape(shape)
        moved = flat(h[at]).astype(f32) + dot(act, node_out[0])
        next_ref[at] = moved.astype(bf16).reshape(shape)

    planes(h.shape[0], body)
    w_one, bias = half_weights(weights, 1)
    edges_forward(next_ref, w_one, bias, sc[0], sums, slopes)
    couple_columns(sums)
    write_faces(sc, sums, faces, counts)


def turn_kernel(counts, sizes, sc, edge_w, node_in, node_out, biases, sums_in, h, g_ref, *refs):
    weights = (edge_w, node_in, node_out, biases)
    n = sum(counts)
    halo, refs = refs[:n], refs[n:]
    scaled_ref, act_ref, dpn_ref, sums = refs[:4]
    faces, (work, inv) = refs[4:-2], refs[-2:]
    add_halo(sc, sums_in, halo, work, counts)
    write_inverse(sc, inv, sizes)
    shape = (chunk_of(h.shape[0]),) + h.shape[1:]
    live = live_rows(sc, h)

    def body(x):
        at = pl.ds(x, chunk_of(h.shape[0]))
        sums_at = flat(scale_planes(sc, inv, x, work[at], h.shape[0], sizes[0]))
        scaled, act, slope = node_forward(sums_at, flat(h[at]), weights, 1)
        scaled_ref[at] = scaled.reshape(shape)
        act_ref[at] = act.reshape(shape)
        grad = flat((g_ref[at].astype(f32) * live).astype(bf16))
        dpn = node_slopes(grad, slope, weights, 1)
        dpn_ref[at] = dpn.reshape(shape)
        node_share(sc, x, inv, sizes[0], dpn, weights, 1, sums)

    planes(h.shape[0], body)
    couple_columns(sums)
    write_faces(sc, sums, faces, counts)


def live_rows(sc, h):
    return (lax.broadcasted_iota(jnp.int32, (1, 1, h.shape[2], 128), 2) < sc[0] * NODES).astype(f32)


def products_kernel(sc, node_in, h, g_ref, scaled, act, dpn, base, grads):
    grads[...] = jnp.zeros_like(grads)
    live = live_rows(sc, h)

    def body(x):
        at = pl.ds(x, chunk_of(h.shape[0]))
        grad = (g_ref[at].astype(f32) * live).astype(bf16)
        node_products(flat(grad), flat(h[at]), flat(scaled[at]), flat(act[at]), flat(dpn[at]), grads)
        dx = dot_rt(flat(dpn[at]), node_in[1, pl.ds(0, 128)])
        base[at] = grad.astype(f32) + dx.reshape(grad.shape)

    planes(h.shape[0], body)


def edge_parts(counts, sc, weights, layer, sums_in, halo, h, slopes, work, grads, row):
    add_halo(sc, sums_in, halo, work, counts)
    shape = (chunk_of(h.shape[0]),) + h.shape[1:]
    w_two = twice(weights[0][layer, 1])

    def to_q(x):
        at = pl.ds(x, chunk_of(h.shape[0]))
        work[at] = dot_rt(split_cols(flat(work[at])), w_two).reshape(shape)

    planes(h.shape[0], to_q)
    edges_backward(work, slopes, work, grads.at[pl.ds(row + 128, NODES)])


def edge_product(h, x, pair, grads, row):
    both = dot_t(flat(h[pl.ds(x, chunk_of(h.shape[0]))]), pair)
    grads[pl.ds(row, 128)] += both[:, :128] + both[:, 128:]


def join_kernel(
    counts, sizes, sc, edge_w, node_in, node_out, biases,
    sums_in, h, base_in, slopes, h0, scaled0, act0, slope0, grads1, *refs
):
    weights = (edge_w, node_in, node_out, biases)
    n = sum(counts)
    halo, refs = refs[:n], refs[n:]
    grad_ref, dpn_ref, sums, keep, send = refs[:5]
    faces, (work, inv, grads) = refs[5:-3], refs[-3:]
    write_inverse(sc, inv, sizes)
    grads[...] = jnp.zeros_like(grads)
    grads[pl.ds(512 + 2 * NODES, grads1.shape[0])] = grads1[...]

    row = 384 + NODES
    shape = (chunk_of(h.shape[0]),) + h.shape[1:]
    edge_parts(counts, sc, weights, 1, sums_in, halo, h, slopes, work, grads, row)
    w_one = twice(edge_w[1, 0])

    def body(x):
        at = pl.ds(x, chunk_of(h.shape[0]))
        pair = split_cols(flat(work[at]))
        edge_product(h, x, pair, grads, row)
        grad = (flat(base_in[at]) + dot_rt(pair, w_one)).astype(bf16)
        dpn = node_slopes(grad, flat(slope0[at]), weights, 0)
        node_products(grad, flat(h0[at]), flat(scaled0[at]), flat(act0[at]), dpn, grads)
        grad_ref[at] = grad.reshape(shape)
        dpn_ref[at] = dpn.reshape(shape)
        node_share(sc, x, inv, sizes[0], dpn, weights, 0, sums)

    planes(h.shape[0], body)
    couple_columns(sums)
    write_faces(sc, sums, faces, counts)
    write_halves(sc, halving_steps(sizes)[0], grads, keep, send)


def last_kernel(counts, sizes, sc, edge_w, node_in, node_out, biases, sums_in, h, slopes, *refs):
    n = sum(counts)
    halo, (edges, grads) = refs[:n], refs[n:]
    grads[...] = jnp.zeros_like(grads)
    edge_parts(counts, sc, (edge_w,), 0, sums_in, halo, h, slopes, edges, grads, 0)

    def body(x):
        edge_product(h, x, split_cols(flat(edges[pl.ds(x, chunk_of(edges.shape[0]))])), grads, 0)

    planes(h.shape[0], body)


def state_kernel(sc, edge_w, node_in, grad_in, dpn, edges, grad_ref):
    shape = (chunk_of(edges.shape[0]),) + edges.shape[1:]
    weight = jnp.concatenate([twice(edge_w[0, 0]), node_in[0, pl.ds(0, 128)]], 1)

    def body(x):
        at = pl.ds(x, chunk_of(edges.shape[0]))
        parts = jnp.concatenate([split_cols(flat(edges[at])), flat(dpn[at])], -1)
        grad_ref[at] = (flat(grad_in[at]).astype(f32) + dot_rt(parts, weight)).astype(bf16).reshape(shape)

    planes(edges.shape[0], body)


def finish_kernel(scale, last_rows, step, sc, edge_w, node_in, value, got, *refs):
    edge_grads, in_grads, out_grads, bias_grads, both = refs
    width = edge_w.shape[-1]
    join_kernel_of(step, last_rows, sc, value, got, both)

    def rows_of(part, start, count=width):
        ref, offset = part
        return ref[pl.ds(offset + start, count)] * scale

    def bias_of(part, start):
        return jnp.sum(rows_of(part, start, NODES), 0, keepdims=True)

    end = 3 * width
    last, sum0 = (both, 0), (both, last_rows)
    sum1 = (both, last_rows + 512 + 2 * NODES)
    firsts = ((last, 0), (sum0, end + NODES))
    for layer, part in enumerate((sum0, sum1)):
        out_grads[layer] = rows_of(part, 0)
        in_grads[layer, pl.ds(0, width)] = rows_of(part, width).T
        bias_grads[layer, pl.ds(1, 1)] = bias_of(part, end)
        source, start = firsts[layer]
        edge_grads[layer, 0] = rows_of(source, start)
        bias_grads[layer, pl.ds(0, 1)] = bias_of(source, start + width)
        mixed = rows_of(part, 2 * width).T
        high = mixed.astype(bf16)
        low = (mixed - high.astype(f32)).astype(bf16)
        lower = node_in[layer, pl.ds(width, width)]
        edge_grads[layer, 1] = dot_rt(high, lower) + dot_rt(low, lower)
        w_two = edge_w[layer, 1]
        in_grads[layer, pl.ds(width, width)] = dot_t(w_two, high) + dot_t(w_two, low)


def call(kernel, name, inputs, outs, scratch=(), flops=0, aliases=None):
    total = sum(math.prod(o.shape) * o.dtype.itemsize for o in outs)
    total += sum(math.prod(i.shape) * i.dtype.itemsize for i in inputs)
    return pl.pallas_call(
        kernel,
        name=name,
        out_shape=tuple(outs),
        in_specs=[SM] + [VM] * (len(inputs) - 1),
        out_specs=tuple([VM] * len(outs)),
        scratch_shapes=list(scratch),
        input_output_aliases=aliases or {},
        compiler_params=pltpu.CompilerParams(vmem_limit_bytes=VMEM_LIMIT),
        cost_estimate=pl.CostEstimate(flops=flops, bytes_accessed=total, transcendentals=0),
    )(*inputs)


def pairs(size, kind):
    matched = [pair for low in range(kind, size - 1, 2) for pair in ((low, low + 1), (low + 1, low))]
    alone = set(range(size)) - {source for source, target in matched}
    return matched + [(i, i) for i in sorted(alone)]


def hops(size):
    found = []
    hop = 1
    while hop < size:
        found.append(hop)
        hop *= 2
    return found


def halving_steps(sizes):
    return [(1, hop) for hop in hops(sizes[1])] + [(0, hop) for hop in hops(sizes[0])]


def whole_steps(sizes):
    along_z = hops(sizes[2])
    return [(2, along_z[k : k + 2]) for k in range(0, len(along_z), 2)]


def padded_rows(rows, sizes):
    unit = NODES << len(halving_steps(sizes))
    return -(-rows // unit) * unit


def bit_of(sc_ref, step):
    axis, hop = step
    return (sc_ref[1 + axis] // hop) % 2


def write_halves(sc_ref, step, from_ref, keep, send):
    half = keep.shape[0]
    bit = bit_of(sc_ref, step)
    keep[...] = from_ref[pl.ds(pl.multiple_of(bit * half, NODES), half)]
    send[...] = from_ref[pl.ds(pl.multiple_of((1 - bit) * half, NODES), half)]


def halve_kernel(step, sc, keep_in, got, keep, send, total):
    total[...] = keep_in[...] + got[...]
    write_halves(sc, step, total, keep, send)


def add_kernel(sc, *refs):
    total = refs[0][...] + refs[1][...]
    for ref in refs[2:-1]:
        total = total + ref[...]
    refs[-1][...] = total


def join_kernel_of(step, start, sc, value, got, out):
    half = value.shape[0] - start
    bit = bit_of(sc, step)
    if start:
        out[pl.ds(0, start)] = value[pl.ds(0, start)] + got[pl.ds(0, start)]
    out[pl.ds(pl.multiple_of(start + bit * half, NODES), half)] = value[pl.ds(start, half)]
    out[pl.ds(pl.multiple_of(start + (1 - bit) * half, NODES), half)] = got[pl.ds(start, half)]


def stack_kernel(sc, first, left, right, out):
    rows = first.shape[0]
    out[pl.ds(0, rows)] = first[...]
    out[pl.ds(rows, left.shape[0])] = left[...] + right[...]


def swap(value, step):
    axis = ("gx", "gy", "gz")[step[0]]
    return lax.ppermute(value, axis, [(i, i ^ step[1]) for i in range(lax.axis_size(axis))])


def rows_like(rows, width=128):
    return jax.ShapeDtypeStruct((rows, width), f32)


def halve(sc, sizes, keep, send):
    steps = halving_steps(sizes)
    got = swap(send, steps[0])
    for step in steps[1:]:
        keep, got = yield keep, got
        half = rows_like(keep.shape[0] // 2)
        keep, send = call(
            functools.partial(halve_kernel, step), "halve", (sc, keep, got), [half, half],
            [pltpu.VMEM(keep.shape, f32)],
        )
        got = swap(send, step)
    keep, got = yield keep, got
    return keep, got


class Background:
    def __init__(self):
        self.active = {}

    def add(self, name, steps):
        self.active[name] = [steps, None]

    def advance(self, entry, tied):
        steps, pending = entry
        try:
            entry[1] = next(steps) if pending is None else steps.send(tied)
        except StopIteration:
            entry[0] = None

    def beside(self, anchor):
        for entry in self.active.values():
            steps, pending = entry
            if steps is None:
                continue
            if pending is None:
                self.advance(entry, None)
            elif pending[1] is not None:
                anchor, tied = lax.optimization_barrier((anchor, pending))
                self.advance(entry, tied)
        return anchor

    def finish(self, name):
        entry = self.active[name]
        while entry[0] is not None:
            done = entry[1]
            if done is not None and done[1] is None:
                return done[0]
            self.advance(entry, done)
        return entry[1]


def on_device(state, cotangent, counts, edge_weights, node_in, node_out, biases):
    x_len, y_len, slots, nodes, width = state.shape
    rows = slots * nodes
    grid = (x_len, y_len, rows, width)
    axes = ("gx", "gy", "gz")
    sizes = tuple(lax.axis_size(a) for a in axes)
    trades = Trades(min(size - 1, 2) for size in sizes)
    trades.sizes = sizes
    nx, ny, nz = trades
    h0 = state.reshape(grid)
    g2 = cotangent.reshape(grid)
    sc = jnp.stack([counts[0]] + [lax.axis_index(a).astype(jnp.int32) for a in axes])

    def sds(shape, kind=f32):
        return jax.ShapeDtypeStruct(shape, kind)

    face_x = sds((y_len, rows, width))
    face_y = sds((x_len, rows, width))
    face_z = sds((x_len, y_len, width))
    face_outs = [face_y] * ny + [face_z] * nz
    full = sds(grid)
    full16 = sds(grid, bf16)
    full3 = sds((3,) + grid)
    work = pltpu.VMEM(grid, f32)
    inv = pltpu.VMEM((y_len, rows, width), f32)
    matmul = 2 * math.prod(grid) * width
    weights = (edge_weights, node_in, node_out, biases)

    def run(kernel, name, inputs, outs, scratch, flops):
        body = functools.partial(kernel, trades, sizes)
        return call(body, name, (sc, *weights, *inputs), outs, scratch, flops * matmul)

    def trade(faces, axis):
        size = lax.axis_size(axis)
        got = [lax.ppermute(face, axis, pairs(size, kind)) for kind, face in reversed(list(enumerate(faces)))]
        return got[::-1]

    background = Background()

    pair = pltpu.VMEM((2,) + grid[1:], f32)

    def first_trade(kernel, name, inputs, scratch, flops):
        faces = call(functools.partial(kernel, trades, sizes), name, (sc, *inputs), [face_x] * nx, scratch, flops)
        return trade(faces, "gx")

    def exchange(got_x, faces, work=None, held=()):
        fix = functools.partial(fix_y_kernel, trades)
        faces_y = call(fix, "fix_y", (sc, *got_x, *faces[:ny]), [face_y] * ny)
        got_y = trade(background.beside(faces_y), "gy")
        fix = functools.partial(fix_z_kernel, trades)
        faces_z = call(fix, "fix_z", (sc, *got_x, *got_y[::-1], *faces[ny:]), [face_z] * nz)
        faces_z = background.beside(faces_z)
        done = None
        if work is not None:
            faces_z, held = lax.optimization_barrier((faces_z, held))
            done = work(*held)
        got_z = trade(faces_z, "gz")
        got_z, done = lax.optimization_barrier((got_z, done))
        return (*got_x, *got_y, *got_z), done

    def to_slopes(half):
        return call(slope_kernel, "slopes", (sc, half), [full3], [], matmul, {1: 0})[0]

    def products(*held):
        return call(
            products_kernel, "nodes1_products", (sc, node_in, *held), [full, rows_like(3 * width + NODES)], [], 6 * matmul
        )

    got_x = first_trade(first_face_kernel, "face0", (edge_weights, biases, h0), [], matmul // 8)
    sums, slopes0, *faces = call(
        functools.partial(first_kernel, trades, sizes), "edges0", (sc, edge_weights, biases, h0),
        [full, full3] + face_outs, [], 3 * matmul,
    )
    halo, slopes0 = exchange(got_x, faces, to_slopes, (slopes0,))
    inputs = (*weights, sums, h0, *halo)
    got_x = first_trade(middle_face_kernel, "face1", inputs, [pair, inv], matmul // 4)
    scaled0, act0, slope0, h1, sums, slopes1, *faces = run(
        middle_kernel, "nodes0_edges1", (sums, h0, *halo),
        [full16, full16, full, full16, full, full3] + face_outs, [work, inv], 8,
    )
    halo, slopes1 = exchange(got_x, faces, to_slopes, (slopes1,))
    inputs = (*weights, sums, h1, g2, *halo)
    got_x = first_trade(turn_face_kernel, "face2", inputs, [pair, inv], matmul // 4)
    scaled1, act1, dpn1, sums, *faces = run(
        turn_kernel, "nodes1_back", (sums, h1, g2, *halo), [full16] * 3 + [full] + face_outs, [work, inv], 7
    )
    halo, (base, grads1) = exchange(got_x, faces, products, (h1, g2, scaled1, act1, dpn1))
    inputs = (*weights, sums, base, slopes1, slope0, *halo)
    got_x = first_trade(join_face_kernel, "face3", inputs, [pair, inv], matmul // 4)
    grad_rows = padded_rows(7 * width + 3 * NODES, sizes)
    half = rows_like(grad_rows // 2)
    grad_in, dpn0, sums, keep, send, *faces = run(
        join_kernel, "edges1_back_nodes0_back",
        (sums, h1, base, slopes1, h0, scaled0, act0, slope0, grads1, *halo),
        [full16, full16, full, half, half] + face_outs, [work, inv, pltpu.VMEM((grad_rows, width), f32)], 12,
    )
    background.add("sums", halve(sc, sizes, keep, send))
    halo, _ = exchange(got_x, faces)
    tail_rows = width + NODES
    edges, last = run(last_kernel, "edges0_back", (sums, h0, slopes0, *halo), [full, rows_like(tail_rows)], [], 6)
    keep, got = background.finish("sums")
    (value,) = call(stack_kernel, "stack", (sc, last, keep, got), [rows_like(tail_rows + keep.shape[0])])
    value, grad_in, dpn0, edges = lax.optimization_barrier((value, grad_in, dpn0, edges))
    (grad0,) = call(
        state_kernel, "state_grad", (sc, edge_weights, node_in, grad_in, dpn0, edges), [full16], [], 4 * matmul
    )
    for axis, together in whole_steps(sizes):
        partners = [sum(c) for n in range(1, len(together) + 1) for c in itertools.combinations(together, n)]
        got = [swap(value, (axis, partner)) for partner in partners]
        (value,) = call(add_kernel, "add", (sc, value, *got), [rows_like(value.shape[0])])
        value, grad0 = lax.optimization_barrier((value, grad0))
    first, *rest = halving_steps(sizes)
    for step in reversed(rest):
        out = rows_like(2 * value.shape[0] - tail_rows)
        body = functools.partial(join_kernel_of, step, tail_rows)
        (value,) = call(body, "join", (sc, value, swap(value, step)), [out])
    layers_all = 3 * slots * sizes[2] // 4
    nodes_all = x_len * sizes[0] * y_len * sizes[1] * layers_all * nodes
    scale = 1.0 / math.sqrt(nodes_all)
    edge_grads, in_grads, out_grads, bias_grads = call(
        functools.partial(finish_kernel, scale, tail_rows, first), "finish",
        (sc, edge_weights, node_in, value, swap(value, first)),
        [sds(edge_weights.shape), sds(node_in.shape), sds(node_out.shape), sds(biases.shape)],
        [pltpu.VMEM((2 * value.shape[0] - tail_rows, width), f32)],
    )
    return grad0.reshape(state.shape), edge_grads, in_grads, out_grads, bias_grads


def solution(mesh):
    return jax.shard_map(
        on_device,
        mesh=mesh,
        in_specs=(
            P("gx", "gy", "gz", None, None),
            P("gx", "gy", "gz", None, None),
            P("gz"),
            P(),
            P(),
            P(),
            P(),
        ),
        out_specs=(P("gx", "gy", "gz", None, None), P(), P(), P(), P()),
        check_vma=False,
    )
```

```python
import functools
import itertools
import math

import jax
import jax.numpy as jnp
from jax import lax
from jax.experimental import pallas as pl
from jax.experimental.pallas import tpu as pltpu
from jax.sharding import PartitionSpec as P

f32 = jnp.float32
bf16 = jnp.bfloat16
NODES = 8
VMEM_LIMIT = 12 * 1024 * 1024
VM = pl.BlockSpec(memory_space=pltpu.VMEM)
SM = pl.BlockSpec(memory_space=pltpu.SMEM)


def dot(left, right):
    return lax.dot_general(left, right, (((1,), (0,)), ((), ())), preferred_element_type=f32)


def dot_t(left, right):
    return lax.dot_general(left, right, (((0,), (0,)), ((), ())), preferred_element_type=f32)


def dot_rt(left, right):
    return lax.dot_general(left, right, (((1,), (1,)), ((), ())), preferred_element_type=f32)


def silu_half(half):
    th = jnp.tanh(half)
    prod = half * th
    return half + prod, (0.5 + 0.5 * th) * ((1.0 + half) - prod)


def split_cols(value):
    high = value.astype(bf16)
    low = (value - high.astype(f32)).astype(bf16)
    return jnp.concatenate([high, low], -1)


def up(value):
    return pltpu.roll(value, NODES - 1, 1)


def down(value):
    return pltpu.roll(value, 1, 1)


def flat(value):
    return value.reshape(-1, value.shape[-1])


def node_rows(value):
    return value.reshape(-1, NODES, value.shape[-1])


def row_ids():
    return lax.broadcasted_iota(jnp.int32, (1, NODES, 128), 1)


def couple_slots(plane, filled):
    count, rows, width = plane.shape
    slots = rows // NODES
    parts = plane.reshape(count, slots, NODES, width)
    ids = row_ids()
    done = []
    for s in range(slots):
        here = parts[:, s]
        if s + 1 < slots:
            take = (ids == NODES - 1) & (s + 1 < filled)
            here = here + jnp.where(take, up(parts[:, s + 1]), 0.0)
        if s > 0:
            here = here + jnp.where(ids == 0, down(parts[:, s - 1]), 0.0)
            here = jnp.where(s < filled, here, 0.0)
        done.append(here[:, None])
    return jnp.concatenate(done, 1).reshape(plane.shape)


def elements(x_len, y_len, body):
    ey = y_len // NODES
    total = (x_len // NODES) * ey

    def step(e, carry):
        x0 = pl.multiple_of((e // ey) * NODES, NODES)
        y0 = pl.multiple_of((e % ey) * NODES, NODES)
        body(x0, y0)
        return carry

    lax.fori_loop(0, total, step, 0)


def edge_dots(parts, weight, weight_both):
    rows, width = parts[0].shape[1:]
    if len(parts) == 2:
        return dot(flat(jnp.concatenate(parts, 0)), weight).reshape(-1, rows, width)
    both = dot(jnp.concatenate([flat(parts[0]), flat(parts[2])], -1), weight_both)
    between = dot(flat(parts[1]), weight).reshape(-1, rows, width)
    first, last = (both[:, k : k + width].reshape(-1, rows, width) for k in (0, width))
    return jnp.concatenate([first, between, last], 0)


def edges_forward(h_ref, w_one, half_bias, filled, sum_ref, half_ref):
    x_len, y_len, rows, width = h_ref.shape
    blank = jnp.zeros_like(w_one)
    w_both = jnp.concatenate([jnp.concatenate([w_one, blank], 1), jnp.concatenate([blank, w_one], 1)], 0)
    inner = row_ids() < NODES - 1

    def body(x0, y0):
        ys = pl.ds(y0, NODES)
        prev = None
        here = h_ref[x0, ys].astype(f32)
        for i in range(NODES):
            parts = []
            nxt = None
            if i < NODES - 1:
                nxt = h_ref[x0 + i + 1, ys].astype(f32)
                parts.append((nxt - here).astype(bf16))
            parts.append((here[1:] - here[:-1]).astype(bf16))
            cols = node_rows(here)
            parts.append((up(cols) - cols).reshape(here.shape).astype(bf16))
            half = edge_dots(parts, w_one, w_both) + half_bias
            act = (half + half * jnp.tanh(half)).astype(bf16).astype(f32)
            at = 0
            total = prev
            prev = None
            if i < NODES - 1:
                prev = act[:NODES]
                total = -prev if total is None else total - prev
                half_ref[0, x0 + i, ys] = half[:NODES]
                at = NODES
            along_y = act[at : at + NODES - 1]
            half_ref[1, x0 + i, pl.ds(y0, NODES - 1)] = half[at : at + NODES - 1]
            at += NODES - 1
            along_z = jnp.where(inner, node_rows(act[at:]), 0.0)
            half_ref[2, x0 + i, ys] = half[at:]
            total = total + (down(along_z) - along_z).reshape(here.shape)
            total = jnp.concatenate(
                [
                    total[:1] - along_y[:1],
                    total[1:-1] + (along_y[:-1] - along_y[1:]),
                    total[-1:] + along_y[-1:],
                ],
                0,
            )
            sum_ref[x0 + i, ys] = couple_slots(total, filled)
            here = nxt

    elements(x_len, y_len, body)


def slope_kernel(sc, half_in, slope_out):
    inner = row_ids() < NODES - 1

    def step(x, carry):
        for k in range(3):
            slope = silu_half(half_in[k, x])[1]
            if k == 2:
                slope = jnp.where(inner, node_rows(slope), 0.0).reshape(slope.shape)
            slope_out[k, x] = slope
        return carry

    lax.fori_loop(0, half_in.shape[1], step, 0)


def couple_columns(sum_ref):
    x_len, y_len = sum_ref.shape[:2]
    for cut in range(NODES, x_len, NODES):
        both = sum_ref[cut - 1] + sum_ref[cut]
        sum_ref[cut - 1] = both
        sum_ref[cut] = both
    for cut in range(NODES, y_len, NODES):
        both = sum_ref[:, cut - 1] + sum_ref[:, cut]
        sum_ref[:, cut - 1] = both
        sum_ref[:, cut] = both


def face_place(sc_ref, axis, kind, last):
    return jnp.where((sc_ref[1 + axis] + kind) % 2 == 0, last, 0)


def end_rows(values, filled, take_top):
    picked = values(0)
    slots = values.slots
    for s in range(slots):
        picked = jnp.where(take_top & (filled == s + 1), values(s * NODES + NODES - 1), picked)
    return picked


class RowReader:
    def __init__(self, slots, read):
        self.slots = slots
        self.read = read

    def __call__(self, row):
        return self.read(row)


def takes_top(sc_ref, kind):
    return (sc_ref[3] + kind) % 2 == 0


def write_faces(sc_ref, sum_ref, faces, counts):
    x_len, y_len, rows, width = sum_ref.shape
    nx, ny, nz = counts
    reader = RowReader(rows // NODES, lambda row: sum_ref[:, :, row])
    for kind in range(ny):
        faces[kind][...] = sum_ref[:, face_place(sc_ref, 1, kind, y_len - 1)]
    for kind in range(nz):
        faces[ny + kind][...] = end_rows(reader, sc_ref[0], takes_top(sc_ref, kind))


def add_halo(sc_ref, halo, into_ref, counts):
    x_len, y_len, rows, width = into_ref.shape
    nx, ny, nz = counts
    for kind in range(nx):
        into_ref[face_place(sc_ref, 0, kind, x_len - 1)] += halo[kind][...]
    for kind in range(ny):
        into_ref[:, face_place(sc_ref, 1, kind, y_len - 1)] += halo[nx + kind][...]
    if nz:
        got = [halo[nx + ny + kind][...] for kind in range(nz)]
        tops = [takes_top(sc_ref, kind) for kind in range(nz)]
        from_below = sum(jnp.where(top, 0.0, value) for top, value in zip(tops, got))
        from_above = sum(jnp.where(top, value, 0.0) for top, value in zip(tops, got))
        into_ref[:, :, 0] += from_below
        for s in range(rows // NODES):
            into_ref[:, :, s * NODES + NODES - 1] += jnp.where(sc_ref[0] == s + 1, from_above, 0.0)


def fix_y_kernel(counts, sc_ref, *refs):
    nx, ny, nz = counts
    got, faces, outs = refs[:nx], refs[nx : nx + ny], refs[nx + ny :]
    x_len = faces[0].shape[0]
    for k in range(ny):
        outs[k][...] = faces[k][...]
    for kind in range(nx):
        place = face_place(sc_ref, 0, kind, x_len - 1)
        for k in range(ny):
            y_len = got[kind].shape[0]
            outs[k][place] += got[kind][face_place(sc_ref, 1, k, y_len - 1)]


def fix_z_kernel(counts, sc_ref, *refs):
    nx, ny, nz = counts
    got_x, refs = refs[:nx], refs[nx:]
    got_y, refs = refs[:ny][::-1], refs[ny:]
    faces, outs = refs[:nz], refs[nz:]
    x_len, y_len, width = faces[0].shape
    for k in range(nz):
        outs[k][...] = faces[k][...]
    for k in range(nz):
        top = takes_top(sc_ref, k)
        for kind in range(nx):
            ref = got_x[kind]
            reader = RowReader(ref.shape[1] // NODES, lambda row, ref=ref: ref[:, row])
            outs[k][face_place(sc_ref, 0, kind, x_len - 1)] += end_rows(reader, sc_ref[0], top)
        for kind in range(ny):
            ref = got_y[kind]
            reader = RowReader(ref.shape[1] // NODES, lambda row, ref=ref: ref[:, row])
            add = end_rows(reader, sc_ref[0], top)
            first = face_place(sc_ref, 1, kind, 1) == 0
            outs[k][:, 0] += jnp.where(first, add, 0.0)
            outs[k][:, y_len - 1] += jnp.where(first, 0.0, add)


def write_inverse(sc_ref, inv_ref, sizes):
    y_len, rows, width = inv_ref.shape
    filled, at_y, at_z = sc_ref[0], sc_ref[2], sc_ref[3]
    ids = lax.broadcasted_iota(jnp.int32, (rows, width), 0)
    node = ids % NODES
    low = (node == 0) & ((ids >= NODES) | (at_z > 0))
    high = (node == NODES - 1) & ((ids < (filled - 1) * NODES) | (at_z < sizes[2] - 1))
    along_z = jnp.where(low | high, 0.5, 1.0).astype(f32)
    for y in range(y_len):
        inv_ref[y] = along_z * end_factor(y, y_len, at_y, sizes[1])


def end_factor(place, length, position, size):
    whole = place + position * length
    low = (place % NODES == 0) & (whole > 0)
    high = (place % NODES == NODES - 1) & (whole < length * size - 1)
    return jnp.where(low | high, 0.5, 1.0).astype(f32)


def chunk_of(x_len):
    return 2 * NODES if x_len % (2 * NODES) == 0 else NODES


def scale_planes(sc_ref, inv_ref, x, block, x_len, size_x):
    inv = inv_ref[...]
    parts = [block[c] * (inv * end_factor(x + c, x_len, sc_ref[1], size_x)) for c in range(block.shape[0])]
    return jnp.stack(parts, 0)


def node_forward(scaled, feat, weights, layer):
    edge_w, node_in, node_out, biases = weights
    pair = split_cols(scaled)
    w_two = edge_w[layer, 1]
    joined = jnp.concatenate([feat, dot(pair, jnp.concatenate([w_two, w_two], 0)).astype(bf16)], -1)
    half = jnp.bfloat16(0.5)
    act, slope = silu_half(dot(joined, node_in[layer] * half) + 0.5 * biases[layer, pl.ds(1, 1)])
    return pair[:, :128], act.astype(bf16), slope


def node_slopes(grad, slope, weights, layer):
    return (dot_rt(grad, weights[2][layer]) * slope).astype(bf16)


def node_share(sc_ref, x, inv_ref, size_x, dpn, weights, layer, sum_ref):
    shape = (chunk_of(sum_ref.shape[0]),) + sum_ref.shape[1:]
    dx = dot_rt(dpn, weights[1][layer, pl.ds(128, 128)]).reshape(shape)
    share = scale_planes(sc_ref, inv_ref, x, dx, sum_ref.shape[0], size_x)
    joined = couple_slots(share.reshape((-1,) + shape[2:]), sc_ref[0])
    sum_ref[pl.ds(x, shape[0])] = joined.reshape(shape)


def node_products(grad, feat, scaled, act, dpn, grads):
    grads[pl.ds(0, 128)] += dot_t(act, grad)
    both = dot_t(dpn, jnp.concatenate([feat, scaled], -1))
    grads[pl.ds(128, 128)] += both[:, :128]
    grads[pl.ds(256, 128)] += both[:, 128:]
    grads[pl.ds(384, NODES)] += jnp.sum(dpn.astype(f32).reshape(-1, NODES, 128), 0)


def couple_plane(plane):
    y_len = plane.shape[0]
    parts = [plane[y] for y in range(y_len)]
    for cut in range(NODES, y_len, NODES):
        both = parts[cut - 1] + parts[cut]
        parts[cut - 1] = parts[cut] = both
    return jnp.stack(parts, 0)


def along_y(plane, combine):
    return [
        combine(plane[y : y + NODES - 1], plane[y + 1 : y + NODES], y) for y in range(0, plane.shape[0], NODES)
    ]


def spread_plane(sign, edge_x, edges_y, edge_z):
    total = sign * edge_x + (down(edge_z) - edge_z).reshape(edge_x.shape)
    parts = []
    for k, edge in enumerate(edges_y):
        here = total[k * NODES : (k + 1) * NODES]
        parts += [here[:1] - edge[:1], here[1:-1] + (edge[:-1] - edge[1:]), here[-1:] + edge[-1:]]
    return jnp.concatenate(parts, 0)


def plane_forward(low, high, at_high, w_one, half_bias, filled):
    y_len, rows, width = low.shape
    here = jnp.where(at_high, high, low)
    cols = node_rows(here)
    parts = [(high - low).astype(bf16)]
    parts += along_y(here, lambda lower, upper, y: (upper - lower).astype(bf16))
    parts.append((up(cols) - cols).reshape(here.shape).astype(bf16))
    half = dot(flat(jnp.concatenate(parts, 0)), w_one).reshape(-1, rows, width) + half_bias
    act = silu_half(half)[0].astype(bf16).astype(f32)
    at = y_len
    edges_y = []
    for _ in range(y_len // NODES):
        edges_y.append(act[at : at + NODES - 1])
        at += NODES - 1
    edge_z = jnp.where(row_ids() < NODES - 1, node_rows(act[at:]), 0.0)
    total = spread_plane(jnp.where(at_high, 1.0, -1.0), act[:y_len], edges_y, edge_z)
    return couple_plane(couple_slots(total, filled))


def plane_backward(low, high, at_high, slope_x, slope_y, slope_z):
    here = jnp.where(at_high, high, low)
    cols = node_rows(here)
    edge_x = ((high - low) * slope_x).astype(bf16).astype(f32)
    edges_y = along_y(
        here, lambda lower, upper, y: ((upper - lower) * slope_y[y : y + NODES - 1]).astype(bf16).astype(f32)
    )
    edge_z = ((up(cols) - cols) * node_rows(slope_z)).astype(bf16).astype(f32)
    return spread_plane(jnp.where(at_high, 1.0, -1.0), edge_x, edges_y, edge_z)


def face_planes(sc_ref, kind, x_len):
    place = face_place(sc_ref, 0, kind, x_len - 1)
    at_high = place > 0
    return place, jnp.where(at_high, x_len - 2, 0), at_high


def halo_planes(sc_ref, from_ref, halo, kind, start, into_ref, counts):
    x_len, y_len, rows, width = from_ref.shape
    nx, ny, nz = counts
    for c in range(2):
        into_ref[c] = from_ref[start + c]
    into_ref[face_place(sc_ref, 0, kind, x_len - 1) - start] += halo[kind][...]
    for c in range(2):
        for k in range(ny):
            into_ref[c, face_place(sc_ref, 1, k, y_len - 1)] += halo[nx + k][start + c]
        for k in range(nz):
            got = halo[nx + ny + k][start + c]
            top = takes_top(sc_ref, k)
            into_ref[c, :, 0] += jnp.where(top, 0.0, got)
            for s in range(rows // NODES):
                into_ref[c, :, s * NODES + NODES - 1] += jnp.where(top & (sc_ref[0] == s + 1), got, 0.0)


def edges_backward(q_ref, slope_ref, edge_ref, bias_acc):
    x_len, y_len, rows, width = q_ref.shape

    def body(x0, y0):
        ys = pl.ds(y0, NODES)
        prev = None
        here = q_ref[x0, ys]
        bias = jnp.zeros((NODES, width), f32)
        for i in range(NODES):
            total = prev
            prev = None
            nxt = None
            if i < NODES - 1:
                nxt = q_ref[x0 + i + 1, ys]
                prev = ((nxt - here) * slope_ref[0, x0 + i, ys]).astype(bf16).astype(f32)
                total = -prev if total is None else total - prev
                bias = bias + jnp.sum(node_rows(prev), 0)
            along_y = (here[1:] - here[:-1]) * slope_ref[1, x0 + i, pl.ds(y0, NODES - 1)]
            along_y = along_y.astype(bf16).astype(f32)
            cols = node_rows(here)
            along_z = (up(cols) - cols) * node_rows(slope_ref[2, x0 + i, ys])
            along_z = along_z.astype(bf16).astype(f32)
            bias = bias + jnp.sum(node_rows(along_y), 0) + jnp.sum(along_z, 0)
            total = total + (down(along_z) - along_z).reshape(here.shape)
            total = jnp.concatenate(
                [
                    total[:1] - along_y[:1],
                    total[1:-1] + (along_y[:-1] - along_y[1:]),
                    total[-1:] + along_y[-1:],
                ],
                0,
            )
            edge_ref[x0 + i, ys] = total
            here = nxt
        bias_acc[...] += bias

    elements(x_len, y_len, body)


def planes(count, body):
    chunk = chunk_of(count)

    def step(c, carry):
        body(pl.multiple_of(c * chunk, chunk))
        return carry

    lax.fori_loop(0, count // chunk, step, 0)


def half_weights(weights, layer):
    edge_w, node_in, node_out, biases = weights
    return edge_w[layer, 0] * jnp.bfloat16(0.5), 0.5 * biases[layer, pl.ds(0, 1)]


def first_kernel(counts, sizes, sc, edge_w, biases, h, sums, slopes, *faces):
    w_one, bias = half_weights((edge_w, None, None, biases), 0)
    edges_forward(h, w_one, bias, sc[0], sums, slopes)
    couple_columns(sums)
    write_faces(sc, sums, faces, counts)


def first_face_kernel(counts, sizes, sc, edge_w, biases, h, *faces):
    w_one, bias = half_weights((edge_w, None, None, biases), 0)
    for kind, face in enumerate(faces):
        place, start, at_high = face_planes(sc, kind, h.shape[0])
        face[...] = plane_forward(
            h[start].astype(f32), h[start + 1].astype(f32), at_high, w_one, bias, sc[0]
        )


def middle_face_kernel(counts, sizes, sc, edge_w, node_in, node_out, biases, sums_in, h, *refs):
    weights = (edge_w, node_in, node_out, biases)
    n = sum(counts)
    halo, faces, (pair, inv) = refs[:n], refs[n:-2], refs[-2:]
    write_inverse(sc, inv, sizes)
    w_one, bias = half_weights(weights, 1)
    x_len = h.shape[0]
    for kind, face in enumerate(faces):
        place, start, at_high = face_planes(sc, kind, x_len)
        halo_planes(sc, sums_in, halo, kind, start, pair, counts)
        sums_at = flat(scale_planes(sc, inv, start, pair[...], x_len, sizes[0]))
        feat = flat(h[pl.ds(start, 2)])
        scaled, act, slope = node_forward(sums_at, feat, weights, 0)
        moved = (feat.astype(f32) + dot(act, node_out[0])).astype(bf16).astype(f32).reshape(pair.shape)
        face[...] = plane_forward(moved[0], moved[1], at_high, w_one, bias, sc[0])


def face_share(sc, sizes, inv, place, x_len, grad, slope, weights, layer, shape):
    dpn = node_slopes(grad, slope, weights, layer)
    dx = dot_rt(dpn, weights[1][layer, pl.ds(128, 128)]).reshape((1,) + shape)
    share = scale_planes(sc, inv, place, dx, x_len, sizes[0])
    return couple_plane(couple_slots(share[0], sc[0]))


def turn_face_kernel(counts, sizes, sc, edge_w, node_in, node_out, biases, sums_in, h, g_ref, *refs):
    weights = (edge_w, node_in, node_out, biases)
    n = sum(counts)
    halo, faces, (pair, inv) = refs[:n], refs[n:-2], refs[-2:]
    write_inverse(sc, inv, sizes)
    x_len, shape = h.shape[0], h.shape[1:]
    live = (lax.broadcasted_iota(jnp.int32, (1, h.shape[2], 128), 1) < sc[0] * NODES).astype(f32)
    for kind, face in enumerate(faces):
        place, start, at_high = face_planes(sc, kind, x_len)
        halo_planes(sc, sums_in, halo, kind, start, pair, counts)
        plane = pair[place - start][None]
        sums_at = flat(scale_planes(sc, inv, place, plane, x_len, sizes[0]))
        scaled, act, slope = node_forward(sums_at, flat(h[place]), weights, 1)
        grad = flat((g_ref[place].astype(f32) * live).astype(bf16))
        face[...] = face_share(sc, sizes, inv, place, x_len, grad, slope, weights, 1, shape)


def join_face_kernel(counts, sizes, sc, edge_w, node_in, node_out, biases, sums_in, base_in, slopes, slope0, *refs):
    weights = (edge_w, node_in, node_out, biases)
    n = sum(counts)
    halo, faces, (pair, inv) = refs[:n], refs[n:-2], refs[-2:]
    write_inverse(sc, inv, sizes)
    x_len, shape = base_in.shape[0], base_in.shape[1:]
    w_two, w_one = twice(edge_w[1, 1]), twice(edge_w[1, 0])
    for kind, face in enumerate(faces):
        place, start, at_high = face_planes(sc, kind, x_len)
        halo_planes(sc, sums_in, halo, kind, start, pair, counts)
        q = dot_rt(split_cols(flat(pair[...])), w_two).reshape(pair.shape)
        edge = plane_backward(q[0], q[1], at_high, slopes[0, start], slopes[1, place], slopes[2, place])
        grad = (flat(base_in[place]) + dot_rt(split_cols(flat(edge)), w_one)).astype(bf16)
        face[...] = face_share(sc, sizes, inv, place, x_len, grad, flat(slope0[place]), weights, 0, shape)


def twice(weight):
    return jnp.concatenate([weight, weight], 1)


def middle_kernel(counts, sizes, sc, edge_w, node_in, node_out, biases, sums_in, h, *refs):
    weights = (edge_w, node_in, node_out, biases)
    n = sum(counts)
    halo, refs = refs[:n], refs[n:]
    work, scaled_ref, act_ref, slope_ref, next_ref, sums, slopes = refs[:7]
    faces, inv = refs[7:-1], refs[-1]
    add_halo(sc, halo, work, counts)
    write_inverse(sc, inv, sizes)
    shape = (chunk_of(h.shape[0]),) + h.shape[1:]

    def body(x):
        at = pl.ds(x, chunk_of(h.shape[0]))
        sums_at = flat(scale_planes(sc, inv, x, work[at], h.shape[0], sizes[0]))
        scaled, act, slope = node_forward(sums_at, flat(h[at]), weights, 0)
        scaled_ref[at] = scaled.reshape(shape)
        act_ref[at] = act.reshape(shape)
        slope_ref[at] = slope.reshape(shape)
        moved = flat(h[at]).astype(f32) + dot(act, node_out[0])
        next_ref[at] = moved.astype(bf16).reshape(shape)

    planes(h.shape[0], body)
    w_one, bias = half_weights(weights, 1)
    edges_forward(next_ref, w_one, bias, sc[0], sums, slopes)
    couple_columns(sums)
    write_faces(sc, sums, faces, counts)


def turn_kernel(counts, sizes, sc, edge_w, node_in, node_out, biases, sums_in, h, g_ref, *refs):
    weights = (edge_w, node_in, node_out, biases)
    n = sum(counts)
    halo, refs = refs[:n], refs[n:]
    work, scaled_ref, act_ref, dpn_ref, sums = refs[:5]
    faces, inv = refs[5:-1], refs[-1]
    add_halo(sc, halo, work, counts)
    write_inverse(sc, inv, sizes)
    shape = (chunk_of(h.shape[0]),) + h.shape[1:]
    live = live_rows(sc, h)

    def body(x):
        at = pl.ds(x, chunk_of(h.shape[0]))
        sums_at = flat(scale_planes(sc, inv, x, work[at], h.shape[0], sizes[0]))
        scaled, act, slope = node_forward(sums_at, flat(h[at]), weights, 1)
        scaled_ref[at] = scaled.reshape(shape)
        act_ref[at] = act.reshape(shape)
        grad = flat((g_ref[at].astype(f32) * live).astype(bf16))
        dpn = node_slopes(grad, slope, weights, 1)
        dpn_ref[at] = dpn.reshape(shape)
        node_share(sc, x, inv, sizes[0], dpn, weights, 1, sums)

    planes(h.shape[0], body)
    couple_columns(sums)
    write_faces(sc, sums, faces, counts)


def live_rows(sc, h):
    return (lax.broadcasted_iota(jnp.int32, (1, 1, h.shape[2], 128), 2) < sc[0] * NODES).astype(f32)


def products_kernel(sc, node_in, h, g_ref, scaled, act, dpn, base, grads):
    grads[...] = jnp.zeros_like(grads)
    live = live_rows(sc, h)

    def body(x):
        at = pl.ds(x, chunk_of(h.shape[0]))
        grad = (g_ref[at].astype(f32) * live).astype(bf16)
        node_products(flat(grad), flat(h[at]), flat(scaled[at]), flat(act[at]), flat(dpn[at]), grads)
        dx = dot_rt(flat(dpn[at]), node_in[1, pl.ds(0, 128)])
        base[at] = grad.astype(f32) + dx.reshape(grad.shape)

    planes(h.shape[0], body)


def edge_parts(counts, sc, weights, layer, halo, slopes, work, bias):
    add_halo(sc, halo, work, counts)
    shape = (chunk_of(work.shape[0]),) + work.shape[1:]
    w_two = twice(weights[0][layer, 1])

    def to_q(x):
        at = pl.ds(x, chunk_of(work.shape[0]))
        work[at] = dot_rt(split_cols(flat(work[at])), w_two).reshape(shape)

    planes(work.shape[0], to_q)
    edges_backward(work, slopes, work, bias)


def edge_product(h, x, pair, grads, row):
    both = dot_t(flat(h[pl.ds(x, chunk_of(h.shape[0]))]), pair)
    grads[pl.ds(row, 128)] += both[:, :128] + both[:, 128:]


def join_kernel(counts, sizes, sc, edge_w, node_in, node_out, biases, sums_in, base_in, slopes, slope0, *refs):
    weights = (edge_w, node_in, node_out, biases)
    n = sum(counts)
    halo, refs = refs[:n], refs[n:]
    work, grad_ref, dpn_ref, sums, bias = refs[:5]
    faces, inv = refs[5:-1], refs[-1]
    write_inverse(sc, inv, sizes)
    bias[...] = jnp.zeros_like(bias)
    edge_parts(counts, sc, weights, 1, halo, slopes, work, bias)
    w_one = twice(edge_w[1, 0])
    x_len = work.shape[0]
    shape = (chunk_of(x_len),) + work.shape[1:]

    def body(x):
        at = pl.ds(x, chunk_of(x_len))
        pair = split_cols(flat(work[at]))
        grad = (flat(base_in[at]) + dot_rt(pair, w_one)).astype(bf16)
        dpn = node_slopes(grad, flat(slope0[at]), weights, 0)
        grad_ref[at] = grad.reshape(shape)
        dpn_ref[at] = dpn.reshape(shape)
        node_share(sc, x, inv, sizes[0], dpn, weights, 0, sums)

    planes(x_len, body)
    couple_columns(sums)
    write_faces(sc, sums, faces, counts)


def sums_kernel(sizes, sc, h, edges, grad, h0, scaled0, act0, dpn0, grads1, bias, keep, send, grads):
    grads[...] = jnp.zeros_like(grads)
    row = 384 + NODES
    grads[pl.ds(row + 128, NODES)] = bias[...]
    grads[pl.ds(row + 128 + NODES, grads1.shape[0])] = grads1[...]

    def body(x):
        at = pl.ds(x, chunk_of(h.shape[0]))
        edge_product(h, x, split_cols(flat(edges[at])), grads, row)
        node_products(flat(grad[at]), flat(h0[at]), flat(scaled0[at]), flat(act0[at]), flat(dpn0[at]), grads)

    planes(h.shape[0], body)
    write_halves(sc, halving_steps(sizes)[0], grads, keep, send)


def last_kernel(counts, sizes, sc, edge_w, node_in, node_out, biases, sums_in, h, slopes, keep, got, *refs):
    n = sum(counts)
    halo, (edges, grads) = refs[:n], refs[n:]
    start = 128 + NODES
    grads[pl.ds(0, start)] = jnp.zeros((start, 128), f32)
    grads[pl.ds(start, keep.shape[0])] = keep[...] + got[...]
    edge_parts(counts, sc, (edge_w,), 0, halo, slopes, edges, grads.at[pl.ds(128, NODES)])

    def body(x):
        edge_product(h, x, split_cols(flat(edges[pl.ds(x, chunk_of(h.shape[0]))])), grads, 0)

    planes(h.shape[0], body)


def state_kernel(sc, edge_w, node_in, grad_in, dpn, edges, grad_ref):
    shape = (chunk_of(edges.shape[0]),) + edges.shape[1:]
    weight = jnp.concatenate([twice(edge_w[0, 0]), node_in[0, pl.ds(0, 128)]], 1)

    def body(x):
        at = pl.ds(x, chunk_of(edges.shape[0]))
        parts = jnp.concatenate([split_cols(flat(edges[at])), flat(dpn[at])], -1)
        grad_ref[at] = (flat(grad_in[at]).astype(f32) + dot_rt(parts, weight)).astype(bf16).reshape(shape)

    planes(edges.shape[0], body)


def finish_kernel(scale, last_rows, step, sc, edge_w, node_in, value, got, *refs):
    edge_grads, in_grads, out_grads, bias_grads, both = refs
    width = edge_w.shape[-1]
    join_kernel_of(step, last_rows, sc, value, got, both)

    def rows_of(part, start, count=width):
        ref, offset = part
        return ref[pl.ds(offset + start, count)] * scale

    def bias_of(part, start):
        return jnp.sum(rows_of(part, start, NODES), 0, keepdims=True)

    end = 3 * width
    last, sum0 = (both, 0), (both, last_rows)
    sum1 = (both, last_rows + 512 + 2 * NODES)
    firsts = ((last, 0), (sum0, end + NODES))
    for layer, part in enumerate((sum0, sum1)):
        out_grads[layer] = rows_of(part, 0)
        in_grads[layer, pl.ds(0, width)] = rows_of(part, width).T
        bias_grads[layer, pl.ds(1, 1)] = bias_of(part, end)
        source, start = firsts[layer]
        edge_grads[layer, 0] = rows_of(source, start)
        bias_grads[layer, pl.ds(0, 1)] = bias_of(source, start + width)
        mixed = rows_of(part, 2 * width).T
        high = mixed.astype(bf16)
        low = (mixed - high.astype(f32)).astype(bf16)
        lower = node_in[layer, pl.ds(width, width)]
        edge_grads[layer, 1] = dot_rt(high, lower) + dot_rt(low, lower)
        w_two = edge_w[layer, 1]
        in_grads[layer, pl.ds(width, width)] = dot_t(w_two, high) + dot_t(w_two, low)


def call(kernel, name, inputs, outs, scratch=(), flops=0, aliases=None):
    total = sum(math.prod(o.shape) * o.dtype.itemsize for o in outs)
    total += sum(math.prod(i.shape) * i.dtype.itemsize for i in inputs)
    return pl.pallas_call(
        kernel,
        name=name,
        out_shape=tuple(outs),
        in_specs=[SM] + [VM] * (len(inputs) - 1),
        out_specs=tuple([VM] * len(outs)),
        scratch_shapes=list(scratch),
        input_output_aliases=aliases or {},
        compiler_params=pltpu.CompilerParams(vmem_limit_bytes=VMEM_LIMIT),
        cost_estimate=pl.CostEstimate(flops=flops, bytes_accessed=total, transcendentals=0),
    )(*inputs)


def pairs(size, kind):
    return [
        pair for low in range(kind, size - 1, 2) for pair in ((low, low + 1), (low + 1, low))
    ]


def hops(size):
    found = []
    hop = 1
    while hop < size:
        found.append(hop)
        hop *= 2
    return found


def halving_steps(sizes):
    return [(1, hop) for hop in hops(sizes[1])[:1]] + [(0, hop) for hop in hops(sizes[0])]


def whole_steps(sizes):
    return [(2, [hop]) for hop in reversed(hops(sizes[2]))] + [(1, [hop]) for hop in hops(sizes[1])[1:]]


def padded_rows(rows, sizes):
    unit = NODES << len(halving_steps(sizes))
    return -(-rows // unit) * unit


def bit_of(sc_ref, step):
    axis, hop = step
    return (sc_ref[1 + axis] // hop) % 2


def write_halves(sc_ref, step, from_ref, keep, send):
    half = keep.shape[0]
    bit = bit_of(sc_ref, step)
    keep[...] = from_ref[pl.ds(pl.multiple_of(bit * half, NODES), half)]
    send[...] = from_ref[pl.ds(pl.multiple_of((1 - bit) * half, NODES), half)]


def halve_kernel(step, sc, keep_in, got, keep, send, total):
    total[...] = keep_in[...] + got[...]
    write_halves(sc, step, total, keep, send)


def add_kernel(sc, *refs):
    total = refs[0][...] + refs[1][...]
    for ref in refs[2:-1]:
        total = total + ref[...]
    refs[-1][...] = total


def join_kernel_of(step, start, sc, value, got, out):
    half = value.shape[0] - start
    bit = bit_of(sc, step)
    if start:
        out[pl.ds(0, start)] = value[pl.ds(0, start)] + got[pl.ds(0, start)]
    out[pl.ds(pl.multiple_of(start + bit * half, NODES), half)] = value[pl.ds(start, half)]
    out[pl.ds(pl.multiple_of(start + (1 - bit) * half, NODES), half)] = got[pl.ds(start, half)]


def swap(value, step):
    axis = ("gx", "gy", "gz")[step[0]]
    return lax.ppermute(value, axis, [(i, i ^ step[1]) for i in range(lax.axis_size(axis))])


def rows_like(rows, width=128):
    return jax.ShapeDtypeStruct((rows, width), f32)


def halve(sc, sizes, keep, send):
    steps = halving_steps(sizes)
    got = swap(send, steps[0])
    for step in steps[1:]:
        keep, got = yield keep, got
        half = rows_like(keep.shape[0] // 2)
        keep, send = call(
            functools.partial(halve_kernel, step), "halve", (sc, keep, got), [half, half],
            [pltpu.VMEM(keep.shape, f32)],
        )
        got = swap(send, step)
    keep, got = yield keep, got
    return keep, got


class Background:
    def __init__(self):
        self.active = {}

    def add(self, name, steps):
        self.active[name] = [steps, None]

    def advance(self, entry, tied):
        steps, pending = entry
        try:
            entry[1] = next(steps) if pending is None else steps.send(tied)
        except StopIteration:
            entry[0] = None

    def beside(self, anchor):
        for entry in self.active.values():
            steps, pending = entry
            if steps is None:
                continue
            if pending is None:
                self.advance(entry, None)
            elif pending[1] is not None:
                anchor, tied = lax.optimization_barrier((anchor, pending))
                self.advance(entry, tied)
        return anchor

    def finish(self, name):
        entry = self.active[name]
        while entry[0] is not None:
            done = entry[1]
            if done is not None and done[1] is None:
                return done[0]
            self.advance(entry, done)
        return entry[1]


def on_device(state, cotangent, counts, edge_weights, node_in, node_out, biases):
    x_len, y_len, slots, nodes, width = state.shape
    rows = slots * nodes
    grid = (x_len, y_len, rows, width)
    axes = ("gx", "gy", "gz")
    sizes = tuple(lax.axis_size(a) for a in axes)
    trades = tuple(min(size - 1, 2) for size in sizes)
    nx, ny, nz = trades
    h0 = state.reshape(grid)
    g2 = cotangent.reshape(grid)
    sc = jnp.stack([counts[0]] + [lax.axis_index(a).astype(jnp.int32) for a in axes])

    def sds(shape, kind=f32):
        return jax.ShapeDtypeStruct(shape, kind)

    face_x = sds((y_len, rows, width))
    face_y = sds((x_len, rows, width))
    face_z = sds((x_len, y_len, width))
    face_outs = [face_y] * ny + [face_z] * nz
    full = sds(grid)
    full16 = sds(grid, bf16)
    full3 = sds((3,) + grid)
    inv = pltpu.VMEM((y_len, rows, width), f32)
    matmul = 2 * math.prod(grid) * width
    weights = (edge_weights, node_in, node_out, biases)

    in_place = {1 + len(weights): 0}

    def run(kernel, name, inputs, outs, scratch, flops, aliases):
        body = functools.partial(kernel, trades, sizes)
        return call(body, name, (sc, *weights, *inputs), outs, scratch, flops * matmul, aliases)

    def behind(value, others):
        return lax.optimization_barrier((value, others))[0]

    def trade(faces, axis):
        size = lax.axis_size(axis)
        got = [lax.ppermute(face, axis, pairs(size, kind)) for kind, face in reversed(list(enumerate(faces)))]
        return got[::-1]

    background = Background()

    pair = pltpu.VMEM((2,) + grid[1:], f32)

    def first_trade(kernel, name, inputs, scratch, flops):
        faces = call(functools.partial(kernel, trades, sizes), name, (sc, *inputs), [face_x] * nx, scratch, flops)
        return trade(faces, "gx"), faces

    def exchange(got_x, faces, work=None, held=(), early=None, early_held=()):
        fix = functools.partial(fix_y_kernel, trades)
        faces_y = call(fix, "fix_y", (sc, *got_x, *faces[:ny]), [face_y] * ny)
        if early is not None:
            faces_y, early_held = lax.optimization_barrier((faces_y, early_held))
            keep, send = early(*early_held)
        got_y = trade(faces_y, "gy")
        if early is not None:
            got_y, (keep, send) = lax.optimization_barrier((got_y, (keep, send)))
            background.add("sums", halve(sc, sizes, keep, send))
        fix = functools.partial(fix_z_kernel, trades)
        faces_z = call(fix, "fix_z", (sc, *got_x, *got_y[::-1], *faces[ny:]), [face_z] * nz)
        faces_z = background.beside(background.beside(faces_z))
        done = None
        if work is not None:
            faces_z, held = lax.optimization_barrier((faces_z, held))
            done = work(*held)
        got_z = trade(faces_z, "gz")
        got_z, done = lax.optimization_barrier((got_z, done))
        return (*got_x, *got_y, *got_z), done

    def to_slopes(half):
        return call(slope_kernel, "slopes", (sc, half), [full3], [], matmul, {1: 0})[0]

    def products(*held):
        return call(
            products_kernel, "nodes1_products", (sc, node_in, *held), [full, rows_like(3 * width + NODES)], [], 6 * matmul
        )

    got_x, faces_x = first_trade(first_face_kernel, "face0", (edge_weights, biases, h0), [], matmul // 8)
    sums, slopes0, *faces = call(
        functools.partial(first_kernel, trades, sizes), "edges0", (sc, edge_weights, biases, h0),
        [full, full3] + face_outs, [], 3 * matmul,
    )
    halo, slopes0 = exchange(got_x, faces, to_slopes, (slopes0,))
    inputs = (*weights, sums, h0, *halo)
    got_x, faces_x = first_trade(middle_face_kernel, "face1", inputs, [pair, inv], matmul // 4)
    _, scaled0, act0, slope0, h1, sums, slopes1, *faces = run(
        middle_kernel, "nodes0_edges1", (behind(sums, faces_x), h0, *halo),
        [full, full16, full16, full, full16, full, full3] + face_outs, [inv], 8, in_place,
    )
    halo, slopes1 = exchange(got_x, faces, to_slopes, (slopes1,))
    inputs = (*weights, sums, h1, g2, *halo)
    got_x, faces_x = first_trade(turn_face_kernel, "face2", inputs, [pair, inv], matmul // 4)
    _, scaled1, act1, dpn1, sums, *faces = run(
        turn_kernel, "nodes1_back", (behind(sums, faces_x), h1, g2, *halo), [full] + [full16] * 3 + [full] + face_outs,
        [inv], 7, in_place,
    )
    halo, (base, grads1) = exchange(got_x, faces, products, (h1, g2, scaled1, act1, dpn1))
    inputs = (*weights, sums, base, slopes1, slope0, *halo)
    got_x, faces_x = first_trade(join_face_kernel, "face3", inputs, [pair, inv], matmul // 4)
    edges1, grad_in, dpn0, sums, bias1, *faces = run(
        join_kernel, "edges1_back_nodes0_back", (behind(sums, faces_x), base, slopes1, slope0, *halo),
        [full, full16, full16, full, rows_like(NODES)] + face_outs, [inv], 9, in_place,
    )

    def layer_sums(*held):
        total = padded_rows(7 * width + 3 * NODES, sizes)
        return call(
            functools.partial(sums_kernel, sizes), "gradient_sums", (sc, *held), [rows_like(total // 2)] * 2,
            [pltpu.VMEM((total, width), f32)], 5 * matmul,
        )

    held = (h1, edges1, grad_in, h0, scaled0, act0, dpn0, grads1, bias1)
    halo, _ = exchange(got_x, faces, early=layer_sums, early_held=held)
    tail_rows = width + NODES
    keep, got = background.finish("sums")
    edges, value = run(
        last_kernel, "edges0_back", (sums, h0, slopes0, keep, got, *halo), [full, rows_like(tail_rows + keep.shape[0])],
        [], 6, in_place,
    )
    value, grad_in, dpn0, edges = lax.optimization_barrier((value, grad_in, dpn0, edges))
    (grad0,) = call(
        state_kernel, "state_grad", (sc, edge_weights, node_in, grad_in, dpn0, edges), [full16], [], 4 * matmul
    )
    for axis, together in whole_steps(sizes):
        partners = [sum(c) for n in range(1, len(together) + 1) for c in itertools.combinations(together, n)]
        got = [swap(value, (axis, partner)) for partner in partners]
        (value,) = call(add_kernel, "add", (sc, value, *got), [rows_like(value.shape[0])])
        value, grad0 = lax.optimization_barrier((value, grad0))
    first, *rest = halving_steps(sizes)
    for step in reversed(rest):
        out = rows_like(2 * value.shape[0] - tail_rows)
        body = functools.partial(join_kernel_of, step, tail_rows)
        (value,) = call(body, "join", (sc, value, swap(value, step)), [out])
    layers_all = 3 * slots * sizes[2] // 4
    nodes_all = x_len * sizes[0] * y_len * sizes[1] * layers_all * nodes
    scale = 1.0 / math.sqrt(nodes_all)
    edge_grads, in_grads, out_grads, bias_grads = call(
        functools.partial(finish_kernel, scale, tail_rows, first), "finish",
        (sc, edge_weights, node_in, value, swap(value, first)),
        [sds(edge_weights.shape), sds(node_in.shape), sds(node_out.shape), sds(biases.shape)],
        [pltpu.VMEM((2 * value.shape[0] - tail_rows, width), f32)],
    )
    return grad0.reshape(state.shape), edge_grads, in_grads, out_grads, bias_grads


def solution(mesh):
    return jax.shard_map(
        on_device,
        mesh=mesh,
        in_specs=(
            P("gx", "gy", "gz", None, None),
            P("gx", "gy", "gz", None, None),
            P("gz"),
            P(),
            P(),
            P(),
            P(),
        ),
        out_specs=(P("gx", "gy", "gz", None, None), P(), P(), P(), P()),
        check_vma=False,
    )
```

```python
import functools
import itertools
import math

import jax
import jax.numpy as jnp
from jax import lax
from jax.experimental import pallas as pl
from jax.experimental.pallas import tpu as pltpu
from jax.sharding import PartitionSpec as P

f32 = jnp.float32
bf16 = jnp.bfloat16
NODES = 8
VMEM_LIMIT = 12 * 1024 * 1024
VM = pl.BlockSpec(memory_space=pltpu.VMEM)
SM = pl.BlockSpec(memory_space=pltpu.SMEM)


def dot(left, right):
    return lax.dot_general(left, right, (((1,), (0,)), ((), ())), preferred_element_type=f32)


def dot_t(left, right):
    return lax.dot_general(left, right, (((0,), (0,)), ((), ())), preferred_element_type=f32)


def dot_rt(left, right):
    return lax.dot_general(left, right, (((1,), (1,)), ((), ())), preferred_element_type=f32)


def silu_half(half):
    th = jnp.tanh(half)
    prod = half * th
    return half + prod, (0.5 + 0.5 * th) * ((1.0 + half) - prod)


def split_cols(value):
    high = value.astype(bf16)
    low = (value - high.astype(f32)).astype(bf16)
    return jnp.concatenate([high, low], -1)


def up(value):
    return pltpu.roll(value, NODES - 1, 1)


def down(value):
    return pltpu.roll(value, 1, 1)


def flat(value):
    return value.reshape(-1, value.shape[-1])


def node_rows(value):
    return value.reshape(-1, NODES, value.shape[-1])


def row_ids():
    return lax.broadcasted_iota(jnp.int32, (1, NODES, 128), 1)


def couple_slots(plane, filled):
    count, rows, width = plane.shape
    slots = rows // NODES
    parts = plane.reshape(count, slots, NODES, width)
    ids = row_ids()
    done = []
    for s in range(slots):
        here = parts[:, s]
        if s + 1 < slots:
            take = (ids == NODES - 1) & (s + 1 < filled)
            here = here + jnp.where(take, up(parts[:, s + 1]), 0.0)
        if s > 0:
            here = here + jnp.where(ids == 0, down(parts[:, s - 1]), 0.0)
            here = jnp.where(s < filled, here, 0.0)
        done.append(here[:, None])
    return jnp.concatenate(done, 1).reshape(plane.shape)


def elements(x_len, y_len, body):
    ey = y_len // NODES
    total = (x_len // NODES) * ey

    def step(e, carry):
        x0 = pl.multiple_of((e // ey) * NODES, NODES)
        y0 = pl.multiple_of((e % ey) * NODES, NODES)
        body(x0, y0)
        return carry

    lax.fori_loop(0, total, step, 0)


def edge_dots(parts, weight, weight_both):
    rows, width = parts[0].shape[1:]
    if len(parts) == 2:
        return dot(flat(jnp.concatenate(parts, 0)), weight).reshape(-1, rows, width)
    both = dot(jnp.concatenate([flat(parts[0]), flat(parts[2])], -1), weight_both)
    between = dot(flat(parts[1]), weight).reshape(-1, rows, width)
    first, last = (both[:, k : k + width].reshape(-1, rows, width) for k in (0, width))
    return jnp.concatenate([first, between, last], 0)


def edges_forward(h_ref, w_one, half_bias, filled, sum_ref, half_ref):
    x_len, y_len, rows, width = h_ref.shape
    blank = jnp.zeros_like(w_one)
    w_both = jnp.concatenate([jnp.concatenate([w_one, blank], 1), jnp.concatenate([blank, w_one], 1)], 0)
    inner = row_ids() < NODES - 1

    def body(x0, y0):
        ys = pl.ds(y0, NODES)
        prev = None
        here = h_ref[x0, ys].astype(f32)
        for i in range(NODES):
            parts = []
            nxt = None
            if i < NODES - 1:
                nxt = h_ref[x0 + i + 1, ys].astype(f32)
                parts.append((nxt - here).astype(bf16))
            parts.append((here[1:] - here[:-1]).astype(bf16))
            cols = node_rows(here)
            parts.append((up(cols) - cols).reshape(here.shape).astype(bf16))
            half = edge_dots(parts, w_one, w_both) + half_bias
            act = (half + half * jnp.tanh(half)).astype(bf16).astype(f32)
            at = 0
            total = prev
            prev = None
            if i < NODES - 1:
                prev = act[:NODES]
                total = -prev if total is None else total - prev
                half_ref[0, x0 + i, ys] = half[:NODES]
                at = NODES
            along_y = act[at : at + NODES - 1]
            half_ref[1, x0 + i, pl.ds(y0, NODES - 1)] = half[at : at + NODES - 1]
            at += NODES - 1
            along_z = jnp.where(inner, node_rows(act[at:]), 0.0)
            half_ref[2, x0 + i, ys] = half[at:]
            total = total + (down(along_z) - along_z).reshape(here.shape)
            total = jnp.concatenate(
                [
                    total[:1] - along_y[:1],
                    total[1:-1] + (along_y[:-1] - along_y[1:]),
                    total[-1:] + along_y[-1:],
                ],
                0,
            )
            sum_ref[x0 + i, ys] = couple_slots(total, filled)
            here = nxt

    elements(x_len, y_len, body)


def slope_kernel(sc, half_in, slope_out):
    inner = row_ids() < NODES - 1

    def step(x, carry):
        for k in range(3):
            slope = silu_half(half_in[k, x])[1]
            if k == 2:
                slope = jnp.where(inner, node_rows(slope), 0.0).reshape(slope.shape)
            slope_out[k, x] = slope
        return carry

    lax.fori_loop(0, half_in.shape[1], step, 0)


def couple_columns(sum_ref):
    x_len, y_len = sum_ref.shape[:2]
    for cut in range(NODES, x_len, NODES):
        both = sum_ref[cut - 1] + sum_ref[cut]
        sum_ref[cut - 1] = both
        sum_ref[cut] = both
    for cut in range(NODES, y_len, NODES):
        both = sum_ref[:, cut - 1] + sum_ref[:, cut]
        sum_ref[:, cut - 1] = both
        sum_ref[:, cut] = both


def face_place(sc_ref, axis, kind, last):
    return jnp.where((sc_ref[1 + axis] + kind) % 2 == 0, last, 0)


def end_rows(values, filled, take_top):
    picked = values(0)
    slots = values.slots
    for s in range(slots):
        picked = jnp.where(take_top & (filled == s + 1), values(s * NODES + NODES - 1), picked)
    return picked


class RowReader:
    def __init__(self, slots, read):
        self.slots = slots
        self.read = read

    def __call__(self, row):
        return self.read(row)


def takes_top(sc_ref, kind):
    return (sc_ref[3] + kind) % 2 == 0


def write_faces(sc_ref, sum_ref, faces, counts):
    x_len, y_len, rows, width = sum_ref.shape
    nx, ny, nz = counts
    reader = RowReader(rows // NODES, lambda row: sum_ref[:, :, row])
    for kind in range(ny):
        faces[kind][...] = sum_ref[:, face_place(sc_ref, 1, kind, y_len - 1)]
    for kind in range(nz):
        faces[ny + kind][...] = end_rows(reader, sc_ref[0], takes_top(sc_ref, kind))


def add_halo(sc_ref, halo, into_ref, counts):
    x_len, y_len, rows, width = into_ref.shape
    nx, ny, nz = counts
    for kind in range(nx):
        into_ref[face_place(sc_ref, 0, kind, x_len - 1)] += halo[kind][...]
    for kind in range(ny):
        into_ref[:, face_place(sc_ref, 1, kind, y_len - 1)] += halo[nx + kind][...]
    if nz:
        got = [halo[nx + ny + kind][...] for kind in range(nz)]
        tops = [takes_top(sc_ref, kind) for kind in range(nz)]
        from_below = sum(jnp.where(top, 0.0, value) for top, value in zip(tops, got))
        from_above = sum(jnp.where(top, value, 0.0) for top, value in zip(tops, got))
        into_ref[:, :, 0] += from_below
        for s in range(rows // NODES):
            into_ref[:, :, s * NODES + NODES - 1] += jnp.where(sc_ref[0] == s + 1, from_above, 0.0)


def fix_y_kernel(counts, sc_ref, *refs):
    nx, ny, nz = counts
    got, faces, outs = refs[:nx], refs[nx : nx + ny], refs[nx + ny :]
    x_len = faces[0].shape[0]
    for kind in range(nx):
        place = face_place(sc_ref, 0, kind, x_len - 1)
        for k in range(ny):
            y_len = got[kind].shape[0]
            outs[k][place] += got[kind][face_place(sc_ref, 1, k, y_len - 1)]


def fix_z_kernel(counts, sc_ref, *refs):
    nx, ny, nz = counts
    got_x, refs = refs[:nx], refs[nx:]
    got_y, refs = refs[:ny][::-1], refs[ny:]
    faces, outs = refs[:nz], refs[nz:]
    x_len, y_len, width = faces[0].shape
    for k in range(nz):
        top = takes_top(sc_ref, k)
        for kind in range(nx):
            ref = got_x[kind]
            reader = RowReader(ref.shape[1] // NODES, lambda row, ref=ref: ref[:, row])
            outs[k][face_place(sc_ref, 0, kind, x_len - 1)] += end_rows(reader, sc_ref[0], top)
        for kind in range(ny):
            ref = got_y[kind]
            reader = RowReader(ref.shape[1] // NODES, lambda row, ref=ref: ref[:, row])
            add = end_rows(reader, sc_ref[0], top)
            first = face_place(sc_ref, 1, kind, 1) == 0
            outs[k][:, 0] += jnp.where(first, add, 0.0)
            outs[k][:, y_len - 1] += jnp.where(first, 0.0, add)


def write_inverse(sc_ref, inv_ref, sizes):
    y_len, rows, width = inv_ref.shape
    filled, at_y, at_z = sc_ref[0], sc_ref[2], sc_ref[3]
    ids = lax.broadcasted_iota(jnp.int32, (rows, width), 0)
    node = ids % NODES
    low = (node == 0) & ((ids >= NODES) | (at_z > 0))
    high = (node == NODES - 1) & ((ids < (filled - 1) * NODES) | (at_z < sizes[2] - 1))
    along_z = jnp.where(low | high, 0.5, 1.0).astype(f32)
    for y in range(y_len):
        inv_ref[y] = along_z * end_factor(y, y_len, at_y, sizes[1])


def end_factor(place, length, position, size):
    whole = place + position * length
    low = (place % NODES == 0) & (whole > 0)
    high = (place % NODES == NODES - 1) & (whole < length * size - 1)
    return jnp.where(low | high, 0.5, 1.0).astype(f32)


def chunk_of(x_len):
    return 2 * NODES if x_len % (2 * NODES) == 0 else NODES


def scale_planes(sc_ref, inv_ref, x, block, x_len, size_x):
    inv = inv_ref[...]
    parts = [block[c] * (inv * end_factor(x + c, x_len, sc_ref[1], size_x)) for c in range(block.shape[0])]
    return jnp.stack(parts, 0)


def node_forward(scaled, feat, weights, layer):
    edge_w, node_in, node_out, biases = weights
    pair = split_cols(scaled)
    w_two = edge_w[layer, 1]
    joined = jnp.concatenate([feat, dot(pair, jnp.concatenate([w_two, w_two], 0)).astype(bf16)], -1)
    half = jnp.bfloat16(0.5)
    act, slope = silu_half(dot(joined, node_in[layer] * half) + 0.5 * biases[layer, pl.ds(1, 1)])
    return pair[:, :128], act.astype(bf16), slope


def node_slopes(grad, slope, weights, layer):
    return (dot_rt(grad, weights[2][layer]) * slope).astype(bf16)


def node_share(sc_ref, x, inv_ref, size_x, dpn, weights, layer, sum_ref):
    shape = (chunk_of(sum_ref.shape[0]),) + sum_ref.shape[1:]
    dx = dot_rt(dpn, weights[1][layer, pl.ds(128, 128)]).reshape(shape)
    share = scale_planes(sc_ref, inv_ref, x, dx, sum_ref.shape[0], size_x)
    joined = couple_slots(share.reshape((-1,) + shape[2:]), sc_ref[0])
    sum_ref[pl.ds(x, shape[0])] = joined.reshape(shape)


def node_products(grad, feat, scaled, act, dpn, grads):
    grads[pl.ds(0, 128)] += dot_t(act, grad)
    both = dot_t(dpn, jnp.concatenate([feat, scaled], -1))
    grads[pl.ds(128, 128)] += both[:, :128]
    grads[pl.ds(256, 128)] += both[:, 128:]
    grads[pl.ds(384, NODES)] += jnp.sum(dpn.astype(f32).reshape(-1, NODES, 128), 0)


def couple_plane(plane):
    y_len = plane.shape[0]
    parts = [plane[y] for y in range(y_len)]
    for cut in range(NODES, y_len, NODES):
        both = parts[cut - 1] + parts[cut]
        parts[cut - 1] = parts[cut] = both
    return jnp.stack(parts, 0)


def along_y(plane, combine):
    return [
        combine(plane[y : y + NODES - 1], plane[y + 1 : y + NODES], y) for y in range(0, plane.shape[0], NODES)
    ]


def spread_plane(sign, edge_x, edges_y, edge_z):
    total = sign * edge_x + (down(edge_z) - edge_z).reshape(edge_x.shape)
    parts = []
    for k, edge in enumerate(edges_y):
        here = total[k * NODES : (k + 1) * NODES]
        parts += [here[:1] - edge[:1], here[1:-1] + (edge[:-1] - edge[1:]), here[-1:] + edge[-1:]]
    return jnp.concatenate(parts, 0)


def plane_forward(low, high, at_high, w_one, half_bias, filled):
    y_len, rows, width = low.shape
    here = jnp.where(at_high, high, low)
    cols = node_rows(here)
    parts = [(high - low).astype(bf16)]
    parts += along_y(here, lambda lower, upper, y: (upper - lower).astype(bf16))
    parts.append((up(cols) - cols).reshape(here.shape).astype(bf16))
    half = dot(flat(jnp.concatenate(parts, 0)), w_one).reshape(-1, rows, width) + half_bias
    act = silu_half(half)[0].astype(bf16).astype(f32)
    at = y_len
    edges_y = []
    for _ in range(y_len // NODES):
        edges_y.append(act[at : at + NODES - 1])
        at += NODES - 1
    edge_z = jnp.where(row_ids() < NODES - 1, node_rows(act[at:]), 0.0)
    total = spread_plane(jnp.where(at_high, 1.0, -1.0), act[:y_len], edges_y, edge_z)
    return couple_plane(couple_slots(total, filled))


def plane_backward(low, high, at_high, slope_x, slope_y, slope_z):
    here = jnp.where(at_high, high, low)
    cols = node_rows(here)
    edge_x = ((high - low) * slope_x).astype(bf16).astype(f32)
    edges_y = along_y(
        here, lambda lower, upper, y: ((upper - lower) * slope_y[y : y + NODES - 1]).astype(bf16).astype(f32)
    )
    edge_z = ((up(cols) - cols) * node_rows(slope_z)).astype(bf16).astype(f32)
    return spread_plane(jnp.where(at_high, 1.0, -1.0), edge_x, edges_y, edge_z)


def face_planes(sc_ref, kind, x_len):
    place = face_place(sc_ref, 0, kind, x_len - 1)
    at_high = place > 0
    return place, jnp.where(at_high, x_len - 2, 0), at_high


def halo_planes(sc_ref, from_ref, halo, kind, start, into_ref, counts):
    x_len, y_len, rows, width = from_ref.shape
    nx, ny, nz = counts
    for c in range(2):
        into_ref[c] = from_ref[start + c]
    into_ref[face_place(sc_ref, 0, kind, x_len - 1) - start] += halo[kind][...]
    for c in range(2):
        for k in range(ny):
            into_ref[c, face_place(sc_ref, 1, k, y_len - 1)] += halo[nx + k][start + c]
        for k in range(nz):
            got = halo[nx + ny + k][start + c]
            top = takes_top(sc_ref, k)
            into_ref[c, :, 0] += jnp.where(top, 0.0, got)
            for s in range(rows // NODES):
                into_ref[c, :, s * NODES + NODES - 1] += jnp.where(top & (sc_ref[0] == s + 1), got, 0.0)


def edges_backward(q_ref, slope_ref, edge_ref, bias_acc):
    x_len, y_len, rows, width = q_ref.shape

    def body(x0, y0):
        ys = pl.ds(y0, NODES)
        prev = None
        here = q_ref[x0, ys]
        bias = jnp.zeros((NODES, width), f32)
        for i in range(NODES):
            total = prev
            prev = None
            nxt = None
            if i < NODES - 1:
                nxt = q_ref[x0 + i + 1, ys]
                prev = ((nxt - here) * slope_ref[0, x0 + i, ys]).astype(bf16).astype(f32)
                total = -prev if total is None else total - prev
                bias = bias + jnp.sum(node_rows(prev), 0)
            along_y = (here[1:] - here[:-1]) * slope_ref[1, x0 + i, pl.ds(y0, NODES - 1)]
            along_y = along_y.astype(bf16).astype(f32)
            cols = node_rows(here)
            along_z = (up(cols) - cols) * node_rows(slope_ref[2, x0 + i, ys])
            along_z = along_z.astype(bf16).astype(f32)
            bias = bias + jnp.sum(node_rows(along_y), 0) + jnp.sum(along_z, 0)
            total = total + (down(along_z) - along_z).reshape(here.shape)
            total = jnp.concatenate(
                [
                    total[:1] - along_y[:1],
                    total[1:-1] + (along_y[:-1] - along_y[1:]),
                    total[-1:] + along_y[-1:],
                ],
                0,
            )
            edge_ref[x0 + i, ys] = total
            here = nxt
        bias_acc[...] += bias

    elements(x_len, y_len, body)


def planes(count, body):
    chunk = chunk_of(count)

    def step(c, carry):
        body(pl.multiple_of(c * chunk, chunk))
        return carry

    lax.fori_loop(0, count // chunk, step, 0)


def half_weights(weights, layer):
    edge_w, node_in, node_out, biases = weights
    return edge_w[layer, 0] * jnp.bfloat16(0.5), 0.5 * biases[layer, pl.ds(0, 1)]


def first_kernel(counts, sizes, sc, edge_w, biases, h, sums, slopes, *faces):
    w_one, bias = half_weights((edge_w, None, None, biases), 0)
    edges_forward(h, w_one, bias, sc[0], sums, slopes)
    couple_columns(sums)
    write_faces(sc, sums, faces, counts)


def first_face_kernel(counts, sizes, sc, edge_w, biases, h, *faces):
    w_one, bias = half_weights((edge_w, None, None, biases), 0)
    for kind, face in enumerate(faces):
        place, start, at_high = face_planes(sc, kind, h.shape[0])
        face[...] = plane_forward(
            h[start].astype(f32), h[start + 1].astype(f32), at_high, w_one, bias, sc[0]
        )


def middle_face_kernel(counts, sizes, sc, edge_w, node_in, node_out, biases, sums_in, h, *refs):
    weights = (edge_w, node_in, node_out, biases)
    n = sum(counts)
    halo, faces, (pair, inv) = refs[:n], refs[n:-2], refs[-2:]
    write_inverse(sc, inv, sizes)
    w_one, bias = half_weights(weights, 1)
    x_len = h.shape[0]
    for kind, face in enumerate(faces):
        place, start, at_high = face_planes(sc, kind, x_len)
        halo_planes(sc, sums_in, halo, kind, start, pair, counts)
        sums_at = flat(scale_planes(sc, inv, start, pair[...], x_len, sizes[0]))
        feat = flat(h[pl.ds(start, 2)])
        scaled, act, slope = node_forward(sums_at, feat, weights, 0)
        moved = (feat.astype(f32) + dot(act, node_out[0])).astype(bf16).astype(f32).reshape(pair.shape)
        face[...] = plane_forward(moved[0], moved[1], at_high, w_one, bias, sc[0])


def face_share(sc, sizes, inv, place, x_len, grad, slope, weights, layer, shape):
    dpn = node_slopes(grad, slope, weights, layer)
    dx = dot_rt(dpn, weights[1][layer, pl.ds(128, 128)]).reshape((1,) + shape)
    share = scale_planes(sc, inv, place, dx, x_len, sizes[0])
    return couple_plane(couple_slots(share[0], sc[0]))


def turn_face_kernel(counts, sizes, sc, edge_w, node_in, node_out, biases, sums_in, h, g_ref, *refs):
    weights = (edge_w, node_in, node_out, biases)
    n = sum(counts)
    halo, faces, (pair, inv) = refs[:n], refs[n:-2], refs[-2:]
    write_inverse(sc, inv, sizes)
    x_len, shape = h.shape[0], h.shape[1:]
    live = (lax.broadcasted_iota(jnp.int32, (1, h.shape[2], 128), 1) < sc[0] * NODES).astype(f32)
    for kind, face in enumerate(faces):
        place, start, at_high = face_planes(sc, kind, x_len)
        halo_planes(sc, sums_in, halo, kind, start, pair, counts)
        plane = pair[place - start][None]
        sums_at = flat(scale_planes(sc, inv, place, plane, x_len, sizes[0]))
        scaled, act, slope = node_forward(sums_at, flat(h[place]), weights, 1)
        grad = flat((g_ref[place].astype(f32) * live).astype(bf16))
        face[...] = face_share(sc, sizes, inv, place, x_len, grad, slope, weights, 1, shape)


def join_face_kernel(counts, sizes, sc, edge_w, node_in, node_out, biases, sums_in, base_in, slopes, slope0, *refs):
    weights = (edge_w, node_in, node_out, biases)
    n = sum(counts)
    halo, faces, (pair, inv) = refs[:n], refs[n:-2], refs[-2:]
    write_inverse(sc, inv, sizes)
    x_len, shape = base_in.shape[0], base_in.shape[1:]
    w_two, w_one = twice(edge_w[1, 1]), twice(edge_w[1, 0])
    for kind, face in enumerate(faces):
        place, start, at_high = face_planes(sc, kind, x_len)
        halo_planes(sc, sums_in, halo, kind, start, pair, counts)
        q = dot_rt(split_cols(flat(pair[...])), w_two).reshape(pair.shape)
        edge = plane_backward(q[0], q[1], at_high, slopes[0, start], slopes[1, place], slopes[2, place])
        grad = (flat(base_in[place]) + dot_rt(split_cols(flat(edge)), w_one)).astype(bf16)
        face[...] = face_share(sc, sizes, inv, place, x_len, grad, flat(slope0[place]), weights, 0, shape)


def twice(weight):
    return jnp.concatenate([weight, weight], 1)


def middle_kernel(counts, sizes, sc, edge_w, node_in, node_out, biases, sums_in, h, *refs):
    weights = (edge_w, node_in, node_out, biases)
    n = sum(counts)
    halo, refs = refs[:n], refs[n:]
    work, scaled_ref, act_ref, slope_ref, next_ref, sums, slopes = refs[:7]
    faces, inv = refs[7:-1], refs[-1]
    add_halo(sc, halo, work, counts)
    write_inverse(sc, inv, sizes)
    shape = (chunk_of(h.shape[0]),) + h.shape[1:]

    def body(x):
        at = pl.ds(x, chunk_of(h.shape[0]))
        sums_at = flat(scale_planes(sc, inv, x, work[at], h.shape[0], sizes[0]))
        scaled, act, slope = node_forward(sums_at, flat(h[at]), weights, 0)
        scaled_ref[at] = scaled.reshape(shape)
        act_ref[at] = act.reshape(shape)
        slope_ref[at] = slope.reshape(shape)
        moved = flat(h[at]).astype(f32) + dot(act, node_out[0])
        next_ref[at] = moved.astype(bf16).reshape(shape)

    planes(h.shape[0], body)
    w_one, bias = half_weights(weights, 1)
    edges_forward(next_ref, w_one, bias, sc[0], sums, slopes)
    couple_columns(sums)
    write_faces(sc, sums, faces, counts)


def turn_kernel(counts, sizes, sc, edge_w, node_in, node_out, biases, sums_in, h, g_ref, *refs):
    weights = (edge_w, node_in, node_out, biases)
    n = sum(counts)
    halo, refs = refs[:n], refs[n:]
    work, scaled_ref, act_ref, dpn_ref, sums = refs[:5]
    faces, inv = refs[5:-1], refs[-1]
    add_halo(sc, halo, work, counts)
    write_inverse(sc, inv, sizes)
    shape = (chunk_of(h.shape[0]),) + h.shape[1:]
    live = live_rows(sc, h)

    def body(x):
        at = pl.ds(x, chunk_of(h.shape[0]))
        sums_at = flat(scale_planes(sc, inv, x, work[at], h.shape[0], sizes[0]))
        scaled, act, slope = node_forward(sums_at, flat(h[at]), weights, 1)
        scaled_ref[at] = scaled.reshape(shape)
        act_ref[at] = act.reshape(shape)
        grad = flat((g_ref[at].astype(f32) * live).astype(bf16))
        dpn = node_slopes(grad, slope, weights, 1)
        dpn_ref[at] = dpn.reshape(shape)
        node_share(sc, x, inv, sizes[0], dpn, weights, 1, sums)

    planes(h.shape[0], body)
    couple_columns(sums)
    write_faces(sc, sums, faces, counts)


def live_rows(sc, h):
    return (lax.broadcasted_iota(jnp.int32, (1, 1, h.shape[2], 128), 2) < sc[0] * NODES).astype(f32)


def products_kernel(sc, node_in, h, g_ref, scaled, act, dpn, base, grads):
    grads[...] = jnp.zeros_like(grads)
    live = live_rows(sc, h)

    def body(x):
        at = pl.ds(x, chunk_of(h.shape[0]))
        grad = (g_ref[at].astype(f32) * live).astype(bf16)
        node_products(flat(grad), flat(h[at]), flat(scaled[at]), flat(act[at]), flat(dpn[at]), grads)
        dx = dot_rt(flat(dpn[at]), node_in[1, pl.ds(0, 128)])
        base[at] = grad.astype(f32) + dx.reshape(grad.shape)

    planes(h.shape[0], body)


def edge_parts(counts, sc, weights, layer, halo, slopes, work, bias):
    add_halo(sc, halo, work, counts)
    shape = (chunk_of(work.shape[0]),) + work.shape[1:]
    w_two = twice(weights[0][layer, 1])

    def to_q(x):
        at = pl.ds(x, chunk_of(work.shape[0]))
        work[at] = dot_rt(split_cols(flat(work[at])), w_two).reshape(shape)

    planes(work.shape[0], to_q)
    edges_backward(work, slopes, work, bias)


def edge_product(h, x, pair, grads, row):
    both = dot_t(flat(h[pl.ds(x, chunk_of(h.shape[0]))]), pair)
    grads[pl.ds(row, 128)] += both[:, :128] + both[:, 128:]


def join_kernel(counts, sizes, sc, edge_w, node_in, node_out, biases, sums_in, base_in, slopes, slope0, *refs):
    weights = (edge_w, node_in, node_out, biases)
    n = sum(counts)
    halo, refs = refs[:n], refs[n:]
    work, grad_ref, dpn_ref, sums, bias = refs[:5]
    faces, inv = refs[5:-1], refs[-1]
    write_inverse(sc, inv, sizes)
    bias[...] = jnp.zeros_like(bias)
    edge_parts(counts, sc, weights, 1, halo, slopes, work, bias)
    w_one = twice(edge_w[1, 0])
    x_len = work.shape[0]
    shape = (chunk_of(x_len),) + work.shape[1:]

    def body(x):
        at = pl.ds(x, chunk_of(x_len))
        pair = split_cols(flat(work[at]))
        grad = (flat(base_in[at]) + dot_rt(pair, w_one)).astype(bf16)
        dpn = node_slopes(grad, flat(slope0[at]), weights, 0)
        grad_ref[at] = grad.reshape(shape)
        dpn_ref[at] = dpn.reshape(shape)
        node_share(sc, x, inv, sizes[0], dpn, weights, 0, sums)

    planes(x_len, body)
    couple_columns(sums)
    write_faces(sc, sums, faces, counts)


def sums_kernel(sizes, sc, h, edges, grad, h0, scaled0, act0, dpn0, grads1, bias, keep, send, grads):
    grads[...] = jnp.zeros_like(grads)
    row = 384 + NODES
    grads[pl.ds(row + 128, NODES)] = bias[...]
    grads[pl.ds(row + 128 + NODES, grads1.shape[0])] = grads1[...]

    def body(x):
        at = pl.ds(x, chunk_of(h.shape[0]))
        edge_product(h, x, split_cols(flat(edges[at])), grads, row)
        node_products(flat(grad[at]), flat(h0[at]), flat(scaled0[at]), flat(act0[at]), flat(dpn0[at]), grads)

    planes(h.shape[0], body)
    write_halves(sc, halving_steps(sizes)[0], grads, keep, send)


def last_kernel(counts, sizes, sc, edge_w, node_in, node_out, biases, sums_in, h, slopes, *refs):
    n = sum(counts)
    halo, (edges, grads) = refs[:n], refs[n:]
    grads[...] = jnp.zeros_like(grads)
    edge_parts(counts, sc, (edge_w,), 0, halo, slopes, edges, grads.at[pl.ds(128, NODES)])

    def body(x):
        edge_product(h, x, split_cols(flat(edges[pl.ds(x, chunk_of(h.shape[0]))])), grads, 0)

    planes(h.shape[0], body)


def state_kernel(sc, edge_w, node_in, grad_in, dpn, edges, grad_ref):
    shape = (chunk_of(edges.shape[0]),) + edges.shape[1:]
    weight = jnp.concatenate([twice(edge_w[0, 0]), node_in[0, pl.ds(0, 128)]], 1)

    def body(x):
        at = pl.ds(x, chunk_of(edges.shape[0]))
        parts = jnp.concatenate([split_cols(flat(edges[at])), flat(dpn[at])], -1)
        grad_ref[at] = (flat(grad_in[at]).astype(f32) + dot_rt(parts, weight)).astype(bf16).reshape(shape)

    planes(edges.shape[0], body)


def finish_kernel(scale, last_rows, step, sc, edge_w, node_in, value, got, *refs):
    edge_grads, in_grads, out_grads, bias_grads, both = refs
    width = edge_w.shape[-1]
    join_kernel_of(step, last_rows, sc, value, got, both)

    def rows_of(part, start, count=width):
        ref, offset = part
        return ref[pl.ds(offset + start, count)] * scale

    def bias_of(part, start):
        return jnp.sum(rows_of(part, start, NODES), 0, keepdims=True)

    end = 3 * width
    last, sum0 = (both, 0), (both, last_rows)
    sum1 = (both, last_rows + 512 + 2 * NODES)
    firsts = ((last, 0), (sum0, end + NODES))
    for layer, part in enumerate((sum0, sum1)):
        out_grads[layer] = rows_of(part, 0)
        in_grads[layer, pl.ds(0, width)] = rows_of(part, width).T
        bias_grads[layer, pl.ds(1, 1)] = bias_of(part, end)
        source, start = firsts[layer]
        edge_grads[layer, 0] = rows_of(source, start)
        bias_grads[layer, pl.ds(0, 1)] = bias_of(source, start + width)
        mixed = rows_of(part, 2 * width).T
        high = mixed.astype(bf16)
        low = (mixed - high.astype(f32)).astype(bf16)
        lower = node_in[layer, pl.ds(width, width)]
        edge_grads[layer, 1] = dot_rt(high, lower) + dot_rt(low, lower)
        w_two = edge_w[layer, 1]
        in_grads[layer, pl.ds(width, width)] = dot_t(w_two, high) + dot_t(w_two, low)


def call(kernel, name, inputs, outs, scratch=(), flops=0, aliases=None):
    total = sum(math.prod(o.shape) * o.dtype.itemsize for o in outs)
    total += sum(math.prod(i.shape) * i.dtype.itemsize for i in inputs)
    return pl.pallas_call(
        kernel,
        name=name,
        out_shape=tuple(outs),
        in_specs=[SM] + [VM] * (len(inputs) - 1),
        out_specs=tuple([VM] * len(outs)),
        scratch_shapes=list(scratch),
        input_output_aliases=aliases or {},
        compiler_params=pltpu.CompilerParams(vmem_limit_bytes=VMEM_LIMIT),
        cost_estimate=pl.CostEstimate(flops=flops, bytes_accessed=total, transcendentals=0),
    )(*inputs)


def pairs(size, kind):
    return [
        pair for low in range(kind, size - 1, 2) for pair in ((low, low + 1), (low + 1, low))
    ]


def hops(size):
    found = []
    hop = 1
    while hop < size:
        found.append(hop)
        hop *= 2
    return found


def halving_steps(sizes):
    return [(1, hop) for hop in hops(sizes[1])[:1]] + [(0, hop) for hop in hops(sizes[0])]


def whole_steps(sizes):
    along_z = hops(sizes[2])
    steps = [(2, along_z[k : k + 2]) for k in range(0, len(along_z), 2)]
    return steps + [(1, [hop]) for hop in hops(sizes[1])[1:]]


def padded_rows(rows, sizes):
    unit = NODES << len(halving_steps(sizes))
    return -(-rows // unit) * unit


def bit_of(sc_ref, step):
    axis, hop = step
    return (sc_ref[1 + axis] // hop) % 2


def write_halves(sc_ref, step, from_ref, keep, send):
    half = keep.shape[0]
    bit = bit_of(sc_ref, step)
    keep[...] = from_ref[pl.ds(pl.multiple_of(bit * half, NODES), half)]
    send[...] = from_ref[pl.ds(pl.multiple_of((1 - bit) * half, NODES), half)]


def halve_kernel(step, sc, keep_in, got, keep, send, total):
    total[...] = keep_in[...] + got[...]
    write_halves(sc, step, total, keep, send)


def add_kernel(sc, *refs):
    total = refs[0][...] + refs[1][...]
    for ref in refs[2:-1]:
        total = total + ref[...]
    refs[-1][...] = total


def join_kernel_of(step, start, sc, value, got, out):
    half = value.shape[0] - start
    bit = bit_of(sc, step)
    if start:
        out[pl.ds(0, start)] = value[pl.ds(0, start)] + got[pl.ds(0, start)]
    out[pl.ds(pl.multiple_of(start + bit * half, NODES), half)] = value[pl.ds(start, half)]
    out[pl.ds(pl.multiple_of(start + (1 - bit) * half, NODES), half)] = got[pl.ds(start, half)]


def stack_kernel(sc, first, left, right, out):
    rows = first.shape[0]
    out[pl.ds(0, rows)] = first[...]
    out[pl.ds(rows, left.shape[0])] = left[...] + right[...]


def swap(value, step):
    axis = ("gx", "gy", "gz")[step[0]]
    return lax.ppermute(value, axis, [(i, i ^ step[1]) for i in range(lax.axis_size(axis))])


def rows_like(rows, width=128):
    return jax.ShapeDtypeStruct((rows, width), f32)


def halve(sc, sizes, keep, send):
    steps = halving_steps(sizes)
    got = swap(send, steps[0])
    for step in steps[1:]:
        keep, got = yield keep, got
        half = rows_like(keep.shape[0] // 2)
        keep, send = call(
            functools.partial(halve_kernel, step), "halve", (sc, keep, got), [half, half],
            [pltpu.VMEM(keep.shape, f32)],
        )
        got = swap(send, step)
    keep, got = yield keep, got
    return keep, got


class Background:
    def __init__(self):
        self.active = {}

    def add(self, name, steps):
        self.active[name] = [steps, None]

    def advance(self, entry, tied):
        steps, pending = entry
        try:
            entry[1] = next(steps) if pending is None else steps.send(tied)
        except StopIteration:
            entry[0] = None

    def beside(self, anchor):
        for entry in self.active.values():
            steps, pending = entry
            if steps is None:
                continue
            if pending is None:
                self.advance(entry, None)
            elif pending[1] is not None:
                anchor, tied = lax.optimization_barrier((anchor, pending))
                self.advance(entry, tied)
        return anchor

    def finish(self, name):
        entry = self.active[name]
        while entry[0] is not None:
            done = entry[1]
            if done is not None and done[1] is None:
                return done[0]
            self.advance(entry, done)
        return entry[1]


def on_device(state, cotangent, counts, edge_weights, node_in, node_out, biases):
    x_len, y_len, slots, nodes, width = state.shape
    rows = slots * nodes
    grid = (x_len, y_len, rows, width)
    axes = ("gx", "gy", "gz")
    sizes = tuple(lax.axis_size(a) for a in axes)
    trades = tuple(min(size - 1, 2) for size in sizes)
    nx, ny, nz = trades
    h0 = state.reshape(grid)
    g2 = cotangent.reshape(grid)
    sc = jnp.stack([counts[0]] + [lax.axis_index(a).astype(jnp.int32) for a in axes])

    def sds(shape, kind=f32):
        return jax.ShapeDtypeStruct(shape, kind)

    face_x = sds((y_len, rows, width))
    face_y = sds((x_len, rows, width))
    face_z = sds((x_len, y_len, width))
    face_outs = [face_y] * ny + [face_z] * nz
    full = sds(grid)
    full16 = sds(grid, bf16)
    full3 = sds((3,) + grid)
    inv = pltpu.VMEM((y_len, rows, width), f32)
    matmul = 2 * math.prod(grid) * width
    weights = (edge_weights, node_in, node_out, biases)

    in_place = {1 + len(weights): 0}

    def run(kernel, name, inputs, outs, scratch, flops, aliases):
        body = functools.partial(kernel, trades, sizes)
        return call(body, name, (sc, *weights, *inputs), outs, scratch, flops * matmul, aliases)

    def behind(value, others):
        return lax.optimization_barrier((value, others))[0]

    def trade(faces, axis):
        size = lax.axis_size(axis)
        got = [lax.ppermute(face, axis, pairs(size, kind)) for kind, face in reversed(list(enumerate(faces)))]
        return got[::-1]

    background = Background()

    pair = pltpu.VMEM((2,) + grid[1:], f32)

    def first_trade(kernel, name, inputs, scratch, flops):
        faces = call(functools.partial(kernel, trades, sizes), name, (sc, *inputs), [face_x] * nx, scratch, flops)
        return trade(faces, "gx"), faces

    def exchange(got_x, faces, work=None, held=(), early=None, early_held=()):
        fix = functools.partial(fix_y_kernel, trades)
        same = {1 + nx + k: k for k in range(ny)}
        faces_y = call(fix, "fix_y", (sc, *got_x, *faces[:ny]), [face_y] * ny, aliases=same)
        if early is not None:
            faces_y, early_held = lax.optimization_barrier((faces_y, early_held))
            keep, send = early(*early_held)
        got_y = trade(faces_y, "gy")
        if early is not None:
            got_y, (keep, send) = lax.optimization_barrier((got_y, (keep, send)))
            background.add("sums", halve(sc, sizes, keep, send))
            background.beside(got_y)
        fix = functools.partial(fix_z_kernel, trades)
        same = {1 + nx + ny + k: k for k in range(nz)}
        faces_z = call(fix, "fix_z", (sc, *got_x, *got_y[::-1], *faces[ny:]), [face_z] * nz, aliases=same)
        background.beside(faces_z)
        done = None
        if work is not None:
            faces_z, held = lax.optimization_barrier((faces_z, held))
            done = work(*held)
        got_z = trade(faces_z, "gz")
        got_z, done = lax.optimization_barrier((got_z, done))
        return (*got_x, *got_y, *got_z), done

    def to_slopes(half):
        return call(slope_kernel, "slopes", (sc, half), [full3], [], matmul, {1: 0})[0]

    def products(*held):
        return call(
            products_kernel, "nodes1_products", (sc, node_in, *held), [full, rows_like(3 * width + NODES)], [], 6 * matmul
        )

    got_x, faces_x = first_trade(first_face_kernel, "face0", (edge_weights, biases, h0), [], matmul // 8)
    sums, slopes0, *faces = call(
        functools.partial(first_kernel, trades, sizes), "edges0", (sc, edge_weights, biases, h0),
        [full, full3] + face_outs, [], 3 * matmul,
    )
    halo, slopes0 = exchange(got_x, faces, to_slopes, (slopes0,))
    inputs = (*weights, sums, h0, *halo)
    got_x, faces_x = first_trade(middle_face_kernel, "face1", inputs, [pair, inv], matmul // 4)
    _, scaled0, act0, slope0, h1, sums, slopes1, *faces = run(
        middle_kernel, "nodes0_edges1", (behind(sums, faces_x), h0, *halo),
        [full, full16, full16, full, full16, full, full3] + face_outs, [inv], 8, in_place,
    )
    halo, slopes1 = exchange(got_x, faces, to_slopes, (slopes1,))
    inputs = (*weights, sums, h1, g2, *halo)
    got_x, faces_x = first_trade(turn_face_kernel, "face2", inputs, [pair, inv], matmul // 4)
    _, scaled1, act1, dpn1, sums, *faces = run(
        turn_kernel, "nodes1_back", (behind(sums, faces_x), h1, g2, *halo), [full] + [full16] * 3 + [full] + face_outs,
        [inv], 7, in_place,
    )
    halo, (base, grads1) = exchange(got_x, faces, products, (h1, g2, scaled1, act1, dpn1))
    inputs = (*weights, sums, base, slopes1, slope0, *halo)
    got_x, faces_x = first_trade(join_face_kernel, "face3", inputs, [pair, inv], matmul // 4)
    edges1, grad_in, dpn0, sums, bias1, *faces = run(
        join_kernel, "edges1_back_nodes0_back", (behind(sums, faces_x), base, slopes1, slope0, *halo),
        [full, full16, full16, full, rows_like(NODES)] + face_outs, [inv], 9, in_place,
    )

    def layer_sums(*held):
        total = padded_rows(7 * width + 3 * NODES, sizes)
        return call(
            functools.partial(sums_kernel, sizes), "gradient_sums", (sc, *held), [rows_like(total // 2)] * 2,
            [pltpu.VMEM((total, width), f32)], 5 * matmul,
        )

    held = (h1, edges1, grad_in, h0, scaled0, act0, dpn0, grads1, bias1)
    halo, _ = exchange(got_x, faces, early=layer_sums, early_held=held)
    tail_rows = width + NODES
    edges, last = run(
        last_kernel, "edges0_back", (sums, h0, slopes0, *halo), [full, rows_like(tail_rows)], [], 6, in_place
    )
    keep, got = background.finish("sums")
    (value,) = call(stack_kernel, "stack", (sc, last, keep, got), [rows_like(tail_rows + keep.shape[0])])
    value, grad_in, dpn0, edges = lax.optimization_barrier((value, grad_in, dpn0, edges))
    (grad0,) = call(
        state_kernel, "state_grad", (sc, edge_weights, node_in, grad_in, dpn0, edges), [full16], [], 4 * matmul
    )
    for axis, together in whole_steps(sizes):
        partners = [sum(c) for n in range(1, len(together) + 1) for c in itertools.combinations(together, n)]
        got = [swap(value, (axis, partner)) for partner in partners]
        (value,) = call(add_kernel, "add", (sc, value, *got), [rows_like(value.shape[0])])
        value, grad0 = lax.optimization_barrier((value, grad0))
    first, *rest = halving_steps(sizes)
    for step in reversed(rest):
        out = rows_like(2 * value.shape[0] - tail_rows)
        body = functools.partial(join_kernel_of, step, tail_rows)
        (value,) = call(body, "join", (sc, value, swap(value, step)), [out])
    layers_all = 3 * slots * sizes[2] // 4
    nodes_all = x_len * sizes[0] * y_len * sizes[1] * layers_all * nodes
    scale = 1.0 / math.sqrt(nodes_all)
    edge_grads, in_grads, out_grads, bias_grads = call(
        functools.partial(finish_kernel, scale, tail_rows, first), "finish",
        (sc, edge_weights, node_in, value, swap(value, first)),
        [sds(edge_weights.shape), sds(node_in.shape), sds(node_out.shape), sds(biases.shape)],
        [pltpu.VMEM((2 * value.shape[0] - tail_rows, width), f32)],
    )
    return grad0.reshape(state.shape), edge_grads, in_grads, out_grads, bias_grads


def solution(mesh):
    return jax.shard_map(
        on_device,
        mesh=mesh,
        in_specs=(
            P("gx", "gy", "gz", None, None),
            P("gx", "gy", "gz", None, None),
            P("gz"),
            P(),
            P(),
            P(),
            P(),
        ),
        out_specs=(P("gx", "gy", "gz", None, None), P(), P(), P(), P()),
        check_vma=False,
    )
```

```python
import functools
import math

import jax
import jax.numpy as jnp
from jax import lax
from jax.experimental import pallas as pl
from jax.experimental.pallas import tpu as pltpu
from jax.sharding import PartitionSpec as P

f32 = jnp.float32
bf16 = jnp.bfloat16
NODES = 8
VMEM_LIMIT = 12 * 1024 * 1024
VM = pl.BlockSpec(memory_space=pltpu.VMEM)
SM = pl.BlockSpec(memory_space=pltpu.SMEM)


def dot(left, right):
    return lax.dot_general(left, right, (((1,), (0,)), ((), ())), preferred_element_type=f32)


def dot_t(left, right):
    return lax.dot_general(left, right, (((0,), (0,)), ((), ())), preferred_element_type=f32)


def dot_rt(left, right):
    return lax.dot_general(left, right, (((1,), (1,)), ((), ())), preferred_element_type=f32)


def silu_half(half):
    th = jnp.tanh(half)
    prod = half * th
    return half + prod, (0.5 + 0.5 * th) * ((1.0 + half) - prod)


def split_cols(value):
    high = value.astype(bf16)
    low = (value - high.astype(f32)).astype(bf16)
    return jnp.concatenate([high, low], -1)


def up(value):
    return pltpu.roll(value, NODES - 1, 1)


def down(value):
    return pltpu.roll(value, 1, 1)


def flat(value):
    return value.reshape(-1, value.shape[-1])


def node_rows(value):
    return value.reshape(-1, NODES, value.shape[-1])


def row_ids():
    return lax.broadcasted_iota(jnp.int32, (1, NODES, 128), 1)


def couple_slots(plane, filled):
    count, rows, width = plane.shape
    slots = rows // NODES
    parts = plane.reshape(count, slots, NODES, width)
    ids = row_ids()
    done = []
    for s in range(slots):
        here = parts[:, s]
        if s + 1 < slots:
            take = (ids == NODES - 1) & (s + 1 < filled)
            here = here + jnp.where(take, up(parts[:, s + 1]), 0.0)
        if s > 0:
            here = here + jnp.where(ids == 0, down(parts[:, s - 1]), 0.0)
            here = jnp.where(s < filled, here, 0.0)
        done.append(here[:, None])
    return jnp.concatenate(done, 1).reshape(plane.shape)


def elements(x_len, y_len, body):
    ey = y_len // NODES
    total = (x_len // NODES) * ey

    def step(e, carry):
        x0 = pl.multiple_of((e // ey) * NODES, NODES)
        y0 = pl.multiple_of((e % ey) * NODES, NODES)
        body(x0, y0)
        return carry

    lax.fori_loop(0, total, step, 0)


def edge_dots(parts, weight, weight_both):
    rows, width = parts[0].shape[1:]
    if len(parts) == 2:
        return dot(flat(jnp.concatenate(parts, 0)), weight).reshape(-1, rows, width)
    both = dot(jnp.concatenate([flat(parts[0]), flat(parts[2])], -1), weight_both)
    between = dot(flat(parts[1]), weight).reshape(-1, rows, width)
    first, last = (both[:, k : k + width].reshape(-1, rows, width) for k in (0, width))
    return jnp.concatenate([first, between, last], 0)


def edges_forward(h_ref, w_one, half_bias, filled, sum_ref, half_ref):
    x_len, y_len, rows, width = h_ref.shape
    blank = jnp.zeros_like(w_one)
    w_both = jnp.concatenate([jnp.concatenate([w_one, blank], 1), jnp.concatenate([blank, w_one], 1)], 0)
    inner = row_ids() < NODES - 1

    def body(x0, y0):
        ys = pl.ds(y0, NODES)
        prev = None
        here = h_ref[x0, ys].astype(f32)
        for i in range(NODES):
            parts = []
            nxt = None
            if i < NODES - 1:
                nxt = h_ref[x0 + i + 1, ys].astype(f32)
                parts.append((nxt - here).astype(bf16))
            parts.append((here[1:] - here[:-1]).astype(bf16))
            cols = node_rows(here)
            parts.append((up(cols) - cols).reshape(here.shape).astype(bf16))
            half = edge_dots(parts, w_one, w_both) + half_bias
            act = (half + half * jnp.tanh(half)).astype(bf16).astype(f32)
            at = 0
            total = prev
            prev = None
            if i < NODES - 1:
                prev = act[:NODES]
                total = -prev if total is None else total - prev
                half_ref[0, x0 + i, ys] = half[:NODES]
                at = NODES
            along_y = act[at : at + NODES - 1]
            half_ref[1, x0 + i, pl.ds(y0, NODES - 1)] = half[at : at + NODES - 1]
            at += NODES - 1
            along_z = jnp.where(inner, node_rows(act[at:]), 0.0)
            half_ref[2, x0 + i, ys] = half[at:]
            total = total + (down(along_z) - along_z).reshape(here.shape)
            total = jnp.concatenate(
                [
                    total[:1] - along_y[:1],
                    total[1:-1] + (along_y[:-1] - along_y[1:]),
                    total[-1:] + along_y[-1:],
                ],
                0,
            )
            sum_ref[x0 + i, ys] = couple_slots(total, filled)
            here = nxt

    elements(x_len, y_len, body)


def slope_kernel(sc, half_in, slope_out):
    inner = row_ids() < NODES - 1

    def step(x, carry):
        for k in range(3):
            slope = silu_half(half_in[k, x])[1]
            if k == 2:
                slope = jnp.where(inner, node_rows(slope), 0.0).reshape(slope.shape)
            slope_out[k, x] = slope
        return carry

    lax.fori_loop(0, half_in.shape[1], step, 0)


def couple_columns(sum_ref):
    x_len, y_len = sum_ref.shape[:2]
    for cut in range(NODES, x_len, NODES):
        both = sum_ref[cut - 1] + sum_ref[cut]
        sum_ref[cut - 1] = both
        sum_ref[cut] = both
    for cut in range(NODES, y_len, NODES):
        both = sum_ref[:, cut - 1] + sum_ref[:, cut]
        sum_ref[:, cut - 1] = both
        sum_ref[:, cut] = both


def face_place(sc_ref, axis, kind, last):
    return jnp.where((sc_ref[1 + axis] + kind) % 2 == 0, last, 0)


def end_rows(values, filled, take_top):
    picked = values(0)
    slots = values.slots
    for s in range(slots):
        picked = jnp.where(take_top & (filled == s + 1), values(s * NODES + NODES - 1), picked)
    return picked


class RowReader:
    def __init__(self, slots, read):
        self.slots = slots
        self.read = read

    def __call__(self, row):
        return self.read(row)


def takes_top(sc_ref, kind):
    return (sc_ref[3] + kind) % 2 == 0


def write_faces(sc_ref, sum_ref, faces, counts):
    x_len, y_len, rows, width = sum_ref.shape
    nx, ny, nz = counts
    reader = RowReader(rows // NODES, lambda row: sum_ref[:, :, row])
    for kind in range(ny):
        faces[kind][...] = sum_ref[:, face_place(sc_ref, 1, kind, y_len - 1)]
    for kind in range(nz):
        faces[ny + kind][...] = end_rows(reader, sc_ref[0], takes_top(sc_ref, kind))


def add_halo(sc_ref, halo, into_ref, counts):
    x_len, y_len, rows, width = into_ref.shape
    nx, ny, nz = counts
    for kind in range(nx):
        into_ref[face_place(sc_ref, 0, kind, x_len - 1)] += halo[kind][...]
    for kind in range(ny):
        into_ref[:, face_place(sc_ref, 1, kind, y_len - 1)] += halo[nx + kind][...]
    if nz:
        got = [halo[nx + ny + kind][...] for kind in range(nz)]
        tops = [takes_top(sc_ref, kind) for kind in range(nz)]
        from_below = sum(jnp.where(top, 0.0, value) for top, value in zip(tops, got))
        from_above = sum(jnp.where(top, value, 0.0) for top, value in zip(tops, got))
        into_ref[:, :, 0] += from_below
        for s in range(rows // NODES):
            into_ref[:, :, s * NODES + NODES - 1] += jnp.where(sc_ref[0] == s + 1, from_above, 0.0)


def fix_y_kernel(counts, sc_ref, *refs):
    nx, ny, nz = counts
    got, faces, outs = refs[:nx], refs[nx : nx + ny], refs[nx + ny :]
    x_len = faces[0].shape[0]
    for kind in range(nx):
        place = face_place(sc_ref, 0, kind, x_len - 1)
        for k in range(ny):
            y_len = got[kind].shape[0]
            outs[k][place] += got[kind][face_place(sc_ref, 1, k, y_len - 1)]


def fix_z_kernel(counts, sc_ref, *refs):
    nx, ny, nz = counts
    got_x, refs = refs[:nx], refs[nx:]
    got_y, refs = refs[:ny][::-1], refs[ny:]
    faces, outs = refs[:nz], refs[nz:]
    x_len, y_len, width = faces[0].shape
    for k in range(nz):
        top = takes_top(sc_ref, k)
        for kind in range(nx):
            ref = got_x[kind]
            reader = RowReader(ref.shape[1] // NODES, lambda row, ref=ref: ref[:, row])
            outs[k][face_place(sc_ref, 0, kind, x_len - 1)] += end_rows(reader, sc_ref[0], top)
        for kind in range(ny):
            ref = got_y[kind]
            reader = RowReader(ref.shape[1] // NODES, lambda row, ref=ref: ref[:, row])
            add = end_rows(reader, sc_ref[0], top)
            first = face_place(sc_ref, 1, kind, 1) == 0
            outs[k][:, 0] += jnp.where(first, add, 0.0)
            outs[k][:, y_len - 1] += jnp.where(first, 0.0, add)


def write_inverse(sc_ref, inv_ref, sizes):
    y_len, rows, width = inv_ref.shape
    filled, at_y, at_z = sc_ref[0], sc_ref[2], sc_ref[3]
    ids = lax.broadcasted_iota(jnp.int32, (rows, width), 0)
    node = ids % NODES
    low = (node == 0) & ((ids >= NODES) | (at_z > 0))
    high = (node == NODES - 1) & ((ids < (filled - 1) * NODES) | (at_z < sizes[2] - 1))
    along_z = jnp.where(low | high, 0.5, 1.0).astype(f32)
    for y in range(y_len):
        inv_ref[y] = along_z * end_factor(y, y_len, at_y, sizes[1])


def end_factor(place, length, position, size):
    whole = place + position * length
    low = (place % NODES == 0) & (whole > 0)
    high = (place % NODES == NODES - 1) & (whole < length * size - 1)
    return jnp.where(low | high, 0.5, 1.0).astype(f32)


def chunk_of(x_len):
    return 2 * NODES if x_len % (2 * NODES) == 0 else NODES


def scale_planes(sc_ref, inv_ref, x, block, x_len, size_x):
    inv = inv_ref[...]
    parts = [block[c] * (inv * end_factor(x + c, x_len, sc_ref[1], size_x)) for c in range(block.shape[0])]
    return jnp.stack(parts, 0)


def node_forward(scaled, feat, weights, layer):
    edge_w, node_in, node_out, biases = weights
    pair = split_cols(scaled)
    w_two = edge_w[layer, 1]
    joined = jnp.concatenate([feat, dot(pair, jnp.concatenate([w_two, w_two], 0)).astype(bf16)], -1)
    half = jnp.bfloat16(0.5)
    act, slope = silu_half(dot(joined, node_in[layer] * half) + 0.5 * biases[layer, pl.ds(1, 1)])
    return pair[:, :128], act.astype(bf16), slope


def node_slopes(grad, slope, weights, layer):
    return (dot_rt(grad, weights[2][layer]) * slope).astype(bf16)


def node_share(sc_ref, x, inv_ref, size_x, dpn, weights, layer, sum_ref):
    shape = (chunk_of(sum_ref.shape[0]),) + sum_ref.shape[1:]
    dx = dot_rt(dpn, weights[1][layer, pl.ds(128, 128)]).reshape(shape)
    share = scale_planes(sc_ref, inv_ref, x, dx, sum_ref.shape[0], size_x)
    joined = couple_slots(share.reshape((-1,) + shape[2:]), sc_ref[0])
    sum_ref[pl.ds(x, shape[0])] = joined.reshape(shape)


def node_products(grad, feat, scaled, act, dpn, grads):
    grads[pl.ds(0, 128)] += dot_t(act, grad)
    both = dot_t(dpn, jnp.concatenate([feat, scaled], -1))
    grads[pl.ds(128, 128)] += both[:, :128]
    grads[pl.ds(256, 128)] += both[:, 128:]
    grads[pl.ds(384, NODES)] += jnp.sum(dpn.astype(f32).reshape(-1, NODES, 128), 0)


def couple_plane(plane):
    y_len = plane.shape[0]
    parts = [plane[y] for y in range(y_len)]
    for cut in range(NODES, y_len, NODES):
        both = parts[cut - 1] + parts[cut]
        parts[cut - 1] = parts[cut] = both
    return jnp.stack(parts, 0)


def along_y(plane, combine):
    return [
        combine(plane[y : y + NODES - 1], plane[y + 1 : y + NODES], y) for y in range(0, plane.shape[0], NODES)
    ]


def spread_plane(sign, edge_x, edges_y, edge_z):
    total = sign * edge_x + (down(edge_z) - edge_z).reshape(edge_x.shape)
    parts = []
    for k, edge in enumerate(edges_y):
        here = total[k * NODES : (k + 1) * NODES]
        parts += [here[:1] - edge[:1], here[1:-1] + (edge[:-1] - edge[1:]), here[-1:] + edge[-1:]]
    return jnp.concatenate(parts, 0)


def plane_forward(low, high, at_high, w_one, half_bias, filled):
    y_len, rows, width = low.shape
    here = jnp.where(at_high, high, low)
    cols = node_rows(here)
    parts = [(high - low).astype(bf16)]
    parts += along_y(here, lambda lower, upper, y: (upper - lower).astype(bf16))
    parts.append((up(cols) - cols).reshape(here.shape).astype(bf16))
    half = dot(flat(jnp.concatenate(parts, 0)), w_one).reshape(-1, rows, width) + half_bias
    act = silu_half(half)[0].astype(bf16).astype(f32)
    at = y_len
    edges_y = []
    for _ in range(y_len // NODES):
        edges_y.append(act[at : at + NODES - 1])
        at += NODES - 1
    edge_z = jnp.where(row_ids() < NODES - 1, node_rows(act[at:]), 0.0)
    total = spread_plane(jnp.where(at_high, 1.0, -1.0), act[:y_len], edges_y, edge_z)
    return couple_plane(couple_slots(total, filled))


def plane_backward(low, high, at_high, slope_x, slope_y, slope_z):
    here = jnp.where(at_high, high, low)
    cols = node_rows(here)
    edge_x = ((high - low) * slope_x).astype(bf16).astype(f32)
    edges_y = along_y(
        here, lambda lower, upper, y: ((upper - lower) * slope_y[y : y + NODES - 1]).astype(bf16).astype(f32)
    )
    edge_z = ((up(cols) - cols) * node_rows(slope_z)).astype(bf16).astype(f32)
    return spread_plane(jnp.where(at_high, 1.0, -1.0), edge_x, edges_y, edge_z)


def face_planes(sc_ref, kind, x_len):
    place = face_place(sc_ref, 0, kind, x_len - 1)
    at_high = place > 0
    return place, jnp.where(at_high, x_len - 2, 0), at_high


def halo_planes(sc_ref, from_ref, halo, kind, start, into_ref, counts):
    x_len, y_len, rows, width = from_ref.shape
    nx, ny, nz = counts
    for c in range(2):
        into_ref[c] = from_ref[start + c]
    into_ref[face_place(sc_ref, 0, kind, x_len - 1) - start] += halo[kind][...]
    for c in range(2):
        for k in range(ny):
            into_ref[c, face_place(sc_ref, 1, k, y_len - 1)] += halo[nx + k][start + c]
        for k in range(nz):
            got = halo[nx + ny + k][start + c]
            top = takes_top(sc_ref, k)
            into_ref[c, :, 0] += jnp.where(top, 0.0, got)
            for s in range(rows // NODES):
                into_ref[c, :, s * NODES + NODES - 1] += jnp.where(top & (sc_ref[0] == s + 1), got, 0.0)


def edges_backward(q_ref, slope_ref, edge_ref, bias_acc):
    x_len, y_len, rows, width = q_ref.shape

    def body(x0, y0):
        ys = pl.ds(y0, NODES)
        prev = None
        here = q_ref[x0, ys]
        bias = jnp.zeros((NODES, width), f32)
        for i in range(NODES):
            total = prev
            prev = None
            nxt = None
            if i < NODES - 1:
                nxt = q_ref[x0 + i + 1, ys]
                prev = ((nxt - here) * slope_ref[0, x0 + i, ys]).astype(bf16).astype(f32)
                total = -prev if total is None else total - prev
                bias = bias + jnp.sum(node_rows(prev), 0)
            along_y = (here[1:] - here[:-1]) * slope_ref[1, x0 + i, pl.ds(y0, NODES - 1)]
            along_y = along_y.astype(bf16).astype(f32)
            cols = node_rows(here)
            along_z = (up(cols) - cols) * node_rows(slope_ref[2, x0 + i, ys])
            along_z = along_z.astype(bf16).astype(f32)
            bias = bias + jnp.sum(node_rows(along_y), 0) + jnp.sum(along_z, 0)
            total = total + (down(along_z) - along_z).reshape(here.shape)
            total = jnp.concatenate(
                [
                    total[:1] - along_y[:1],
                    total[1:-1] + (along_y[:-1] - along_y[1:]),
                    total[-1:] + along_y[-1:],
                ],
                0,
            )
            edge_ref[x0 + i, ys] = total
            here = nxt
        bias_acc[...] += bias

    elements(x_len, y_len, body)


def planes(count, body):
    chunk = chunk_of(count)

    def step(c, carry):
        body(pl.multiple_of(c * chunk, chunk))
        return carry

    lax.fori_loop(0, count // chunk, step, 0)


def half_weights(weights, layer):
    edge_w, node_in, node_out, biases = weights
    return edge_w[layer, 0] * jnp.bfloat16(0.5), 0.5 * biases[layer, pl.ds(0, 1)]


def first_kernel(counts, sizes, sc, edge_w, biases, h, sums, slopes, *faces):
    w_one, bias = half_weights((edge_w, None, None, biases), 0)
    edges_forward(h, w_one, bias, sc[0], sums, slopes)
    couple_columns(sums)
    write_faces(sc, sums, faces, counts)


def first_face_kernel(counts, sizes, sc, edge_w, biases, h, *faces):
    w_one, bias = half_weights((edge_w, None, None, biases), 0)
    for kind, face in enumerate(faces):
        place, start, at_high = face_planes(sc, kind, h.shape[0])
        face[...] = plane_forward(
            h[start].astype(f32), h[start + 1].astype(f32), at_high, w_one, bias, sc[0]
        )


def middle_face_kernel(counts, sizes, sc, edge_w, node_in, node_out, biases, sums_in, h, *refs):
    weights = (edge_w, node_in, node_out, biases)
    n = sum(counts)
    halo, faces, (pair, inv) = refs[:n], refs[n:-2], refs[-2:]
    write_inverse(sc, inv, sizes)
    w_one, bias = half_weights(weights, 1)
    x_len = h.shape[0]
    for kind, face in enumerate(faces):
        place, start, at_high = face_planes(sc, kind, x_len)
        halo_planes(sc, sums_in, halo, kind, start, pair, counts)
        sums_at = flat(scale_planes(sc, inv, start, pair[...], x_len, sizes[0]))
        feat = flat(h[pl.ds(start, 2)])
        scaled, act, slope = node_forward(sums_at, feat, weights, 0)
        moved = (feat.astype(f32) + dot(act, node_out[0])).astype(bf16).astype(f32).reshape(pair.shape)
        face[...] = plane_forward(moved[0], moved[1], at_high, w_one, bias, sc[0])


def face_share(sc, sizes, inv, place, x_len, grad, slope, weights, layer, shape):
    dpn = node_slopes(grad, slope, weights, layer)
    dx = dot_rt(dpn, weights[1][layer, pl.ds(128, 128)]).reshape((1,) + shape)
    share = scale_planes(sc, inv, place, dx, x_len, sizes[0])
    return couple_plane(couple_slots(share[0], sc[0]))


def turn_face_kernel(counts, sizes, sc, edge_w, node_in, node_out, biases, sums_in, h, g_ref, *refs):
    weights = (edge_w, node_in, node_out, biases)
    n = sum(counts)
    halo, faces, (pair, inv) = refs[:n], refs[n:-2], refs[-2:]
    write_inverse(sc, inv, sizes)
    x_len, shape = h.shape[0], h.shape[1:]
    live = (lax.broadcasted_iota(jnp.int32, (1, h.shape[2], 128), 1) < sc[0] * NODES).astype(f32)
    for kind, face in enumerate(faces):
        place, start, at_high = face_planes(sc, kind, x_len)
        halo_planes(sc, sums_in, halo, kind, start, pair, counts)
        plane = pair[place - start][None]
        sums_at = flat(scale_planes(sc, inv, place, plane, x_len, sizes[0]))
        scaled, act, slope = node_forward(sums_at, flat(h[place]), weights, 1)
        grad = flat((g_ref[place].astype(f32) * live).astype(bf16))
        face[...] = face_share(sc, sizes, inv, place, x_len, grad, slope, weights, 1, shape)


def join_face_kernel(counts, sizes, sc, edge_w, node_in, node_out, biases, sums_in, base_in, slopes, slope0, *refs):
    weights = (edge_w, node_in, node_out, biases)
    n = sum(counts)
    halo, faces, (pair, inv) = refs[:n], refs[n:-2], refs[-2:]
    write_inverse(sc, inv, sizes)
    x_len, shape = base_in.shape[0], base_in.shape[1:]
    w_two, w_one = twice(edge_w[1, 1]), twice(edge_w[1, 0])
    for kind, face in enumerate(faces):
        place, start, at_high = face_planes(sc, kind, x_len)
        halo_planes(sc, sums_in, halo, kind, start, pair, counts)
        q = dot_rt(split_cols(flat(pair[...])), w_two).reshape(pair.shape)
        edge = plane_backward(q[0], q[1], at_high, slopes[0, start], slopes[1, place], slopes[2, place])
        grad = (flat(base_in[place]) + dot_rt(split_cols(flat(edge)), w_one)).astype(bf16)
        face[...] = face_share(sc, sizes, inv, place, x_len, grad, flat(slope0[place]), weights, 0, shape)


def twice(weight):
    return jnp.concatenate([weight, weight], 1)


def middle_kernel(counts, sizes, sc, edge_w, node_in, node_out, biases, sums_in, h, *refs):
    weights = (edge_w, node_in, node_out, biases)
    n = sum(counts)
    halo, refs = refs[:n], refs[n:]
    work, scaled_ref, act_ref, slope_ref, next_ref, sums, slopes = refs[:7]
    faces, inv = refs[7:-1], refs[-1]
    add_halo(sc, halo, work, counts)
    write_inverse(sc, inv, sizes)
    shape = (chunk_of(h.shape[0]),) + h.shape[1:]

    def body(x):
        at = pl.ds(x, chunk_of(h.shape[0]))
        sums_at = flat(scale_planes(sc, inv, x, work[at], h.shape[0], sizes[0]))
        scaled, act, slope = node_forward(sums_at, flat(h[at]), weights, 0)
        scaled_ref[at] = scaled.reshape(shape)
        act_ref[at] = act.reshape(shape)
        slope_ref[at] = slope.reshape(shape)
        moved = flat(h[at]).astype(f32) + dot(act, node_out[0])
        next_ref[at] = moved.astype(bf16).reshape(shape)

    planes(h.shape[0], body)
    w_one, bias = half_weights(weights, 1)
    edges_forward(next_ref, w_one, bias, sc[0], sums, slopes)
    couple_columns(sums)
    write_faces(sc, sums, faces, counts)


def turn_kernel(counts, sizes, sc, edge_w, node_in, node_out, biases, sums_in, h, g_ref, *refs):
    weights = (edge_w, node_in, node_out, biases)
    n = sum(counts)
    halo, refs = refs[:n], refs[n:]
    work, scaled_ref, act_ref, dpn_ref, sums = refs[:5]
    faces, inv = refs[5:-1], refs[-1]
    add_halo(sc, halo, work, counts)
    write_inverse(sc, inv, sizes)
    shape = (chunk_of(h.shape[0]),) + h.shape[1:]
    live = live_rows(sc, h)

    def body(x):
        at = pl.ds(x, chunk_of(h.shape[0]))
        sums_at = flat(scale_planes(sc, inv, x, work[at], h.shape[0], sizes[0]))
        scaled, act, slope = node_forward(sums_at, flat(h[at]), weights, 1)
        scaled_ref[at] = scaled.reshape(shape)
        act_ref[at] = act.reshape(shape)
        grad = flat((g_ref[at].astype(f32) * live).astype(bf16))
        dpn = node_slopes(grad, slope, weights, 1)
        dpn_ref[at] = dpn.reshape(shape)
        node_share(sc, x, inv, sizes[0], dpn, weights, 1, sums)

    planes(h.shape[0], body)
    couple_columns(sums)
    write_faces(sc, sums, faces, counts)


def live_rows(sc, h):
    return (lax.broadcasted_iota(jnp.int32, (1, 1, h.shape[2], 128), 2) < sc[0] * NODES).astype(f32)


def products_kernel(sc, node_in, h, g_ref, scaled, act, dpn, base, grads):
    grads[...] = jnp.zeros_like(grads)
    live = live_rows(sc, h)

    def body(x):
        at = pl.ds(x, chunk_of(h.shape[0]))
        grad = (g_ref[at].astype(f32) * live).astype(bf16)
        node_products(flat(grad), flat(h[at]), flat(scaled[at]), flat(act[at]), flat(dpn[at]), grads)
        dx = dot_rt(flat(dpn[at]), node_in[1, pl.ds(0, 128)])
        base[at] = grad.astype(f32) + dx.reshape(grad.shape)

    planes(h.shape[0], body)


def edge_parts(counts, sc, weights, layer, halo, slopes, work, bias):
    add_halo(sc, halo, work, counts)
    shape = (chunk_of(work.shape[0]),) + work.shape[1:]
    w_two = twice(weights[0][layer, 1])

    def to_q(x):
        at = pl.ds(x, chunk_of(work.shape[0]))
        work[at] = dot_rt(split_cols(flat(work[at])), w_two).reshape(shape)

    planes(work.shape[0], to_q)
    edges_backward(work, slopes, work, bias)


def edge_product(h, x, pair, grads, row):
    both = dot_t(flat(h[pl.ds(x, chunk_of(h.shape[0]))]), pair)
    grads[pl.ds(row, 128)] += both[:, :128] + both[:, 128:]


def join_kernel(counts, sizes, sc, edge_w, node_in, node_out, biases, sums_in, base_in, slopes, slope0, *refs):
    weights = (edge_w, node_in, node_out, biases)
    n = sum(counts)
    halo, refs = refs[:n], refs[n:]
    work, grad_ref, dpn_ref, sums, bias = refs[:5]
    faces, inv = refs[5:-1], refs[-1]
    write_inverse(sc, inv, sizes)
    bias[...] = jnp.zeros_like(bias)
    edge_parts(counts, sc, weights, 1, halo, slopes, work, bias)
    w_one = twice(edge_w[1, 0])
    x_len = work.shape[0]
    shape = (chunk_of(x_len),) + work.shape[1:]

    def body(x):
        at = pl.ds(x, chunk_of(x_len))
        pair = split_cols(flat(work[at]))
        grad = (flat(base_in[at]) + dot_rt(pair, w_one)).astype(bf16)
        dpn = node_slopes(grad, flat(slope0[at]), weights, 0)
        grad_ref[at] = grad.reshape(shape)
        dpn_ref[at] = dpn.reshape(shape)
        node_share(sc, x, inv, sizes[0], dpn, weights, 0, sums)

    planes(x_len, body)
    couple_columns(sums)
    write_faces(sc, sums, faces, counts)


def sums_kernel(sizes, sc, h, edges, grad, h0, scaled0, act0, dpn0, grads1, bias, keep, send, grads):
    grads[...] = jnp.zeros_like(grads)
    row = 384 + NODES
    grads[pl.ds(row + 128, NODES)] = bias[...]
    grads[pl.ds(row + 128 + NODES, grads1.shape[0])] = grads1[...]

    def body(x):
        at = pl.ds(x, chunk_of(h.shape[0]))
        edge_product(h, x, split_cols(flat(edges[at])), grads, row)
        node_products(flat(grad[at]), flat(h0[at]), flat(scaled0[at]), flat(act0[at]), flat(dpn0[at]), grads)

    planes(h.shape[0], body)
    write_halves(sc, halving_steps(sizes)[0], grads, keep, send)


def last_kernel(counts, sizes, sc, edge_w, node_in, node_out, biases, sums_in, h, slopes, *refs):
    n = sum(counts)
    halo, (edges, grads) = refs[:n], refs[n:]
    grads[...] = jnp.zeros_like(grads)
    edge_parts(counts, sc, (edge_w,), 0, halo, slopes, edges, grads.at[pl.ds(128, NODES)])

    def body(x):
        edge_product(h, x, split_cols(flat(edges[pl.ds(x, chunk_of(h.shape[0]))])), grads, 0)

    planes(h.shape[0], body)


def state_kernel(sc, edge_w, node_in, grad_in, dpn, edges, grad_ref):
    shape = (chunk_of(edges.shape[0]),) + edges.shape[1:]
    weight = jnp.concatenate([twice(edge_w[0, 0]), node_in[0, pl.ds(0, 128)]], 1)

    def body(x):
        at = pl.ds(x, chunk_of(edges.shape[0]))
        parts = jnp.concatenate([split_cols(flat(edges[at])), flat(dpn[at])], -1)
        grad_ref[at] = (flat(grad_in[at]).astype(f32) + dot_rt(parts, weight)).astype(bf16).reshape(shape)

    planes(edges.shape[0], body)


def finish_kernel(scale, last_rows, step, sc, edge_w, node_in, value, got, *refs):
    edge_grads, in_grads, out_grads, bias_grads, both = refs
    width = edge_w.shape[-1]
    join_kernel_of(step, last_rows, sc, value, got, both)

    def rows_of(part, start, count=width):
        ref, offset = part
        return ref[pl.ds(offset + start, count)] * scale

    def bias_of(part, start):
        return jnp.sum(rows_of(part, start, NODES), 0, keepdims=True)

    end = 3 * width
    last, sum0 = (both, 0), (both, last_rows)
    sum1 = (both, last_rows + 512 + 2 * NODES)
    firsts = ((last, 0), (sum0, end + NODES))
    for layer, part in enumerate((sum0, sum1)):
        out_grads[layer] = rows_of(part, 0)
        in_grads[layer, pl.ds(0, width)] = rows_of(part, width).T
        bias_grads[layer, pl.ds(1, 1)] = bias_of(part, end)
        source, start = firsts[layer]
        edge_grads[layer, 0] = rows_of(source, start)
        bias_grads[layer, pl.ds(0, 1)] = bias_of(source, start + width)
        mixed = rows_of(part, 2 * width).T
        high = mixed.astype(bf16)
        low = (mixed - high.astype(f32)).astype(bf16)
        lower = node_in[layer, pl.ds(width, width)]
        edge_grads[layer, 1] = dot_rt(high, lower) + dot_rt(low, lower)
        w_two = edge_w[layer, 1]
        in_grads[layer, pl.ds(width, width)] = dot_t(w_two, high) + dot_t(w_two, low)


def call(kernel, name, inputs, outs, scratch=(), flops=0, aliases=None):
    total = sum(math.prod(o.shape) * o.dtype.itemsize for o in outs)
    total += sum(math.prod(i.shape) * i.dtype.itemsize for i in inputs)
    return pl.pallas_call(
        kernel,
        name=name,
        out_shape=tuple(outs),
        in_specs=[SM] + [VM] * (len(inputs) - 1),
        out_specs=tuple([VM] * len(outs)),
        scratch_shapes=list(scratch),
        input_output_aliases=aliases or {},
        compiler_params=pltpu.CompilerParams(vmem_limit_bytes=VMEM_LIMIT),
        cost_estimate=pl.CostEstimate(flops=flops, bytes_accessed=total, transcendentals=0),
    )(*inputs)


def pairs(size, kind):
    return [
        pair for low in range(kind, size - 1, 2) for pair in ((low, low + 1), (low + 1, low))
    ]


def hops(size):
    found = []
    hop = 1
    while hop < size:
        found.append(hop)
        hop *= 2
    return found


def halving_steps(sizes):
    steps = [(1, hop) for hop in hops(sizes[1])[:1]]
    steps += [(0, hop) for hop in hops(sizes[0])]
    return steps + [(1, hop) for hop in hops(sizes[1])[1:]]


def padded_rows(rows, sizes):
    unit = NODES << len(halving_steps(sizes))
    return -(-rows // unit) * unit


def bit_of(sc_ref, step):
    axis, hop = step
    return (sc_ref[1 + axis] // hop) % 2


def write_halves(sc_ref, step, from_ref, keep, send):
    half = keep.shape[0]
    bit = bit_of(sc_ref, step)
    keep[...] = from_ref[pl.ds(pl.multiple_of(bit * half, NODES), half)]
    send[...] = from_ref[pl.ds(pl.multiple_of((1 - bit) * half, NODES), half)]


def halve_kernel(step, sc, keep_in, got, keep, send, total):
    total[...] = keep_in[...] + got[...]
    write_halves(sc, step, total, keep, send)


def add_kernel(sc, left, right, out):
    out[...] = left[...] + right[...]


def join_kernel_of(step, start, sc, value, got, out):
    half = value.shape[0] - start
    bit = bit_of(sc, step)
    if start:
        out[pl.ds(0, start)] = value[pl.ds(0, start)] + got[pl.ds(0, start)]
    out[pl.ds(pl.multiple_of(start + bit * half, NODES), half)] = value[pl.ds(start, half)]
    out[pl.ds(pl.multiple_of(start + (1 - bit) * half, NODES), half)] = got[pl.ds(start, half)]


def stack_kernel(sc, first, left, right, out):
    rows = first.shape[0]
    out[pl.ds(0, rows)] = first[...]
    out[pl.ds(rows, left.shape[0])] = left[...] + right[...]


def swap(value, step):
    axis = ("gx", "gy", "gz")[step[0]]
    return lax.ppermute(value, axis, [(i, i ^ step[1]) for i in range(lax.axis_size(axis))])


def rows_like(rows, width=128):
    return jax.ShapeDtypeStruct((rows, width), f32)


def halve(sc, sizes, keep, send):
    steps = halving_steps(sizes)
    got = swap(send, steps[0])
    for step in steps[1:]:
        keep, got = yield keep, got
        half = rows_like(keep.shape[0] // 2)
        keep, send = call(
            functools.partial(halve_kernel, step), "halve", (sc, keep, got), [half, half],
            [pltpu.VMEM(keep.shape, f32)],
        )
        got = swap(send, step)
    keep, got = yield keep, got
    return keep, got


class Background:
    def __init__(self):
        self.active = {}

    def add(self, name, steps):
        self.active[name] = [steps, None]

    def advance(self, entry, tied):
        steps, pending = entry
        try:
            entry[1] = next(steps) if pending is None else steps.send(tied)
        except StopIteration:
            entry[0] = None

    def beside(self, anchor):
        for entry in self.active.values():
            steps, pending = entry
            if steps is None:
                continue
            if pending is None:
                self.advance(entry, None)
            elif pending[1] is not None:
                anchor, tied = lax.optimization_barrier((anchor, pending))
                self.advance(entry, tied)
        return anchor

    def finish(self, name):
        entry = self.active[name]
        while entry[0] is not None:
            done = entry[1]
            if done is not None and done[1] is None:
                return done[0]
            self.advance(entry, done)
        return entry[1]


def on_device(state, cotangent, counts, edge_weights, node_in, node_out, biases):
    x_len, y_len, slots, nodes, width = state.shape
    rows = slots * nodes
    grid = (x_len, y_len, rows, width)
    axes = ("gx", "gy", "gz")
    sizes = tuple(lax.axis_size(a) for a in axes)
    trades = tuple(min(size - 1, 2) for size in sizes)
    nx, ny, nz = trades
    h0 = state.reshape(grid)
    g2 = cotangent.reshape(grid)
    sc = jnp.stack([counts[0]] + [lax.axis_index(a).astype(jnp.int32) for a in axes])

    def sds(shape, kind=f32):
        return jax.ShapeDtypeStruct(shape, kind)

    face_x = sds((y_len, rows, width))
    face_y = sds((x_len, rows, width))
    face_z = sds((x_len, y_len, width))
    face_outs = [face_y] * ny + [face_z] * nz
    full = sds(grid)
    full16 = sds(grid, bf16)
    full3 = sds((3,) + grid)
    inv = pltpu.VMEM((y_len, rows, width), f32)
    matmul = 2 * math.prod(grid) * width
    weights = (edge_weights, node_in, node_out, biases)

    in_place = {1 + len(weights): 0}

    def run(kernel, name, inputs, outs, scratch, flops, aliases):
        body = functools.partial(kernel, trades, sizes)
        return call(body, name, (sc, *weights, *inputs), outs, scratch, flops * matmul, aliases)

    def behind(value, others):
        return lax.optimization_barrier((value, others))[0]

    def trade(faces, axis):
        size = lax.axis_size(axis)
        got = [lax.ppermute(face, axis, pairs(size, kind)) for kind, face in reversed(list(enumerate(faces)))]
        return got[::-1]

    background = Background()

    pair = pltpu.VMEM((2,) + grid[1:], f32)

    def first_trade(kernel, name, inputs, scratch, flops):
        faces = call(functools.partial(kernel, trades, sizes), name, (sc, *inputs), [face_x] * nx, scratch, flops)
        return trade(faces, "gx"), faces

    def exchange(got_x, faces, work=None, held=(), early=None, early_held=()):
        fix = functools.partial(fix_y_kernel, trades)
        same = {1 + nx + k: k for k in range(ny)}
        faces_y = call(fix, "fix_y", (sc, *got_x, *faces[:ny]), [face_y] * ny, aliases=same)
        if early is not None:
            faces_y, early_held = lax.optimization_barrier((faces_y, early_held))
            keep, send = early(*early_held)
        got_y = trade(faces_y, "gy")
        if early is not None:
            got_y, (keep, send) = lax.optimization_barrier((got_y, (keep, send)))
            background.add("sums", halve(sc, sizes, keep, send))
            background.beside(got_y)
        fix = functools.partial(fix_z_kernel, trades)
        same = {1 + nx + ny + k: k for k in range(nz)}
        faces_z = call(fix, "fix_z", (sc, *got_x, *got_y[::-1], *faces[ny:]), [face_z] * nz, aliases=same)
        background.beside(faces_z)
        done = None
        if work is not None:
            faces_z, held = lax.optimization_barrier((faces_z, held))
            done = work(*held)
        got_z = trade(faces_z, "gz")
        got_z, done = lax.optimization_barrier((got_z, done))
        return (*got_x, *got_y, *got_z), done

    def to_slopes(half):
        return call(slope_kernel, "slopes", (sc, half), [full3], [], matmul, {1: 0})[0]

    def products(*held):
        return call(
            products_kernel, "nodes1_products", (sc, node_in, *held), [full, rows_like(3 * width + NODES)], [], 6 * matmul
        )

    got_x, faces_x = first_trade(first_face_kernel, "face0", (edge_weights, biases, h0), [], matmul // 8)
    sums, slopes0, *faces = call(
        functools.partial(first_kernel, trades, sizes), "edges0", (sc, edge_weights, biases, h0),
        [full, full3] + face_outs, [], 3 * matmul,
    )
    halo, slopes0 = exchange(got_x, faces, to_slopes, (slopes0,))
    inputs = (*weights, sums, h0, *halo)
    got_x, faces_x = first_trade(middle_face_kernel, "face1", inputs, [pair, inv], matmul // 4)
    _, scaled0, act0, slope0, h1, sums, slopes1, *faces = run(
        middle_kernel, "nodes0_edges1", (behind(sums, faces_x), h0, *halo),
        [full, full16, full16, full, full16, full, full3] + face_outs, [inv], 8, in_place,
    )
    halo, slopes1 = exchange(got_x, faces, to_slopes, (slopes1,))
    inputs = (*weights, sums, h1, g2, *halo)
    got_x, faces_x = first_trade(turn_face_kernel, "face2", inputs, [pair, inv], matmul // 4)
    _, scaled1, act1, dpn1, sums, *faces = run(
        turn_kernel, "nodes1_back", (behind(sums, faces_x), h1, g2, *halo), [full] + [full16] * 3 + [full] + face_outs,
        [inv], 7, in_place,
    )
    halo, (base, grads1) = exchange(got_x, faces, products, (h1, g2, scaled1, act1, dpn1))
    inputs = (*weights, sums, base, slopes1, slope0, *halo)
    got_x, faces_x = first_trade(join_face_kernel, "face3", inputs, [pair, inv], matmul // 4)
    edges1, grad_in, dpn0, sums, bias1, *faces = run(
        join_kernel, "edges1_back_nodes0_back", (behind(sums, faces_x), base, slopes1, slope0, *halo),
        [full, full16, full16, full, rows_like(NODES)] + face_outs, [inv], 9, in_place,
    )

    def layer_sums(*held):
        total = padded_rows(7 * width + 3 * NODES, sizes)
        return call(
            functools.partial(sums_kernel, sizes), "gradient_sums", (sc, *held), [rows_like(total // 2)] * 2,
            [pltpu.VMEM((total, width), f32)], 5 * matmul,
        )

    held = (h1, edges1, grad_in, h0, scaled0, act0, dpn0, grads1, bias1)
    halo, _ = exchange(got_x, faces, early=layer_sums, early_held=held)
    tail_rows = width + NODES
    edges, last = run(
        last_kernel, "edges0_back", (sums, h0, slopes0, *halo), [full, rows_like(tail_rows)], [], 6, in_place
    )
    keep, got = background.finish("sums")
    (value,) = call(stack_kernel, "stack", (sc, last, keep, got), [rows_like(tail_rows + keep.shape[0])])
    value, grad_in, dpn0, edges = lax.optimization_barrier((value, grad_in, dpn0, edges))
    (grad0,) = call(
        state_kernel, "state_grad", (sc, edge_weights, node_in, grad_in, dpn0, edges), [full16], [], 4 * matmul
    )
    for hop in reversed(hops(sizes[2])):
        (value,) = call(add_kernel, "add", (sc, value, swap(value, (2, hop))), [rows_like(value.shape[0])])
        value, grad0 = lax.optimization_barrier((value, grad0))
    first, *rest = halving_steps(sizes)
    for step in reversed(rest):
        out = rows_like(2 * value.shape[0] - tail_rows)
        body = functools.partial(join_kernel_of, step, tail_rows)
        (value,) = call(body, "join", (sc, value, swap(value, step)), [out])
    layers_all = 3 * slots * sizes[2] // 4
    nodes_all = x_len * sizes[0] * y_len * sizes[1] * layers_all * nodes
    scale = 1.0 / math.sqrt(nodes_all)
    edge_grads, in_grads, out_grads, bias_grads = call(
        functools.partial(finish_kernel, scale, tail_rows, first), "finish",
        (sc, edge_weights, node_in, value, swap(value, first)),
        [sds(edge_weights.shape), sds(node_in.shape), sds(node_out.shape), sds(biases.shape)],
        [pltpu.VMEM((2 * value.shape[0] - tail_rows, width), f32)],
    )
    return grad0.reshape(state.shape), edge_grads, in_grads, out_grads, bias_grads


def solution(mesh):
    return jax.shard_map(
        on_device,
        mesh=mesh,
        in_specs=(
            P("gx", "gy", "gz", None, None),
            P("gx", "gy", "gz", None, None),
            P("gz"),
            P(),
            P(),
            P(),
            P(),
        ),
        out_specs=(P("gx", "gy", "gz", None, None), P(), P(), P(), P()),
        check_vma=False,
    )
```

```python
import functools
import math

import jax
import jax.numpy as jnp
from jax import lax
from jax.experimental import pallas as pl
from jax.experimental.pallas import tpu as pltpu
from jax.sharding import PartitionSpec as P

f32 = jnp.float32
bf16 = jnp.bfloat16
NODES = 8
VMEM_LIMIT = 12 * 1024 * 1024
VM = pl.BlockSpec(memory_space=pltpu.VMEM)
SM = pl.BlockSpec(memory_space=pltpu.SMEM)


def dot(left, right):
    return lax.dot_general(left, right, (((1,), (0,)), ((), ())), preferred_element_type=f32)


def dot_t(left, right):
    return lax.dot_general(left, right, (((0,), (0,)), ((), ())), preferred_element_type=f32)


def dot_rt(left, right):
    return lax.dot_general(left, right, (((1,), (1,)), ((), ())), preferred_element_type=f32)


def silu_half(half):
    th = jnp.tanh(half)
    prod = half * th
    return half + prod, (0.5 + 0.5 * th) * ((1.0 + half) - prod)


def split_cols(value):
    high = value.astype(bf16)
    low = (value - high.astype(f32)).astype(bf16)
    return jnp.concatenate([high, low], -1)


def up(value):
    return pltpu.roll(value, NODES - 1, 1)


def down(value):
    return pltpu.roll(value, 1, 1)


def flat(value):
    return value.reshape(-1, value.shape[-1])


def node_rows(value):
    return value.reshape(-1, NODES, value.shape[-1])


def row_ids():
    return lax.broadcasted_iota(jnp.int32, (1, NODES, 128), 1)


def couple_slots(plane, filled):
    count, rows, width = plane.shape
    slots = rows // NODES
    parts = plane.reshape(count, slots, NODES, width)
    ids = row_ids()
    done = []
    for s in range(slots):
        here = parts[:, s]
        if s + 1 < slots:
            take = (ids == NODES - 1) & (s + 1 < filled)
            here = here + jnp.where(take, up(parts[:, s + 1]), 0.0)
        if s > 0:
            here = here + jnp.where(ids == 0, down(parts[:, s - 1]), 0.0)
            here = jnp.where(s < filled, here, 0.0)
        done.append(here[:, None])
    return jnp.concatenate(done, 1).reshape(plane.shape)


def elements(x_len, y_len, body):
    ey = y_len // NODES
    total = (x_len // NODES) * ey

    def step(e, carry):
        x0 = pl.multiple_of((e // ey) * NODES, NODES)
        y0 = pl.multiple_of((e % ey) * NODES, NODES)
        body(x0, y0)
        return carry

    lax.fori_loop(0, total, step, 0, unroll=2 if total % 2 == 0 else 1)


def edge_dots(parts, weight, weight_both):
    rows, width = parts[0].shape[1:]
    if len(parts) == 2:
        return dot(flat(jnp.concatenate(parts, 0)), weight).reshape(-1, rows, width)
    both = dot(jnp.concatenate([flat(parts[0]), flat(parts[2])], -1), weight_both)
    between = dot(flat(parts[1]), weight).reshape(-1, rows, width)
    first, last = (both[:, k : k + width].reshape(-1, rows, width) for k in (0, width))
    return jnp.concatenate([first, between, last], 0)


def edges_forward(h_ref, w_one, half_bias, filled, sum_ref, half_ref):
    x_len, y_len, rows, width = h_ref.shape
    blank = jnp.zeros_like(w_one)
    w_both = jnp.concatenate([jnp.concatenate([w_one, blank], 1), jnp.concatenate([blank, w_one], 1)], 0)
    inner = row_ids() < NODES - 1

    def body(x0, y0):
        ys = pl.ds(y0, NODES)
        prev = None
        here = h_ref[x0, ys].astype(f32)
        for i in range(NODES):
            parts = []
            nxt = None
            if i < NODES - 1:
                nxt = h_ref[x0 + i + 1, ys].astype(f32)
                parts.append((nxt - here).astype(bf16))
            parts.append((here[1:] - here[:-1]).astype(bf16))
            cols = node_rows(here)
            parts.append((up(cols) - cols).reshape(here.shape).astype(bf16))
            half = edge_dots(parts, w_one, w_both) + half_bias
            act = (half + half * jnp.tanh(half)).astype(bf16).astype(f32)
            at = 0
            total = prev
            prev = None
            if i < NODES - 1:
                prev = act[:NODES]
                total = -prev if total is None else total - prev
                half_ref[0, x0 + i, ys] = half[:NODES]
                at = NODES
            along_y = act[at : at + NODES - 1]
            half_ref[1, x0 + i, pl.ds(y0, NODES - 1)] = half[at : at + NODES - 1]
            at += NODES - 1
            along_z = jnp.where(inner, node_rows(act[at:]), 0.0)
            half_ref[2, x0 + i, ys] = half[at:]
            total = total + (down(along_z) - along_z).reshape(here.shape)
            total = jnp.concatenate(
                [
                    total[:1] - along_y[:1],
                    total[1:-1] + (along_y[:-1] - along_y[1:]),
                    total[-1:] + along_y[-1:],
                ],
                0,
            )
            sum_ref[x0 + i, ys] = couple_slots(total, filled)
            here = nxt

    elements(x_len, y_len, body)


def slope_kernel(sc, half_in, slope_out):
    inner = row_ids() < NODES - 1

    def step(x, carry):
        for k in range(3):
            slope = silu_half(half_in[k, x])[1]
            if k == 2:
                slope = jnp.where(inner, node_rows(slope), 0.0).reshape(slope.shape)
            slope_out[k, x] = slope
        return carry

    lax.fori_loop(0, half_in.shape[1], step, 0)


def couple_columns(sum_ref):
    x_len, y_len = sum_ref.shape[:2]
    for cut in range(NODES, x_len, NODES):
        both = sum_ref[cut - 1] + sum_ref[cut]
        sum_ref[cut - 1] = both
        sum_ref[cut] = both
    for cut in range(NODES, y_len, NODES):
        both = sum_ref[:, cut - 1] + sum_ref[:, cut]
        sum_ref[:, cut - 1] = both
        sum_ref[:, cut] = both


def face_place(sc_ref, axis, kind, last):
    return jnp.where((sc_ref[1 + axis] + kind) % 2 == 0, last, 0)


def end_rows(values, filled, take_top):
    picked = values(0)
    slots = values.slots
    for s in range(slots):
        picked = jnp.where(take_top & (filled == s + 1), values(s * NODES + NODES - 1), picked)
    return picked


class RowReader:
    def __init__(self, slots, read):
        self.slots = slots
        self.read = read

    def __call__(self, row):
        return self.read(row)


def takes_top(sc_ref, kind):
    return (sc_ref[3] + kind) % 2 == 0


def write_faces(sc_ref, sum_ref, faces, counts):
    x_len, y_len, rows, width = sum_ref.shape
    nx, ny, nz = counts
    reader = RowReader(rows // NODES, lambda row: sum_ref[:, :, row])
    for kind in range(ny):
        faces[kind][...] = sum_ref[:, face_place(sc_ref, 1, kind, y_len - 1)]
    for kind in range(nz):
        faces[ny + kind][...] = end_rows(reader, sc_ref[0], takes_top(sc_ref, kind))


def add_halo(sc_ref, halo, into_ref, counts):
    x_len, y_len, rows, width = into_ref.shape
    nx, ny, nz = counts
    for kind in range(nx):
        into_ref[face_place(sc_ref, 0, kind, x_len - 1)] += halo[kind][...]
    for kind in range(ny):
        into_ref[:, face_place(sc_ref, 1, kind, y_len - 1)] += halo[nx + kind][...]
    if nz:
        got = [halo[nx + ny + kind][...] for kind in range(nz)]
        tops = [takes_top(sc_ref, kind) for kind in range(nz)]
        from_below = sum(jnp.where(top, 0.0, value) for top, value in zip(tops, got))
        from_above = sum(jnp.where(top, value, 0.0) for top, value in zip(tops, got))
        into_ref[:, :, 0] += from_below
        for s in range(rows // NODES):
            into_ref[:, :, s * NODES + NODES - 1] += jnp.where(sc_ref[0] == s + 1, from_above, 0.0)


def fix_y_kernel(counts, sc_ref, *refs):
    nx, ny, nz = counts
    got, faces, outs = refs[:nx], refs[nx : nx + ny], refs[nx + ny :]
    x_len = faces[0].shape[0]
    for kind in range(nx):
        place = face_place(sc_ref, 0, kind, x_len - 1)
        for k in range(ny):
            y_len = got[kind].shape[0]
            outs[k][place] += got[kind][face_place(sc_ref, 1, k, y_len - 1)]


def fix_z_kernel(counts, sc_ref, *refs):
    nx, ny, nz = counts
    got_x, refs = refs[:nx], refs[nx:]
    got_y, refs = refs[:ny][::-1], refs[ny:]
    faces, outs = refs[:nz], refs[nz:]
    x_len, y_len, width = faces[0].shape
    for k in range(nz):
        top = takes_top(sc_ref, k)
        for kind in range(nx):
            ref = got_x[kind]
            reader = RowReader(ref.shape[1] // NODES, lambda row, ref=ref: ref[:, row])
            outs[k][face_place(sc_ref, 0, kind, x_len - 1)] += end_rows(reader, sc_ref[0], top)
        for kind in range(ny):
            ref = got_y[kind]
            reader = RowReader(ref.shape[1] // NODES, lambda row, ref=ref: ref[:, row])
            add = end_rows(reader, sc_ref[0], top)
            first = face_place(sc_ref, 1, kind, 1) == 0
            outs[k][:, 0] += jnp.where(first, add, 0.0)
            outs[k][:, y_len - 1] += jnp.where(first, 0.0, add)


def write_inverse(sc_ref, inv_ref, sizes):
    y_len, rows, width = inv_ref.shape
    filled, at_y, at_z = sc_ref[0], sc_ref[2], sc_ref[3]
    ids = lax.broadcasted_iota(jnp.int32, (rows, width), 0)
    node = ids % NODES
    low = (node == 0) & ((ids >= NODES) | (at_z > 0))
    high = (node == NODES - 1) & ((ids < (filled - 1) * NODES) | (at_z < sizes[2] - 1))
    along_z = jnp.where(low | high, 0.5, 1.0).astype(f32)
    for y in range(y_len):
        inv_ref[y] = along_z * end_factor(y, y_len, at_y, sizes[1])


def end_factor(place, length, position, size):
    whole = place + position * length
    low = (place % NODES == 0) & (whole > 0)
    high = (place % NODES == NODES - 1) & (whole < length * size - 1)
    return jnp.where(low | high, 0.5, 1.0).astype(f32)


def chunk_of(x_len):
    return 2 * NODES if x_len % (2 * NODES) == 0 else NODES


def scale_planes(sc_ref, inv_ref, x, block, x_len, size_x):
    inv = inv_ref[...]
    parts = [block[c] * (inv * end_factor(x + c, x_len, sc_ref[1], size_x)) for c in range(block.shape[0])]
    return jnp.stack(parts, 0)


def node_forward(scaled, feat, weights, layer):
    edge_w, node_in, node_out, biases = weights
    pair = split_cols(scaled)
    w_two = edge_w[layer, 1]
    joined = jnp.concatenate([feat, dot(pair, jnp.concatenate([w_two, w_two], 0)).astype(bf16)], -1)
    half = jnp.bfloat16(0.5)
    act, slope = silu_half(dot(joined, node_in[layer] * half) + 0.5 * biases[layer, pl.ds(1, 1)])
    return pair[:, :128], act.astype(bf16), slope


def node_slopes(grad, slope, weights, layer):
    return (dot_rt(grad, weights[2][layer]) * slope).astype(bf16)


def node_share(sc_ref, x, inv_ref, size_x, dpn, weights, layer, sum_ref):
    shape = (chunk_of(sum_ref.shape[0]),) + sum_ref.shape[1:]
    dx = dot_rt(dpn, weights[1][layer, pl.ds(128, 128)]).reshape(shape)
    share = scale_planes(sc_ref, inv_ref, x, dx, sum_ref.shape[0], size_x)
    joined = couple_slots(share.reshape((-1,) + shape[2:]), sc_ref[0])
    sum_ref[pl.ds(x, shape[0])] = joined.reshape(shape)


def node_products(grad, feat, scaled, act, dpn, grads):
    grads[pl.ds(0, 128)] += dot_t(act, grad)
    both = dot_t(dpn, jnp.concatenate([feat, scaled], -1))
    grads[pl.ds(128, 128)] += both[:, :128]
    grads[pl.ds(256, 128)] += both[:, 128:]
    grads[pl.ds(384, NODES)] += jnp.sum(dpn.astype(f32).reshape(-1, NODES, 128), 0)


def couple_plane(plane):
    y_len = plane.shape[0]
    parts = [plane[y] for y in range(y_len)]
    for cut in range(NODES, y_len, NODES):
        both = parts[cut - 1] + parts[cut]
        parts[cut - 1] = parts[cut] = both
    return jnp.stack(parts, 0)


def along_y(plane, combine):
    return [
        combine(plane[y : y + NODES - 1], plane[y + 1 : y + NODES], y) for y in range(0, plane.shape[0], NODES)
    ]


def spread_plane(sign, edge_x, edges_y, edge_z):
    total = sign * edge_x + (down(edge_z) - edge_z).reshape(edge_x.shape)
    parts = []
    for k, edge in enumerate(edges_y):
        here = total[k * NODES : (k + 1) * NODES]
        parts += [here[:1] - edge[:1], here[1:-1] + (edge[:-1] - edge[1:]), here[-1:] + edge[-1:]]
    return jnp.concatenate(parts, 0)


def plane_forward(low, high, at_high, w_one, half_bias, filled):
    y_len, rows, width = low.shape
    here = jnp.where(at_high, high, low)
    cols = node_rows(here)
    parts = [(high - low).astype(bf16)]
    parts += along_y(here, lambda lower, upper, y: (upper - lower).astype(bf16))
    parts.append((up(cols) - cols).reshape(here.shape).astype(bf16))
    half = dot(flat(jnp.concatenate(parts, 0)), w_one).reshape(-1, rows, width) + half_bias
    act = silu_half(half)[0].astype(bf16).astype(f32)
    at = y_len
    edges_y = []
    for _ in range(y_len // NODES):
        edges_y.append(act[at : at + NODES - 1])
        at += NODES - 1
    edge_z = jnp.where(row_ids() < NODES - 1, node_rows(act[at:]), 0.0)
    total = spread_plane(jnp.where(at_high, 1.0, -1.0), act[:y_len], edges_y, edge_z)
    return couple_plane(couple_slots(total, filled))


def plane_backward(low, high, at_high, slope_x, slope_y, slope_z):
    here = jnp.where(at_high, high, low)
    cols = node_rows(here)
    edge_x = ((high - low) * slope_x).astype(bf16).astype(f32)
    edges_y = along_y(
        here, lambda lower, upper, y: ((upper - lower) * slope_y[y : y + NODES - 1]).astype(bf16).astype(f32)
    )
    edge_z = ((up(cols) - cols) * node_rows(slope_z)).astype(bf16).astype(f32)
    return spread_plane(jnp.where(at_high, 1.0, -1.0), edge_x, edges_y, edge_z)


def face_planes(sc_ref, kind, x_len):
    place = face_place(sc_ref, 0, kind, x_len - 1)
    at_high = place > 0
    return place, jnp.where(at_high, x_len - 2, 0), at_high


def halo_planes(sc_ref, from_ref, halo, kind, start, into_ref, counts):
    x_len, y_len, rows, width = from_ref.shape
    nx, ny, nz = counts
    for c in range(2):
        into_ref[c] = from_ref[start + c]
    into_ref[face_place(sc_ref, 0, kind, x_len - 1) - start] += halo[kind][...]
    for c in range(2):
        for k in range(ny):
            into_ref[c, face_place(sc_ref, 1, k, y_len - 1)] += halo[nx + k][start + c]
        for k in range(nz):
            got = halo[nx + ny + k][start + c]
            top = takes_top(sc_ref, k)
            into_ref[c, :, 0] += jnp.where(top, 0.0, got)
            for s in range(rows // NODES):
                into_ref[c, :, s * NODES + NODES - 1] += jnp.where(top & (sc_ref[0] == s + 1), got, 0.0)


def edges_backward(q_ref, slope_ref, edge_ref, bias_acc):
    x_len, y_len, rows, width = q_ref.shape

    def body(x0, y0):
        ys = pl.ds(y0, NODES)
        prev = None
        here = q_ref[x0, ys]
        bias = jnp.zeros((NODES, width), f32)
        for i in range(NODES):
            total = prev
            prev = None
            nxt = None
            if i < NODES - 1:
                nxt = q_ref[x0 + i + 1, ys]
                prev = ((nxt - here) * slope_ref[0, x0 + i, ys]).astype(bf16).astype(f32)
                total = -prev if total is None else total - prev
                bias = bias + jnp.sum(node_rows(prev), 0)
            along_y = (here[1:] - here[:-1]) * slope_ref[1, x0 + i, pl.ds(y0, NODES - 1)]
            along_y = along_y.astype(bf16).astype(f32)
            cols = node_rows(here)
            along_z = (up(cols) - cols) * node_rows(slope_ref[2, x0 + i, ys])
            along_z = along_z.astype(bf16).astype(f32)
            bias = bias + jnp.sum(node_rows(along_y), 0) + jnp.sum(along_z, 0)
            total = total + (down(along_z) - along_z).reshape(here.shape)
            total = jnp.concatenate(
                [
                    total[:1] - along_y[:1],
                    total[1:-1] + (along_y[:-1] - along_y[1:]),
                    total[-1:] + along_y[-1:],
                ],
                0,
            )
            edge_ref[x0 + i, ys] = total
            here = nxt
        bias_acc[...] += bias

    elements(x_len, y_len, body)


def planes(count, body):
    chunk = chunk_of(count)

    def step(c, carry):
        body(pl.multiple_of(c * chunk, chunk))
        return carry

    lax.fori_loop(0, count // chunk, step, 0)


def half_weights(weights, layer):
    edge_w, node_in, node_out, biases = weights
    return edge_w[layer, 0] * jnp.bfloat16(0.5), 0.5 * biases[layer, pl.ds(0, 1)]


def first_kernel(counts, sizes, sc, edge_w, biases, h, sums, slopes, *faces):
    w_one, bias = half_weights((edge_w, None, None, biases), 0)
    edges_forward(h, w_one, bias, sc[0], sums, slopes)
    couple_columns(sums)
    write_faces(sc, sums, faces, counts)


def first_face_kernel(counts, sizes, sc, edge_w, biases, h, *faces):
    w_one, bias = half_weights((edge_w, None, None, biases), 0)
    for kind, face in enumerate(faces):
        place, start, at_high = face_planes(sc, kind, h.shape[0])
        face[...] = plane_forward(
            h[start].astype(f32), h[start + 1].astype(f32), at_high, w_one, bias, sc[0]
        )


def middle_face_kernel(counts, sizes, sc, edge_w, node_in, node_out, biases, sums_in, h, *refs):
    weights = (edge_w, node_in, node_out, biases)
    n = sum(counts)
    halo, faces, (pair, inv) = refs[:n], refs[n:-2], refs[-2:]
    write_inverse(sc, inv, sizes)
    w_one, bias = half_weights(weights, 1)
    x_len = h.shape[0]
    for kind, face in enumerate(faces):
        place, start, at_high = face_planes(sc, kind, x_len)
        halo_planes(sc, sums_in, halo, kind, start, pair, counts)
        sums_at = flat(scale_planes(sc, inv, start, pair[...], x_len, sizes[0]))
        feat = flat(h[pl.ds(start, 2)])
        scaled, act, slope = node_forward(sums_at, feat, weights, 0)
        moved = (feat.astype(f32) + dot(act, node_out[0])).astype(bf16).astype(f32).reshape(pair.shape)
        face[...] = plane_forward(moved[0], moved[1], at_high, w_one, bias, sc[0])


def face_share(sc, sizes, inv, place, x_len, grad, slope, weights, layer, shape):
    dpn = node_slopes(grad, slope, weights, layer)
    dx = dot_rt(dpn, weights[1][layer, pl.ds(128, 128)]).reshape((1,) + shape)
    share = scale_planes(sc, inv, place, dx, x_len, sizes[0])
    return couple_plane(couple_slots(share[0], sc[0]))


def turn_face_kernel(counts, sizes, sc, edge_w, node_in, node_out, biases, sums_in, h, g_ref, *refs):
    weights = (edge_w, node_in, node_out, biases)
    n = sum(counts)
    halo, faces, (pair, inv) = refs[:n], refs[n:-2], refs[-2:]
    write_inverse(sc, inv, sizes)
    x_len, shape = h.shape[0], h.shape[1:]
    live = (lax.broadcasted_iota(jnp.int32, (1, h.shape[2], 128), 1) < sc[0] * NODES).astype(f32)
    for kind, face in enumerate(faces):
        place, start, at_high = face_planes(sc, kind, x_len)
        halo_planes(sc, sums_in, halo, kind, start, pair, counts)
        plane = pair[place - start][None]
        sums_at = flat(scale_planes(sc, inv, place, plane, x_len, sizes[0]))
        scaled, act, slope = node_forward(sums_at, flat(h[place]), weights, 1)
        grad = flat((g_ref[place].astype(f32) * live).astype(bf16))
        face[...] = face_share(sc, sizes, inv, place, x_len, grad, slope, weights, 1, shape)


def join_face_kernel(counts, sizes, sc, edge_w, node_in, node_out, biases, sums_in, base_in, slopes, slope0, *refs):
    weights = (edge_w, node_in, node_out, biases)
    n = sum(counts)
    halo, faces, (pair, inv) = refs[:n], refs[n:-2], refs[-2:]
    write_inverse(sc, inv, sizes)
    x_len, shape = base_in.shape[0], base_in.shape[1:]
    w_two, w_one = twice(edge_w[1, 1]), twice(edge_w[1, 0])
    for kind, face in enumerate(faces):
        place, start, at_high = face_planes(sc, kind, x_len)
        halo_planes(sc, sums_in, halo, kind, start, pair, counts)
        q = dot_rt(split_cols(flat(pair[...])), w_two).reshape(pair.shape)
        edge = plane_backward(q[0], q[1], at_high, slopes[0, start], slopes[1, place], slopes[2, place])
        grad = (flat(base_in[place]) + dot_rt(split_cols(flat(edge)), w_one)).astype(bf16)
        face[...] = face_share(sc, sizes, inv, place, x_len, grad, flat(slope0[place]), weights, 0, shape)


def twice(weight):
    return jnp.concatenate([weight, weight], 1)


def middle_kernel(counts, sizes, sc, edge_w, node_in, node_out, biases, sums_in, h, *refs):
    weights = (edge_w, node_in, node_out, biases)
    n = sum(counts)
    halo, refs = refs[:n], refs[n:]
    work, scaled_ref, act_ref, slope_ref, next_ref, sums, slopes = refs[:7]
    faces, inv = refs[7:-1], refs[-1]
    add_halo(sc, halo, work, counts)
    write_inverse(sc, inv, sizes)
    shape = (chunk_of(h.shape[0]),) + h.shape[1:]

    def body(x):
        at = pl.ds(x, chunk_of(h.shape[0]))
        sums_at = flat(scale_planes(sc, inv, x, work[at], h.shape[0], sizes[0]))
        scaled, act, slope = node_forward(sums_at, flat(h[at]), weights, 0)
        scaled_ref[at] = scaled.reshape(shape)
        act_ref[at] = act.reshape(shape)
        slope_ref[at] = slope.reshape(shape)
        moved = flat(h[at]).astype(f32) + dot(act, node_out[0])
        next_ref[at] = moved.astype(bf16).reshape(shape)

    planes(h.shape[0], body)
    w_one, bias = half_weights(weights, 1)
    edges_forward(next_ref, w_one, bias, sc[0], sums, slopes)
    couple_columns(sums)
    write_faces(sc, sums, faces, counts)


def turn_kernel(counts, sizes, sc, edge_w, node_in, node_out, biases, sums_in, h, g_ref, *refs):
    weights = (edge_w, node_in, node_out, biases)
    n = sum(counts)
    halo, refs = refs[:n], refs[n:]
    work, scaled_ref, act_ref, dpn_ref, sums = refs[:5]
    faces, inv = refs[5:-1], refs[-1]
    add_halo(sc, halo, work, counts)
    write_inverse(sc, inv, sizes)
    shape = (chunk_of(h.shape[0]),) + h.shape[1:]
    live = live_rows(sc, h)

    def body(x):
        at = pl.ds(x, chunk_of(h.shape[0]))
        sums_at = flat(scale_planes(sc, inv, x, work[at], h.shape[0], sizes[0]))
        scaled, act, slope = node_forward(sums_at, flat(h[at]), weights, 1)
        scaled_ref[at] = scaled.reshape(shape)
        act_ref[at] = act.reshape(shape)
        grad = flat((g_ref[at].astype(f32) * live).astype(bf16))
        dpn = node_slopes(grad, slope, weights, 1)
        dpn_ref[at] = dpn.reshape(shape)
        node_share(sc, x, inv, sizes[0], dpn, weights, 1, sums)

    planes(h.shape[0], body)
    couple_columns(sums)
    write_faces(sc, sums, faces, counts)


def live_rows(sc, h):
    return (lax.broadcasted_iota(jnp.int32, (1, 1, h.shape[2], 128), 2) < sc[0] * NODES).astype(f32)


def products_kernel(sc, node_in, h, g_ref, scaled, act, dpn, base, grads):
    grads[...] = jnp.zeros_like(grads)
    live = live_rows(sc, h)

    def body(x):
        at = pl.ds(x, chunk_of(h.shape[0]))
        grad = (g_ref[at].astype(f32) * live).astype(bf16)
        node_products(flat(grad), flat(h[at]), flat(scaled[at]), flat(act[at]), flat(dpn[at]), grads)
        dx = dot_rt(flat(dpn[at]), node_in[1, pl.ds(0, 128)])
        base[at] = grad.astype(f32) + dx.reshape(grad.shape)

    planes(h.shape[0], body)


def edge_parts(counts, sc, weights, layer, halo, slopes, work, bias):
    add_halo(sc, halo, work, counts)
    shape = (chunk_of(work.shape[0]),) + work.shape[1:]
    w_two = twice(weights[0][layer, 1])

    def to_q(x):
        at = pl.ds(x, chunk_of(work.shape[0]))
        work[at] = dot_rt(split_cols(flat(work[at])), w_two).reshape(shape)

    planes(work.shape[0], to_q)
    edges_backward(work, slopes, work, bias)


def edge_product(h, x, pair, grads, row):
    both = dot_t(flat(h[pl.ds(x, chunk_of(h.shape[0]))]), pair)
    grads[pl.ds(row, 128)] += both[:, :128] + both[:, 128:]


def join_kernel(counts, sizes, sc, edge_w, node_in, node_out, biases, sums_in, base_in, slopes, slope0, *refs):
    weights = (edge_w, node_in, node_out, biases)
    n = sum(counts)
    halo, refs = refs[:n], refs[n:]
    work, grad_ref, dpn_ref, sums, bias = refs[:5]
    faces, inv = refs[5:-1], refs[-1]
    write_inverse(sc, inv, sizes)
    bias[...] = jnp.zeros_like(bias)
    edge_parts(counts, sc, weights, 1, halo, slopes, work, bias)
    w_one = twice(edge_w[1, 0])
    x_len = work.shape[0]
    shape = (chunk_of(x_len),) + work.shape[1:]

    def body(x):
        at = pl.ds(x, chunk_of(x_len))
        pair = split_cols(flat(work[at]))
        grad = (flat(base_in[at]) + dot_rt(pair, w_one)).astype(bf16)
        dpn = node_slopes(grad, flat(slope0[at]), weights, 0)
        grad_ref[at] = grad.reshape(shape)
        dpn_ref[at] = dpn.reshape(shape)
        node_share(sc, x, inv, sizes[0], dpn, weights, 0, sums)

    planes(x_len, body)
    couple_columns(sums)
    write_faces(sc, sums, faces, counts)


def sums_kernel(sizes, sc, h, edges, grad, h0, scaled0, act0, dpn0, grads1, bias, keep, send, grads):
    grads[...] = jnp.zeros_like(grads)
    row = 384 + NODES
    grads[pl.ds(row + 128, NODES)] = bias[...]
    grads[pl.ds(row + 128 + NODES, grads1.shape[0])] = grads1[...]

    def body(x):
        at = pl.ds(x, chunk_of(h.shape[0]))
        edge_product(h, x, split_cols(flat(edges[at])), grads, row)
        node_products(flat(grad[at]), flat(h0[at]), flat(scaled0[at]), flat(act0[at]), flat(dpn0[at]), grads)

    planes(h.shape[0], body)
    write_halves(sc, halving_steps(sizes)[0], grads, keep, send)


def last_kernel(counts, sizes, sc, edge_w, node_in, node_out, biases, sums_in, h, slopes, *refs):
    n = sum(counts)
    halo, (edges, grads) = refs[:n], refs[n:]
    grads[...] = jnp.zeros_like(grads)
    edge_parts(counts, sc, (edge_w,), 0, halo, slopes, edges, grads.at[pl.ds(128, NODES)])

    def body(x):
        edge_product(h, x, split_cols(flat(edges[pl.ds(x, chunk_of(h.shape[0]))])), grads, 0)

    planes(h.shape[0], body)


def state_kernel(sc, edge_w, node_in, grad_in, dpn, edges, grad_ref):
    shape = (chunk_of(edges.shape[0]),) + edges.shape[1:]
    weight = jnp.concatenate([twice(edge_w[0, 0]), node_in[0, pl.ds(0, 128)]], 1)

    def body(x):
        at = pl.ds(x, chunk_of(edges.shape[0]))
        parts = jnp.concatenate([split_cols(flat(edges[at])), flat(dpn[at])], -1)
        grad_ref[at] = (flat(grad_in[at]).astype(f32) + dot_rt(parts, weight)).astype(bf16).reshape(shape)

    planes(edges.shape[0], body)


def finish_kernel(scale, last_rows, step, sc, edge_w, node_in, value, got, *refs):
    edge_grads, in_grads, out_grads, bias_grads, both = refs
    width = edge_w.shape[-1]
    join_kernel_of(step, last_rows, sc, value, got, both)

    def rows_of(part, start, count=width):
        ref, offset = part
        return ref[pl.ds(offset + start, count)] * scale

    def bias_of(part, start):
        return jnp.sum(rows_of(part, start, NODES), 0, keepdims=True)

    end = 3 * width
    last, sum0 = (both, 0), (both, last_rows)
    sum1 = (both, last_rows + 512 + 2 * NODES)
    firsts = ((last, 0), (sum0, end + NODES))
    for layer, part in enumerate((sum0, sum1)):
        out_grads[layer] = rows_of(part, 0)
        in_grads[layer, pl.ds(0, width)] = rows_of(part, width).T
        bias_grads[layer, pl.ds(1, 1)] = bias_of(part, end)
        source, start = firsts[layer]
        edge_grads[layer, 0] = rows_of(source, start)
        bias_grads[layer, pl.ds(0, 1)] = bias_of(source, start + width)
        mixed = rows_of(part, 2 * width).T
        high = mixed.astype(bf16)
        low = (mixed - high.astype(f32)).astype(bf16)
        lower = node_in[layer, pl.ds(width, width)]
        edge_grads[layer, 1] = dot_rt(high, lower) + dot_rt(low, lower)
        w_two = edge_w[layer, 1]
        in_grads[layer, pl.ds(width, width)] = dot_t(w_two, high) + dot_t(w_two, low)


def call(kernel, name, inputs, outs, scratch=(), flops=0, aliases=None):
    total = sum(math.prod(o.shape) * o.dtype.itemsize for o in outs)
    total += sum(math.prod(i.shape) * i.dtype.itemsize for i in inputs)
    return pl.pallas_call(
        kernel,
        name=name,
        out_shape=tuple(outs),
        in_specs=[SM] + [VM] * (len(inputs) - 1),
        out_specs=tuple([VM] * len(outs)),
        scratch_shapes=list(scratch),
        input_output_aliases=aliases or {},
        compiler_params=pltpu.CompilerParams(vmem_limit_bytes=VMEM_LIMIT),
        cost_estimate=pl.CostEstimate(flops=flops, bytes_accessed=total, transcendentals=0),
    )(*inputs)


def pairs(size, kind):
    return [
        pair for low in range(kind, size - 1, 2) for pair in ((low, low + 1), (low + 1, low))
    ]


def hops(size):
    found = []
    hop = 1
    while hop < size:
        found.append(hop)
        hop *= 2
    return found


def halving_steps(sizes):
    steps = [(1, hop) for hop in hops(sizes[1])[:1]]
    steps += [(0, hop) for hop in hops(sizes[0])]
    return steps + [(1, hop) for hop in hops(sizes[1])[1:]]


def padded_rows(rows, sizes):
    unit = NODES << len(halving_steps(sizes))
    return -(-rows // unit) * unit


def bit_of(sc_ref, step):
    axis, hop = step
    return (sc_ref[1 + axis] // hop) % 2


def write_halves(sc_ref, step, from_ref, keep, send):
    half = keep.shape[0]
    bit = bit_of(sc_ref, step)
    keep[...] = from_ref[pl.ds(pl.multiple_of(bit * half, NODES), half)]
    send[...] = from_ref[pl.ds(pl.multiple_of((1 - bit) * half, NODES), half)]


def halve_kernel(step, sc, keep_in, got, keep, send, total):
    total[...] = keep_in[...] + got[...]
    write_halves(sc, step, total, keep, send)


def join_kernel_of(step, start, sc, value, got, out):
    half = value.shape[0] - start
    bit = bit_of(sc, step)
    if start:
        out[pl.ds(0, start)] = value[pl.ds(0, start)] + got[pl.ds(0, start)]
    out[pl.ds(pl.multiple_of(start + bit * half, NODES), half)] = value[pl.ds(start, half)]
    out[pl.ds(pl.multiple_of(start + (1 - bit) * half, NODES), half)] = got[pl.ds(start, half)]


def stack_kernel(sc, first, left, right, out):
    rows = first.shape[0]
    out[pl.ds(0, rows)] = first[...]
    out[pl.ds(rows, left.shape[0])] = left[...] + right[...]


def swap(value, step):
    axis = ("gx", "gy", "gz")[step[0]]
    return lax.ppermute(value, axis, [(i, i ^ step[1]) for i in range(lax.axis_size(axis))])


def rows_like(rows, width=128):
    return jax.ShapeDtypeStruct((rows, width), f32)


def halve(sc, sizes, keep, send):
    steps = halving_steps(sizes)
    got = swap(send, steps[0])
    for step in steps[1:]:
        keep, got = yield keep, got
        half = rows_like(keep.shape[0] // 2)
        keep, send = call(
            functools.partial(halve_kernel, step), "halve", (sc, keep, got), [half, half],
            [pltpu.VMEM(keep.shape, f32)],
        )
        got = swap(send, step)
    keep, got = yield keep, got
    return keep, got


class Background:
    def __init__(self):
        self.active = {}

    def add(self, name, steps):
        self.active[name] = [steps, None]

    def advance(self, entry, tied):
        steps, pending = entry
        try:
            entry[1] = next(steps) if pending is None else steps.send(tied)
        except StopIteration:
            entry[0] = None

    def beside(self, anchor):
        for entry in self.active.values():
            steps, pending = entry
            if steps is None:
                continue
            if pending is None:
                self.advance(entry, None)
            elif pending[1] is not None:
                anchor, tied = lax.optimization_barrier((anchor, pending))
                self.advance(entry, tied)
        return anchor

    def finish(self, name):
        entry = self.active[name]
        while entry[0] is not None:
            done = entry[1]
            if done is not None and done[1] is None:
                return done[0]
            self.advance(entry, done)
        return entry[1]


def on_device(state, cotangent, counts, edge_weights, node_in, node_out, biases):
    x_len, y_len, slots, nodes, width = state.shape
    rows = slots * nodes
    grid = (x_len, y_len, rows, width)
    axes = ("gx", "gy", "gz")
    sizes = tuple(lax.axis_size(a) for a in axes)
    trades = tuple(min(size - 1, 2) for size in sizes)
    nx, ny, nz = trades
    h0 = state.reshape(grid)
    g2 = cotangent.reshape(grid)
    sc = jnp.stack([counts[0]] + [lax.axis_index(a).astype(jnp.int32) for a in axes])

    def sds(shape, kind=f32):
        return jax.ShapeDtypeStruct(shape, kind)

    face_x = sds((y_len, rows, width))
    face_y = sds((x_len, rows, width))
    face_z = sds((x_len, y_len, width))
    face_outs = [face_y] * ny + [face_z] * nz
    full = sds(grid)
    full16 = sds(grid, bf16)
    full3 = sds((3,) + grid)
    inv = pltpu.VMEM((y_len, rows, width), f32)
    matmul = 2 * math.prod(grid) * width
    weights = (edge_weights, node_in, node_out, biases)

    in_place = {1 + len(weights): 0}

    def run(kernel, name, inputs, outs, scratch, flops, aliases):
        body = functools.partial(kernel, trades, sizes)
        return call(body, name, (sc, *weights, *inputs), outs, scratch, flops * matmul, aliases)

    def behind(value, others):
        return lax.optimization_barrier((value, others))[0]

    def trade(faces, axis):
        size = lax.axis_size(axis)
        got = [lax.ppermute(face, axis, pairs(size, kind)) for kind, face in reversed(list(enumerate(faces)))]
        return got[::-1]

    background = Background()

    pair = pltpu.VMEM((2,) + grid[1:], f32)

    def first_trade(kernel, name, inputs, scratch, flops):
        faces = call(functools.partial(kernel, trades, sizes), name, (sc, *inputs), [face_x] * nx, scratch, flops)
        return trade(faces, "gx"), faces

    def exchange(got_x, faces, work=None, held=(), early=None, early_held=()):
        fix = functools.partial(fix_y_kernel, trades)
        same = {1 + nx + k: k for k in range(ny)}
        faces_y = call(fix, "fix_y", (sc, *got_x, *faces[:ny]), [face_y] * ny, aliases=same)
        if early is not None:
            faces_y, early_held = lax.optimization_barrier((faces_y, early_held))
            keep, send = early(*early_held)
        got_y = trade(faces_y, "gy")
        if early is not None:
            got_y, (keep, send) = lax.optimization_barrier((got_y, (keep, send)))
            background.add("sums", halve(sc, sizes, keep, send))
            background.beside(got_y)
        fix = functools.partial(fix_z_kernel, trades)
        same = {1 + nx + ny + k: k for k in range(nz)}
        faces_z = call(fix, "fix_z", (sc, *got_x, *got_y[::-1], *faces[ny:]), [face_z] * nz, aliases=same)
        background.beside(faces_z)
        done = None
        if work is not None:
            faces_z, held = lax.optimization_barrier((faces_z, held))
            done = work(*held)
        got_z = trade(faces_z, "gz")
        got_z, done = lax.optimization_barrier((got_z, done))
        return (*got_x, *got_y, *got_z), done

    def to_slopes(half):
        return call(slope_kernel, "slopes", (sc, half), [full3], [], matmul, {1: 0})[0]

    def products(*held):
        return call(
            products_kernel, "nodes1_products", (sc, node_in, *held), [full, rows_like(3 * width + NODES)], [], 6 * matmul
        )

    got_x, faces_x = first_trade(first_face_kernel, "face0", (edge_weights, biases, h0), [], matmul // 8)
    sums, slopes0, *faces = call(
        functools.partial(first_kernel, trades, sizes), "edges0", (sc, edge_weights, biases, h0),
        [full, full3] + face_outs, [], 3 * matmul,
    )
    halo, slopes0 = exchange(got_x, faces, to_slopes, (slopes0,))
    inputs = (*weights, sums, h0, *halo)
    got_x, faces_x = first_trade(middle_face_kernel, "face1", inputs, [pair, inv], matmul // 4)
    _, scaled0, act0, slope0, h1, sums, slopes1, *faces = run(
        middle_kernel, "nodes0_edges1", (behind(sums, faces_x), h0, *halo),
        [full, full16, full16, full, full16, full, full3] + face_outs, [inv], 8, in_place,
    )
    halo, slopes1 = exchange(got_x, faces, to_slopes, (slopes1,))
    inputs = (*weights, sums, h1, g2, *halo)
    got_x, faces_x = first_trade(turn_face_kernel, "face2", inputs, [pair, inv], matmul // 4)
    _, scaled1, act1, dpn1, sums, *faces = run(
        turn_kernel, "nodes1_back", (behind(sums, faces_x), h1, g2, *halo), [full] + [full16] * 3 + [full] + face_outs,
        [inv], 7, in_place,
    )
    halo, (base, grads1) = exchange(got_x, faces, products, (h1, g2, scaled1, act1, dpn1))
    inputs = (*weights, sums, base, slopes1, slope0, *halo)
    got_x, faces_x = first_trade(join_face_kernel, "face3", inputs, [pair, inv], matmul // 4)
    edges1, grad_in, dpn0, sums, bias1, *faces = run(
        join_kernel, "edges1_back_nodes0_back", (behind(sums, faces_x), base, slopes1, slope0, *halo),
        [full, full16, full16, full, rows_like(NODES)] + face_outs, [inv], 9, in_place,
    )

    def layer_sums(*held):
        total = padded_rows(7 * width + 3 * NODES, sizes)
        return call(
            functools.partial(sums_kernel, sizes), "gradient_sums", (sc, *held), [rows_like(total // 2)] * 2,
            [pltpu.VMEM((total, width), f32)], 5 * matmul,
        )

    held = (h1, edges1, grad_in, h0, scaled0, act0, dpn0, grads1, bias1)
    halo, _ = exchange(got_x, faces, early=layer_sums, early_held=held)
    tail_rows = width + NODES
    edges, last = run(
        last_kernel, "edges0_back", (sums, h0, slopes0, *halo), [full, rows_like(tail_rows)], [], 6, in_place
    )
    keep, got = background.finish("sums")
    (value,) = call(stack_kernel, "stack", (sc, last, keep, got), [rows_like(tail_rows + keep.shape[0])])
    value, grad_in, dpn0, edges = lax.optimization_barrier((value, grad_in, dpn0, edges))
    (grad0,) = call(
        state_kernel, "state_grad", (sc, edge_weights, node_in, grad_in, dpn0, edges), [full16], [], 4 * matmul
    )
    for hop in reversed(hops(sizes[2])):
        value = value + swap(value, (2, hop))
        value, grad0 = lax.optimization_barrier((value, grad0))
    first, *rest = halving_steps(sizes)
    for step in reversed(rest):
        out = rows_like(2 * value.shape[0] - tail_rows)
        body = functools.partial(join_kernel_of, step, tail_rows)
        (value,) = call(body, "join", (sc, value, swap(value, step)), [out])
    layers_all = 3 * slots * sizes[2] // 4
    nodes_all = x_len * sizes[0] * y_len * sizes[1] * layers_all * nodes
    scale = 1.0 / math.sqrt(nodes_all)
    edge_grads, in_grads, out_grads, bias_grads = call(
        functools.partial(finish_kernel, scale, tail_rows, first), "finish",
        (sc, edge_weights, node_in, value, swap(value, first)),
        [sds(edge_weights.shape), sds(node_in.shape), sds(node_out.shape), sds(biases.shape)],
        [pltpu.VMEM((2 * value.shape[0] - tail_rows, width), f32)],
    )
    return grad0.reshape(state.shape), edge_grads, in_grads, out_grads, bias_grads


def solution(mesh):
    return jax.shard_map(
        on_device,
        mesh=mesh,
        in_specs=(
            P("gx", "gy", "gz", None, None),
            P("gx", "gy", "gz", None, None),
            P("gz"),
            P(),
            P(),
            P(),
            P(),
        ),
        out_specs=(P("gx", "gy", "gz", None, None), P(), P(), P(), P()),
        check_vma=False,
    )
```

```python
import functools
import math

import jax
import jax.numpy as jnp
from jax import lax
from jax.experimental import pallas as pl
from jax.experimental.pallas import tpu as pltpu
from jax.sharding import PartitionSpec as P

f32 = jnp.float32
bf16 = jnp.bfloat16
NODES = 8
VMEM_LIMIT = 12 * 1024 * 1024
VM = pl.BlockSpec(memory_space=pltpu.VMEM)
SM = pl.BlockSpec(memory_space=pltpu.SMEM)


def dot(left, right):
    return lax.dot_general(left, right, (((1,), (0,)), ((), ())), preferred_element_type=f32)


def dot_t(left, right):
    return lax.dot_general(left, right, (((0,), (0,)), ((), ())), preferred_element_type=f32)


def dot_rt(left, right):
    return lax.dot_general(left, right, (((1,), (1,)), ((), ())), preferred_element_type=f32)


def silu_half(half):
    th = jnp.tanh(half)
    prod = half * th
    return half + prod, (0.5 + 0.5 * th) * ((1.0 + half) - prod)


def split_cols(value):
    high = value.astype(bf16)
    low = (value - high.astype(f32)).astype(bf16)
    return jnp.concatenate([high, low], -1)


def up(value):
    return pltpu.roll(value, NODES - 1, 1)


def down(value):
    return pltpu.roll(value, 1, 1)


def flat(value):
    return value.reshape(-1, value.shape[-1])


def node_rows(value):
    return value.reshape(-1, NODES, value.shape[-1])


def row_ids():
    return lax.broadcasted_iota(jnp.int32, (1, NODES, 128), 1)


def couple_slots(plane, filled):
    count, rows, width = plane.shape
    slots = rows // NODES
    parts = plane.reshape(count, slots, NODES, width)
    ids = row_ids()
    done = []
    for s in range(slots):
        here = parts[:, s]
        if s + 1 < slots:
            take = (ids == NODES - 1) & (s + 1 < filled)
            here = here + jnp.where(take, up(parts[:, s + 1]), 0.0)
        if s > 0:
            here = here + jnp.where(ids == 0, down(parts[:, s - 1]), 0.0)
            here = jnp.where(s < filled, here, 0.0)
        done.append(here[:, None])
    return jnp.concatenate(done, 1).reshape(plane.shape)


def elements(x_len, y_len, body, unroll=1):
    ey = y_len // NODES
    total = (x_len // NODES) * ey

    def step(e, carry):
        x0 = pl.multiple_of((e // ey) * NODES, NODES)
        y0 = pl.multiple_of((e % ey) * NODES, NODES)
        body(x0, y0)
        return carry

    lax.fori_loop(0, total, step, 0, unroll=unroll if total % unroll == 0 else 1)


def edge_dots(parts, weight, weight_both):
    rows, width = parts[0].shape[1:]
    if len(parts) == 2:
        return dot(flat(jnp.concatenate(parts, 0)), weight).reshape(-1, rows, width)
    both = dot(jnp.concatenate([flat(parts[0]), flat(parts[2])], -1), weight_both)
    between = dot(flat(parts[1]), weight).reshape(-1, rows, width)
    first, last = (both[:, k : k + width].reshape(-1, rows, width) for k in (0, width))
    return jnp.concatenate([first, between, last], 0)


def edges_forward(h_ref, w_one, half_bias, filled, sum_ref, half_ref):
    x_len, y_len, rows, width = h_ref.shape
    blank = jnp.zeros_like(w_one)
    w_both = jnp.concatenate([jnp.concatenate([w_one, blank], 1), jnp.concatenate([blank, w_one], 1)], 0)
    inner = row_ids() < NODES - 1

    def body(x0, y0):
        ys = pl.ds(y0, NODES)
        prev = None
        here = h_ref[x0, ys].astype(f32)
        for i in range(NODES):
            parts = []
            nxt = None
            if i < NODES - 1:
                nxt = h_ref[x0 + i + 1, ys].astype(f32)
                parts.append((nxt - here).astype(bf16))
            parts.append((here[1:] - here[:-1]).astype(bf16))
            cols = node_rows(here)
            parts.append((up(cols) - cols).reshape(here.shape).astype(bf16))
            half = edge_dots(parts, w_one, w_both) + half_bias
            act = (half + half * jnp.tanh(half)).astype(bf16).astype(f32)
            at = 0
            total = prev
            prev = None
            if i < NODES - 1:
                prev = act[:NODES]
                total = -prev if total is None else total - prev
                half_ref[0, x0 + i, ys] = half[:NODES]
                at = NODES
            along_y = act[at : at + NODES - 1]
            half_ref[1, x0 + i, pl.ds(y0, NODES - 1)] = half[at : at + NODES - 1]
            at += NODES - 1
            along_z = jnp.where(inner, node_rows(act[at:]), 0.0)
            half_ref[2, x0 + i, ys] = half[at:]
            total = total + (down(along_z) - along_z).reshape(here.shape)
            total = jnp.concatenate(
                [
                    total[:1] - along_y[:1],
                    total[1:-1] + (along_y[:-1] - along_y[1:]),
                    total[-1:] + along_y[-1:],
                ],
                0,
            )
            sum_ref[x0 + i, ys] = couple_slots(total, filled)
            here = nxt

    elements(x_len, y_len, body, 2)


def slope_kernel(sc, half_in, slope_out):
    inner = row_ids() < NODES - 1

    def step(x, carry):
        for k in range(3):
            slope = silu_half(half_in[k, x])[1]
            if k == 2:
                slope = jnp.where(inner, node_rows(slope), 0.0).reshape(slope.shape)
            slope_out[k, x] = slope
        return carry

    lax.fori_loop(0, half_in.shape[1], step, 0)


def couple_columns(sum_ref):
    x_len, y_len = sum_ref.shape[:2]
    for cut in range(NODES, x_len, NODES):
        both = sum_ref[cut - 1] + sum_ref[cut]
        sum_ref[cut - 1] = both
        sum_ref[cut] = both
    for cut in range(NODES, y_len, NODES):
        both = sum_ref[:, cut - 1] + sum_ref[:, cut]
        sum_ref[:, cut - 1] = both
        sum_ref[:, cut] = both


def face_place(sc_ref, axis, kind, last):
    return jnp.where((sc_ref[1 + axis] + kind) % 2 == 0, last, 0)


def end_rows(values, filled, take_top):
    picked = values(0)
    slots = values.slots
    for s in range(slots):
        picked = jnp.where(take_top & (filled == s + 1), values(s * NODES + NODES - 1), picked)
    return picked


class RowReader:
    def __init__(self, slots, read):
        self.slots = slots
        self.read = read

    def __call__(self, row):
        return self.read(row)


def takes_top(sc_ref, kind):
    return (sc_ref[3] + kind) % 2 == 0


def write_faces(sc_ref, sum_ref, faces, counts):
    x_len, y_len, rows, width = sum_ref.shape
    nx, ny, nz = counts
    reader = RowReader(rows // NODES, lambda row: sum_ref[:, :, row])
    for kind in range(ny):
        faces[kind][...] = sum_ref[:, face_place(sc_ref, 1, kind, y_len - 1)]
    for kind in range(nz):
        faces[ny + kind][...] = end_rows(reader, sc_ref[0], takes_top(sc_ref, kind))


def add_halo(sc_ref, halo, into_ref, counts):
    x_len, y_len, rows, width = into_ref.shape
    nx, ny, nz = counts
    for kind in range(nx):
        into_ref[face_place(sc_ref, 0, kind, x_len - 1)] += halo[kind][...]
    for kind in range(ny):
        into_ref[:, face_place(sc_ref, 1, kind, y_len - 1)] += halo[nx + kind][...]
    if nz:
        got = [halo[nx + ny + kind][...] for kind in range(nz)]
        tops = [takes_top(sc_ref, kind) for kind in range(nz)]
        from_below = sum(jnp.where(top, 0.0, value) for top, value in zip(tops, got))
        from_above = sum(jnp.where(top, value, 0.0) for top, value in zip(tops, got))
        into_ref[:, :, 0] += from_below
        for s in range(rows // NODES):
            into_ref[:, :, s * NODES + NODES - 1] += jnp.where(sc_ref[0] == s + 1, from_above, 0.0)


def fix_y_kernel(counts, sc_ref, *refs):
    nx, ny, nz = counts
    got, faces, outs = refs[:nx], refs[nx : nx + ny], refs[nx + ny :]
    x_len = faces[0].shape[0]
    for kind in range(nx):
        place = face_place(sc_ref, 0, kind, x_len - 1)
        for k in range(ny):
            y_len = got[kind].shape[0]
            outs[k][place] += got[kind][face_place(sc_ref, 1, k, y_len - 1)]


def fix_z_kernel(counts, sc_ref, *refs):
    nx, ny, nz = counts
    got_x, refs = refs[:nx], refs[nx:]
    got_y, refs = refs[:ny][::-1], refs[ny:]
    faces, outs = refs[:nz], refs[nz:]
    x_len, y_len, width = faces[0].shape
    for k in range(nz):
        top = takes_top(sc_ref, k)
        for kind in range(nx):
            ref = got_x[kind]
            reader = RowReader(ref.shape[1] // NODES, lambda row, ref=ref: ref[:, row])
            outs[k][face_place(sc_ref, 0, kind, x_len - 1)] += end_rows(reader, sc_ref[0], top)
        for kind in range(ny):
            ref = got_y[kind]
            reader = RowReader(ref.shape[1] // NODES, lambda row, ref=ref: ref[:, row])
            add = end_rows(reader, sc_ref[0], top)
            first = face_place(sc_ref, 1, kind, 1) == 0
            outs[k][:, 0] += jnp.where(first, add, 0.0)
            outs[k][:, y_len - 1] += jnp.where(first, 0.0, add)


def write_inverse(sc_ref, inv_ref, sizes):
    y_len, rows, width = inv_ref.shape
    filled, at_y, at_z = sc_ref[0], sc_ref[2], sc_ref[3]
    ids = lax.broadcasted_iota(jnp.int32, (rows, width), 0)
    node = ids % NODES
    low = (node == 0) & ((ids >= NODES) | (at_z > 0))
    high = (node == NODES - 1) & ((ids < (filled - 1) * NODES) | (at_z < sizes[2] - 1))
    along_z = jnp.where(low | high, 0.5, 1.0).astype(f32)
    for y in range(y_len):
        inv_ref[y] = along_z * end_factor(y, y_len, at_y, sizes[1])


def end_factor(place, length, position, size):
    whole = place + position * length
    low = (place % NODES == 0) & (whole > 0)
    high = (place % NODES == NODES - 1) & (whole < length * size - 1)
    return jnp.where(low | high, 0.5, 1.0).astype(f32)


def chunk_of(x_len):
    return 2 * NODES if x_len % (2 * NODES) == 0 else NODES


def scale_planes(sc_ref, inv_ref, x, block, x_len, size_x):
    inv = inv_ref[...]
    parts = [block[c] * (inv * end_factor(x + c, x_len, sc_ref[1], size_x)) for c in range(block.shape[0])]
    return jnp.stack(parts, 0)


def node_forward(scaled, feat, weights, layer):
    edge_w, node_in, node_out, biases = weights
    pair = split_cols(scaled)
    w_two = edge_w[layer, 1]
    joined = jnp.concatenate([feat, dot(pair, jnp.concatenate([w_two, w_two], 0)).astype(bf16)], -1)
    half = jnp.bfloat16(0.5)
    act, slope = silu_half(dot(joined, node_in[layer] * half) + 0.5 * biases[layer, pl.ds(1, 1)])
    return pair[:, :128], act.astype(bf16), slope


def node_slopes(grad, slope, weights, layer):
    return (dot_rt(grad, weights[2][layer]) * slope).astype(bf16)


def node_share(sc_ref, x, inv_ref, size_x, dpn, weights, layer, sum_ref):
    shape = (chunk_of(sum_ref.shape[0]),) + sum_ref.shape[1:]
    dx = dot_rt(dpn, weights[1][layer, pl.ds(128, 128)]).reshape(shape)
    share = scale_planes(sc_ref, inv_ref, x, dx, sum_ref.shape[0], size_x)
    joined = couple_slots(share.reshape((-1,) + shape[2:]), sc_ref[0])
    sum_ref[pl.ds(x, shape[0])] = joined.reshape(shape)


def node_products(grad, feat, scaled, act, dpn, grads):
    grads[pl.ds(0, 128)] += dot_t(act, grad)
    both = dot_t(dpn, jnp.concatenate([feat, scaled], -1))
    grads[pl.ds(128, 128)] += both[:, :128]
    grads[pl.ds(256, 128)] += both[:, 128:]
    grads[pl.ds(384, NODES)] += jnp.sum(dpn.astype(f32).reshape(-1, NODES, 128), 0)


def couple_plane(plane):
    y_len = plane.shape[0]
    parts = [plane[y] for y in range(y_len)]
    for cut in range(NODES, y_len, NODES):
        both = parts[cut - 1] + parts[cut]
        parts[cut - 1] = parts[cut] = both
    return jnp.stack(parts, 0)


def along_y(plane, combine):
    return [
        combine(plane[y : y + NODES - 1], plane[y + 1 : y + NODES], y) for y in range(0, plane.shape[0], NODES)
    ]


def spread_plane(sign, edge_x, edges_y, edge_z):
    total = sign * edge_x + (down(edge_z) - edge_z).reshape(edge_x.shape)
    parts = []
    for k, edge in enumerate(edges_y):
        here = total[k * NODES : (k + 1) * NODES]
        parts += [here[:1] - edge[:1], here[1:-1] + (edge[:-1] - edge[1:]), here[-1:] + edge[-1:]]
    return jnp.concatenate(parts, 0)


def plane_forward(low, high, at_high, w_one, half_bias, filled):
    y_len, rows, width = low.shape
    here = jnp.where(at_high, high, low)
    cols = node_rows(here)
    parts = [(high - low).astype(bf16)]
    parts += along_y(here, lambda lower, upper, y: (upper - lower).astype(bf16))
    parts.append((up(cols) - cols).reshape(here.shape).astype(bf16))
    half = dot(flat(jnp.concatenate(parts, 0)), w_one).reshape(-1, rows, width) + half_bias
    act = silu_half(half)[0].astype(bf16).astype(f32)
    at = y_len
    edges_y = []
    for _ in range(y_len // NODES):
        edges_y.append(act[at : at + NODES - 1])
        at += NODES - 1
    edge_z = jnp.where(row_ids() < NODES - 1, node_rows(act[at:]), 0.0)
    total = spread_plane(jnp.where(at_high, 1.0, -1.0), act[:y_len], edges_y, edge_z)
    return couple_plane(couple_slots(total, filled))


def plane_backward(low, high, at_high, slope_x, slope_y, slope_z):
    here = jnp.where(at_high, high, low)
    cols = node_rows(here)
    edge_x = ((high - low) * slope_x).astype(bf16).astype(f32)
    edges_y = along_y(
        here, lambda lower, upper, y: ((upper - lower) * slope_y[y : y + NODES - 1]).astype(bf16).astype(f32)
    )
    edge_z = ((up(cols) - cols) * node_rows(slope_z)).astype(bf16).astype(f32)
    return spread_plane(jnp.where(at_high, 1.0, -1.0), edge_x, edges_y, edge_z)


def face_planes(sc_ref, kind, x_len):
    place = face_place(sc_ref, 0, kind, x_len - 1)
    at_high = place > 0
    return place, jnp.where(at_high, x_len - 2, 0), at_high


def halo_planes(sc_ref, from_ref, halo, kind, start, into_ref, counts):
    x_len, y_len, rows, width = from_ref.shape
    nx, ny, nz = counts
    for c in range(2):
        into_ref[c] = from_ref[start + c]
    into_ref[face_place(sc_ref, 0, kind, x_len - 1) - start] += halo[kind][...]
    for c in range(2):
        for k in range(ny):
            into_ref[c, face_place(sc_ref, 1, k, y_len - 1)] += halo[nx + k][start + c]
        for k in range(nz):
            got = halo[nx + ny + k][start + c]
            top = takes_top(sc_ref, k)
            into_ref[c, :, 0] += jnp.where(top, 0.0, got)
            for s in range(rows // NODES):
                into_ref[c, :, s * NODES + NODES - 1] += jnp.where(top & (sc_ref[0] == s + 1), got, 0.0)


def edges_backward(q_ref, slope_ref, edge_ref, bias_acc):
    x_len, y_len, rows, width = q_ref.shape

    def body(x0, y0):
        ys = pl.ds(y0, NODES)
        prev = None
        here = q_ref[x0, ys]
        bias = jnp.zeros((NODES, width), f32)
        for i in range(NODES):
            total = prev
            prev = None
            nxt = None
            if i < NODES - 1:
                nxt = q_ref[x0 + i + 1, ys]
                prev = ((nxt - here) * slope_ref[0, x0 + i, ys]).astype(bf16).astype(f32)
                total = -prev if total is None else total - prev
                bias = bias + jnp.sum(node_rows(prev), 0)
            along_y = (here[1:] - here[:-1]) * slope_ref[1, x0 + i, pl.ds(y0, NODES - 1)]
            along_y = along_y.astype(bf16).astype(f32)
            cols = node_rows(here)
            along_z = (up(cols) - cols) * node_rows(slope_ref[2, x0 + i, ys])
            along_z = along_z.astype(bf16).astype(f32)
            bias = bias + jnp.sum(node_rows(along_y), 0) + jnp.sum(along_z, 0)
            total = total + (down(along_z) - along_z).reshape(here.shape)
            total = jnp.concatenate(
                [
                    total[:1] - along_y[:1],
                    total[1:-1] + (along_y[:-1] - along_y[1:]),
                    total[-1:] + along_y[-1:],
                ],
                0,
            )
            edge_ref[x0 + i, ys] = total
            here = nxt
        bias_acc[...] += bias

    elements(x_len, y_len, body)


def planes(count, body):
    chunk = chunk_of(count)

    def step(c, carry):
        body(pl.multiple_of(c * chunk, chunk))
        return carry

    lax.fori_loop(0, count // chunk, step, 0)


def half_weights(weights, layer):
    edge_w, node_in, node_out, biases = weights
    return edge_w[layer, 0] * jnp.bfloat16(0.5), 0.5 * biases[layer, pl.ds(0, 1)]


def first_kernel(counts, sizes, sc, edge_w, biases, h, sums, slopes, *faces):
    w_one, bias = half_weights((edge_w, None, None, biases), 0)
    edges_forward(h, w_one, bias, sc[0], sums, slopes)
    couple_columns(sums)
    write_faces(sc, sums, faces, counts)


def first_face_kernel(counts, sizes, sc, edge_w, biases, h, *faces):
    w_one, bias = half_weights((edge_w, None, None, biases), 0)
    for kind, face in enumerate(faces):
        place, start, at_high = face_planes(sc, kind, h.shape[0])
        face[...] = plane_forward(
            h[start].astype(f32), h[start + 1].astype(f32), at_high, w_one, bias, sc[0]
        )


def middle_face_kernel(counts, sizes, sc, edge_w, node_in, node_out, biases, sums_in, h, *refs):
    weights = (edge_w, node_in, node_out, biases)
    n = sum(counts)
    halo, faces, (pair, inv) = refs[:n], refs[n:-2], refs[-2:]
    write_inverse(sc, inv, sizes)
    w_one, bias = half_weights(weights, 1)
    x_len = h.shape[0]
    for kind, face in enumerate(faces):
        place, start, at_high = face_planes(sc, kind, x_len)
        halo_planes(sc, sums_in, halo, kind, start, pair, counts)
        sums_at = flat(scale_planes(sc, inv, start, pair[...], x_len, sizes[0]))
        feat = flat(h[pl.ds(start, 2)])
        scaled, act, slope = node_forward(sums_at, feat, weights, 0)
        moved = (feat.astype(f32) + dot(act, node_out[0])).astype(bf16).astype(f32).reshape(pair.shape)
        face[...] = plane_forward(moved[0], moved[1], at_high, w_one, bias, sc[0])


def face_share(sc, sizes, inv, place, x_len, grad, slope, weights, layer, shape):
    dpn = node_slopes(grad, slope, weights, layer)
    dx = dot_rt(dpn, weights[1][layer, pl.ds(128, 128)]).reshape((1,) + shape)
    share = scale_planes(sc, inv, place, dx, x_len, sizes[0])
    return couple_plane(couple_slots(share[0], sc[0]))


def turn_face_kernel(counts, sizes, sc, edge_w, node_in, node_out, biases, sums_in, h, g_ref, *refs):
    weights = (edge_w, node_in, node_out, biases)
    n = sum(counts)
    halo, faces, (pair, inv) = refs[:n], refs[n:-2], refs[-2:]
    write_inverse(sc, inv, sizes)
    x_len, shape = h.shape[0], h.shape[1:]
    live = (lax.broadcasted_iota(jnp.int32, (1, h.shape[2], 128), 1) < sc[0] * NODES).astype(f32)
    for kind, face in enumerate(faces):
        place, start, at_high = face_planes(sc, kind, x_len)
        halo_planes(sc, sums_in, halo, kind, start, pair, counts)
        plane = pair[place - start][None]
        sums_at = flat(scale_planes(sc, inv, place, plane, x_len, sizes[0]))
        scaled, act, slope = node_forward(sums_at, flat(h[place]), weights, 1)
        grad = flat((g_ref[place].astype(f32) * live).astype(bf16))
        face[...] = face_share(sc, sizes, inv, place, x_len, grad, slope, weights, 1, shape)


def join_face_kernel(counts, sizes, sc, edge_w, node_in, node_out, biases, sums_in, base_in, slopes, slope0, *refs):
    weights = (edge_w, node_in, node_out, biases)
    n = sum(counts)
    halo, faces, (pair, inv) = refs[:n], refs[n:-2], refs[-2:]
    write_inverse(sc, inv, sizes)
    x_len, shape = base_in.shape[0], base_in.shape[1:]
    w_two, w_one = twice(edge_w[1, 1]), twice(edge_w[1, 0])
    for kind, face in enumerate(faces):
        place, start, at_high = face_planes(sc, kind, x_len)
        halo_planes(sc, sums_in, halo, kind, start, pair, counts)
        q = dot_rt(split_cols(flat(pair[...])), w_two).reshape(pair.shape)
        edge = plane_backward(q[0], q[1], at_high, slopes[0, start], slopes[1, place], slopes[2, place])
        grad = (flat(base_in[place]) + dot_rt(split_cols(flat(edge)), w_one)).astype(bf16)
        face[...] = face_share(sc, sizes, inv, place, x_len, grad, flat(slope0[place]), weights, 0, shape)


def twice(weight):
    return jnp.concatenate([weight, weight], 1)


def middle_kernel(counts, sizes, sc, edge_w, node_in, node_out, biases, sums_in, h, *refs):
    weights = (edge_w, node_in, node_out, biases)
    n = sum(counts)
    halo, refs = refs[:n], refs[n:]
    work, scaled_ref, act_ref, slope_ref, next_ref, sums, slopes = refs[:7]
    faces, inv = refs[7:-1], refs[-1]
    add_halo(sc, halo, work, counts)
    write_inverse(sc, inv, sizes)
    shape = (chunk_of(h.shape[0]),) + h.shape[1:]

    def body(x):
        at = pl.ds(x, chunk_of(h.shape[0]))
        sums_at = flat(scale_planes(sc, inv, x, work[at], h.shape[0], sizes[0]))
        scaled, act, slope = node_forward(sums_at, flat(h[at]), weights, 0)
        scaled_ref[at] = scaled.reshape(shape)
        act_ref[at] = act.reshape(shape)
        slope_ref[at] = slope.reshape(shape)
        moved = flat(h[at]).astype(f32) + dot(act, node_out[0])
        next_ref[at] = moved.astype(bf16).reshape(shape)

    planes(h.shape[0], body)
    w_one, bias = half_weights(weights, 1)
    edges_forward(next_ref, w_one, bias, sc[0], sums, slopes)
    couple_columns(sums)
    write_faces(sc, sums, faces, counts)


def turn_kernel(counts, sizes, sc, edge_w, node_in, node_out, biases, sums_in, h, g_ref, *refs):
    weights = (edge_w, node_in, node_out, biases)
    n = sum(counts)
    halo, refs = refs[:n], refs[n:]
    work, scaled_ref, act_ref, dpn_ref, sums = refs[:5]
    faces, inv = refs[5:-1], refs[-1]
    add_halo(sc, halo, work, counts)
    write_inverse(sc, inv, sizes)
    shape = (chunk_of(h.shape[0]),) + h.shape[1:]
    live = live_rows(sc, h)

    def body(x):
        at = pl.ds(x, chunk_of(h.shape[0]))
        sums_at = flat(scale_planes(sc, inv, x, work[at], h.shape[0], sizes[0]))
        scaled, act, slope = node_forward(sums_at, flat(h[at]), weights, 1)
        scaled_ref[at] = scaled.reshape(shape)
        act_ref[at] = act.reshape(shape)
        grad = flat((g_ref[at].astype(f32) * live).astype(bf16))
        dpn = node_slopes(grad, slope, weights, 1)
        dpn_ref[at] = dpn.reshape(shape)
        node_share(sc, x, inv, sizes[0], dpn, weights, 1, sums)

    planes(h.shape[0], body)
    couple_columns(sums)
    write_faces(sc, sums, faces, counts)


def live_rows(sc, h):
    return (lax.broadcasted_iota(jnp.int32, (1, 1, h.shape[2], 128), 2) < sc[0] * NODES).astype(f32)


def products_kernel(sc, node_in, h, g_ref, scaled, act, dpn, base, grads):
    grads[...] = jnp.zeros_like(grads)
    live = live_rows(sc, h)

    def body(x):
        at = pl.ds(x, chunk_of(h.shape[0]))
        grad = (g_ref[at].astype(f32) * live).astype(bf16)
        node_products(flat(grad), flat(h[at]), flat(scaled[at]), flat(act[at]), flat(dpn[at]), grads)
        dx = dot_rt(flat(dpn[at]), node_in[1, pl.ds(0, 128)])
        base[at] = grad.astype(f32) + dx.reshape(grad.shape)

    planes(h.shape[0], body)


def edge_parts(counts, sc, weights, layer, halo, slopes, work, bias):
    add_halo(sc, halo, work, counts)
    shape = (chunk_of(work.shape[0]),) + work.shape[1:]
    w_two = twice(weights[0][layer, 1])

    def to_q(x):
        at = pl.ds(x, chunk_of(work.shape[0]))
        work[at] = dot_rt(split_cols(flat(work[at])), w_two).reshape(shape)

    planes(work.shape[0], to_q)
    edges_backward(work, slopes, work, bias)


def edge_product(h, x, pair, grads, row):
    both = dot_t(flat(h[pl.ds(x, chunk_of(h.shape[0]))]), pair)
    grads[pl.ds(row, 128)] += both[:, :128] + both[:, 128:]


def join_kernel(counts, sizes, sc, edge_w, node_in, node_out, biases, sums_in, base_in, slopes, slope0, *refs):
    weights = (edge_w, node_in, node_out, biases)
    n = sum(counts)
    halo, refs = refs[:n], refs[n:]
    work, grad_ref, dpn_ref, sums, bias = refs[:5]
    faces, inv = refs[5:-1], refs[-1]
    write_inverse(sc, inv, sizes)
    bias[...] = jnp.zeros_like(bias)
    edge_parts(counts, sc, weights, 1, halo, slopes, work, bias)
    w_one = twice(edge_w[1, 0])
    x_len = work.shape[0]
    shape = (chunk_of(x_len),) + work.shape[1:]

    def body(x):
        at = pl.ds(x, chunk_of(x_len))
        pair = split_cols(flat(work[at]))
        grad = (flat(base_in[at]) + dot_rt(pair, w_one)).astype(bf16)
        dpn = node_slopes(grad, flat(slope0[at]), weights, 0)
        grad_ref[at] = grad.reshape(shape)
        dpn_ref[at] = dpn.reshape(shape)
        node_share(sc, x, inv, sizes[0], dpn, weights, 0, sums)

    planes(x_len, body)
    couple_columns(sums)
    write_faces(sc, sums, faces, counts)


def sums_kernel(sizes, sc, h, edges, grad, h0, scaled0, act0, dpn0, grads1, bias, keep, send, grads):
    grads[...] = jnp.zeros_like(grads)
    row = 384 + NODES
    grads[pl.ds(row + 128, NODES)] = bias[...]
    grads[pl.ds(row + 128 + NODES, grads1.shape[0])] = grads1[...]

    def body(x):
        at = pl.ds(x, chunk_of(h.shape[0]))
        edge_product(h, x, split_cols(flat(edges[at])), grads, row)
        node_products(flat(grad[at]), flat(h0[at]), flat(scaled0[at]), flat(act0[at]), flat(dpn0[at]), grads)

    planes(h.shape[0], body)
    write_halves(sc, halving_steps(sizes)[0], grads, keep, send)


def last_kernel(counts, sizes, sc, edge_w, node_in, node_out, biases, sums_in, h, slopes, *refs):
    n = sum(counts)
    halo, (edges, grads, second) = refs[:n], refs[n:]
    grads[...] = jnp.zeros_like(grads)
    for k, step in enumerate(halving_steps(sizes)):
        second[k] = jnp.full(second.shape[1:], bit_of(sc, step), jnp.int32)
    edge_parts(counts, sc, (edge_w,), 0, halo, slopes, edges, grads.at[pl.ds(128, NODES)])

    def body(x):
        edge_product(h, x, split_cols(flat(edges[pl.ds(x, chunk_of(h.shape[0]))])), grads, 0)

    planes(h.shape[0], body)


def state_kernel(sc, edge_w, node_in, grad_in, dpn, edges, grad_ref):
    shape = (chunk_of(edges.shape[0]),) + edges.shape[1:]
    weight = jnp.concatenate([twice(edge_w[0, 0]), node_in[0, pl.ds(0, 128)]], 1)

    def body(x):
        at = pl.ds(x, chunk_of(edges.shape[0]))
        parts = jnp.concatenate([split_cols(flat(edges[at])), flat(dpn[at])], -1)
        grad_ref[at] = (flat(grad_in[at]).astype(f32) + dot_rt(parts, weight)).astype(bf16).reshape(shape)

    planes(edges.shape[0], body)


def finish_kernel(scale, last_rows, step, sc, edge_w, node_in, value, got, *refs):
    edge_grads, in_grads, out_grads, bias_grads, both = refs
    width = edge_w.shape[-1]
    join_kernel_of(step, last_rows, sc, value, got, both)

    def rows_of(part, start, count=width):
        ref, offset = part
        return ref[pl.ds(offset + start, count)] * scale

    def bias_of(part, start):
        return jnp.sum(rows_of(part, start, NODES), 0, keepdims=True)

    end = 3 * width
    last, sum0 = (both, 0), (both, last_rows)
    sum1 = (both, last_rows + 512 + 2 * NODES)
    firsts = ((last, 0), (sum0, end + NODES))
    for layer, part in enumerate((sum0, sum1)):
        out_grads[layer] = rows_of(part, 0)
        in_grads[layer, pl.ds(0, width)] = rows_of(part, width).T
        bias_grads[layer, pl.ds(1, 1)] = bias_of(part, end)
        source, start = firsts[layer]
        edge_grads[layer, 0] = rows_of(source, start)
        bias_grads[layer, pl.ds(0, 1)] = bias_of(source, start + width)
        mixed = rows_of(part, 2 * width).T
        high = mixed.astype(bf16)
        low = (mixed - high.astype(f32)).astype(bf16)
        lower = node_in[layer, pl.ds(width, width)]
        edge_grads[layer, 1] = dot_rt(high, lower) + dot_rt(low, lower)
        w_two = edge_w[layer, 1]
        in_grads[layer, pl.ds(width, width)] = dot_t(w_two, high) + dot_t(w_two, low)


def call(kernel, name, inputs, outs, scratch=(), flops=0, aliases=None):
    total = sum(math.prod(o.shape) * o.dtype.itemsize for o in outs)
    total += sum(math.prod(i.shape) * i.dtype.itemsize for i in inputs)
    return pl.pallas_call(
        kernel,
        name=name,
        out_shape=tuple(outs),
        in_specs=[SM] + [VM] * (len(inputs) - 1),
        out_specs=tuple([VM] * len(outs)),
        scratch_shapes=list(scratch),
        input_output_aliases=aliases or {},
        compiler_params=pltpu.CompilerParams(vmem_limit_bytes=VMEM_LIMIT),
        cost_estimate=pl.CostEstimate(flops=flops, bytes_accessed=total, transcendentals=0),
    )(*inputs)


def pairs(size, kind):
    return [
        pair for low in range(kind, size - 1, 2) for pair in ((low, low + 1), (low + 1, low))
    ]


def hops(size):
    found = []
    hop = 1
    while hop < size:
        found.append(hop)
        hop *= 2
    return found


def halving_steps(sizes):
    steps = [(1, hop) for hop in hops(sizes[1])[:1]]
    steps += [(0, hop) for hop in hops(sizes[0])]
    return steps + [(1, hop) for hop in hops(sizes[1])[1:]]


def padded_rows(rows, sizes):
    unit = NODES << len(halving_steps(sizes))
    return -(-rows // unit) * unit


def bit_of(sc_ref, step):
    axis, hop = step
    return (sc_ref[1 + axis] // hop) % 2


def write_halves(sc_ref, step, from_ref, keep, send):
    half = keep.shape[0]
    bit = bit_of(sc_ref, step)
    keep[...] = from_ref[pl.ds(pl.multiple_of(bit * half, NODES), half)]
    send[...] = from_ref[pl.ds(pl.multiple_of((1 - bit) * half, NODES), half)]


def halve_kernel(step, sc, keep_in, got, keep, send, total):
    total[...] = keep_in[...] + got[...]
    write_halves(sc, step, total, keep, send)


def join_kernel_of(step, start, sc, value, got, out):
    half = value.shape[0] - start
    bit = bit_of(sc, step)
    if start:
        out[pl.ds(0, start)] = value[pl.ds(0, start)] + got[pl.ds(0, start)]
    out[pl.ds(pl.multiple_of(start + bit * half, NODES), half)] = value[pl.ds(start, half)]
    out[pl.ds(pl.multiple_of(start + (1 - bit) * half, NODES), half)] = got[pl.ds(start, half)]


def swap(value, step):
    axis = ("gx", "gy", "gz")[step[0]]
    return lax.ppermute(value, axis, [(i, i ^ step[1]) for i in range(lax.axis_size(axis))])


def rows_like(rows, width=128):
    return jax.ShapeDtypeStruct((rows, width), f32)


def halve(sc, sizes, keep, send):
    steps = halving_steps(sizes)
    got = swap(send, steps[0])
    for step in steps[1:]:
        keep, got = yield keep, got
        half = rows_like(keep.shape[0] // 2)
        keep, send = call(
            functools.partial(halve_kernel, step), "halve", (sc, keep, got), [half, half],
            [pltpu.VMEM(keep.shape, f32)],
        )
        got = swap(send, step)
    keep, got = yield keep, got
    return keep, got


class Background:
    def __init__(self):
        self.active = {}

    def add(self, name, steps):
        self.active[name] = [steps, None]

    def advance(self, entry, tied):
        steps, pending = entry
        try:
            entry[1] = next(steps) if pending is None else steps.send(tied)
        except StopIteration:
            entry[0] = None

    def beside(self, anchor):
        for entry in self.active.values():
            steps, pending = entry
            if steps is None:
                continue
            if pending is None:
                self.advance(entry, None)
            elif pending[1] is not None:
                anchor, tied = lax.optimization_barrier((anchor, pending))
                self.advance(entry, tied)
        return anchor

    def finish(self, name):
        entry = self.active[name]
        while entry[0] is not None:
            done = entry[1]
            if done is not None and done[1] is None:
                return done[0]
            self.advance(entry, done)
        return entry[1]


def on_device(state, cotangent, counts, edge_weights, node_in, node_out, biases):
    x_len, y_len, slots, nodes, width = state.shape
    rows = slots * nodes
    grid = (x_len, y_len, rows, width)
    axes = ("gx", "gy", "gz")
    sizes = tuple(lax.axis_size(a) for a in axes)
    trades = tuple(min(size - 1, 2) for size in sizes)
    nx, ny, nz = trades
    h0 = state.reshape(grid)
    g2 = cotangent.reshape(grid)
    sc = jnp.stack([counts[0]] + [lax.axis_index(a).astype(jnp.int32) for a in axes])

    def sds(shape, kind=f32):
        return jax.ShapeDtypeStruct(shape, kind)

    face_x = sds((y_len, rows, width))
    face_y = sds((x_len, rows, width))
    face_z = sds((x_len, y_len, width))
    face_outs = [face_y] * ny + [face_z] * nz
    full = sds(grid)
    full16 = sds(grid, bf16)
    full3 = sds((3,) + grid)
    inv = pltpu.VMEM((y_len, rows, width), f32)
    matmul = 2 * math.prod(grid) * width
    weights = (edge_weights, node_in, node_out, biases)

    in_place = {1 + len(weights): 0}

    def run(kernel, name, inputs, outs, scratch, flops, aliases):
        body = functools.partial(kernel, trades, sizes)
        return call(body, name, (sc, *weights, *inputs), outs, scratch, flops * matmul, aliases)

    def behind(value, others):
        return lax.optimization_barrier((value, others))[0]

    def trade(faces, axis):
        size = lax.axis_size(axis)
        got = [lax.ppermute(face, axis, pairs(size, kind)) for kind, face in reversed(list(enumerate(faces)))]
        return got[::-1]

    background = Background()

    pair = pltpu.VMEM((2,) + grid[1:], f32)

    def first_trade(kernel, name, inputs, scratch, flops):
        faces = call(functools.partial(kernel, trades, sizes), name, (sc, *inputs), [face_x] * nx, scratch, flops)
        return trade(faces, "gx"), faces

    def exchange(got_x, faces, work=None, held=(), early=None, early_held=()):
        fix = functools.partial(fix_y_kernel, trades)
        same = {1 + nx + k: k for k in range(ny)}
        faces_y = call(fix, "fix_y", (sc, *got_x, *faces[:ny]), [face_y] * ny, aliases=same)
        if early is not None:
            faces_y, early_held = lax.optimization_barrier((faces_y, early_held))
            keep, send = early(*early_held)
        got_y = trade(faces_y, "gy")
        if early is not None:
            got_y, (keep, send) = lax.optimization_barrier((got_y, (keep, send)))
            background.add("sums", halve(sc, sizes, keep, send))
            background.beside(got_y)
        fix = functools.partial(fix_z_kernel, trades)
        same = {1 + nx + ny + k: k for k in range(nz)}
        faces_z = call(fix, "fix_z", (sc, *got_x, *got_y[::-1], *faces[ny:]), [face_z] * nz, aliases=same)
        background.beside(faces_z)
        done = None
        if work is not None:
            faces_z, held = lax.optimization_barrier((faces_z, held))
            done = work(*held)
        got_z = trade(faces_z, "gz")
        got_z, done = lax.optimization_barrier((got_z, done))
        return (*got_x, *got_y, *got_z), done

    def to_slopes(half):
        return call(slope_kernel, "slopes", (sc, half), [full3], [], matmul, {1: 0})[0]

    def products(*held):
        return call(
            products_kernel, "nodes1_products", (sc, node_in, *held), [full, rows_like(3 * width + NODES)], [], 6 * matmul
        )

    got_x, faces_x = first_trade(first_face_kernel, "face0", (edge_weights, biases, h0), [], matmul // 8)
    sums, slopes0, *faces = call(
        functools.partial(first_kernel, trades, sizes), "edges0", (sc, edge_weights, biases, h0),
        [full, full3] + face_outs, [], 3 * matmul,
    )
    halo, slopes0 = exchange(got_x, faces, to_slopes, (slopes0,))
    inputs = (*weights, sums, h0, *halo)
    got_x, faces_x = first_trade(middle_face_kernel, "face1", inputs, [pair, inv], matmul // 4)
    _, scaled0, act0, slope0, h1, sums, slopes1, *faces = run(
        middle_kernel, "nodes0_edges1", (behind(sums, faces_x), h0, *halo),
        [full, full16, full16, full, full16, full, full3] + face_outs, [inv], 8, in_place,
    )
    halo, slopes1 = exchange(got_x, faces, to_slopes, (slopes1,))
    inputs = (*weights, sums, h1, g2, *halo)
    got_x, faces_x = first_trade(turn_face_kernel, "face2", inputs, [pair, inv], matmul // 4)
    _, scaled1, act1, dpn1, sums, *faces = run(
        turn_kernel, "nodes1_back", (behind(sums, faces_x), h1, g2, *halo), [full] + [full16] * 3 + [full] + face_outs,
        [inv], 7, in_place,
    )
    halo, (base, grads1) = exchange(got_x, faces, products, (h1, g2, scaled1, act1, dpn1))
    inputs = (*weights, sums, base, slopes1, slope0, *halo)
    got_x, faces_x = first_trade(join_face_kernel, "face3", inputs, [pair, inv], matmul // 4)
    edges1, grad_in, dpn0, sums, bias1, *faces = run(
        join_kernel, "edges1_back_nodes0_back", (behind(sums, faces_x), base, slopes1, slope0, *halo),
        [full, full16, full16, full, rows_like(NODES)] + face_outs, [inv], 9, in_place,
    )

    def layer_sums(*held):
        total = padded_rows(7 * width + 3 * NODES, sizes)
        return call(
            functools.partial(sums_kernel, sizes), "gradient_sums", (sc, *held), [rows_like(total // 2)] * 2,
            [pltpu.VMEM((total, width), f32)], 5 * matmul,
        )

    held = (h1, edges1, grad_in, h0, scaled0, act0, dpn0, grads1, bias1)
    halo, _ = exchange(got_x, faces, early=layer_sums, early_held=held)
    tail_rows = width + NODES
    steps = halving_steps(sizes)
    edges, last, second = run(
        last_kernel, "edges0_back", (sums, h0, slopes0, *halo),
        [full, rows_like(tail_rows), sds((len(steps), NODES, width), jnp.int32)], [], 6, in_place,
    )
    keep, got = background.finish("sums")
    value = jnp.concatenate([last, keep + got], 0)
    value, grad_in, dpn0, edges = lax.optimization_barrier((value, grad_in, dpn0, edges))
    (grad0,) = call(
        state_kernel, "state_grad", (sc, edge_weights, node_in, grad_in, dpn0, edges), [full16], [], 4 * matmul
    )
    for hop in reversed(hops(sizes[2])):
        value = value + swap(value, (2, hop))
        value, grad0 = lax.optimization_barrier((value, grad0))
    for k in reversed(range(1, len(steps))):
        got = swap(value, steps[k])
        mine, other = value[tail_rows:], got[tail_rows:]
        joined = jnp.where(
            second[k, :1] == 0, jnp.concatenate([mine, other], 0), jnp.concatenate([other, mine], 0)
        )
        value = jnp.concatenate([value[:tail_rows] + got[:tail_rows], joined], 0)
    layers_all = 3 * slots * sizes[2] // 4
    nodes_all = x_len * sizes[0] * y_len * sizes[1] * layers_all * nodes
    scale = 1.0 / math.sqrt(nodes_all)
    edge_grads, in_grads, out_grads, bias_grads = call(
        functools.partial(finish_kernel, scale, tail_rows, steps[0]), "finish",
        (sc, edge_weights, node_in, value, swap(value, steps[0])),
        [sds(edge_weights.shape), sds(node_in.shape), sds(node_out.shape), sds(biases.shape)],
        [pltpu.VMEM((2 * value.shape[0] - tail_rows, width), f32)],
    )
    return grad0.reshape(state.shape), edge_grads, in_grads, out_grads, bias_grads


def solution(mesh):
    return jax.shard_map(
        on_device,
        mesh=mesh,
        in_specs=(
            P("gx", "gy", "gz", None, None),
            P("gx", "gy", "gz", None, None),
            P("gz"),
            P(),
            P(),
            P(),
            P(),
        ),
        out_specs=(P("gx", "gy", "gz", None, None), P(), P(), P(), P()),
        check_vma=False,
    )
```

```python
import functools
import math

import jax
import jax.numpy as jnp
from jax import lax
from jax.experimental import pallas as pl
from jax.experimental.layout import Layout, with_layout_constraint
from jax.experimental.pallas import tpu as pltpu
from jax.sharding import PartitionSpec as P

f32 = jnp.float32
bf16 = jnp.bfloat16
NODES = 8
VMEM_LIMIT = 12 * 1024 * 1024
VM = pl.BlockSpec(memory_space=pltpu.VMEM)
SM = pl.BlockSpec(memory_space=pltpu.SMEM)


def dot(left, right):
    return lax.dot_general(left, right, (((1,), (0,)), ((), ())), preferred_element_type=f32)


def dot_t(left, right):
    return lax.dot_general(left, right, (((0,), (0,)), ((), ())), preferred_element_type=f32)


def dot_rt(left, right):
    return lax.dot_general(left, right, (((1,), (1,)), ((), ())), preferred_element_type=f32)


def silu_half(half):
    th = jnp.tanh(half)
    prod = half * th
    return half + prod, (0.5 + 0.5 * th) * ((1.0 + half) - prod)


def split_cols(value):
    high = value.astype(bf16)
    low = (value - high.astype(f32)).astype(bf16)
    return jnp.concatenate([high, low], -1)


def up(value):
    return pltpu.roll(value, NODES - 1, 1)


def down(value):
    return pltpu.roll(value, 1, 1)


def flat(value):
    return value.reshape(-1, value.shape[-1])


def node_rows(value):
    return value.reshape(-1, NODES, value.shape[-1])


def row_ids():
    return lax.broadcasted_iota(jnp.int32, (1, NODES, 128), 1)


def couple_slots(plane, filled):
    count, rows, width = plane.shape
    slots = rows // NODES
    parts = plane.reshape(count, slots, NODES, width)
    ids = row_ids()
    done = []
    for s in range(slots):
        here = parts[:, s]
        if s + 1 < slots:
            take = (ids == NODES - 1) & (s + 1 < filled)
            here = here + jnp.where(take, up(parts[:, s + 1]), 0.0)
        if s > 0:
            here = here + jnp.where(ids == 0, down(parts[:, s - 1]), 0.0)
            here = jnp.where(s < filled, here, 0.0)
        done.append(here[:, None])
    return jnp.concatenate(done, 1).reshape(plane.shape)


def elements(x_len, y_len, body, unroll=1):
    ey = y_len // NODES
    total = (x_len // NODES) * ey

    def step(e, carry):
        x0 = pl.multiple_of((e // ey) * NODES, NODES)
        y0 = pl.multiple_of((e % ey) * NODES, NODES)
        body(x0, y0)
        return carry

    lax.fori_loop(0, total, step, 0, unroll=unroll if total % unroll == 0 else 1)


def edge_dots(parts, weight, weight_both):
    rows, width = parts[0].shape[1:]
    if len(parts) == 2:
        return dot(flat(jnp.concatenate(parts, 0)), weight).reshape(-1, rows, width)
    both = dot(jnp.concatenate([flat(parts[0]), flat(parts[2])], -1), weight_both)
    between = dot(flat(parts[1]), weight).reshape(-1, rows, width)
    first, last = (both[:, k : k + width].reshape(-1, rows, width) for k in (0, width))
    return jnp.concatenate([first, between, last], 0)


def edges_forward(h_ref, w_one, half_bias, filled, sum_ref, half_ref):
    x_len, y_len, rows, width = h_ref.shape
    blank = jnp.zeros_like(w_one)
    w_both = jnp.concatenate([jnp.concatenate([w_one, blank], 1), jnp.concatenate([blank, w_one], 1)], 0)
    inner = row_ids() < NODES - 1

    def body(x0, y0):
        ys = pl.ds(y0, NODES)
        prev = None
        here = h_ref[x0, ys].astype(f32)
        for i in range(NODES):
            parts = []
            nxt = None
            if i < NODES - 1:
                nxt = h_ref[x0 + i + 1, ys].astype(f32)
                parts.append((nxt - here).astype(bf16))
            parts.append((here[1:] - here[:-1]).astype(bf16))
            cols = node_rows(here)
            parts.append((up(cols) - cols).reshape(here.shape).astype(bf16))
            half = edge_dots(parts, w_one, w_both) + half_bias
            act = (half + half * jnp.tanh(half)).astype(bf16).astype(f32)
            at = 0
            total = prev
            prev = None
            if i < NODES - 1:
                prev = act[:NODES]
                total = -prev if total is None else total - prev
                half_ref[0, x0 + i, ys] = half[:NODES]
                at = NODES
            along_y = act[at : at + NODES - 1]
            half_ref[1, x0 + i, pl.ds(y0, NODES - 1)] = half[at : at + NODES - 1]
            at += NODES - 1
            along_z = jnp.where(inner, node_rows(act[at:]), 0.0)
            half_ref[2, x0 + i, ys] = half[at:]
            total = total + (down(along_z) - along_z).reshape(here.shape)
            total = jnp.concatenate(
                [
                    total[:1] - along_y[:1],
                    total[1:-1] + (along_y[:-1] - along_y[1:]),
                    total[-1:] + along_y[-1:],
                ],
                0,
            )
            sum_ref[x0 + i, ys] = couple_slots(total, filled)
            here = nxt

    elements(x_len, y_len, body, 2)


def slope_kernel(sc, half_in, slope_out):
    inner = row_ids() < NODES - 1

    def step(x, carry):
        for k in range(3):
            slope = silu_half(half_in[k, x])[1]
            if k == 2:
                slope = jnp.where(inner, node_rows(slope), 0.0).reshape(slope.shape)
            slope_out[k, x] = slope
        return carry

    lax.fori_loop(0, half_in.shape[1], step, 0)


def couple_columns(sum_ref):
    x_len, y_len = sum_ref.shape[:2]
    for cut in range(NODES, x_len, NODES):
        both = sum_ref[cut - 1] + sum_ref[cut]
        sum_ref[cut - 1] = both
        sum_ref[cut] = both
    for cut in range(NODES, y_len, NODES):
        both = sum_ref[:, cut - 1] + sum_ref[:, cut]
        sum_ref[:, cut - 1] = both
        sum_ref[:, cut] = both


def face_place(sc_ref, axis, kind, last):
    return jnp.where((sc_ref[1 + axis] + kind) % 2 == 0, last, 0)


def end_rows(values, filled, take_top):
    picked = values(0)
    slots = values.slots
    for s in range(slots):
        picked = jnp.where(take_top & (filled == s + 1), values(s * NODES + NODES - 1), picked)
    return picked


class RowReader:
    def __init__(self, slots, read):
        self.slots = slots
        self.read = read

    def __call__(self, row):
        return self.read(row)


def takes_top(sc_ref, kind):
    return (sc_ref[3] + kind) % 2 == 0


def write_faces(sc_ref, sum_ref, faces, counts):
    x_len, y_len, rows, width = sum_ref.shape
    nx, ny, nz = counts
    reader = RowReader(rows // NODES, lambda row: sum_ref[:, :, row])
    for kind in range(ny):
        faces[kind][...] = sum_ref[:, face_place(sc_ref, 1, kind, y_len - 1)]
    for kind in range(nz):
        faces[ny + kind][...] = end_rows(reader, sc_ref[0], takes_top(sc_ref, kind))


def add_halo(sc_ref, halo, into_ref, counts):
    x_len, y_len, rows, width = into_ref.shape
    nx, ny, nz = counts
    for kind in range(nx):
        into_ref[face_place(sc_ref, 0, kind, x_len - 1)] += halo[kind][...]
    for kind in range(ny):
        into_ref[:, face_place(sc_ref, 1, kind, y_len - 1)] += halo[nx + kind][...]
    if nz:
        got = [halo[nx + ny + kind][...] for kind in range(nz)]
        tops = [takes_top(sc_ref, kind) for kind in range(nz)]
        from_below = sum(jnp.where(top, 0.0, value) for top, value in zip(tops, got))
        from_above = sum(jnp.where(top, value, 0.0) for top, value in zip(tops, got))
        into_ref[:, :, 0] += from_below
        for s in range(rows // NODES):
            into_ref[:, :, s * NODES + NODES - 1] += jnp.where(sc_ref[0] == s + 1, from_above, 0.0)


def add_line(flag, axis, kind, face, line):
    place = lax.broadcasted_iota(jnp.int32, face.shape, axis)
    last = face.shape[axis] - 1
    here = (flag["low", axis, kind] & (place == 0)) | (flag["high", axis, kind] & (place == last))
    return face + jnp.where(here, jnp.expand_dims(line, axis), 0.0)


def corrected_y(counts, flag, got_x, faces):
    nx, ny, nz = counts
    done = []
    for k, face in enumerate(faces):
        for kind, got in enumerate(got_x):
            line = jnp.where(flag["high", 1, k], got[-1], got[0])
            face = add_line(flag, 0, kind, face, line)
        done.append(face)
    return done


def corrected_z(counts, flag, got_x, got_y, faces):
    done = []
    for k, face in enumerate(faces):

        def layer(got):
            picked = got[:, 0]
            for s in range(got.shape[1] // NODES):
                picked = jnp.where(flag["top", k, s], got[:, s * NODES + NODES - 1], picked)
            return picked

        for kind, got in enumerate(got_x):
            line = layer(got)
            face = add_line(flag, 0, kind, face, line)
        for kind, got in enumerate(got_y):
            line = layer(got)
            face = add_line(flag, 1, kind, face, line)
        done.append(face)
    return done


def write_inverse(sc_ref, inv_ref, sizes):
    y_len, rows, width = inv_ref.shape
    filled, at_y, at_z = sc_ref[0], sc_ref[2], sc_ref[3]
    ids = lax.broadcasted_iota(jnp.int32, (rows, width), 0)
    node = ids % NODES
    low = (node == 0) & ((ids >= NODES) | (at_z > 0))
    high = (node == NODES - 1) & ((ids < (filled - 1) * NODES) | (at_z < sizes[2] - 1))
    along_z = jnp.where(low | high, 0.5, 1.0).astype(f32)
    for y in range(y_len):
        inv_ref[y] = along_z * end_factor(y, y_len, at_y, sizes[1])


def end_factor(place, length, position, size):
    whole = place + position * length
    low = (place % NODES == 0) & (whole > 0)
    high = (place % NODES == NODES - 1) & (whole < length * size - 1)
    return jnp.where(low | high, 0.5, 1.0).astype(f32)


def chunk_of(x_len):
    return 2 * NODES if x_len % (2 * NODES) == 0 else NODES


def scale_planes(sc_ref, inv_ref, x, block, x_len, size_x):
    inv = inv_ref[...]
    parts = [block[c] * (inv * end_factor(x + c, x_len, sc_ref[1], size_x)) for c in range(block.shape[0])]
    return jnp.stack(parts, 0)


def node_forward(scaled, feat, weights, layer):
    edge_w, node_in, node_out, biases = weights
    pair = split_cols(scaled)
    w_two = edge_w[layer, 1]
    joined = jnp.concatenate([feat, dot(pair, jnp.concatenate([w_two, w_two], 0)).astype(bf16)], -1)
    half = jnp.bfloat16(0.5)
    act, slope = silu_half(dot(joined, node_in[layer] * half) + 0.5 * biases[layer, pl.ds(1, 1)])
    return pair[:, :128], act.astype(bf16), slope


def node_slopes(grad, slope, weights, layer):
    return (dot_rt(grad, weights[2][layer]) * slope).astype(bf16)


def node_share(sc_ref, x, inv_ref, size_x, dpn, weights, layer, sum_ref):
    shape = (chunk_of(sum_ref.shape[0]),) + sum_ref.shape[1:]
    dx = dot_rt(dpn, weights[1][layer, pl.ds(128, 128)]).reshape(shape)
    share = scale_planes(sc_ref, inv_ref, x, dx, sum_ref.shape[0], size_x)
    joined = couple_slots(share.reshape((-1,) + shape[2:]), sc_ref[0])
    sum_ref[pl.ds(x, shape[0])] = joined.reshape(shape)


def node_products(grad, feat, scaled, act, dpn, grads):
    grads[pl.ds(0, 128)] += dot_t(act, grad)
    both = dot_t(dpn, jnp.concatenate([feat, scaled], -1))
    grads[pl.ds(128, 128)] += both[:, :128]
    grads[pl.ds(256, 128)] += both[:, 128:]
    grads[pl.ds(384, NODES)] += jnp.sum(dpn.astype(f32).reshape(-1, NODES, 128), 0)


def couple_plane(plane):
    y_len = plane.shape[0]
    parts = [plane[y] for y in range(y_len)]
    for cut in range(NODES, y_len, NODES):
        both = parts[cut - 1] + parts[cut]
        parts[cut - 1] = parts[cut] = both
    return jnp.stack(parts, 0)


def along_y(plane, combine):
    return [
        combine(plane[y : y + NODES - 1], plane[y + 1 : y + NODES], y) for y in range(0, plane.shape[0], NODES)
    ]


def spread_plane(sign, edge_x, edges_y, edge_z):
    total = sign * edge_x + (down(edge_z) - edge_z).reshape(edge_x.shape)
    parts = []
    for k, edge in enumerate(edges_y):
        here = total[k * NODES : (k + 1) * NODES]
        parts += [here[:1] - edge[:1], here[1:-1] + (edge[:-1] - edge[1:]), here[-1:] + edge[-1:]]
    return jnp.concatenate(parts, 0)


def plane_forward(low, high, at_high, w_one, half_bias, filled):
    y_len, rows, width = low.shape
    here = jnp.where(at_high, high, low)
    cols = node_rows(here)
    parts = [(high - low).astype(bf16)]
    parts += along_y(here, lambda lower, upper, y: (upper - lower).astype(bf16))
    parts.append((up(cols) - cols).reshape(here.shape).astype(bf16))
    half = dot(flat(jnp.concatenate(parts, 0)), w_one).reshape(-1, rows, width) + half_bias
    act = silu_half(half)[0].astype(bf16).astype(f32)
    at = y_len
    edges_y = []
    for _ in range(y_len // NODES):
        edges_y.append(act[at : at + NODES - 1])
        at += NODES - 1
    edge_z = jnp.where(row_ids() < NODES - 1, node_rows(act[at:]), 0.0)
    total = spread_plane(jnp.where(at_high, 1.0, -1.0), act[:y_len], edges_y, edge_z)
    return couple_plane(couple_slots(total, filled))


def plane_backward(low, high, at_high, slope_x, slope_y, slope_z):
    here = jnp.where(at_high, high, low)
    cols = node_rows(here)
    edge_x = ((high - low) * slope_x).astype(bf16).astype(f32)
    edges_y = along_y(
        here, lambda lower, upper, y: ((upper - lower) * slope_y[y : y + NODES - 1]).astype(bf16).astype(f32)
    )
    edge_z = ((up(cols) - cols) * node_rows(slope_z)).astype(bf16).astype(f32)
    return spread_plane(jnp.where(at_high, 1.0, -1.0), edge_x, edges_y, edge_z)


def face_planes(sc_ref, kind, x_len):
    place = face_place(sc_ref, 0, kind, x_len - 1)
    at_high = place > 0
    return place, jnp.where(at_high, x_len - 2, 0), at_high


def halo_planes(sc_ref, from_ref, halo, kind, start, into_ref, counts):
    x_len, y_len, rows, width = from_ref.shape
    nx, ny, nz = counts
    for c in range(2):
        into_ref[c] = from_ref[start + c]
    into_ref[face_place(sc_ref, 0, kind, x_len - 1) - start] += halo[kind][...]
    for c in range(2):
        for k in range(ny):
            into_ref[c, face_place(sc_ref, 1, k, y_len - 1)] += halo[nx + k][start + c]
        for k in range(nz):
            got = halo[nx + ny + k][start + c]
            top = takes_top(sc_ref, k)
            into_ref[c, :, 0] += jnp.where(top, 0.0, got)
            for s in range(rows // NODES):
                into_ref[c, :, s * NODES + NODES - 1] += jnp.where(top & (sc_ref[0] == s + 1), got, 0.0)


def edges_backward(q_ref, slope_ref, edge_ref, bias_acc):
    x_len, y_len, rows, width = q_ref.shape

    def body(x0, y0):
        ys = pl.ds(y0, NODES)
        prev = None
        here = q_ref[x0, ys]
        bias = jnp.zeros((NODES, width), f32)
        for i in range(NODES):
            total = prev
            prev = None
            nxt = None
            if i < NODES - 1:
                nxt = q_ref[x0 + i + 1, ys]
                prev = ((nxt - here) * slope_ref[0, x0 + i, ys]).astype(bf16).astype(f32)
                total = -prev if total is None else total - prev
                bias = bias + jnp.sum(node_rows(prev), 0)
            along_y = (here[1:] - here[:-1]) * slope_ref[1, x0 + i, pl.ds(y0, NODES - 1)]
            along_y = along_y.astype(bf16).astype(f32)
            cols = node_rows(here)
            along_z = (up(cols) - cols) * node_rows(slope_ref[2, x0 + i, ys])
            along_z = along_z.astype(bf16).astype(f32)
            bias = bias + jnp.sum(node_rows(along_y), 0) + jnp.sum(along_z, 0)
            total = total + (down(along_z) - along_z).reshape(here.shape)
            total = jnp.concatenate(
                [
                    total[:1] - along_y[:1],
                    total[1:-1] + (along_y[:-1] - along_y[1:]),
                    total[-1:] + along_y[-1:],
                ],
                0,
            )
            edge_ref[x0 + i, ys] = total
            here = nxt
        bias_acc[...] += bias

    elements(x_len, y_len, body)


def planes(count, body):
    chunk = chunk_of(count)

    def step(c, carry):
        body(pl.multiple_of(c * chunk, chunk))
        return carry

    lax.fori_loop(0, count // chunk, step, 0)


def half_weights(weights, layer):
    edge_w, node_in, node_out, biases = weights
    return edge_w[layer, 0] * jnp.bfloat16(0.5), 0.5 * biases[layer, pl.ds(0, 1)]


def first_kernel(counts, sizes, sc, edge_w, biases, h, sums, slopes, *faces):
    w_one, bias = half_weights((edge_w, None, None, biases), 0)
    edges_forward(h, w_one, bias, sc[0], sums, slopes)
    couple_columns(sums)
    write_faces(sc, sums, faces, counts)


def flag_values(sc, counts, sizes, slots):
    found = {}
    for axis, number in enumerate(counts):
        for kind in range(number):
            even = (sc[1 + axis] + kind) % 2 == 0
            found["high", axis, kind] = even
            found["low", axis, kind] = jnp.logical_not(even)
    for kind in range(counts[2]):
        for s in range(slots):
            found["top", kind, s] = takes_top(sc, kind) & (sc[0] == s + 1)
    for step in halving_steps(sizes):
        found["bit", step] = bit_of(sc, step) == 1
    return found


def first_face_kernel(counts, sizes, sc, edge_w, biases, h, *refs):
    faces, flags = refs[:-1], refs[-1]
    for k, value in enumerate(flag_values(sc, counts, sizes, h.shape[2] // NODES).values()):
        flags[k] = jnp.full(flags.shape[1:], value.astype(jnp.int32), jnp.int32)
    w_one, bias = half_weights((edge_w, None, None, biases), 0)
    for kind, face in enumerate(faces):
        place, start, at_high = face_planes(sc, kind, h.shape[0])
        face[...] = plane_forward(
            h[start].astype(f32), h[start + 1].astype(f32), at_high, w_one, bias, sc[0]
        )


def middle_face_kernel(counts, sizes, sc, edge_w, node_in, node_out, biases, sums_in, h, *refs):
    weights = (edge_w, node_in, node_out, biases)
    n = sum(counts)
    halo, faces, (pair, inv) = refs[:n], refs[n:-2], refs[-2:]
    write_inverse(sc, inv, sizes)
    w_one, bias = half_weights(weights, 1)
    x_len = h.shape[0]
    for kind, face in enumerate(faces):
        place, start, at_high = face_planes(sc, kind, x_len)
        halo_planes(sc, sums_in, halo, kind, start, pair, counts)
        sums_at = flat(scale_planes(sc, inv, start, pair[...], x_len, sizes[0]))
        feat = flat(h[pl.ds(start, 2)])
        scaled, act, slope = node_forward(sums_at, feat, weights, 0)
        moved = (feat.astype(f32) + dot(act, node_out[0])).astype(bf16).astype(f32).reshape(pair.shape)
        face[...] = plane_forward(moved[0], moved[1], at_high, w_one, bias, sc[0])


def face_share(sc, sizes, inv, place, x_len, grad, slope, weights, layer, shape):
    dpn = node_slopes(grad, slope, weights, layer)
    dx = dot_rt(dpn, weights[1][layer, pl.ds(128, 128)]).reshape((1,) + shape)
    share = scale_planes(sc, inv, place, dx, x_len, sizes[0])
    return couple_plane(couple_slots(share[0], sc[0]))


def turn_face_kernel(counts, sizes, sc, edge_w, node_in, node_out, biases, sums_in, h, g_ref, *refs):
    weights = (edge_w, node_in, node_out, biases)
    n = sum(counts)
    halo, faces, (pair, inv) = refs[:n], refs[n:-2], refs[-2:]
    write_inverse(sc, inv, sizes)
    x_len, shape = h.shape[0], h.shape[1:]
    live = (lax.broadcasted_iota(jnp.int32, (1, h.shape[2], 128), 1) < sc[0] * NODES).astype(f32)
    for kind, face in enumerate(faces):
        place, start, at_high = face_planes(sc, kind, x_len)
        halo_planes(sc, sums_in, halo, kind, start, pair, counts)
        plane = pair[place - start][None]
        sums_at = flat(scale_planes(sc, inv, place, plane, x_len, sizes[0]))
        scaled, act, slope = node_forward(sums_at, flat(h[place]), weights, 1)
        grad = flat((g_ref[place].astype(f32) * live).astype(bf16))
        face[...] = face_share(sc, sizes, inv, place, x_len, grad, slope, weights, 1, shape)


def join_face_kernel(counts, sizes, sc, edge_w, node_in, node_out, biases, sums_in, base_in, slopes, slope0, *refs):
    weights = (edge_w, node_in, node_out, biases)
    n = sum(counts)
    halo, faces, (pair, inv) = refs[:n], refs[n:-2], refs[-2:]
    write_inverse(sc, inv, sizes)
    x_len, shape = base_in.shape[0], base_in.shape[1:]
    w_two, w_one = twice(edge_w[1, 1]), twice(edge_w[1, 0])
    for kind, face in enumerate(faces):
        place, start, at_high = face_planes(sc, kind, x_len)
        halo_planes(sc, sums_in, halo, kind, start, pair, counts)
        q = dot_rt(split_cols(flat(pair[...])), w_two).reshape(pair.shape)
        edge = plane_backward(q[0], q[1], at_high, slopes[0, start], slopes[1, place], slopes[2, place])
        grad = (flat(base_in[place]) + dot_rt(split_cols(flat(edge)), w_one)).astype(bf16)
        face[...] = face_share(sc, sizes, inv, place, x_len, grad, flat(slope0[place]), weights, 0, shape)


def twice(weight):
    return jnp.concatenate([weight, weight], 1)


def middle_kernel(counts, sizes, sc, edge_w, node_in, node_out, biases, sums_in, h, *refs):
    weights = (edge_w, node_in, node_out, biases)
    n = sum(counts)
    halo, refs = refs[:n], refs[n:]
    work, scaled_ref, act_ref, slope_ref, next_ref, sums, slopes = refs[:7]
    faces, inv = refs[7:-1], refs[-1]
    add_halo(sc, halo, work, counts)
    write_inverse(sc, inv, sizes)
    shape = (chunk_of(h.shape[0]),) + h.shape[1:]

    def body(x):
        at = pl.ds(x, chunk_of(h.shape[0]))
        sums_at = flat(scale_planes(sc, inv, x, work[at], h.shape[0], sizes[0]))
        scaled, act, slope = node_forward(sums_at, flat(h[at]), weights, 0)
        scaled_ref[at] = scaled.reshape(shape)
        act_ref[at] = act.reshape(shape)
        slope_ref[at] = slope.reshape(shape)
        moved = flat(h[at]).astype(f32) + dot(act, node_out[0])
        next_ref[at] = moved.astype(bf16).reshape(shape)

    planes(h.shape[0], body)
    w_one, bias = half_weights(weights, 1)
    edges_forward(next_ref, w_one, bias, sc[0], sums, slopes)
    couple_columns(sums)
    write_faces(sc, sums, faces, counts)


def turn_kernel(counts, sizes, sc, edge_w, node_in, node_out, biases, sums_in, h, g_ref, *refs):
    weights = (edge_w, node_in, node_out, biases)
    n = sum(counts)
    halo, refs = refs[:n], refs[n:]
    work, scaled_ref, act_ref, dpn_ref, sums = refs[:5]
    faces, inv = refs[5:-1], refs[-1]
    add_halo(sc, halo, work, counts)
    write_inverse(sc, inv, sizes)
    shape = (chunk_of(h.shape[0]),) + h.shape[1:]
    live = live_rows(sc, h)

    def body(x):
        at = pl.ds(x, chunk_of(h.shape[0]))
        sums_at = flat(scale_planes(sc, inv, x, work[at], h.shape[0], sizes[0]))
        scaled, act, slope = node_forward(sums_at, flat(h[at]), weights, 1)
        scaled_ref[at] = scaled.reshape(shape)
        act_ref[at] = act.reshape(shape)
        grad = flat((g_ref[at].astype(f32) * live).astype(bf16))
        dpn = node_slopes(grad, slope, weights, 1)
        dpn_ref[at] = dpn.reshape(shape)
        node_share(sc, x, inv, sizes[0], dpn, weights, 1, sums)

    planes(h.shape[0], body)
    couple_columns(sums)
    write_faces(sc, sums, faces, counts)


def live_rows(sc, h):
    return (lax.broadcasted_iota(jnp.int32, (1, 1, h.shape[2], 128), 2) < sc[0] * NODES).astype(f32)


def products_kernel(sc, node_in, h, g_ref, scaled, act, dpn, base, grads):
    grads[...] = jnp.zeros_like(grads)
    live = live_rows(sc, h)

    def body(x):
        at = pl.ds(x, chunk_of(h.shape[0]))
        grad = (g_ref[at].astype(f32) * live).astype(bf16)
        node_products(flat(grad), flat(h[at]), flat(scaled[at]), flat(act[at]), flat(dpn[at]), grads)
        dx = dot_rt(flat(dpn[at]), node_in[1, pl.ds(0, 128)])
        base[at] = grad.astype(f32) + dx.reshape(grad.shape)

    planes(h.shape[0], body)


def edge_parts(counts, sc, weights, layer, halo, slopes, work, bias):
    add_halo(sc, halo, work, counts)
    shape = (chunk_of(work.shape[0]),) + work.shape[1:]
    w_two = twice(weights[0][layer, 1])

    def to_q(x):
        at = pl.ds(x, chunk_of(work.shape[0]))
        work[at] = dot_rt(split_cols(flat(work[at])), w_two).reshape(shape)

    planes(work.shape[0], to_q)
    edges_backward(work, slopes, work, bias)


def edge_product(h, x, pair, grads, row):
    both = dot_t(flat(h[pl.ds(x, chunk_of(h.shape[0]))]), pair)
    grads[pl.ds(row, 128)] += both[:, :128] + both[:, 128:]


def join_kernel(counts, sizes, sc, edge_w, node_in, node_out, biases, sums_in, base_in, slopes, slope0, *refs):
    weights = (edge_w, node_in, node_out, biases)
    n = sum(counts)
    halo, refs = refs[:n], refs[n:]
    work, grad_ref, dpn_ref, sums, bias = refs[:5]
    faces, inv = refs[5:-1], refs[-1]
    write_inverse(sc, inv, sizes)
    bias[...] = jnp.zeros_like(bias)
    edge_parts(counts, sc, weights, 1, halo, slopes, work, bias)
    w_one = twice(edge_w[1, 0])
    x_len = work.shape[0]
    shape = (chunk_of(x_len),) + work.shape[1:]

    def body(x):
        at = pl.ds(x, chunk_of(x_len))
        pair = split_cols(flat(work[at]))
        grad = (flat(base_in[at]) + dot_rt(pair, w_one)).astype(bf16)
        dpn = node_slopes(grad, flat(slope0[at]), weights, 0)
        grad_ref[at] = grad.reshape(shape)
        dpn_ref[at] = dpn.reshape(shape)
        node_share(sc, x, inv, sizes[0], dpn, weights, 0, sums)

    planes(x_len, body)
    couple_columns(sums)
    write_faces(sc, sums, faces, counts)


def sums_kernel(sizes, sc, h, edges, grad, h0, scaled0, act0, dpn0, grads1, bias, keep, send, grads):
    grads[...] = jnp.zeros_like(grads)
    row = 384 + NODES
    grads[pl.ds(row + 128, NODES)] = bias[...]
    grads[pl.ds(row + 128 + NODES, grads1.shape[0])] = grads1[...]

    def body(x):
        at = pl.ds(x, chunk_of(h.shape[0]))
        edge_product(h, x, split_cols(flat(edges[at])), grads, row)
        node_products(flat(grad[at]), flat(h0[at]), flat(scaled0[at]), flat(act0[at]), flat(dpn0[at]), grads)

    planes(h.shape[0], body)
    write_halves(sc, halving_steps(sizes)[0], grads, keep, send)


def last_kernel(counts, sizes, sc, edge_w, node_in, node_out, biases, sums_in, h, slopes, *refs):
    n = sum(counts)
    halo, (edges, grads) = refs[:n], refs[n:]
    grads[...] = jnp.zeros_like(grads)
    edge_parts(counts, sc, (edge_w,), 0, halo, slopes, edges, grads.at[pl.ds(128, NODES)])

    def body(x):
        edge_product(h, x, split_cols(flat(edges[pl.ds(x, chunk_of(h.shape[0]))])), grads, 0)

    planes(h.shape[0], body)


def state_kernel(sc, edge_w, node_in, grad_in, dpn, edges, grad_ref):
    shape = (chunk_of(edges.shape[0]),) + edges.shape[1:]
    weight = jnp.concatenate([twice(edge_w[0, 0]), node_in[0, pl.ds(0, 128)]], 1)

    def body(x):
        at = pl.ds(x, chunk_of(edges.shape[0]))
        parts = jnp.concatenate([split_cols(flat(edges[at])), flat(dpn[at])], -1)
        grad_ref[at] = (flat(grad_in[at]).astype(f32) + dot_rt(parts, weight)).astype(bf16).reshape(shape)

    planes(edges.shape[0], body)


def finish_kernel(scale, last_rows, step, sc, edge_w, node_in, value, got, *refs):
    edge_grads, in_grads, out_grads, bias_grads, both = refs
    width = edge_w.shape[-1]
    join_kernel_of(step, last_rows, sc, value, got, both)

    def rows_of(part, start, count=width):
        ref, offset = part
        return ref[pl.ds(offset + start, count)] * scale

    def bias_of(part, start):
        return jnp.sum(rows_of(part, start, NODES), 0, keepdims=True)

    end = 3 * width
    last, sum0 = (both, 0), (both, last_rows)
    sum1 = (both, last_rows + 512 + 2 * NODES)
    firsts = ((last, 0), (sum0, end + NODES))
    for layer, part in enumerate((sum0, sum1)):
        out_grads[layer] = rows_of(part, 0)
        in_grads[layer, pl.ds(0, width)] = rows_of(part, width).T
        bias_grads[layer, pl.ds(1, 1)] = bias_of(part, end)
        source, start = firsts[layer]
        edge_grads[layer, 0] = rows_of(source, start)
        bias_grads[layer, pl.ds(0, 1)] = bias_of(source, start + width)
        mixed = rows_of(part, 2 * width).T
        high = mixed.astype(bf16)
        low = (mixed - high.astype(f32)).astype(bf16)
        lower = node_in[layer, pl.ds(width, width)]
        edge_grads[layer, 1] = dot_rt(high, lower) + dot_rt(low, lower)
        w_two = edge_w[layer, 1]
        in_grads[layer, pl.ds(width, width)] = dot_t(w_two, high) + dot_t(w_two, low)


def call(kernel, name, inputs, outs, scratch=(), flops=0, aliases=None):
    total = sum(math.prod(o.shape) * o.dtype.itemsize for o in outs)
    total += sum(math.prod(i.shape) * i.dtype.itemsize for i in inputs)
    return pl.pallas_call(
        kernel,
        name=name,
        out_shape=tuple(outs),
        in_specs=[SM] + [VM] * (len(inputs) - 1),
        out_specs=tuple([VM] * len(outs)),
        scratch_shapes=list(scratch),
        input_output_aliases=aliases or {},
        compiler_params=pltpu.CompilerParams(vmem_limit_bytes=VMEM_LIMIT),
        cost_estimate=pl.CostEstimate(flops=flops, bytes_accessed=total, transcendentals=0),
    )(*inputs)


def pairs(size, kind):
    return [
        pair for low in range(kind, size - 1, 2) for pair in ((low, low + 1), (low + 1, low))
    ]


def hops(size):
    found = []
    hop = 1
    while hop < size:
        found.append(hop)
        hop *= 2
    return found


def halving_steps(sizes):
    steps = [(1, hop) for hop in hops(sizes[1])[:1]]
    steps += [(0, hop) for hop in hops(sizes[0])]
    return steps + [(1, hop) for hop in hops(sizes[1])[1:]]


def padded_rows(rows, sizes):
    unit = NODES << len(halving_steps(sizes))
    return -(-rows // unit) * unit


def bit_of(sc_ref, step):
    axis, hop = step
    return (sc_ref[1 + axis] // hop) % 2


def write_halves(sc_ref, step, from_ref, keep, send):
    half = keep.shape[0]
    bit = bit_of(sc_ref, step)
    keep[...] = from_ref[pl.ds(pl.multiple_of(bit * half, NODES), half)]
    send[...] = from_ref[pl.ds(pl.multiple_of((1 - bit) * half, NODES), half)]


def join_kernel_of(step, start, sc, value, got, out):
    half = value.shape[0] - start
    bit = bit_of(sc, step)
    if start:
        out[pl.ds(0, start)] = value[pl.ds(0, start)] + got[pl.ds(0, start)]
    out[pl.ds(pl.multiple_of(start + bit * half, NODES), half)] = value[pl.ds(start, half)]
    out[pl.ds(pl.multiple_of(start + (1 - bit) * half, NODES), half)] = got[pl.ds(start, half)]


def swap(value, step):
    axis = ("gx", "gy", "gz")[step[0]]
    return lax.ppermute(value, axis, [(i, i ^ step[1]) for i in range(lax.axis_size(axis))])


def rows_like(rows, width=128):
    return jax.ShapeDtypeStruct((rows, width), f32)


def halve(flag, sizes, keep, send):
    steps = halving_steps(sizes)
    got = swap(send, steps[0])
    for step in steps[1:]:
        keep, got = yield keep, got
        total = keep + got
        half = total.shape[0] // 2
        first, second = total[:half], total[half:]
        keep = jnp.where(flag["bit", step], second, first)
        send = jnp.where(flag["bit", step], first, second)
        got = swap(send, step)
    keep, got = yield keep, got
    return keep, got


class Background:
    def __init__(self):
        self.active = {}

    def add(self, name, steps):
        self.active[name] = [steps, None]

    def advance(self, entry, tied):
        steps, pending = entry
        try:
            entry[1] = next(steps) if pending is None else steps.send(tied)
        except StopIteration:
            entry[0] = None

    def beside(self, anchor):
        for entry in self.active.values():
            steps, pending = entry
            if steps is None:
                continue
            if pending is None:
                self.advance(entry, None)
            elif pending[1] is not None:
                anchor, tied = lax.optimization_barrier((anchor, pending))
                self.advance(entry, tied)
        return anchor

    def finish(self, name):
        entry = self.active[name]
        while entry[0] is not None:
            done = entry[1]
            if done is not None and done[1] is None:
                return done[0]
            self.advance(entry, done)
        return entry[1]


def on_device(state, cotangent, counts, edge_weights, node_in, node_out, biases):
    x_len, y_len, slots, nodes, width = state.shape
    rows = slots * nodes
    grid = (x_len, y_len, rows, width)
    axes = ("gx", "gy", "gz")
    sizes = tuple(lax.axis_size(a) for a in axes)
    trades = tuple(min(size - 1, 2) for size in sizes)
    nx, ny, nz = trades
    h0 = state.reshape(grid)
    g2 = cotangent.reshape(grid)
    sc = jnp.stack([counts[0]] + [lax.axis_index(a).astype(jnp.int32) for a in axes])

    def sds(shape, kind=f32):
        return jax.ShapeDtypeStruct(shape, kind)

    face_x = sds((y_len, rows, width))
    face_y = sds((x_len, rows, width))
    face_z = sds((x_len, y_len, width))
    face_outs = [face_y] * ny + [face_z] * nz
    full = sds(grid)
    full16 = sds(grid, bf16)
    full3 = sds((3,) + grid)
    inv = pltpu.VMEM((y_len, rows, width), f32)
    matmul = 2 * math.prod(grid) * width
    weights = (edge_weights, node_in, node_out, biases)

    in_place = {1 + len(weights): 0}

    def run(kernel, name, inputs, outs, scratch, flops, aliases):
        body = functools.partial(kernel, trades, sizes)
        return call(body, name, (sc, *weights, *inputs), outs, scratch, flops * matmul, aliases)

    def behind(value, others):
        return lax.optimization_barrier((value, others))[0]

    def trade(faces, axis):
        size = lax.axis_size(axis)
        got = [lax.ppermute(face, axis, pairs(size, kind)) for kind, face in reversed(list(enumerate(faces)))]
        return [with_layout_constraint(value, Layout(major_to_minor=(0, 1, 2))) for value in got[::-1]]

    background = Background()

    pair = pltpu.VMEM((2,) + grid[1:], f32)

    def first_trade(kernel, name, inputs, scratch, flops):
        faces = call(functools.partial(kernel, trades, sizes), name, (sc, *inputs), [face_x] * nx, scratch, flops)
        return trade(faces, "gx"), faces

    def exchange(got_x, faces, work=None, held=(), early=None, early_held=()):
        faces_y = corrected_y(trades, flag, got_x, faces[:ny])
        if early is not None:
            faces_y, early_held = lax.optimization_barrier((faces_y, early_held))
            keep, send = early(*early_held)
        got_y = trade(faces_y, "gy")
        if early is not None:
            got_y, (keep, send) = lax.optimization_barrier((got_y, (keep, send)))
            background.add("sums", halve(flag, sizes, keep, send))
            background.beside(got_y)
        faces_z = corrected_z(trades, flag, got_x, got_y, faces[ny:])
        background.beside(faces_z)
        done = None
        if work is not None:
            faces_z, held = lax.optimization_barrier((faces_z, held))
            done = work(*held)
        got_z = trade(faces_z, "gz")
        got_z, done = lax.optimization_barrier((got_z, done))
        return (*got_x, *got_y, *got_z), done

    def to_slopes(half):
        return call(slope_kernel, "slopes", (sc, half), [full3], [], matmul, {1: 0})[0]

    def products(*held):
        return call(
            products_kernel, "nodes1_products", (sc, node_in, *held), [full, rows_like(3 * width + NODES)], [], 6 * matmul
        )

    names = list(flag_values([jnp.int32(0)] * 4, trades, sizes, slots))
    *faces_x, flag_rows = call(
        functools.partial(first_face_kernel, trades, sizes), "face0", (sc, edge_weights, biases, h0),
        [face_x] * nx + [sds((len(names), NODES, width), jnp.int32)], [], matmul // 8,
    )
    flag = {name: flag_rows[k, 0] == 1 for k, name in enumerate(names)}
    got_x = trade(faces_x, "gx")
    sums, slopes0, *faces = call(
        functools.partial(first_kernel, trades, sizes), "edges0", (sc, edge_weights, biases, h0),
        [full, full3] + face_outs, [], 3 * matmul,
    )
    halo, slopes0 = exchange(got_x, faces, to_slopes, (slopes0,))
    inputs = (*weights, sums, h0, *halo)
    got_x, faces_x = first_trade(middle_face_kernel, "face1", inputs, [pair, inv], matmul // 4)
    _, scaled0, act0, slope0, h1, sums, slopes1, *faces = run(
        middle_kernel, "nodes0_edges1", (behind(sums, faces_x), h0, *halo),
        [full, full16, full16, full, full16, full, full3] + face_outs, [inv], 8, in_place,
    )
    halo, slopes1 = exchange(got_x, faces, to_slopes, (slopes1,))
    inputs = (*weights, sums, h1, g2, *halo)
    got_x, faces_x = first_trade(turn_face_kernel, "face2", inputs, [pair, inv], matmul // 4)
    _, scaled1, act1, dpn1, sums, *faces = run(
        turn_kernel, "nodes1_back", (behind(sums, faces_x), h1, g2, *halo), [full] + [full16] * 3 + [full] + face_outs,
        [inv], 7, in_place,
    )
    halo, (base, grads1) = exchange(got_x, faces, products, (h1, g2, scaled1, act1, dpn1))
    inputs = (*weights, sums, base, slopes1, slope0, *halo)
    got_x, faces_x = first_trade(join_face_kernel, "face3", inputs, [pair, inv], matmul // 4)
    edges1, grad_in, dpn0, sums, bias1, *faces = run(
        join_kernel, "edges1_back_nodes0_back", (behind(sums, faces_x), base, slopes1, slope0, *halo),
        [full, full16, full16, full, rows_like(NODES)] + face_outs, [inv], 9, in_place,
    )

    def layer_sums(*held):
        total = padded_rows(7 * width + 3 * NODES, sizes)
        return call(
            functools.partial(sums_kernel, sizes), "gradient_sums", (sc, *held), [rows_like(total // 2)] * 2,
            [pltpu.VMEM((total, width), f32)], 5 * matmul,
        )

    held = (h1, edges1, grad_in, h0, scaled0, act0, dpn0, grads1, bias1)
    halo, _ = exchange(got_x, faces, early=layer_sums, early_held=held)
    tail_rows = width + NODES
    steps = halving_steps(sizes)
    edges, last = run(
        last_kernel, "edges0_back", (sums, h0, slopes0, *halo), [full, rows_like(tail_rows)], [], 6, in_place
    )
    keep, got = background.finish("sums")
    value = jnp.concatenate([last, keep + got], 0)
    value, grad_in, dpn0, edges = lax.optimization_barrier((value, grad_in, dpn0, edges))
    (grad0,) = call(
        state_kernel, "state_grad", (sc, edge_weights, node_in, grad_in, dpn0, edges), [full16], [], 4 * matmul
    )
    for hop in reversed(hops(sizes[2])):
        value = value + swap(value, (2, hop))
        value, grad0 = lax.optimization_barrier((value, grad0))
    for k in reversed(range(1, len(steps))):
        got = swap(value, steps[k])
        mine, other = value[tail_rows:], got[tail_rows:]
        joined = jnp.where(
            flag["bit", steps[k]], jnp.concatenate([other, mine], 0), jnp.concatenate([mine, other], 0)
        )
        value = jnp.concatenate([value[:tail_rows] + got[:tail_rows], joined], 0)
    layers_all = 3 * slots * sizes[2] // 4
    nodes_all = x_len * sizes[0] * y_len * sizes[1] * layers_all * nodes
    scale = 1.0 / math.sqrt(nodes_all)
    edge_grads, in_grads, out_grads, bias_grads = call(
        functools.partial(finish_kernel, scale, tail_rows, steps[0]), "finish",
        (sc, edge_weights, node_in, value, swap(value, steps[0])),
        [sds(edge_weights.shape), sds(node_in.shape), sds(node_out.shape), sds(biases.shape)],
        [pltpu.VMEM((2 * value.shape[0] - tail_rows, width), f32)],
    )
    return grad0.reshape(state.shape), edge_grads, in_grads, out_grads, bias_grads


def solution(mesh):
    return jax.shard_map(
        on_device,
        mesh=mesh,
        in_specs=(
            P("gx", "gy", "gz", None, None),
            P("gx", "gy", "gz", None, None),
            P("gz"),
            P(),
            P(),
            P(),
            P(),
        ),
        out_specs=(P("gx", "gy", "gz", None, None), P(), P(), P(), P()),
        check_vma=False,
    )
```
